32 devices in a mesh: groups: 2 (over y), dp: 16 (over z, x, core).
Axes of the slice: x: 2, y: 2, z: 4, core: 2. Of those that a mesh axis runs over, the one named last changes fastest.
Arguments:
- activations: bfloat16 [128, 64, 8192], P(('groups', 'dp')), parts along dimension 0, may hold values from -6 to 6
- out_grads: bfloat16 [128, 64, 8192], P(('groups', 'dp')), parts along dimension 0, may hold values from -6 to 6
- project_in: bfloat16 [8192, 32], replicated, may hold values from -0.0625 to 0.0625
- project_out: bfloat16 [8192, 32], replicated, may hold values from -0.0625 to 0.0625
- lengths: int32 [128], P(('groups', 'dp')), parts along dimension 0, may hold values from 16 to 64, as said below
- query_index: int32 [32], P('groups'), parts along dimension 0, may hold values from 0 to 63, as said below
Outputs:
- scores: float32 [128, 16], P(('groups', 'dp')), parts along dimension 0
The draws below stay inside these ranges and needn't reach their ends.
There are 2 independent parts, one for each index of `groups`. The reference program is written for one: setup_inputs(seed, part) draws one part's arguments, and reference() takes and returns one part's arrays. A program takes and returns all parts, laid end to end along the dimension named above; an argument that names none is the same for every part. Nothing has to cross between parts.
Inputs may be any that keep to these rules, and one draw needn't show every extreme that they name: `lengths`: some examples have exactly 64 live positions and some exactly 16. `query_index`: distinct example numbers; 0 and 63 are always among them.
All inputs are finite; a program needn't handle non-finite values.
Results may differ from the reference program's by a relative error of at most 0.0003.
Values sent between devices are 32-bit elements; how exact they have to be, the bound alone decides.
No kernel may reach another device: no remote copies, remote signals or barrier semaphores. Data moves between devices by JAX's collectives and lax.ppermute only.
A program may use at most 128 MiB of HBM per device.

```python
import jax
import jax.numpy as jnp
from jax import lax

D = 8192
RANK = 32
SEQ = 64
FISH = 1024
EXAMPLES = 64
NQ = 16


def draw_lengths(key, part):
    key = jax.random.fold_in(key, 11)
    drawn = jax.random.randint(key, (EXAMPLES,), SEQ // 4, SEQ + 1, dtype=jnp.int32)
    positions = jnp.arange(EXAMPLES, dtype=jnp.int32)
    drawn = jnp.where(positions % 3 == 0, SEQ, drawn)
    return jnp.where(positions % 3 == 1, SEQ // 4, drawn).astype(jnp.int32)


def draw_query_index(key, part):
    key = jax.random.fold_in(key, 23)
    first_key = jax.random.fold_in(key, 1)
    second_key = jax.random.fold_in(key, 2)
    middle = jax.random.permutation(first_key, EXAMPLES - 2).astype(jnp.int32) + 1
    picked = jnp.concatenate([jnp.array([0, EXAMPLES - 1], dtype=jnp.int32), middle[:NQ - 2]])
    order = jax.random.permutation(second_key, NQ)
    return picked[order].astype(jnp.int32)


def block_levels(rng, shape, shards, low, largest):
    def one(dim, shards_of):
        draws = jax.random.uniform(jax.random.fold_in(jax.random.fold_in(rng, 6), dim), (shards_of,), jnp.float32, low / len(shards), largest / len(shards))
        return jnp.repeat(jnp.exp(draws), shape[dim] // shards_of).reshape((-1,) + (1,) * (len(shape) - dim - 1))

    gain = one(*shards[0])
    for cut in shards[1:]:
        gain = gain * one(*cut)
    return gain


def normal_values(own_key, dims, scale, limit, split=(), kind=jnp.bfloat16):
    entries = scale * jax.random.normal(own_key, dims, jnp.float32)
    if split:
        entries = entries * block_levels(own_key, dims, split, -0.22, 0.18)
    return jnp.clip(entries, -limit, limit).astype(kind)


def setup_inputs(seed: int = 0, part: int = 0) -> dict:
    seeds = jax.random.split(jax.random.key(seed), 7)
    part_splits = jax.random.split(jax.random.fold_in(seeds[6], part), 7)
    return {
        "activations": normal_values(part_splits[0], (EXAMPLES, SEQ, D), 1.0, 6.0, ((0, 16),)),
        "out_grads": normal_values(part_splits[1], (EXAMPLES, SEQ, D), 1.0, 6.0, ((0, 16),)),
        "project_in": normal_values(seeds[2], (D, RANK), D ** -0.5, 0.0625),
        "project_out": normal_values(seeds[3], (D, RANK), D ** -0.5, 0.0625),
        "lengths": draw_lengths(jax.random.fold_in(jax.random.fold_in(seeds[6], part), 71), part),
        "query_index": draw_query_index(jax.random.fold_in(jax.random.fold_in(seeds[6], part), 71), part),
    }


damp_ratio = 0.5

def sketch_rows(activations, out_grads, project_in, project_out, lengths):
    count, seq_len, width = activations.shape
    rank_dim = project_in.shape[1]
    feat = jnp.dot(activations.reshape(count * seq_len, width).astype(jnp.float32), project_in.astype(jnp.float32), preferred_element_type=jnp.float32).reshape(count, seq_len, rank_dim)
    grad = jnp.dot(out_grads.reshape(count * seq_len, width).astype(jnp.float32), project_out.astype(jnp.float32), preferred_element_type=jnp.float32).reshape(count, seq_len, rank_dim)
    padding = (jnp.arange(seq_len, dtype=jnp.int32)[None, :] < lengths[:, None]).astype(jnp.float32)
    grad = grad * padding[:, :, None]
    outer = jnp.einsum('esi,esj->eij', grad, feat, precision=lax.Precision.HIGHEST)
    return outer.reshape(count, rank_dim * rank_dim)

def reference(activations, out_grads, project_in, project_out, lengths, query_index):
    sketches = sketch_rows(activations, out_grads, project_in, project_out, lengths)
    fisher = jnp.dot(sketches.T, sketches, precision=lax.Precision.HIGHEST)
    damping = damp_ratio * jnp.sum(sketches * sketches) / FISH
    queries = sketches[query_index.astype(jnp.int32)]
    system = fisher + damping * jnp.eye(FISH, dtype=jnp.float32)
    solved = jnp.linalg.solve(system, queries.T)
    return jnp.dot(sketches, solved, precision=lax.Precision.HIGHEST)
```

```python
import functools

import jax
import jax.numpy as jnp
from jax import lax
from jax.experimental import pallas as pl
from jax.experimental.pallas import tpu as pltpu
from jax.sharding import PartitionSpec as P

damp_ratio = 0.5
LANES = 128
SUBLANES = 8
NT = (((1,), (1,)), ((), ()))


def sketch_kernel(chunks, seq_len, act_hbm, out_hbm, pin_hbm, pout_hbm, lengths_ref, sketch_ref, act, out, pin, pout, sems):
    rows, width = act.shape
    rank_dim = pin.shape[0]
    step = width // chunks
    copies = []
    for c in range(chunks):
        cols = pl.ds(c * step, step)
        copies.append(
            [
                pltpu.make_async_copy(src.at[:, cols], dst.at[:, cols], sems.at[n, c])
                for n, (src, dst) in enumerate(
                    ((pin_hbm, pin), (act_hbm, act), (pout_hbm, pout), (out_hbm, out))
                )
            ]
        )
        for copy in copies[-1]:
            copy.start()
    feat = jnp.zeros((rank_dim, rows), jnp.float32)
    grad = jnp.zeros((rank_dim, rows), jnp.float32)
    for c in range(chunks):
        cols = slice(c * step, (c + 1) * step)
        for copy in copies[c]:
            copy.wait()
        feat = feat + lax.dot_general(pin[:, cols], act[:, cols], NT, preferred_element_type=jnp.float32)
        grad = grad + lax.dot_general(pout[:, cols], out[:, cols], NT, preferred_element_type=jnp.float32)
    count = rows // seq_len
    reps = LANES // rank_dim
    position = lax.broadcasted_iota(jnp.int32, (rank_dim, rows), 1)
    masked = []
    for e in range(count):
        first = e * seq_len
        live = (position >= first) & (position < first + lengths_ref[e])
        masked.append(jnp.where(live, grad, 0.0))
    outer = lax.dot_general(
        jnp.concatenate(masked, axis=0),
        jnp.concatenate([feat] * reps, axis=0),
        NT,
        precision=lax.Precision.HIGHEST,
        preferred_element_type=jnp.float32,
    )
    band = lax.broadcasted_iota(jnp.int32, (SUBLANES, LANES), 1) // rank_dim
    for e in range(count):
        entry = outer[e * rank_dim : e * rank_dim + SUBLANES]
        for b in range(1, reps):
            first = e * rank_dim + b * SUBLANES
            entry = jnp.where(band == b, outer[first : first + SUBLANES], entry)
        sketch_ref[e * SUBLANES : (e + 1) * SUBLANES] = entry


def sketch_rows(activations, out_grads, project_in, project_out, lengths):
    count, seq_len, width = activations.shape
    rank_dim = project_in.shape[1]
    rows = count * seq_len
    chunks = 8
    return pl.pallas_call(
        functools.partial(sketch_kernel, chunks, seq_len),
        out_shape=jax.ShapeDtypeStruct((count * SUBLANES, LANES), jnp.float32),
        in_specs=[pl.BlockSpec(memory_space=pl.ANY)] * 4 + [pl.BlockSpec(memory_space=pltpu.SMEM)],
        out_specs=pl.BlockSpec(memory_space=pltpu.VMEM),
        scratch_shapes=[
            pltpu.VMEM((rows, width), jnp.bfloat16),
            pltpu.VMEM((rows, width), jnp.bfloat16),
            pltpu.VMEM((rank_dim, width), jnp.bfloat16),
            pltpu.VMEM((rank_dim, width), jnp.bfloat16),
            pltpu.SemaphoreType.DMA((4, chunks)),
        ],
        compiler_params=pltpu.CompilerParams(vmem_limit_bytes=24 * 2**20),
    )(
        activations.reshape(rows, width),
        out_grads.reshape(rows, width),
        project_in.T,
        project_out.T,
        lengths,
    )


def solve_kernel(nq, per_dev, axis, tiles_ref, query_ref, scores_ref, extended, solved):
    examples = tiles_ref.shape[0] // SUBLANES
    wide = examples + nq
    fisher_dim = SUBLANES * LANES
    extended[: examples * SUBLANES] = tiles_ref[...]
    for q in range(nq):
        first = pl.multiple_of(query_ref[q] * SUBLANES, SUBLANES)
        extended[(examples + q) * SUBLANES : (examples + q + 1) * SUBLANES] = tiles_ref[pl.ds(first, SUBLANES)]
    extended[wide * SUBLANES :] = jnp.zeros((LANES * SUBLANES - wide * SUBLANES, LANES), jnp.float32)
    right = jnp.concatenate([extended[pl.ds(s, LANES, stride=SUBLANES)] for s in range(SUBLANES)], axis=1)
    system = lax.dot_general(
        right[:examples], right, NT, precision=lax.Precision.HIGHEST, preferred_element_type=jnp.float32
    )
    row = lax.broadcasted_iota(jnp.int32, system.shape, 0)
    col = lax.broadcasted_iota(jnp.int32, system.shape, 1)
    diagonal = row == col
    trace = jnp.sum(jnp.where(diagonal, system, 0.0))
    damping = damp_ratio * trace / fisher_dim
    system = jnp.where(diagonal, system + damping, system)
    for k in range(examples):
        pivot_row = system[k : k + 1]
        scaled = pivot_row / system[k : k + 1, k : k + 1]
        system = jnp.where(row == k, scaled, system - system[:, k : k + 1] * scaled)
    solved[...] = system
    first = lax.axis_index(axis) * per_dev
    mine = solved[pl.ds(first, per_dev)]
    scores_ref[...] = mine[:, examples : examples + nq]


def gram_scores(tiles, query_index, per_dev, axis):
    examples = tiles.shape[0] // SUBLANES
    nq = query_index.shape[0]
    return pl.pallas_call(
        functools.partial(solve_kernel, nq, per_dev, axis),
        out_shape=jax.ShapeDtypeStruct((per_dev, nq), jnp.float32),
        in_specs=[pl.BlockSpec(memory_space=pltpu.VMEM), pl.BlockSpec(memory_space=pltpu.SMEM)],
        out_specs=pl.BlockSpec(memory_space=pltpu.VMEM),
        scratch_shapes=[
            pltpu.VMEM((LANES * SUBLANES, LANES), jnp.float32),
            pltpu.VMEM((examples, LANES), jnp.float32),
        ],
    )(tiles, query_index)


def large_scores(tiles, query_index, per_dev, axis):
    sketches = tiles.reshape(-1, SUBLANES * LANES)
    gram = jnp.dot(sketches, sketches.T, precision=lax.Precision.HIGHEST)
    examples, fisher_dim = sketches.shape
    damping = damp_ratio * jnp.trace(gram) / fisher_dim
    factor = jnp.linalg.cholesky(gram + damping * jnp.eye(examples, dtype=jnp.float32))
    mine = lax.dynamic_slice_in_dim(gram, lax.axis_index(axis) * per_dev, per_dev, 0)
    half = lax.linalg.triangular_solve(factor, mine.T, left_side=True, lower=True)
    solved = lax.linalg.triangular_solve(factor, half, left_side=True, lower=True, transpose_a=True)
    selector = (query_index[:, None] == jnp.arange(examples, dtype=jnp.int32)[None, :]).astype(jnp.float32)
    return jnp.dot(selector, solved, precision=lax.Precision.HIGHEST).T


def local(activations, out_grads, project_in, project_out, lengths, query_index):
    per_dev = activations.shape[0]
    tiles = sketch_rows(activations, out_grads, project_in, project_out, lengths)
    every = lax.all_gather(tiles, "dp", axis=0, tiled=True)
    examples = every.shape[0] // SUBLANES
    if examples + query_index.shape[0] <= LANES:
        return gram_scores(every, query_index, per_dev, "dp")
    return large_scores(every, query_index, per_dev, "dp")


def solution(mesh):
    return jax.shard_map(
        local,
        mesh=mesh,
        in_specs=(
            P(("groups", "dp"), None, None),
            P(("groups", "dp"), None, None),
            P(),
            P(),
            P(("groups", "dp")),
            P("groups"),
        ),
        out_specs=P(("groups", "dp"), None),
        check_vma=False,
    )
```

```python
import functools

import jax
import jax.numpy as jnp
from jax import lax
from jax.experimental import pallas as pl
from jax.experimental.pallas import tpu as pltpu
from jax.sharding import PartitionSpec as P

damp_ratio = 0.5
LANES = 128
SUBLANES = 8
NT = (((1,), (1,)), ((), ()))


def sketch_kernel(chunks, seq_len, act_hbm, out_hbm, pin_hbm, pout_hbm, lengths_ref, sketch_ref, act, out, pin, pout, sems):
    rows, width = act.shape
    rank_dim = pin.shape[0]
    step = width // chunks
    copies = []
    for c in range(chunks):
        cols = pl.ds(c * step, step)
        copies.append(
            [
                pltpu.make_async_copy(src.at[:, cols], dst.at[:, cols], sems.at[n, c])
                for n, (src, dst) in enumerate(
                    ((pin_hbm, pin), (act_hbm, act), (pout_hbm, pout), (out_hbm, out))
                )
            ]
        )
        for copy in copies[-1]:
            copy.start()
    feat = jnp.zeros((rank_dim, rows), jnp.float32)
    grad = jnp.zeros((rank_dim, rows), jnp.float32)
    for c in range(chunks):
        cols = slice(c * step, (c + 1) * step)
        for copy in copies[c]:
            copy.wait()
        feat = feat + lax.dot_general(pin[:, cols], act[:, cols], NT, preferred_element_type=jnp.float32)
        grad = grad + lax.dot_general(pout[:, cols], out[:, cols], NT, preferred_element_type=jnp.float32)
    count = rows // seq_len
    reps = LANES // rank_dim
    position = lax.broadcasted_iota(jnp.int32, (rank_dim, rows), 1)
    masked = []
    for e in range(count):
        first = e * seq_len
        live = (position >= first) & (position < first + lengths_ref[e])
        masked.append(jnp.where(live, grad, 0.0))
    outer = lax.dot_general(
        jnp.concatenate(masked, axis=0),
        jnp.concatenate([feat] * reps, axis=0),
        NT,
        precision=lax.Precision.HIGHEST,
        preferred_element_type=jnp.float32,
    )
    band = lax.broadcasted_iota(jnp.int32, (SUBLANES, LANES), 1) // rank_dim
    for e in range(count):
        entry = outer[e * rank_dim : e * rank_dim + SUBLANES]
        for b in range(1, reps):
            first = e * rank_dim + b * SUBLANES
            entry = jnp.where(band == b, outer[first : first + SUBLANES], entry)
        sketch_ref[e * SUBLANES : (e + 1) * SUBLANES] = entry


def sketch_rows(activations, out_grads, project_in, project_out, lengths):
    count, seq_len, width = activations.shape
    rank_dim = project_in.shape[1]
    rows = count * seq_len
    chunks = 8
    return pl.pallas_call(
        functools.partial(sketch_kernel, chunks, seq_len),
        out_shape=jax.ShapeDtypeStruct((count * SUBLANES, LANES), jnp.float32),
        in_specs=[pl.BlockSpec(memory_space=pltpu.HBM)] * 4 + [pl.BlockSpec(memory_space=pltpu.SMEM)],
        out_specs=pl.BlockSpec(memory_space=pltpu.VMEM),
        scratch_shapes=[
            pltpu.VMEM((rows, width), jnp.bfloat16),
            pltpu.VMEM((rows, width), jnp.bfloat16),
            pltpu.VMEM((rank_dim, width), jnp.bfloat16),
            pltpu.VMEM((rank_dim, width), jnp.bfloat16),
            pltpu.SemaphoreType.DMA((4, chunks)),
        ],
    )(
        activations.reshape(rows, width),
        out_grads.reshape(rows, width),
        project_in.T,
        project_out.T,
        lengths,
    )


def solve_kernel(nq, per_dev, axis, *refs):
    tiles, (query_ref, scores_ref, extended) = refs[:-3], refs[-3:]
    block = per_dev * SUBLANES
    examples = len(tiles) * per_dev
    wide = examples + nq
    fisher_dim = SUBLANES * LANES
    me = lax.axis_index(axis)
    for slot, tile in enumerate(tiles):
        extended[slot * block : (slot + 1) * block] = tile[...]
    for q in range(nq):
        number = query_ref[q]
        place = (number // per_dev ^ me) * per_dev + number % per_dev
        first = pl.multiple_of(place * SUBLANES, SUBLANES)
        extended[(examples + q) * SUBLANES : (examples + q + 1) * SUBLANES] = extended[pl.ds(first, SUBLANES)]
    extended[wide * SUBLANES :] = jnp.zeros((LANES * SUBLANES - wide * SUBLANES, LANES), jnp.float32)
    right = jnp.concatenate([extended[pl.ds(s, LANES, stride=SUBLANES)] for s in range(SUBLANES)], axis=1)
    system = lax.dot_general(
        right[:examples], right, NT, precision=lax.Precision.HIGHEST, preferred_element_type=jnp.float32
    )
    row = lax.broadcasted_iota(jnp.int32, system.shape, 0)
    col = lax.broadcasted_iota(jnp.int32, system.shape, 1)
    diagonal = row == col
    trace = jnp.sum(jnp.where(diagonal, system, 0.0))
    damping = damp_ratio * trace / fisher_dim
    system = jnp.where(diagonal, system + damping, system)
    for k in range(examples):
        pivot_row = system[k : k + 1]
        scaled = pivot_row / system[k : k + 1, k : k + 1]
        system = jnp.where(row == k, scaled, system - system[:, k : k + 1] * scaled)
    scores_ref[...] = system[:per_dev, examples : examples + nq]


def gram_scores(tiles, query_index, axis):
    block = tiles[0].shape[0]
    per_dev = block // SUBLANES
    nq = query_index.shape[0]
    return pl.pallas_call(
        functools.partial(solve_kernel, nq, per_dev, axis),
        out_shape=jax.ShapeDtypeStruct((per_dev, nq), jnp.float32),
        in_specs=[pl.BlockSpec(memory_space=pltpu.VMEM)] * len(tiles) + [pl.BlockSpec(memory_space=pltpu.SMEM)],
        out_specs=pl.BlockSpec(memory_space=pltpu.VMEM),
        scratch_shapes=[pltpu.VMEM((LANES * SUBLANES, LANES), jnp.float32)],
    )(*tiles, query_index)


def gather_xor(tiles, axis, size):
    return [tiles] + [lax.ppermute(tiles, axis, [(i, i ^ s) for i in range(size)]) for s in range(1, size)]


def large_scores(tiles, query_index, per_dev, axis):
    sketches = tiles.reshape(-1, SUBLANES * LANES)
    gram = jnp.dot(sketches, sketches.T, precision=lax.Precision.HIGHEST)
    examples, fisher_dim = sketches.shape
    damping = damp_ratio * jnp.trace(gram) / fisher_dim
    factor = jnp.linalg.cholesky(gram + damping * jnp.eye(examples, dtype=jnp.float32))
    mine = lax.dynamic_slice_in_dim(gram, lax.axis_index(axis) * per_dev, per_dev, 0)
    half = lax.linalg.triangular_solve(factor, mine.T, left_side=True, lower=True)
    solved = lax.linalg.triangular_solve(factor, half, left_side=True, lower=True, transpose_a=True)
    selector = (query_index[:, None] == jnp.arange(examples, dtype=jnp.int32)[None, :]).astype(jnp.float32)
    return jnp.dot(selector, solved, precision=lax.Precision.HIGHEST).T


def local(activations, out_grads, project_in, project_out, lengths, query_index):
    per_dev = activations.shape[0]
    tiles = sketch_rows(activations, out_grads, project_in, project_out, lengths)
    size = lax.axis_size("dp")
    if size * per_dev + query_index.shape[0] <= LANES:
        return gram_scores(gather_xor(tiles, "dp", size), query_index, "dp")
    return large_scores(lax.all_gather(tiles, "dp", axis=0, tiled=True), query_index, per_dev, "dp")


def solution(mesh):
    return jax.shard_map(
        local,
        mesh=mesh,
        in_specs=(
            P(("groups", "dp"), None, None),
            P(("groups", "dp"), None, None),
            P(),
            P(),
            P(("groups", "dp")),
            P("groups"),
        ),
        out_specs=P(("groups", "dp"), None),
        check_vma=False,
    )
```

```python
import functools

import jax
import jax.numpy as jnp
from jax import lax
from jax.experimental import pallas as pl
from jax.experimental.pallas import tpu as pltpu
from jax.sharding import PartitionSpec as P

damp_ratio = 0.5
LANES = 128
SUBLANES = 8
NT = (((1,), (1,)), ((), ()))


def sketch_kernel(chunks, seq_len, copies_out, act_hbm, out_hbm, pin_hbm, pout_hbm, lengths_ref, sketch_ref, act, out, pin, pout, sems):
    rows, width = act.shape
    rank_dim = pin.shape[0]
    step = width // chunks
    copies = []
    for c in range(chunks):
        cols = pl.ds(c * step, step)
        copies.append(
            [
                pltpu.make_async_copy(src.at[:, cols], dst.at[:, cols], sems.at[n, c])
                for n, (src, dst) in enumerate(
                    ((pin_hbm, pin), (act_hbm, act), (pout_hbm, pout), (out_hbm, out))
                )
            ]
        )
        for copy in copies[-1]:
            copy.start()
    feat = jnp.zeros((rank_dim, rows), jnp.float32)
    grad = jnp.zeros((rank_dim, rows), jnp.float32)
    for c in range(chunks):
        cols = slice(c * step, (c + 1) * step)
        for copy in copies[c]:
            copy.wait()
        feat = feat + lax.dot_general(pin[:, cols], act[:, cols], NT, preferred_element_type=jnp.float32)
        grad = grad + lax.dot_general(pout[:, cols], out[:, cols], NT, preferred_element_type=jnp.float32)
    count = rows // seq_len
    reps = LANES // rank_dim
    position = lax.broadcasted_iota(jnp.int32, (rank_dim, rows), 1)
    masked = []
    for e in range(count):
        first = e * seq_len
        live = (position >= first) & (position < first + lengths_ref[e])
        masked.append(jnp.where(live, grad, 0.0))
    outer = lax.dot_general(
        jnp.concatenate(masked, axis=0),
        jnp.concatenate([feat] * reps, axis=0),
        NT,
        precision=lax.Precision.HIGHEST,
        preferred_element_type=jnp.float32,
    )
    band = lax.broadcasted_iota(jnp.int32, (SUBLANES, LANES), 1) // rank_dim
    for e in range(count):
        entry = outer[e * rank_dim : e * rank_dim + SUBLANES]
        for b in range(1, reps):
            first = e * rank_dim + b * SUBLANES
            entry = jnp.where(band == b, outer[first : first + SUBLANES], entry)
        for n in range(copies_out):
            first = (n * count + e) * SUBLANES
            sketch_ref[first : first + SUBLANES] = entry


def sketch_rows(activations, out_grads, project_in, project_out, lengths, copies_out):
    count, seq_len, width = activations.shape
    rank_dim = project_in.shape[1]
    rows = count * seq_len
    chunks = 8
    return pl.pallas_call(
        functools.partial(sketch_kernel, chunks, seq_len, copies_out),
        out_shape=jax.ShapeDtypeStruct((copies_out * count * SUBLANES, LANES), jnp.float32),
        in_specs=[pl.BlockSpec(memory_space=pltpu.HBM)] * 4 + [pl.BlockSpec(memory_space=pltpu.SMEM)],
        out_specs=pl.BlockSpec(memory_space=pltpu.VMEM),
        scratch_shapes=[
            pltpu.VMEM((rows, width), jnp.bfloat16),
            pltpu.VMEM((rows, width), jnp.bfloat16),
            pltpu.VMEM((rank_dim, width), jnp.bfloat16),
            pltpu.VMEM((rank_dim, width), jnp.bfloat16),
            pltpu.SemaphoreType.DMA((4, chunks)),
        ],
    )(
        activations.reshape(rows, width),
        out_grads.reshape(rows, width),
        project_in.T,
        project_out.T,
        lengths,
    )


def solve_kernel(nq, per_dev, axis, tiles_ref, query_ref, scores_ref, extended):
    block = per_dev * SUBLANES
    size = tiles_ref.shape[0] // block
    examples = size * per_dev
    wide = examples + nq
    fisher_dim = SUBLANES * LANES
    me = lax.axis_index(axis)
    for slot in range(size):
        first = pl.multiple_of((me ^ slot) * block, block)
        extended[slot * block : (slot + 1) * block] = tiles_ref[pl.ds(first, block)]
    for q in range(nq):
        number = query_ref[q]
        first = pl.multiple_of(number * SUBLANES, SUBLANES)
        extended[(examples + q) * SUBLANES : (examples + q + 1) * SUBLANES] = tiles_ref[pl.ds(first, SUBLANES)]
    extended[wide * SUBLANES :] = jnp.zeros((LANES * SUBLANES - wide * SUBLANES, LANES), jnp.float32)
    right = jnp.concatenate([extended[pl.ds(s, LANES, stride=SUBLANES)] for s in range(SUBLANES)], axis=1)
    system = lax.dot_general(
        right[:examples], right, NT, precision=lax.Precision.HIGHEST, preferred_element_type=jnp.float32
    )
    row = lax.broadcasted_iota(jnp.int32, system.shape, 0)
    col = lax.broadcasted_iota(jnp.int32, system.shape, 1)
    diagonal = row == col
    trace = jnp.sum(jnp.where(diagonal, system, 0.0))
    damping = damp_ratio * trace / fisher_dim
    system = jnp.where(diagonal, system + damping, system)
    for k in range(examples):
        pivot_row = system[k : k + 1]
        scaled = pivot_row / system[k : k + 1, k : k + 1]
        system = jnp.where(row == k, scaled, system - system[:, k : k + 1] * scaled)
    scores_ref[...] = system[:per_dev, examples : examples + nq]


def gram_scores(tiles, query_index, per_dev, axis):
    nq = query_index.shape[0]
    return pl.pallas_call(
        functools.partial(solve_kernel, nq, per_dev, axis),
        out_shape=jax.ShapeDtypeStruct((per_dev, nq), jnp.float32),
        in_specs=[pl.BlockSpec(memory_space=pltpu.VMEM), pl.BlockSpec(memory_space=pltpu.SMEM)],
        out_specs=pl.BlockSpec(memory_space=pltpu.VMEM),
        scratch_shapes=[pltpu.VMEM((LANES * SUBLANES, LANES), jnp.float32)],
        compiler_params=pltpu.CompilerParams(vmem_limit_bytes=8 * 2**20),
    )(tiles, query_index)


def large_scores(tiles, query_index, per_dev, axis):
    sketches = tiles.reshape(-1, SUBLANES * LANES)
    gram = jnp.dot(sketches, sketches.T, precision=lax.Precision.HIGHEST)
    examples, fisher_dim = sketches.shape
    damping = damp_ratio * jnp.trace(gram) / fisher_dim
    factor = jnp.linalg.cholesky(gram + damping * jnp.eye(examples, dtype=jnp.float32))
    mine = lax.dynamic_slice_in_dim(gram, lax.axis_index(axis) * per_dev, per_dev, 0)
    half = lax.linalg.triangular_solve(factor, mine.T, left_side=True, lower=True)
    solved = lax.linalg.triangular_solve(factor, half, left_side=True, lower=True, transpose_a=True)
    selector = (query_index[:, None] == jnp.arange(examples, dtype=jnp.int32)[None, :]).astype(jnp.float32)
    return jnp.dot(selector, solved, precision=lax.Precision.HIGHEST).T


def local(activations, out_grads, project_in, project_out, lengths, query_index):
    per_dev = activations.shape[0]
    size = lax.axis_size("dp")
    small = size * per_dev + query_index.shape[0] <= LANES
    copies_out = size if small else 1
    tiles = sketch_rows(activations, out_grads, project_in, project_out, lengths, copies_out)
    if small:
        every = lax.all_to_all(tiles, "dp", split_axis=0, concat_axis=0, tiled=True)
        return gram_scores(every, query_index, per_dev, "dp")
    return large_scores(lax.all_gather(tiles, "dp", axis=0, tiled=True), query_index, per_dev, "dp")


def solution(mesh):
    return jax.shard_map(
        local,
        mesh=mesh,
        in_specs=(
            P(("groups", "dp"), None, None),
            P(("groups", "dp"), None, None),
            P(),
            P(),
            P(("groups", "dp")),
            P("groups"),
        ),
        out_specs=P(("groups", "dp"), None),
        check_vma=False,
    )
```

```python
import functools

import jax
import jax.numpy as jnp
from jax import lax
from jax.experimental import pallas as pl
from jax.experimental.pallas import tpu as pltpu
from jax.sharding import PartitionSpec as P

damp_ratio = 0.5
LANES = 128
SUBLANES = 8
NT = (((1,), (1,)), ((), ()))


def sketch_kernel(chunks, seq_len, act_hbm, out_hbm, pin_hbm, pout_hbm, lengths_ref, sketch_ref, act, out, pin, pout, sems):
    rows, width = act.shape
    rank_dim = pin.shape[0]
    step = width // chunks
    copies = []
    for c in range(chunks):
        cols = pl.ds(c * step, step)
        copies.append(
            [
                pltpu.make_async_copy(src.at[:, cols], dst.at[:, cols], sems.at[n, c])
                for n, (src, dst) in enumerate(
                    ((pin_hbm, pin), (act_hbm, act), (pout_hbm, pout), (out_hbm, out))
                )
            ]
        )
        for copy in copies[-1]:
            copy.start()
    feat = jnp.zeros((rank_dim, rows), jnp.float32)
    grad = jnp.zeros((rank_dim, rows), jnp.float32)
    for c in range(chunks):
        cols = slice(c * step, (c + 1) * step)
        for copy in copies[c]:
            copy.wait()
        feat = feat + lax.dot_general(pin[:, cols], act[:, cols], NT, preferred_element_type=jnp.float32)
        grad = grad + lax.dot_general(pout[:, cols], out[:, cols], NT, preferred_element_type=jnp.float32)
    count = rows // seq_len
    reps = LANES // rank_dim
    position = lax.broadcasted_iota(jnp.int32, (rank_dim, rows), 1)
    masked = []
    for e in range(count):
        first = e * seq_len
        live = (position >= first) & (position < first + lengths_ref[e])
        masked.append(jnp.where(live, grad, 0.0))
    outer = lax.dot_general(
        jnp.concatenate(masked, axis=0),
        jnp.concatenate([feat] * reps, axis=0),
        NT,
        precision=lax.Precision.HIGHEST,
        preferred_element_type=jnp.float32,
    )
    band = lax.broadcasted_iota(jnp.int32, (SUBLANES, LANES), 1) // rank_dim
    for e in range(count):
        entry = outer[e * rank_dim : e * rank_dim + SUBLANES]
        for b in range(1, reps):
            first = e * rank_dim + b * SUBLANES
            entry = jnp.where(band == b, outer[first : first + SUBLANES], entry)
        sketch_ref[e * SUBLANES : (e + 1) * SUBLANES] = entry


def sketch_rows(activations, out_grads, project_in, project_out, lengths):
    count, seq_len, width = activations.shape
    rank_dim = project_in.shape[1]
    rows = count * seq_len
    chunks = 8
    return pl.pallas_call(
        functools.partial(sketch_kernel, chunks, seq_len),
        out_shape=jax.ShapeDtypeStruct((count * SUBLANES, LANES), jnp.float32),
        in_specs=[pl.BlockSpec(memory_space=pltpu.HBM)] * 4 + [pl.BlockSpec(memory_space=pltpu.SMEM)],
        out_specs=pl.BlockSpec(memory_space=pltpu.VMEM),
        scratch_shapes=[
            pltpu.VMEM((rows, width), jnp.bfloat16),
            pltpu.VMEM((rows, width), jnp.bfloat16),
            pltpu.VMEM((rank_dim, width), jnp.bfloat16),
            pltpu.VMEM((rank_dim, width), jnp.bfloat16),
            pltpu.SemaphoreType.DMA((4, chunks)),
        ],
    )(
        activations.reshape(rows, width),
        out_grads.reshape(rows, width),
        project_in.T,
        project_out.T,
        lengths,
    )


def solve_kernel(nq, per_dev, inner, axis, *refs):
    tiles, (query_ref, scores_ref, extended) = refs[:-3], refs[-3:]
    block = tiles[0].shape[0]
    examples = len(tiles) * block // SUBLANES
    outer = examples // (inner * per_dev)
    wide = examples + nq
    fisher_dim = SUBLANES * LANES
    me = lax.axis_index(axis)
    for slot, tile in enumerate(tiles):
        extended[slot * block : (slot + 1) * block] = tile[...]
    for q in range(nq):
        number = query_ref[q]
        slot = (number // per_dev) ^ me
        place = ((slot % inner) * outer + slot // inner) * per_dev + number % per_dev
        first = pl.multiple_of(place * SUBLANES, SUBLANES)
        extended[(examples + q) * SUBLANES : (examples + q + 1) * SUBLANES] = extended[pl.ds(first, SUBLANES)]
    extended[wide * SUBLANES :] = jnp.zeros((LANES * SUBLANES - wide * SUBLANES, LANES), jnp.float32)
    right = jnp.concatenate([extended[pl.ds(s, LANES, stride=SUBLANES)] for s in range(SUBLANES)], axis=1)
    system = lax.dot_general(
        right[:examples], right, NT, precision=lax.Precision.HIGHEST, preferred_element_type=jnp.float32
    )
    row = lax.broadcasted_iota(jnp.int32, system.shape, 0)
    col = lax.broadcasted_iota(jnp.int32, system.shape, 1)
    diagonal = row == col
    trace = jnp.sum(jnp.where(diagonal, system, 0.0))
    damping = damp_ratio * trace / fisher_dim
    system = jnp.where(diagonal, system + damping, system)
    for k in range(examples):
        pivot_row = system[k : k + 1]
        scaled = pivot_row / system[k : k + 1, k : k + 1]
        system = jnp.where(row == k, scaled, system - system[:, k : k + 1] * scaled)
    scores_ref[...] = system[:per_dev, examples : examples + nq]


def gram_scores(tiles, query_index, per_dev, inner, axis):
    nq = query_index.shape[0]
    return pl.pallas_call(
        functools.partial(solve_kernel, nq, per_dev, inner, axis),
        out_shape=jax.ShapeDtypeStruct((per_dev, nq), jnp.float32),
        in_specs=[pl.BlockSpec(memory_space=pltpu.VMEM)] * len(tiles) + [pl.BlockSpec(memory_space=pltpu.SMEM)],
        out_specs=pl.BlockSpec(memory_space=pltpu.VMEM),
        scratch_shapes=[pltpu.VMEM((LANES * SUBLANES, LANES), jnp.float32)],
        compiler_params=pltpu.CompilerParams(vmem_limit_bytes=8 * 2**20),
    )(*tiles, query_index)


def gather_xor(tiles, axis, size, inner):
    def swap(block, slot):
        return lax.ppermute(block, axis, [(i, i ^ slot) for i in range(size)])

    column = jnp.concatenate([tiles] + [swap(tiles, slot) for slot in range(inner, size, inner)], axis=0)
    return [column] + [swap(column, slot) for slot in range(1, inner)]


def large_scores(tiles, query_index, per_dev, axis):
    sketches = tiles.reshape(-1, SUBLANES * LANES)
    gram = jnp.dot(sketches, sketches.T, precision=lax.Precision.HIGHEST)
    examples, fisher_dim = sketches.shape
    damping = damp_ratio * jnp.trace(gram) / fisher_dim
    factor = jnp.linalg.cholesky(gram + damping * jnp.eye(examples, dtype=jnp.float32))
    mine = lax.dynamic_slice_in_dim(gram, lax.axis_index(axis) * per_dev, per_dev, 0)
    half = lax.linalg.triangular_solve(factor, mine.T, left_side=True, lower=True)
    solved = lax.linalg.triangular_solve(factor, half, left_side=True, lower=True, transpose_a=True)
    selector = (query_index[:, None] == jnp.arange(examples, dtype=jnp.int32)[None, :]).astype(jnp.float32)
    return jnp.dot(selector, solved, precision=lax.Precision.HIGHEST).T


def local(activations, out_grads, project_in, project_out, lengths, query_index):
    per_dev = activations.shape[0]
    size = lax.axis_size("dp")
    tiles = sketch_rows(activations, out_grads, project_in, project_out, lengths)
    if size * per_dev + query_index.shape[0] <= LANES:
        inner = 4
        return gram_scores(gather_xor(tiles, "dp", size, inner), query_index, per_dev, inner, "dp")
    return large_scores(lax.all_gather(tiles, "dp", axis=0, tiled=True), query_index, per_dev, "dp")


def solution(mesh):
    return jax.shard_map(
        local,
        mesh=mesh,
        in_specs=(
            P(("groups", "dp"), None, None),
            P(("groups", "dp"), None, None),
            P(),
            P(),
            P(("groups", "dp")),
            P("groups"),
        ),
        out_specs=P(("groups", "dp"), None),
        check_vma=False,
    )
```

```python
import functools

import jax
import jax.numpy as jnp
from jax import lax
from jax.experimental import pallas as pl
from jax.experimental.pallas import tpu as pltpu
from jax.sharding import PartitionSpec as P

damp_ratio = 0.5
AXES = ("outer", "inner")
LANES = 128
SUBLANES = 8
NT = (((1,), (1,)), ((), ()))


def sketch_kernel(chunks, seq_len, act_hbm, out_hbm, pin_hbm, pout_hbm, lengths_ref, sketch_ref, act, out, pin, pout, sems):
    rows, width = act.shape
    rank_dim = pin.shape[0]
    step = width // chunks
    copies = []
    for c in range(chunks):
        cols = pl.ds(c * step, step)
        copies.append(
            [
                pltpu.make_async_copy(src.at[:, cols], dst.at[:, cols], sems.at[n, c])
                for n, (src, dst) in enumerate(
                    ((pin_hbm, pin), (act_hbm, act), (pout_hbm, pout), (out_hbm, out))
                )
            ]
        )
        for copy in copies[-1]:
            copy.start()
    feat = jnp.zeros((rank_dim, rows), jnp.float32)
    grad = jnp.zeros((rank_dim, rows), jnp.float32)
    for c in range(chunks):
        cols = slice(c * step, (c + 1) * step)
        for copy in copies[c]:
            copy.wait()
        feat = feat + lax.dot_general(pin[:, cols], act[:, cols], NT, preferred_element_type=jnp.float32)
        grad = grad + lax.dot_general(pout[:, cols], out[:, cols], NT, preferred_element_type=jnp.float32)
    count = rows // seq_len
    reps = LANES // rank_dim
    position = lax.broadcasted_iota(jnp.int32, (rank_dim, rows), 1)
    masked = []
    for e in range(count):
        first = e * seq_len
        live = (position >= first) & (position < first + lengths_ref[e])
        masked.append(jnp.where(live, grad, 0.0))
    outer = lax.dot_general(
        jnp.concatenate(masked, axis=0),
        jnp.concatenate([feat] * reps, axis=0),
        NT,
        precision=lax.Precision.HIGHEST,
        preferred_element_type=jnp.float32,
    )
    band = lax.broadcasted_iota(jnp.int32, (SUBLANES, LANES), 1) // rank_dim
    for e in range(count):
        entry = outer[e * rank_dim : e * rank_dim + SUBLANES]
        for b in range(1, reps):
            first = e * rank_dim + b * SUBLANES
            entry = jnp.where(band == b, outer[first : first + SUBLANES], entry)
        sketch_ref[e * SUBLANES : (e + 1) * SUBLANES] = entry


def sketch_rows(activations, out_grads, project_in, project_out, lengths):
    count, seq_len, width = activations.shape
    rank_dim = project_in.shape[1]
    rows = count * seq_len
    chunks = 8
    return pl.pallas_call(
        functools.partial(sketch_kernel, chunks, seq_len),
        out_shape=jax.ShapeDtypeStruct((count * SUBLANES, LANES), jnp.float32),
        in_specs=[pl.BlockSpec(memory_space=pltpu.HBM)] * 4 + [pl.BlockSpec(memory_space=pltpu.SMEM)],
        out_specs=pl.BlockSpec(memory_space=pltpu.VMEM),
        scratch_shapes=[
            pltpu.VMEM((rows, width), jnp.bfloat16),
            pltpu.VMEM((rows, width), jnp.bfloat16),
            pltpu.VMEM((rank_dim, width), jnp.bfloat16),
            pltpu.VMEM((rank_dim, width), jnp.bfloat16),
            pltpu.SemaphoreType.DMA((4, chunks)),
        ],
    )(
        activations.reshape(rows, width),
        out_grads.reshape(rows, width),
        project_in.T,
        project_out.T,
        lengths,
    )


def solve_kernel(nq, per_dev, place_of, tiles_ref, query_ref, scores_ref, extended, solved):
    examples = tiles_ref.shape[0] // SUBLANES
    wide = examples + nq
    fisher_dim = SUBLANES * LANES
    extended[: examples * SUBLANES] = tiles_ref[...]
    for q in range(nq):
        number = query_ref[q]
        place = place_of(number // per_dev) * per_dev + number % per_dev
        first = pl.multiple_of(place * SUBLANES, SUBLANES)
        extended[(examples + q) * SUBLANES : (examples + q + 1) * SUBLANES] = tiles_ref[pl.ds(first, SUBLANES)]
    extended[wide * SUBLANES :] = jnp.zeros((LANES * SUBLANES - wide * SUBLANES, LANES), jnp.float32)
    right = jnp.concatenate([extended[pl.ds(s, LANES, stride=SUBLANES)] for s in range(SUBLANES)], axis=1)
    system = lax.dot_general(
        right[:examples], right, NT, precision=lax.Precision.HIGHEST, preferred_element_type=jnp.float32
    )
    row = lax.broadcasted_iota(jnp.int32, system.shape, 0)
    col = lax.broadcasted_iota(jnp.int32, system.shape, 1)
    diagonal = row == col
    trace = jnp.sum(jnp.where(diagonal, system, 0.0))
    damping = damp_ratio * trace / fisher_dim
    system = jnp.where(diagonal, system + damping, system)
    for k in range(examples):
        pivot_row = system[k : k + 1]
        scaled = pivot_row / system[k : k + 1, k : k + 1]
        system = jnp.where(row == k, scaled, system - system[:, k : k + 1] * scaled)
    solved[...] = system
    first = place_of(lax.axis_index(AXES)) * per_dev
    scores_ref[...] = solved[pl.ds(first, per_dev)][:, examples : examples + nq]


def gram_scores(tiles, query_index, per_dev, place_of):
    nq = query_index.shape[0]
    return pl.pallas_call(
        functools.partial(solve_kernel, nq, per_dev, place_of),
        out_shape=jax.ShapeDtypeStruct((per_dev, nq), jnp.float32),
        in_specs=[pl.BlockSpec(memory_space=pltpu.VMEM), pl.BlockSpec(memory_space=pltpu.SMEM)],
        out_specs=pl.BlockSpec(memory_space=pltpu.VMEM),
        scratch_shapes=[
            pltpu.VMEM((LANES * SUBLANES, LANES), jnp.float32),
            pltpu.VMEM((tiles.shape[0] // SUBLANES, LANES), jnp.float32),
        ],
        compiler_params=pltpu.CompilerParams(vmem_limit_bytes=8 * 2**20),
    )(tiles, query_index)


def large_scores(tiles, query_index, per_dev, axis):
    sketches = tiles.reshape(-1, SUBLANES * LANES)
    gram = jnp.dot(sketches, sketches.T, precision=lax.Precision.HIGHEST)
    examples, fisher_dim = sketches.shape
    damping = damp_ratio * jnp.trace(gram) / fisher_dim
    factor = jnp.linalg.cholesky(gram + damping * jnp.eye(examples, dtype=jnp.float32))
    mine = lax.dynamic_slice_in_dim(gram, lax.axis_index(axis) * per_dev, per_dev, 0)
    half = lax.linalg.triangular_solve(factor, mine.T, left_side=True, lower=True)
    solved = lax.linalg.triangular_solve(factor, half, left_side=True, lower=True, transpose_a=True)
    selector = (query_index[:, None] == jnp.arange(examples, dtype=jnp.int32)[None, :]).astype(jnp.float32)
    return jnp.dot(selector, solved, precision=lax.Precision.HIGHEST).T


def local(activations, out_grads, project_in, project_out, lengths, query_index):
    per_dev = activations.shape[0]
    outer, inner = (lax.axis_size(name) for name in AXES)
    tiles = sketch_rows(activations, out_grads, project_in, project_out, lengths)
    if outer * inner * per_dev + query_index.shape[0] <= LANES:
        column = lax.all_gather(tiles, "outer", axis=0, tiled=True)
        every = lax.all_gather(column, "inner", axis=0, tiled=True)
        return gram_scores(every, query_index, per_dev, lambda p: p % inner * outer + p // inner)
    return large_scores(lax.all_gather(tiles, AXES, axis=0, tiled=True), query_index, per_dev, AXES)


def solution(mesh):
    groups, size = mesh.shape["groups"], mesh.shape["dp"]
    inner = 4
    cut = jax.sharding.Mesh(mesh.devices.reshape(groups, size // inner, inner), ("groups",) + AXES)
    every = ("groups",) + AXES
    return jax.shard_map(
        local,
        mesh=cut,
        in_specs=(P(every, None, None), P(every, None, None), P(), P(), P(every), P("groups")),
        out_specs=P(every, None),
        check_vma=False,
    )
```

```python
import functools

import jax
import jax.numpy as jnp
from jax import lax
from jax.experimental import pallas as pl
from jax.experimental.pallas import tpu as pltpu
from jax.sharding import PartitionSpec as P

damp_ratio = 0.5
LANES = 128
SUBLANES = 8
NT = (((1,), (1,)), ((), ()))


def sketch_kernel(chunks, seq_len, act_hbm, out_hbm, pin_hbm, pout_hbm, lengths_ref, sketch_ref, act, out, pin, pout, sems):
    rows, width = act.shape
    rank_dim = pin.shape[0]
    step = width // chunks
    copies = []
    for c in range(chunks):
        cols = pl.ds(c * step, step)
        copies.append(
            [
                pltpu.make_async_copy(src.at[:, cols], dst.at[:, cols], sems.at[n, c])
                for n, (src, dst) in enumerate(
                    ((pin_hbm, pin), (act_hbm, act), (pout_hbm, pout), (out_hbm, out))
                )
            ]
        )
        for copy in copies[-1]:
            copy.start()
    feat = jnp.zeros((rows, rank_dim), jnp.float32)
    grad = jnp.zeros((rows, rank_dim), jnp.float32)
    for c in range(chunks):
        cols = slice(c * step, (c + 1) * step)
        for copy in copies[c]:
            copy.wait()
        feat = feat + lax.dot_general(act[:, cols], pin[:, cols], NT, preferred_element_type=jnp.float32)
        grad = grad + lax.dot_general(out[:, cols], pout[:, cols], NT, preferred_element_type=jnp.float32)
    count = rows // seq_len
    reps = LANES // rank_dim
    position = lax.broadcasted_iota(jnp.int32, (rows, rank_dim), 0)
    masked = []
    for e in range(count):
        first = e * seq_len
        live = (position >= first) & (position < first + lengths_ref[e])
        masked.append(jnp.where(live, grad, 0.0))
    outer = lax.dot_general(
        jnp.concatenate(masked, axis=1),
        jnp.concatenate([feat] * reps, axis=1),
        (((0,), (0,)), ((), ())),
        precision=lax.Precision.HIGHEST,
        preferred_element_type=jnp.float32,
    )
    band = lax.broadcasted_iota(jnp.int32, (SUBLANES, LANES), 1) // rank_dim
    for e in range(count):
        entry = outer[e * rank_dim : e * rank_dim + SUBLANES]
        for b in range(1, reps):
            first = e * rank_dim + b * SUBLANES
            entry = jnp.where(band == b, outer[first : first + SUBLANES], entry)
        sketch_ref[e * SUBLANES : (e + 1) * SUBLANES] = entry


def sketch_rows(activations, out_grads, project_in, project_out, lengths):
    count, seq_len, width = activations.shape
    rank_dim = project_in.shape[1]
    rows = count * seq_len
    chunks = 8
    return pl.pallas_call(
        functools.partial(sketch_kernel, chunks, seq_len),
        out_shape=jax.ShapeDtypeStruct((count * SUBLANES, LANES), jnp.float32),
        in_specs=[pl.BlockSpec(memory_space=pltpu.HBM)] * 4 + [pl.BlockSpec(memory_space=pltpu.SMEM)],
        out_specs=pl.BlockSpec(memory_space=pltpu.VMEM),
        scratch_shapes=[
            pltpu.VMEM((rows, width), jnp.bfloat16),
            pltpu.VMEM((rows, width), jnp.bfloat16),
            pltpu.VMEM((rank_dim, width), jnp.bfloat16),
            pltpu.VMEM((rank_dim, width), jnp.bfloat16),
            pltpu.SemaphoreType.DMA((4, chunks)),
        ],
    )(
        activations.reshape(rows, width),
        out_grads.reshape(rows, width),
        project_in.T,
        project_out.T,
        lengths,
    )


def eliminate(system, count):
    row = lax.broadcasted_iota(jnp.int32, (SUBLANES, system.shape[1]), 0)
    shape = system.shape
    for k in range(0, count, 4):
        cols = [jnp.broadcast_to(system[:, k + j : k + j + 1], shape) for j in range(4)]
        rows = [system[k + i : k + i + 1] for i in range(4)]
        p = [[cols[j][k + i : k + i + 1] for j in range(4)] for i in range(4)]
        scale = 1.0 / (p[0][0] * p[1][1] - p[0][1] * p[0][1])
        a, b, c = p[1][1] * scale, -p[0][1] * scale, p[0][0] * scale
        y = [
            [a * p[0][2] + b * p[1][2], a * p[0][3] + b * p[1][3]],
            [b * p[0][2] + c * p[1][2], b * p[0][3] + c * p[1][3]],
        ]
        s00 = p[2][2] - (p[0][2] * y[0][0] + p[1][2] * y[1][0])
        s01 = p[2][3] - (p[0][2] * y[0][1] + p[1][2] * y[1][1])
        s11 = p[3][3] - (p[0][3] * y[0][1] + p[1][3] * y[1][1])
        scale = 1.0 / (s00 * s11 - s01 * s01)
        d, e, f = s11 * scale, -s01 * scale, s00 * scale
        z0 = a * rows[0] + b * rows[1]
        z1 = b * rows[0] + c * rows[1]
        t0 = rows[2] - (p[0][2] * z0 + p[1][2] * z1)
        t1 = rows[3] - (p[0][3] * z0 + p[1][3] * z1)
        w2 = d * t0 + e * t1
        w3 = e * t0 + f * t1
        w0 = z0 - (y[0][0] * w2 + y[0][1] * w3)
        w1 = z1 - (y[1][0] * w2 + y[1][1] * w3)
        done = [w0, w1, w2, w3]
        parts = []
        for r in range(0, count, SUBLANES):
            own = slice(r, r + SUBLANES)
            part = system[own] - (cols[0][own] * w0 + cols[1][own] * w1) - (cols[2][own] * w2 + cols[3][own] * w3)
            if r <= k < r + SUBLANES:
                for i in range(4):
                    part = jnp.where(row == k - r + i, done[i], part)
            parts.append(part)
        system = jnp.concatenate(parts, axis=0)
    return system


def solve_kernel(nq, per_dev, inner, axis, *refs):
    tiles, (query_ref, scores_ref, extended) = refs[:-3], refs[-3:]
    block = tiles[0].shape[0]
    examples = len(tiles) * block // SUBLANES
    outer = examples // (inner * per_dev)
    wide = examples + nq
    fisher_dim = SUBLANES * LANES
    me = lax.axis_index(axis)
    for slot, tile in enumerate(tiles):
        extended[slot * block : (slot + 1) * block] = tile[...]
    for q in range(nq):
        number = query_ref[q]
        slot = (number // per_dev) ^ me
        place = ((slot % inner) * outer + slot // inner) * per_dev + number % per_dev
        first = pl.multiple_of(place * SUBLANES, SUBLANES)
        extended[(examples + q) * SUBLANES : (examples + q + 1) * SUBLANES] = extended[pl.ds(first, SUBLANES)]
    extended[wide * SUBLANES :] = jnp.zeros((LANES * SUBLANES - wide * SUBLANES, LANES), jnp.float32)
    right = jnp.concatenate([extended[pl.ds(s, LANES, stride=SUBLANES)] for s in range(SUBLANES)], axis=1)
    system = lax.dot_general(
        right[:examples], right, NT, precision=lax.Precision.HIGHEST, preferred_element_type=jnp.float32
    )
    row = lax.broadcasted_iota(jnp.int32, system.shape, 0)
    col = lax.broadcasted_iota(jnp.int32, system.shape, 1)
    diagonal = row == col
    trace = jnp.sum(jnp.where(diagonal, system, 0.0))
    damping = damp_ratio * trace / fisher_dim
    system = jnp.where(diagonal, system + damping, system)
    system = eliminate(system, examples)
    scores_ref[...] = system[:per_dev, examples : examples + nq]


def gram_scores(tiles, query_index, per_dev, inner, axis):
    nq = query_index.shape[0]
    return pl.pallas_call(
        functools.partial(solve_kernel, nq, per_dev, inner, axis),
        out_shape=jax.ShapeDtypeStruct((per_dev, nq), jnp.float32),
        in_specs=[pl.BlockSpec(memory_space=pltpu.VMEM)] * len(tiles) + [pl.BlockSpec(memory_space=pltpu.SMEM)],
        out_specs=pl.BlockSpec(memory_space=pltpu.VMEM),
        scratch_shapes=[pltpu.VMEM((LANES * SUBLANES, LANES), jnp.float32)],
        compiler_params=pltpu.CompilerParams(vmem_limit_bytes=8 * 2**20),
    )(*tiles, query_index)


def gather_xor(tiles, axis, size, inner):
    def swap(block, slot):
        return lax.ppermute(block, axis, [(i, i ^ slot) for i in range(size)])

    column = jnp.concatenate([tiles] + [swap(tiles, slot) for slot in range(inner, size, inner)], axis=0)
    return [column] + [swap(column, slot) for slot in range(1, inner)]


def large_scores(tiles, query_index, per_dev, axis):
    sketches = tiles.reshape(-1, SUBLANES * LANES)
    gram = jnp.dot(sketches, sketches.T, precision=lax.Precision.HIGHEST)
    examples, fisher_dim = sketches.shape
    damping = damp_ratio * jnp.trace(gram) / fisher_dim
    factor = jnp.linalg.cholesky(gram + damping * jnp.eye(examples, dtype=jnp.float32))
    mine = lax.dynamic_slice_in_dim(gram, lax.axis_index(axis) * per_dev, per_dev, 0)
    half = lax.linalg.triangular_solve(factor, mine.T, left_side=True, lower=True)
    solved = lax.linalg.triangular_solve(factor, half, left_side=True, lower=True, transpose_a=True)
    selector = (query_index[:, None] == jnp.arange(examples, dtype=jnp.int32)[None, :]).astype(jnp.float32)
    return jnp.dot(selector, solved, precision=lax.Precision.HIGHEST).T


def local(activations, out_grads, project_in, project_out, lengths, query_index):
    per_dev = activations.shape[0]
    size = lax.axis_size("dp")
    tiles = sketch_rows(activations, out_grads, project_in, project_out, lengths)
    if size * per_dev + query_index.shape[0] <= LANES:
        inner = 4
        return gram_scores(gather_xor(tiles, "dp", size, inner), query_index, per_dev, inner, "dp")
    return large_scores(lax.all_gather(tiles, "dp", axis=0, tiled=True), query_index, per_dev, "dp")


def solution(mesh):
    return jax.shard_map(
        local,
        mesh=mesh,
        in_specs=(
            P(("groups", "dp"), None, None),
            P(("groups", "dp"), None, None),
            P(),
            P(),
            P(("groups", "dp")),
            P("groups"),
        ),
        out_specs=P(("groups", "dp"), None),
        check_vma=False,
    )
```

```python
import functools

import jax
import jax.numpy as jnp
from jax import lax
from jax.experimental import pallas as pl
from jax.experimental.pallas import tpu as pltpu
from jax.sharding import PartitionSpec as P

damp_ratio = 0.5
AXES = ("outer", "inner")
LANES = 128
SUBLANES = 8
NT = (((1,), (1,)), ((), ()))


def sketch_kernel(chunks, seq_len, copies_out, act_hbm, out_hbm, pin_hbm, pout_hbm, lengths_ref, sketch_ref, act, out, pin, pout, sems):
    rows, width = act.shape
    rank_dim = pin.shape[0]
    step = width // chunks
    copies = []
    for c in range(chunks):
        cols = pl.ds(c * step, step)
        copies.append(
            [
                pltpu.make_async_copy(src.at[:, cols], dst.at[:, cols], sems.at[n, c])
                for n, (src, dst) in enumerate(
                    ((pin_hbm, pin), (act_hbm, act), (pout_hbm, pout), (out_hbm, out))
                )
            ]
        )
        for copy in copies[-1]:
            copy.start()
    feat = jnp.zeros((rows, rank_dim), jnp.float32)
    grad = jnp.zeros((rows, rank_dim), jnp.float32)
    for c in range(chunks):
        cols = slice(c * step, (c + 1) * step)
        for copy in copies[c]:
            copy.wait()
        feat = feat + lax.dot_general(act[:, cols], pin[:, cols], NT, preferred_element_type=jnp.float32)
        grad = grad + lax.dot_general(out[:, cols], pout[:, cols], NT, preferred_element_type=jnp.float32)
    count = rows // seq_len
    reps = LANES // rank_dim
    position = lax.broadcasted_iota(jnp.int32, (rows, rank_dim), 0)
    masked = []
    for e in range(count):
        first = e * seq_len
        live = (position >= first) & (position < first + lengths_ref[e])
        masked.append(jnp.where(live, grad, 0.0))
    outer = lax.dot_general(
        jnp.concatenate(masked, axis=1),
        jnp.concatenate([feat] * reps, axis=1),
        (((0,), (0,)), ((), ())),
        precision=lax.Precision.HIGHEST,
        preferred_element_type=jnp.float32,
    )
    band = lax.broadcasted_iota(jnp.int32, (SUBLANES, LANES), 1) // rank_dim
    for e in range(count):
        entry = outer[e * rank_dim : e * rank_dim + SUBLANES]
        for b in range(1, reps):
            first = e * rank_dim + b * SUBLANES
            entry = jnp.where(band == b, outer[first : first + SUBLANES], entry)
        for n in range(copies_out):
            first = (n * count + e) * SUBLANES
            sketch_ref[first : first + SUBLANES] = entry


def sketch_rows(activations, out_grads, project_in, project_out, lengths, copies_out):
    count, seq_len, width = activations.shape
    rank_dim = project_in.shape[1]
    rows = count * seq_len
    chunks = 8
    return pl.pallas_call(
        functools.partial(sketch_kernel, chunks, seq_len, copies_out),
        out_shape=jax.ShapeDtypeStruct((copies_out * count * SUBLANES, LANES), jnp.float32),
        in_specs=[pl.BlockSpec(memory_space=pltpu.HBM)] * 4 + [pl.BlockSpec(memory_space=pltpu.SMEM)],
        out_specs=pl.BlockSpec(memory_space=pltpu.VMEM),
        scratch_shapes=[
            pltpu.VMEM((rows, width), jnp.bfloat16),
            pltpu.VMEM((rows, width), jnp.bfloat16),
            pltpu.VMEM((rank_dim, width), jnp.bfloat16),
            pltpu.VMEM((rank_dim, width), jnp.bfloat16),
            pltpu.SemaphoreType.DMA((4, chunks)),
        ],
        compiler_params=pltpu.CompilerParams(vmem_limit_bytes=241 * 2**18),
    )(
        activations.reshape(rows, width),
        out_grads.reshape(rows, width),
        project_in.T,
        project_out.T,
        lengths,
    )


def eliminate(system, count):
    row = lax.broadcasted_iota(jnp.int32, (SUBLANES, system.shape[1]), 0)
    shape = system.shape
    for k in range(0, count, 4):
        cols = [jnp.broadcast_to(system[:, k + j : k + j + 1], shape) for j in range(4)]
        rows = [system[k + i : k + i + 1] for i in range(4)]
        p = [[cols[j][k + i : k + i + 1] for j in range(4)] for i in range(4)]
        scale = 1.0 / (p[0][0] * p[1][1] - p[0][1] * p[0][1])
        a, b, c = p[1][1] * scale, -p[0][1] * scale, p[0][0] * scale
        y = [
            [a * p[0][2] + b * p[1][2], a * p[0][3] + b * p[1][3]],
            [b * p[0][2] + c * p[1][2], b * p[0][3] + c * p[1][3]],
        ]
        s00 = p[2][2] - (p[0][2] * y[0][0] + p[1][2] * y[1][0])
        s01 = p[2][3] - (p[0][2] * y[0][1] + p[1][2] * y[1][1])
        s11 = p[3][3] - (p[0][3] * y[0][1] + p[1][3] * y[1][1])
        scale = 1.0 / (s00 * s11 - s01 * s01)
        d, e, f = s11 * scale, -s01 * scale, s00 * scale
        z0 = a * rows[0] + b * rows[1]
        z1 = b * rows[0] + c * rows[1]
        t0 = rows[2] - (p[0][2] * z0 + p[1][2] * z1)
        t1 = rows[3] - (p[0][3] * z0 + p[1][3] * z1)
        w2 = d * t0 + e * t1
        w3 = e * t0 + f * t1
        w0 = z0 - (y[0][0] * w2 + y[0][1] * w3)
        w1 = z1 - (y[1][0] * w2 + y[1][1] * w3)
        done = [w0, w1, w2, w3]
        parts = []
        for r in range(0, count, SUBLANES):
            own = slice(r, r + SUBLANES)
            part = system[own] - (cols[0][own] * w0 + cols[1][own] * w1) - (cols[2][own] * w2 + cols[3][own] * w3)
            if r <= k < r + SUBLANES:
                for i in range(4):
                    part = jnp.where(row == k - r + i, done[i], part)
            parts.append(part)
        system = jnp.concatenate(parts, axis=0)
    return system


def solve_kernel(nq, per_dev, *refs):
    tiles, (query_ref, scores_ref, extended, solved) = refs[:-4], refs[-4:]
    block = tiles[0].shape[0]
    inner = len(tiles)
    examples = inner * block // SUBLANES
    outer = examples // (inner * per_dev)
    wide = examples + nq
    fisher_dim = SUBLANES * LANES
    mine_outer, mine_inner = (lax.axis_index(name) for name in AXES)
    for slot, tile in enumerate(tiles):
        extended[slot * block : (slot + 1) * block] = tile[...]
    for q in range(nq):
        number = query_ref[q]
        device = number // per_dev
        place = ((device % inner ^ mine_inner) * outer + device // inner) * per_dev + number % per_dev
        first = pl.multiple_of(place * SUBLANES, SUBLANES)
        extended[(examples + q) * SUBLANES : (examples + q + 1) * SUBLANES] = extended[pl.ds(first, SUBLANES)]
    extended[wide * SUBLANES :] = jnp.zeros((LANES * SUBLANES - wide * SUBLANES, LANES), jnp.float32)
    right = jnp.concatenate([extended[pl.ds(s, LANES, stride=SUBLANES)] for s in range(SUBLANES)], axis=1)
    system = lax.dot_general(
        right[:examples], right, NT, precision=lax.Precision.HIGHEST, preferred_element_type=jnp.float32
    )
    row = lax.broadcasted_iota(jnp.int32, system.shape, 0)
    col = lax.broadcasted_iota(jnp.int32, system.shape, 1)
    diagonal = row == col
    trace = jnp.sum(jnp.where(diagonal, system, 0.0))
    damping = damp_ratio * trace / fisher_dim
    system = jnp.where(diagonal, system + damping, system)
    system = eliminate(system, examples)
    solved[...] = system
    scores_ref[...] = solved[pl.ds(mine_outer * per_dev, per_dev)][:, examples : examples + nq]


def gram_scores(tiles, query_index, per_dev):
    nq = query_index.shape[0]
    examples = len(tiles) * tiles[0].shape[0] // SUBLANES
    return pl.pallas_call(
        functools.partial(solve_kernel, nq, per_dev),
        out_shape=jax.ShapeDtypeStruct((per_dev, nq), jnp.float32),
        in_specs=[pl.BlockSpec(memory_space=pltpu.VMEM)] * len(tiles) + [pl.BlockSpec(memory_space=pltpu.SMEM)],
        out_specs=pl.BlockSpec(memory_space=pltpu.VMEM),
        scratch_shapes=[
            pltpu.VMEM((LANES * SUBLANES, LANES), jnp.float32),
            pltpu.VMEM((examples, LANES), jnp.float32),
        ],
        compiler_params=pltpu.CompilerParams(vmem_limit_bytes=8 * 2**20),
    )(*tiles, query_index)


def large_scores(tiles, query_index, per_dev, axis):
    sketches = tiles.reshape(-1, SUBLANES * LANES)
    gram = jnp.dot(sketches, sketches.T, precision=lax.Precision.HIGHEST)
    examples, fisher_dim = sketches.shape
    damping = damp_ratio * jnp.trace(gram) / fisher_dim
    factor = jnp.linalg.cholesky(gram + damping * jnp.eye(examples, dtype=jnp.float32))
    mine = lax.dynamic_slice_in_dim(gram, lax.axis_index(axis) * per_dev, per_dev, 0)
    half = lax.linalg.triangular_solve(factor, mine.T, left_side=True, lower=True)
    solved = lax.linalg.triangular_solve(factor, half, left_side=True, lower=True, transpose_a=True)
    selector = (query_index[:, None] == jnp.arange(examples, dtype=jnp.int32)[None, :]).astype(jnp.float32)
    return jnp.dot(selector, solved, precision=lax.Precision.HIGHEST).T


def local(activations, out_grads, project_in, project_out, lengths, query_index):
    per_dev = activations.shape[0]
    outer, inner = (lax.axis_size(name) for name in AXES)
    small = outer * inner * per_dev + query_index.shape[0] <= LANES
    tiles = sketch_rows(activations, out_grads, project_in, project_out, lengths, outer if small else 1)
    if not small:
        return large_scores(lax.all_gather(tiles, AXES, axis=0, tiled=True), query_index, per_dev, AXES)
    column = lax.all_to_all(tiles, "outer", split_axis=0, concat_axis=0, tiled=True)
    columns = [column] + [
        lax.ppermute(column, "inner", [(i, i ^ slot) for i in range(inner)]) for slot in range(1, inner)
    ]
    return gram_scores(columns, query_index, per_dev)


def solution(mesh):
    groups, size = mesh.shape["groups"], mesh.shape["dp"]
    inner = 4
    cut = jax.sharding.Mesh(mesh.devices.reshape(groups, size // inner, inner), ("groups",) + AXES)
    every = ("groups",) + AXES
    return jax.shard_map(
        local,
        mesh=cut,
        in_specs=(P(every, None, None), P(every, None, None), P(), P(), P(every), P("groups")),
        out_specs=P(every, None),
        check_vma=False,
    )
```

```python
import functools

import jax
import jax.numpy as jnp
from jax import lax
from jax.experimental import pallas as pl
from jax.experimental.pallas import tpu as pltpu
from jax.sharding import PartitionSpec as P

damp_ratio = 0.5
LANES = 128
SUBLANES = 8
NT = (((1,), (1,)), ((), ()))


def sketch_kernel(chunks, seq_len, act_hbm, out_hbm, pin_hbm, pout_hbm, lengths_hbm, sketch_ref, act, out, pin, pout, lengths_ref, sems, lengths_sem):
    rows, width = act.shape
    rank_dim = pin.shape[0]
    step = width // chunks
    lengths_copy = pltpu.make_async_copy(lengths_hbm, lengths_ref, lengths_sem)
    lengths_copy.start()
    copies = []
    for c in range(chunks):
        cols = pl.ds(c * step, step)
        copies.append(
            [
                pltpu.make_async_copy(src.at[:, cols], dst.at[:, cols], sems.at[n, c])
                for n, (src, dst) in enumerate(
                    ((pin_hbm, pin), (act_hbm, act), (pout_hbm, pout), (out_hbm, out))
                )
            ]
        )
        for copy in copies[-1]:
            copy.start()
    feat = jnp.zeros((rows, rank_dim), jnp.float32)
    grad = jnp.zeros((rows, rank_dim), jnp.float32)
    for c in range(chunks):
        cols = slice(c * step, (c + 1) * step)
        for copy in copies[c]:
            copy.wait()
        feat = feat + lax.dot_general(act[:, cols], pin[:, cols], NT, preferred_element_type=jnp.float32)
        grad = grad + lax.dot_general(out[:, cols], pout[:, cols], NT, preferred_element_type=jnp.float32)
    count = rows // seq_len
    reps = LANES // rank_dim
    lengths_copy.wait()
    position = lax.broadcasted_iota(jnp.int32, (rows, rank_dim), 0)
    masked = []
    for e in range(count):
        first = e * seq_len
        live = (position >= first) & (position < first + lengths_ref[e])
        masked.append(jnp.where(live, grad, 0.0))
    outer = lax.dot_general(
        jnp.concatenate(masked, axis=1),
        jnp.concatenate([feat] * reps, axis=1),
        (((0,), (0,)), ((), ())),
        precision=lax.Precision.HIGHEST,
        preferred_element_type=jnp.float32,
    )
    band = lax.broadcasted_iota(jnp.int32, (SUBLANES, LANES), 1) // rank_dim
    for e in range(count):
        entry = outer[e * rank_dim : e * rank_dim + SUBLANES]
        for b in range(1, reps):
            first = e * rank_dim + b * SUBLANES
            entry = jnp.where(band == b, outer[first : first + SUBLANES], entry)
        sketch_ref[e * SUBLANES : (e + 1) * SUBLANES] = entry


def sketch_rows(activations, out_grads, project_in, project_out, lengths):
    count, seq_len, width = activations.shape
    rank_dim = project_in.shape[1]
    rows = count * seq_len
    chunks = 8
    return pl.pallas_call(
        functools.partial(sketch_kernel, chunks, seq_len),
        out_shape=jax.ShapeDtypeStruct((count * SUBLANES, LANES), jnp.float32),
        in_specs=[pl.BlockSpec(memory_space=pltpu.HBM)] * 5,
        out_specs=pl.BlockSpec(memory_space=pltpu.VMEM),
        scratch_shapes=[
            pltpu.VMEM((rows, width), jnp.bfloat16),
            pltpu.VMEM((rows, width), jnp.bfloat16),
            pltpu.VMEM((rank_dim, width), jnp.bfloat16),
            pltpu.VMEM((rank_dim, width), jnp.bfloat16),
            pltpu.SMEM((count,), jnp.int32),
            pltpu.SemaphoreType.DMA((4, chunks)),
            pltpu.SemaphoreType.DMA,
        ],
        compiler_params=pltpu.CompilerParams(vmem_limit_bytes=16 * 2**20),
    )(
        *(
            pltpu.with_memory_space_constraint(operand, pltpu.HBM)
            for operand in (
                activations.reshape(rows, width),
                out_grads.reshape(rows, width),
                project_in.T,
                project_out.T,
                lengths,
            )
        ),
    )


def eliminate(system, count):
    row = lax.broadcasted_iota(jnp.int32, (SUBLANES, system.shape[1]), 0)
    shape = system.shape
    for k in range(0, count, 4):
        cols = [jnp.broadcast_to(system[:, k + j : k + j + 1], shape) for j in range(4)]
        rows = [system[k + i : k + i + 1] for i in range(4)]
        p = [[cols[j][k + i : k + i + 1] for j in range(4)] for i in range(4)]
        scale = 1.0 / (p[0][0] * p[1][1] - p[0][1] * p[0][1])
        a, b, c = p[1][1] * scale, -p[0][1] * scale, p[0][0] * scale
        y = [
            [a * p[0][2] + b * p[1][2], a * p[0][3] + b * p[1][3]],
            [b * p[0][2] + c * p[1][2], b * p[0][3] + c * p[1][3]],
        ]
        s00 = p[2][2] - (p[0][2] * y[0][0] + p[1][2] * y[1][0])
        s01 = p[2][3] - (p[0][2] * y[0][1] + p[1][2] * y[1][1])
        s11 = p[3][3] - (p[0][3] * y[0][1] + p[1][3] * y[1][1])
        scale = 1.0 / (s00 * s11 - s01 * s01)
        d, e, f = s11 * scale, -s01 * scale, s00 * scale
        z0 = a * rows[0] + b * rows[1]
        z1 = b * rows[0] + c * rows[1]
        t0 = rows[2] - (p[0][2] * z0 + p[1][2] * z1)
        t1 = rows[3] - (p[0][3] * z0 + p[1][3] * z1)
        w2 = d * t0 + e * t1
        w3 = e * t0 + f * t1
        w0 = z0 - (y[0][0] * w2 + y[0][1] * w3)
        w1 = z1 - (y[1][0] * w2 + y[1][1] * w3)
        done = [w0, w1, w2, w3]
        parts = []
        for r in range(0, count, SUBLANES):
            own = slice(r, r + SUBLANES)
            part = system[own] - (cols[0][own] * w0 + cols[1][own] * w1) - (cols[2][own] * w2 + cols[3][own] * w3)
            if r <= k < r + SUBLANES:
                for i in range(4):
                    part = jnp.where(row == k - r + i, done[i], part)
            parts.append(part)
        system = jnp.concatenate(parts, axis=0)
    return system


def solve_kernel(nq, per_dev, inner, axis, *refs):
    tiles, (query_ref, scores_ref, extended) = refs[:-3], refs[-3:]
    block = tiles[0].shape[0]
    examples = len(tiles) * block // SUBLANES
    outer = examples // (inner * per_dev)
    wide = examples + nq
    fisher_dim = SUBLANES * LANES
    me = lax.axis_index(axis)
    for slot, tile in enumerate(tiles):
        extended[slot * block : (slot + 1) * block] = tile[...]
    for q in range(nq):
        number = query_ref[q]
        slot = (number // per_dev) ^ me
        place = (gray(slot % inner) * outer + gray(slot // inner)) * per_dev + number % per_dev
        first = pl.multiple_of(place * SUBLANES, SUBLANES)
        extended[(examples + q) * SUBLANES : (examples + q + 1) * SUBLANES] = extended[pl.ds(first, SUBLANES)]
    extended[wide * SUBLANES :] = jnp.zeros((LANES * SUBLANES - wide * SUBLANES, LANES), jnp.float32)
    right = jnp.concatenate([extended[pl.ds(s, LANES, stride=SUBLANES)] for s in range(SUBLANES)], axis=1)
    system = lax.dot_general(
        right[:examples], right, NT, precision=lax.Precision.HIGHEST, preferred_element_type=jnp.float32
    )
    row = lax.broadcasted_iota(jnp.int32, system.shape, 0)
    col = lax.broadcasted_iota(jnp.int32, system.shape, 1)
    diagonal = row == col
    trace = jnp.sum(jnp.where(diagonal, system, 0.0))
    damping = damp_ratio * trace / fisher_dim
    system = jnp.where(diagonal, system + damping, system)
    system = eliminate(system, examples)
    scores_ref[...] = system[:per_dev, examples : examples + nq]


def gram_scores(tiles, query_index, per_dev, inner, axis):
    nq = query_index.shape[0]
    return pl.pallas_call(
        functools.partial(solve_kernel, nq, per_dev, inner, axis),
        out_shape=jax.ShapeDtypeStruct((per_dev, nq), jnp.float32),
        in_specs=[pl.BlockSpec(memory_space=pltpu.VMEM)] * len(tiles) + [pl.BlockSpec(memory_space=pltpu.SMEM)],
        out_specs=pl.BlockSpec(memory_space=pltpu.VMEM),
        scratch_shapes=[pltpu.VMEM((LANES * SUBLANES, LANES), jnp.float32)],
        compiler_params=pltpu.CompilerParams(vmem_limit_bytes=8 * 2**20),
    )(*tiles, query_index)


def gray(n):
    return n ^ (n >> 1)


def gather_xor(tiles, axis, size, inner):
    def swap_all(block, unit, count):
        order = sorted(range(1, count), key=gray)
        return [block] + [lax.ppermute(block, axis, [(i, i ^ n * unit) for i in range(size)]) for n in order]

    return swap_all(jnp.concatenate(swap_all(tiles, inner, size // inner), axis=0), 1, inner)


def large_scores(tiles, query_index, per_dev, axis):
    sketches = tiles.reshape(-1, SUBLANES * LANES)
    gram = jnp.dot(sketches, sketches.T, precision=lax.Precision.HIGHEST)
    examples, fisher_dim = sketches.shape
    damping = damp_ratio * jnp.trace(gram) / fisher_dim
    factor = jnp.linalg.cholesky(gram + damping * jnp.eye(examples, dtype=jnp.float32))
    mine = lax.dynamic_slice_in_dim(gram, lax.axis_index(axis) * per_dev, per_dev, 0)
    half = lax.linalg.triangular_solve(factor, mine.T, left_side=True, lower=True)
    solved = lax.linalg.triangular_solve(factor, half, left_side=True, lower=True, transpose_a=True)
    selector = (query_index[:, None] == jnp.arange(examples, dtype=jnp.int32)[None, :]).astype(jnp.float32)
    return jnp.dot(selector, solved, precision=lax.Precision.HIGHEST).T


def local(activations, out_grads, project_in, project_out, lengths, query_index):
    per_dev = activations.shape[0]
    size = lax.axis_size("dp")
    tiles = sketch_rows(activations, out_grads, project_in, project_out, lengths)
    if size * per_dev + query_index.shape[0] <= LANES:
        inner = 4
        return gram_scores(gather_xor(tiles, "dp", size, inner), query_index, per_dev, inner, "dp")
    return large_scores(lax.all_gather(tiles, "dp", axis=0, tiled=True), query_index, per_dev, "dp")


def solution(mesh):
    return jax.shard_map(
        local,
        mesh=mesh,
        in_specs=(
            P(("groups", "dp"), None, None),
            P(("groups", "dp"), None, None),
            P(),
            P(),
            P(("groups", "dp")),
            P("groups"),
        ),
        out_specs=P(("groups", "dp"), None),
        check_vma=False,
    )
```

```python
import functools

import jax
import jax.numpy as jnp
from jax import lax
from jax.experimental import pallas as pl
from jax.experimental.pallas import tpu as pltpu
from jax.sharding import PartitionSpec as P

damp_ratio = 0.5
LANES = 128
SUBLANES = 8
NT = (((1,), (1,)), ((), ()))


def sketch_kernel(chunks, seq_len, act_hbm, out_hbm, pin_hbm, pout_hbm, lengths_hbm, sketch_ref, act, out, pin, pout, lengths_ref, sems, lengths_sem):
    rows, width = act.shape
    rank_dim = pin.shape[0]
    step = width // chunks
    lengths_copy = pltpu.make_async_copy(lengths_hbm, lengths_ref, lengths_sem)
    lengths_copy.start()
    copies = []
    for c in range(chunks):
        cols = pl.ds(c * step, step)
        copies.append(
            [
                pltpu.make_async_copy(src.at[:, cols], dst.at[:, cols], sems.at[n, c])
                for n, (src, dst) in enumerate(
                    ((pin_hbm, pin), (act_hbm, act), (pout_hbm, pout), (out_hbm, out))
                )
            ]
        )
        for copy in copies[-1]:
            copy.start()
    feat = jnp.zeros((rows, rank_dim), jnp.float32)
    grad = jnp.zeros((rows, rank_dim), jnp.float32)
    for c in range(chunks):
        cols = slice(c * step, (c + 1) * step)
        for copy in copies[c]:
            copy.wait()
        feat = feat + lax.dot_general(act[:, cols], pin[:, cols], NT, preferred_element_type=jnp.float32)
        grad = grad + lax.dot_general(out[:, cols], pout[:, cols], NT, preferred_element_type=jnp.float32)
    count = rows // seq_len
    reps = LANES // rank_dim
    lengths_copy.wait()
    position = lax.broadcasted_iota(jnp.int32, (rows, rank_dim), 0)
    masked = []
    for e in range(count):
        first = e * seq_len
        live = (position >= first) & (position < first + lengths_ref[e])
        masked.append(jnp.where(live, grad, 0.0))
    outer = lax.dot_general(
        jnp.concatenate(masked, axis=1),
        jnp.concatenate([feat] * reps, axis=1),
        (((0,), (0,)), ((), ())),
        precision=lax.Precision.HIGHEST,
        preferred_element_type=jnp.float32,
    )
    band = lax.broadcasted_iota(jnp.int32, (SUBLANES, LANES), 1) // rank_dim
    for e in range(count):
        entry = outer[e * rank_dim : e * rank_dim + SUBLANES]
        for b in range(1, reps):
            first = e * rank_dim + b * SUBLANES
            entry = jnp.where(band == b, outer[first : first + SUBLANES], entry)
        sketch_ref[e * SUBLANES : (e + 1) * SUBLANES] = entry


def sketch_rows(activations, out_grads, project_in, project_out, lengths):
    count, seq_len, width = activations.shape
    rank_dim = project_in.shape[1]
    rows = count * seq_len
    chunks = 8
    return pl.pallas_call(
        functools.partial(sketch_kernel, chunks, seq_len),
        out_shape=jax.ShapeDtypeStruct((count * SUBLANES, LANES), jnp.float32),
        in_specs=[pl.BlockSpec(memory_space=pltpu.HBM)] * 5,
        out_specs=pl.BlockSpec(memory_space=pltpu.VMEM),
        scratch_shapes=[
            pltpu.VMEM((rows, width), jnp.bfloat16),
            pltpu.VMEM((rows, width), jnp.bfloat16),
            pltpu.VMEM((rank_dim, width), jnp.bfloat16),
            pltpu.VMEM((rank_dim, width), jnp.bfloat16),
            pltpu.SMEM((count,), jnp.int32),
            pltpu.SemaphoreType.DMA((4, chunks)),
            pltpu.SemaphoreType.DMA,
        ],
        compiler_params=pltpu.CompilerParams(vmem_limit_bytes=16 * 2**20),
    )(
        *(
            pltpu.with_memory_space_constraint(operand, pltpu.HBM)
            for operand in (
                activations.reshape(rows, width),
                out_grads.reshape(rows, width),
                project_in.T,
                project_out.T,
                lengths,
            )
        ),
    )


def reciprocal(x):
    guess = pl.reciprocal(x, approx=True)
    guess = guess * (2.0 - x * guess)
    return guess * (2.0 - x * guess)


def pivot_solver(p):
    scale = reciprocal(p[0][0] * p[1][1] - p[0][1] * p[0][1])
    a, b, c = p[1][1] * scale, p[0][1] * scale, p[0][0] * scale
    y = [
        [a * p[0][2] - b * p[1][2], a * p[0][3] - b * p[1][3]],
        [c * p[1][2] - b * p[0][2], c * p[1][3] - b * p[0][3]],
    ]
    s00 = p[2][2] - (p[0][2] * y[0][0] + p[1][2] * y[1][0])
    s01 = p[2][3] - (p[0][2] * y[0][1] + p[1][2] * y[1][1])
    s11 = p[3][3] - (p[0][3] * y[0][1] + p[1][3] * y[1][1])
    scale = reciprocal(s00 * s11 - s01 * s01)
    d, e, f = s11 * scale, s01 * scale, s00 * scale

    def solve(r):
        z0 = a * r[0] - b * r[1]
        z1 = c * r[1] - b * r[0]
        t0 = r[2] - (y[0][0] * r[0] + y[1][0] * r[1])
        t1 = r[3] - (y[0][1] * r[0] + y[1][1] * r[1])
        w2 = d * t0 - e * t1
        w3 = f * t1 - e * t0
        return z0 - (y[0][0] * w2 + y[0][1] * w3), z1 - (y[1][0] * w2 + y[1][1] * w3), w2, w3

    return solve


def eliminate(system):
    step = 4
    count = len(system) * SUBLANES
    row = lax.broadcasted_iota(jnp.int32, (SUBLANES, LANES), 0)

    def spread(column):
        return [jnp.broadcast_to(tile[:, column : column + 1], tile.shape) for tile in system]

    def row_of(tiles, number):
        tile = tiles[number // SUBLANES]
        return jnp.broadcast_to(tile[number % SUBLANES : number % SUBLANES + 1], tile.shape)

    def update(tiles, columns, done, first):
        updated = []
        for n, tile in enumerate(tiles):
            tile = tile - (columns[0][n] * done[0] + columns[1][n] * done[1]) - (columns[2][n] * done[2] + columns[3][n] * done[3])
            if n == first // SUBLANES:
                for i in range(step):
                    tile = jnp.where(row == first % SUBLANES + i, done[i], tile)
            updated.append(tile)
        return updated

    columns = [spread(j) for j in range(step)]
    for first in range(0, count, step):
        pivots = range(first, first + step)
        solve = pivot_solver([[row_of(column, i) for column in columns] for i in pivots])
        following = []
        if first + step < count:
            for j in range(first + step, first + 2 * step):
                column = spread(j)
                following.append(update(column, columns, solve([row_of(column, i) for i in pivots]), first))
        system = update(system, columns, solve([row_of(system, i) for i in pivots]), first)
        columns = following
    return system


def solve_kernel(per_dev, inner, axis, *refs):
    tiles, (query_ref, scores_ref, gram_ref) = refs[:-3], refs[-3:]
    nq = query_ref.shape[1]
    part = tiles[0].shape[0] // SUBLANES
    examples = len(tiles) * part
    outer = examples // (inner * per_dev)
    fisher_dim = SUBLANES * LANES
    gram_ref[...] = jnp.zeros(gram_ref.shape, jnp.float32)
    slot = (query_ref[...] // per_dev) ^ lax.axis_index(axis)
    place = (gray(slot % inner) * outer + gray(slot // inner)) * per_dev + query_ref[...] % per_dev
    rest = LANES - examples - nq
    place = jnp.concatenate(
        [jnp.zeros((1, examples), jnp.int32), place] + ([jnp.zeros((1, rest), jnp.int32)] if rest else []), axis=1
    )
    lane = lax.broadcasted_iota(jnp.int32, (SUBLANES, LANES), 1)
    source = jnp.where(lane < examples, lane, jnp.broadcast_to(place, lane.shape))
    sketches = jnp.concatenate(
        [
            jnp.concatenate([tile[pl.ds(s, part, stride=SUBLANES)] for tile in tiles], axis=0)
            for s in range(SUBLANES)
        ],
        axis=1,
    )
    squares = jnp.sum(jnp.sum(sketches * sketches, axis=0, keepdims=True), axis=1, keepdims=True)
    scale = jnp.broadcast_to(1.0 / squares, (SUBLANES, LANES))
    gram_ref[:, :examples] = lax.dot_general(
        sketches, sketches, NT, precision=lax.Precision.HIGHEST, preferred_element_type=jnp.float32
    )
    row = lax.broadcasted_iota(jnp.int32, (SUBLANES, LANES), 0)
    system = []
    for first in range(0, examples, SUBLANES):
        tile = jnp.take_along_axis(gram_ref[first : first + SUBLANES], source, axis=1) * scale
        system.append(jnp.where(lane == row + first, tile + damp_ratio / fisher_dim, tile))
    scores_ref[...] = eliminate(system)[0][:per_dev, examples : examples + nq]


def gram_scores(tiles, query_index, per_dev, inner, axis):
    nq = query_index.shape[0]
    examples = len(tiles) * tiles[0].shape[0] // SUBLANES
    return pl.pallas_call(
        functools.partial(solve_kernel, per_dev, inner, axis),
        out_shape=jax.ShapeDtypeStruct((per_dev, nq), jnp.float32),
        in_specs=[pl.BlockSpec(memory_space=pltpu.VMEM)] * (len(tiles) + 1),
        out_specs=pl.BlockSpec(memory_space=pltpu.VMEM),
        scratch_shapes=[pltpu.VMEM((examples, LANES), jnp.float32)],
        compiler_params=pltpu.CompilerParams(vmem_limit_bytes=8 * 2**20),
    )(*tiles, query_index.reshape(1, nq))


def gray(n):
    return n ^ (n >> 1)


def gather_xor(tiles, axis, size, inner):
    def swap(block, slot):
        return lax.ppermute(block, axis, [(i, i ^ slot) for i in range(size)])

    order = sorted(range(1, size // inner), key=gray)
    column = jnp.concatenate([tiles] + [swap(tiles, n * inner) for n in order], axis=0)
    across = swap(column, 2)
    return [column, swap(column, 1), swap(across, 1), across]


def large_scores(tiles, query_index, per_dev, axis):
    sketches = tiles.reshape(-1, SUBLANES * LANES)
    gram = jnp.dot(sketches, sketches.T, precision=lax.Precision.HIGHEST)
    examples, fisher_dim = sketches.shape
    damping = damp_ratio * jnp.trace(gram) / fisher_dim
    factor = jnp.linalg.cholesky(gram + damping * jnp.eye(examples, dtype=jnp.float32))
    mine = lax.dynamic_slice_in_dim(gram, lax.axis_index(axis) * per_dev, per_dev, 0)
    half = lax.linalg.triangular_solve(factor, mine.T, left_side=True, lower=True)
    solved = lax.linalg.triangular_solve(factor, half, left_side=True, lower=True, transpose_a=True)
    selector = (query_index[:, None] == jnp.arange(examples, dtype=jnp.int32)[None, :]).astype(jnp.float32)
    return jnp.dot(selector, solved, precision=lax.Precision.HIGHEST).T


def local(activations, out_grads, project_in, project_out, lengths, query_index):
    per_dev = activations.shape[0]
    size = lax.axis_size("dp")
    tiles = sketch_rows(activations, out_grads, project_in, project_out, lengths)
    if size * per_dev + query_index.shape[0] <= LANES:
        inner = 4
        return gram_scores(gather_xor(tiles, "dp", size, inner), query_index, per_dev, inner, "dp")
    return large_scores(lax.all_gather(tiles, "dp", axis=0, tiled=True), query_index, per_dev, "dp")


def solution(mesh):
    return jax.shard_map(
        local,
        mesh=mesh,
        in_specs=(
            P(("groups", "dp"), None, None),
            P(("groups", "dp"), None, None),
            P(),
            P(),
            P(("groups", "dp")),
            P("groups"),
        ),
        out_specs=P(("groups", "dp"), None),
        check_vma=False,
    )
```

```python
import functools

import jax
import jax.numpy as jnp
from jax import lax
from jax.experimental import pallas as pl
from jax.experimental.pallas import tpu as pltpu
from jax.sharding import PartitionSpec as P

damp_ratio = 0.5
LANES = 128
SUBLANES = 8
NT = (((1,), (1,)), ((), ()))


def sketch_kernel(chunks, floor, act_hbm, out_hbm, pin_hbm, pout_hbm, lengths_hbm, sketch_ref, act, out, pin, pout, lengths_ref, sems, lengths_sem):
    count, seq_len, width = act.shape
    rank_dim = pin.shape[0]
    rows = count * seq_len
    step = width // chunks
    lengths_copy = pltpu.make_async_copy(lengths_hbm, lengths_ref, lengths_sem)
    lengths_copy.start()

    def tail(c, e, n):
        src, dst = ((act_hbm, act), (out_hbm, out))[n]
        part = (e, pl.ds(floor, seq_len - floor), pl.ds(c * step, step))
        return pltpu.make_async_copy(src.at[part], dst.at[part], sems.at[c, 4 + 2 * e + n])

    heads = []
    for c in range(chunks):
        cols = pl.ds(c * step, step)
        head = (slice(None), pl.ds(0, floor), cols)
        heads.append(
            [
                pltpu.make_async_copy(src.at[part], dst.at[part], sems.at[c, n])
                for n, (src, dst, part) in enumerate(
                    (
                        (pin_hbm, pin, (slice(None), cols)),
                        (act_hbm, act, head),
                        (pout_hbm, pout, (slice(None), cols)),
                        (out_hbm, out, head),
                    )
                )
            ]
        )

    def start_heads(c):
        for copy in heads[c]:
            copy.start()

    def start_tails(c):
        for e in range(count):

            @pl.when(lengths_ref[e] > floor)
            def _():
                tail(c, e, 0).start()
                tail(c, e, 1).start()

    for c in range(2):
        start_heads(c)
    lengths_copy.wait()
    for c in range(chunks):
        if c >= 2:
            start_heads(c)
        start_tails(c)
    feat = jnp.zeros((rows, rank_dim), jnp.float32)
    grad = jnp.zeros((rows, rank_dim), jnp.float32)
    for c in range(chunks):
        cols = slice(c * step, (c + 1) * step)
        for copy in heads[c]:
            copy.wait()
        for e in range(count):

            @pl.when(lengths_ref[e] > floor)
            def _():
                tail(c, e, 0).wait()
                tail(c, e, 1).wait()

        feat = feat + lax.dot_general(
            act[:, :, cols].reshape(rows, step), pin[:, cols], NT, preferred_element_type=jnp.float32
        )
        grad = grad + lax.dot_general(
            out[:, :, cols].reshape(rows, step), pout[:, cols], NT, preferred_element_type=jnp.float32
        )
    reps = LANES // rank_dim
    position = lax.broadcasted_iota(jnp.int32, (rows, rank_dim), 0)
    masked = []
    live_any = jnp.zeros((rows, rank_dim), jnp.bool_)
    for e in range(count):
        first = e * seq_len
        live = (position >= first) & (position < first + lengths_ref[e])
        masked.append(jnp.where(live, grad, 0.0))
        live_any = live_any | live
    feat = jnp.where(live_any, feat, 0.0)
    outer = lax.dot_general(
        jnp.concatenate(masked, axis=1),
        jnp.concatenate([feat] * reps, axis=1),
        (((0,), (0,)), ((), ())),
        precision=lax.Precision.HIGHEST,
        preferred_element_type=jnp.float32,
    )
    band = lax.broadcasted_iota(jnp.int32, (SUBLANES, LANES), 1) // rank_dim
    for e in range(count):
        entry = outer[e * rank_dim : e * rank_dim + SUBLANES]
        for b in range(1, reps):
            first = e * rank_dim + b * SUBLANES
            entry = jnp.where(band == b, outer[first : first + SUBLANES], entry)
        sketch_ref[e * SUBLANES : (e + 1) * SUBLANES] = entry


def sketch_rows(activations, out_grads, project_in, project_out, lengths):
    count, seq_len, width = activations.shape
    rank_dim = project_in.shape[1]
    chunks = 8
    floor = 16
    return pl.pallas_call(
        functools.partial(sketch_kernel, chunks, floor),
        out_shape=jax.ShapeDtypeStruct((count * SUBLANES, LANES), jnp.float32),
        in_specs=[pl.BlockSpec(memory_space=pltpu.HBM)] * 5,
        out_specs=pl.BlockSpec(memory_space=pltpu.VMEM),
        scratch_shapes=[
            pltpu.VMEM((count, seq_len, width), jnp.bfloat16),
            pltpu.VMEM((count, seq_len, width), jnp.bfloat16),
            pltpu.VMEM((rank_dim, width), jnp.bfloat16),
            pltpu.VMEM((rank_dim, width), jnp.bfloat16),
            pltpu.SMEM((count,), jnp.int32),
            pltpu.SemaphoreType.DMA((chunks, 4 + 2 * count)),
            pltpu.SemaphoreType.DMA,
        ],
        compiler_params=pltpu.CompilerParams(vmem_limit_bytes=16 * 2**20),
    )(
        *(
            pltpu.with_memory_space_constraint(operand, pltpu.HBM)
            for operand in (activations, out_grads, project_in.T, project_out.T, lengths)
        )
    )


def reciprocal(x):
    guess = pl.reciprocal(x, approx=True)
    guess = guess * (2.0 - x * guess)
    return guess * (2.0 - x * guess)


def pivot_solver(p):
    scale = reciprocal(p[0][0] * p[1][1] - p[0][1] * p[0][1])
    a, b, c = p[1][1] * scale, p[0][1] * scale, p[0][0] * scale
    y = [
        [a * p[0][2] - b * p[1][2], a * p[0][3] - b * p[1][3]],
        [c * p[1][2] - b * p[0][2], c * p[1][3] - b * p[0][3]],
    ]
    s00 = p[2][2] - (p[0][2] * y[0][0] + p[1][2] * y[1][0])
    s01 = p[2][3] - (p[0][2] * y[0][1] + p[1][2] * y[1][1])
    s11 = p[3][3] - (p[0][3] * y[0][1] + p[1][3] * y[1][1])
    scale = reciprocal(s00 * s11 - s01 * s01)
    d, e, f = s11 * scale, s01 * scale, s00 * scale

    def solve(r):
        z0 = a * r[0] - b * r[1]
        z1 = c * r[1] - b * r[0]
        t0 = r[2] - (y[0][0] * r[0] + y[1][0] * r[1])
        t1 = r[3] - (y[0][1] * r[0] + y[1][1] * r[1])
        w2 = d * t0 - e * t1
        w3 = f * t1 - e * t0
        return z0 - (y[0][0] * w2 + y[0][1] * w3), z1 - (y[1][0] * w2 + y[1][1] * w3), w2, w3

    return solve


def solve_first(system):
    step = 4

    def spread(column):
        return [jnp.broadcast_to(tile[:, column : column + 1], tile.shape) for tile in system]

    def row_of(tiles, number):
        tile = tiles[number // SUBLANES]
        return jnp.broadcast_to(tile[number % SUBLANES : number % SUBLANES + 1], tile.shape)

    def update(tiles, columns, done):
        return [
            tile - (c0 * done[0] + c1 * done[1]) - (c2 * done[2] + c3 * done[3])
            for tile, c0, c1, c2, c3 in zip(tiles, *columns)
        ]

    count = len(system) * SUBLANES
    columns = [spread(j) for j in range(count - step, count)]
    for first in range(count - step, 0, -step):
        pivots = range(first, first + step)
        left = pl.cdiv(first, SUBLANES)
        solve = pivot_solver([[row_of(column, i) for column in columns] for i in pivots])
        following = []
        for j in range(first - step, first):
            column = spread(j)
            done = solve([row_of(column, i) for i in pivots])
            following.append(update(column[:left], [c[:left] for c in columns], done))
        done = solve([row_of(system, i) for i in pivots])
        system = update(system[:left], [c[:left] for c in columns], done)
        columns = following
    solve = pivot_solver([[row_of(column, i) for column in columns] for i in range(step)])
    return solve([row_of(system, i) for i in range(step)])


def solve_kernel(per_dev, inner, axis, *refs):
    tiles, (query_ref, scores_ref, gram_ref) = refs[:-3], refs[-3:]
    nq = query_ref.shape[1]
    part = tiles[0].shape[0] // SUBLANES
    examples = len(tiles) * part
    outer = examples // (inner * per_dev)
    fisher_dim = SUBLANES * LANES
    gram_ref[...] = jnp.zeros(gram_ref.shape, jnp.float32)
    slot = (query_ref[...] // per_dev) ^ lax.axis_index(axis)
    place = (gray(slot % inner) * outer + gray(slot // inner)) * per_dev + query_ref[...] % per_dev
    rest = LANES - examples - nq
    place = jnp.concatenate(
        [jnp.zeros((1, examples), jnp.int32), place] + ([jnp.zeros((1, rest), jnp.int32)] if rest else []), axis=1
    )
    lane = lax.broadcasted_iota(jnp.int32, (SUBLANES, LANES), 1)
    source = jnp.where(lane < examples, lane, jnp.broadcast_to(place, lane.shape))
    sketches = jnp.concatenate(
        [
            jnp.concatenate([tile[pl.ds(s, part, stride=SUBLANES)] for tile in tiles], axis=0)
            for s in range(SUBLANES)
        ],
        axis=1,
    )
    squares = jnp.sum(jnp.sum(sketches * sketches, axis=0, keepdims=True), axis=1, keepdims=True)
    scale = jnp.broadcast_to(1.0 / squares, (SUBLANES, LANES))
    gram_ref[:, :examples] = lax.dot_general(
        sketches, sketches, NT, precision=lax.Precision.HIGHEST, preferred_element_type=jnp.float32
    )
    row = lax.broadcasted_iota(jnp.int32, (SUBLANES, LANES), 0)
    system = []
    for first in range(0, examples, SUBLANES):
        tile = jnp.take_along_axis(gram_ref[first : first + SUBLANES], source, axis=1) * scale
        system.append(jnp.where(lane == row + first, tile + damp_ratio / fisher_dim, tile))
    solved = solve_first(system)
    scores = solved[0]
    for i in range(1, len(solved)):
        scores = jnp.where(row == i, solved[i], scores)
    scores_ref[...] = scores[:per_dev, examples : examples + nq]


def gram_scores(tiles, query_index, per_dev, inner, axis):
    nq = query_index.shape[0]
    examples = len(tiles) * tiles[0].shape[0] // SUBLANES
    return pl.pallas_call(
        functools.partial(solve_kernel, per_dev, inner, axis),
        out_shape=jax.ShapeDtypeStruct((per_dev, nq), jnp.float32),
        in_specs=[pl.BlockSpec(memory_space=pltpu.VMEM)] * (len(tiles) + 1),
        out_specs=pl.BlockSpec(memory_space=pltpu.VMEM),
        scratch_shapes=[pltpu.VMEM((examples, LANES), jnp.float32)],
        compiler_params=pltpu.CompilerParams(vmem_limit_bytes=8 * 2**20),
    )(*tiles, query_index.reshape(1, nq))


def gray(n):
    return n ^ (n >> 1)


def gather_xor(tiles, axis, size, inner):
    def swap_all(block, unit, count):
        order = sorted(range(1, count), key=gray)
        return [block] + [lax.ppermute(block, axis, [(i, i ^ n * unit) for i in range(size)]) for n in order]

    return swap_all(jnp.concatenate(swap_all(tiles, inner, size // inner), axis=0), 1, inner)


def large_scores(tiles, query_index, per_dev, axis):
    sketches = tiles.reshape(-1, SUBLANES * LANES)
    gram = jnp.dot(sketches, sketches.T, precision=lax.Precision.HIGHEST)
    examples, fisher_dim = sketches.shape
    damping = damp_ratio * jnp.trace(gram) / fisher_dim
    factor = jnp.linalg.cholesky(gram + damping * jnp.eye(examples, dtype=jnp.float32))
    mine = lax.dynamic_slice_in_dim(gram, lax.axis_index(axis) * per_dev, per_dev, 0)
    half = lax.linalg.triangular_solve(factor, mine.T, left_side=True, lower=True)
    solved = lax.linalg.triangular_solve(factor, half, left_side=True, lower=True, transpose_a=True)
    selector = (query_index[:, None] == jnp.arange(examples, dtype=jnp.int32)[None, :]).astype(jnp.float32)
    return jnp.dot(selector, solved, precision=lax.Precision.HIGHEST).T


def local(activations, out_grads, project_in, project_out, lengths, query_index):
    per_dev = activations.shape[0]
    size = lax.axis_size("dp")
    tiles = sketch_rows(activations, out_grads, project_in, project_out, lengths)
    if size * per_dev + query_index.shape[0] <= LANES:
        inner = 4
        return gram_scores(gather_xor(tiles, "dp", size, inner), query_index, per_dev, inner, "dp")
    return large_scores(lax.all_gather(tiles, "dp", axis=0, tiled=True), query_index, per_dev, "dp")


def solution(mesh):
    return jax.shard_map(
        local,
        mesh=mesh,
        in_specs=(
            P(("groups", "dp"), None, None),
            P(("groups", "dp"), None, None),
            P(),
            P(),
            P(("groups", "dp")),
            P("groups"),
        ),
        out_specs=P(("groups", "dp"), None),
        check_vma=False,
    )
```

```python
import functools

import jax
import jax.numpy as jnp
from jax import lax
from jax.experimental import pallas as pl
from jax.experimental.pallas import tpu as pltpu
from jax.sharding import PartitionSpec as P

damp_ratio = 0.5
LANES = 128
SUBLANES = 8
NT = (((1,), (1,)), ((), ()))


def sketch_kernel(bounds, floor, act_hbm, out_hbm, pin_hbm, pout_hbm, lengths_hbm, sketch_ref, act, out, pin, pout, lengths_ref, sems, lengths_sem):
    count, seq_len, width = act.shape
    rank_dim = pin.shape[0]
    rows = count * seq_len
    chunks = len(bounds) - 1
    columns = [pl.ds(a, b - a) for a, b in zip(bounds, bounds[1:])]
    lengths_copy = pltpu.make_async_copy(lengths_hbm, lengths_ref, lengths_sem)
    lengths_copy.start()

    def tail(c, e, n):
        src, dst = ((act_hbm, act), (out_hbm, out))[n]
        part = (e, pl.ds(floor, seq_len - floor), columns[c])
        return pltpu.make_async_copy(src.at[part], dst.at[part], sems.at[c, 4 + 2 * e + n])

    heads = []
    for c in range(chunks):
        cols = columns[c]
        head = (slice(None), pl.ds(0, floor), cols)
        heads.append(
            [
                pltpu.make_async_copy(src.at[part], dst.at[part], sems.at[c, n])
                for n, (src, dst, part) in enumerate(
                    (
                        (pin_hbm, pin, (slice(None), cols)),
                        (act_hbm, act, head),
                        (pout_hbm, pout, (slice(None), cols)),
                        (out_hbm, out, head),
                    )
                )
            ]
        )

    for c in range(chunks):
        for copy in heads[c]:
            copy.start()
    lengths_copy.wait()
    for c in range(chunks):
        for e in range(count):

            @pl.when(lengths_ref[e] > floor)
            def _():
                tail(c, e, 0).start()
                tail(c, e, 1).start()

    feat = jnp.zeros((rows, rank_dim), jnp.float32)
    grad = jnp.zeros((rows, rank_dim), jnp.float32)
    for c in range(chunks):
        cols = slice(bounds[c], bounds[c + 1])
        step = bounds[c + 1] - bounds[c]
        for copy in heads[c]:
            copy.wait()
        for e in range(count):

            @pl.when(lengths_ref[e] > floor)
            def _():
                tail(c, e, 0).wait()
                tail(c, e, 1).wait()

        feat = feat + lax.dot_general(
            act[:, :, cols].reshape(rows, step), pin[:, cols], NT, preferred_element_type=jnp.float32
        )
        grad = grad + lax.dot_general(
            out[:, :, cols].reshape(rows, step), pout[:, cols], NT, preferred_element_type=jnp.float32
        )
    reps = LANES // rank_dim
    position = lax.broadcasted_iota(jnp.int32, (rows, rank_dim), 0)
    masked = []
    live_any = jnp.zeros((rows, rank_dim), jnp.bool_)
    for e in range(count):
        first = e * seq_len
        live = (position >= first) & (position < first + lengths_ref[e])
        masked.append(jnp.where(live, grad, 0.0))
        live_any = live_any | live
    feat = jnp.where(live_any, feat, 0.0)
    outer = lax.dot_general(
        jnp.concatenate(masked, axis=1),
        jnp.concatenate([feat] * reps, axis=1),
        (((0,), (0,)), ((), ())),
        precision=lax.Precision.HIGHEST,
        preferred_element_type=jnp.float32,
    )
    band = lax.broadcasted_iota(jnp.int32, (SUBLANES, LANES), 1) // rank_dim
    for e in range(count):
        entry = outer[e * rank_dim : e * rank_dim + SUBLANES]
        for b in range(1, reps):
            first = e * rank_dim + b * SUBLANES
            entry = jnp.where(band == b, outer[first : first + SUBLANES], entry)
        sketch_ref[e * SUBLANES : (e + 1) * SUBLANES] = entry


def sketch_rows(activations, out_grads, project_in, project_out, lengths):
    count, seq_len, width = activations.shape
    rank_dim = project_in.shape[1]
    unit = width // 16
    bounds = (0, 5 * unit, 10 * unit, 14 * unit, width)
    chunks = len(bounds) - 1
    floor = 16
    return pl.pallas_call(
        functools.partial(sketch_kernel, bounds, floor),
        out_shape=jax.ShapeDtypeStruct((count * SUBLANES, LANES), jnp.float32),
        in_specs=[pl.BlockSpec(memory_space=pltpu.HBM)] * 5,
        out_specs=pl.BlockSpec(memory_space=pltpu.VMEM),
        scratch_shapes=[
            pltpu.VMEM((count, seq_len, width), jnp.bfloat16),
            pltpu.VMEM((count, seq_len, width), jnp.bfloat16),
            pltpu.VMEM((rank_dim, width), jnp.bfloat16),
            pltpu.VMEM((rank_dim, width), jnp.bfloat16),
            pltpu.SMEM((count,), jnp.int32),
            pltpu.SemaphoreType.DMA((chunks, 4 + 2 * count)),
            pltpu.SemaphoreType.DMA,
        ],
        compiler_params=pltpu.CompilerParams(vmem_limit_bytes=16 * 2**20),
    )(
        *(
            pltpu.with_memory_space_constraint(operand, pltpu.HBM)
            for operand in (activations, out_grads, project_in.T, project_out.T, lengths)
        )
    )


def solve_first(system):
    step = 4

    def spread(column):
        return [jnp.broadcast_to(tile[:, column : column + 1], tile.shape) for tile in system]

    def row_of(tiles, number):
        tile = tiles[number // SUBLANES]
        return jnp.broadcast_to(tile[number % SUBLANES : number % SUBLANES + 1], tile.shape)

    def factor(columns, first):
        p = {(i, j): row_of(columns[j], first + i) for j in range(step) for i in range(j + 1)}
        lower, inverse = {}, []
        for k in range(step):
            inverse.append(pl.reciprocal(p[k, k]))
            for i in range(k + 1, step):
                lower[i, k] = p[k, i] * inverse[k]
            for i in range(k + 1, step):
                for j in range(i, step):
                    p[i, j] = p[i, j] - lower[i, k] * p[k, j]
        return lower, inverse

    def forward(lower, parts):
        parts = list(parts)
        for k in range(step):
            for i in range(k + 1, step):
                parts[i] = [part - lower[i, k] * other for part, other in zip(parts[i], parts[k])]
        return parts

    def update(tiles, columns, lower, inverse, rows):
        rows = forward(lower, [[r] for r in rows])
        for column, row, scale in zip(columns, rows, inverse):
            done = row[0] * scale
            tiles = [tile - c * done for tile, c in zip(tiles, column)]
        return tiles

    count = len(system) * SUBLANES
    columns = [spread(j) for j in range(count - step, count)]
    for first in range(count - step, 0, -step):
        pivots = range(first, first + step)
        left = pl.cdiv(first, SUBLANES)
        lower, inverse = factor(columns, first)
        columns = forward(lower, [c[:left] for c in columns])
        following = []
        for j in range(first - step, first):
            column = spread(j)
            following.append(update(column[:left], columns, lower, inverse, [row_of(column, i) for i in pivots]))
        system = update(system[:left], columns, lower, inverse, [row_of(system, i) for i in pivots])
        columns = following
    lower, inverse = factor(columns, 0)
    rows = forward(lower, [[row_of(system, i)] for i in range(step)])
    solved = [row[0] * scale for row, scale in zip(rows, inverse)]
    for k in reversed(range(step)):
        for i in range(k):
            solved[i] = solved[i] - lower[k, i] * solved[k]
    return solved


def solve_kernel(per_dev, inner, axis, *refs):
    tiles, (query_ref, scores_ref, gram_ref) = refs[:-3], refs[-3:]
    nq = query_ref.shape[1]
    part = tiles[0].shape[0] // SUBLANES
    examples = len(tiles) * part
    outer = examples // (inner * per_dev)
    fisher_dim = SUBLANES * LANES
    gram_ref[...] = jnp.zeros(gram_ref.shape, jnp.float32)
    slot = (query_ref[...] // per_dev) ^ lax.axis_index(axis)
    place = (gray(slot % inner) * outer + gray(slot // inner)) * per_dev + query_ref[...] % per_dev
    rest = LANES - examples - nq
    place = jnp.concatenate(
        [jnp.zeros((1, examples), jnp.int32), place] + ([jnp.zeros((1, rest), jnp.int32)] if rest else []), axis=1
    )
    lane = lax.broadcasted_iota(jnp.int32, (SUBLANES, LANES), 1)
    source = jnp.where(lane < examples, lane, jnp.broadcast_to(place, lane.shape))
    sketches = jnp.concatenate(
        [
            jnp.concatenate([tile[pl.ds(s, part, stride=SUBLANES)] for tile in tiles], axis=0)
            for s in range(SUBLANES)
        ],
        axis=1,
    )
    squares = jnp.sum(jnp.sum(sketches * sketches, axis=0, keepdims=True), axis=1, keepdims=True)
    scale = jnp.broadcast_to(1.0 / squares, (SUBLANES, LANES))
    gram_ref[:, :examples] = lax.dot_general(
        sketches, sketches, NT, precision=lax.Precision.HIGHEST, preferred_element_type=jnp.float32
    )
    row = lax.broadcasted_iota(jnp.int32, (SUBLANES, LANES), 0)
    system = []
    for first in range(0, examples, SUBLANES):
        tile = jnp.take_along_axis(gram_ref[first : first + SUBLANES], source, axis=1) * scale
        system.append(jnp.where(lane == row + first, tile + damp_ratio / fisher_dim, tile))
    solved = solve_first(system)
    scores = solved[0]
    for i in range(1, len(solved)):
        scores = jnp.where(row == i, solved[i], scores)
    scores_ref[...] = scores[:per_dev, examples : examples + nq]


def gram_scores(tiles, query_index, per_dev, inner, axis):
    nq = query_index.shape[0]
    examples = len(tiles) * tiles[0].shape[0] // SUBLANES
    return pl.pallas_call(
        functools.partial(solve_kernel, per_dev, inner, axis),
        out_shape=jax.ShapeDtypeStruct((per_dev, nq), jnp.float32),
        in_specs=[pl.BlockSpec(memory_space=pltpu.VMEM)] * (len(tiles) + 1),
        out_specs=pl.BlockSpec(memory_space=pltpu.VMEM),
        scratch_shapes=[pltpu.VMEM((examples, LANES), jnp.float32)],
        compiler_params=pltpu.CompilerParams(vmem_limit_bytes=8 * 2**20),
    )(*tiles, query_index.reshape(1, nq))


def gray(n):
    return n ^ (n >> 1)


def gather_xor(tiles, axis, size, inner):
    def swap_all(block, unit, count):
        order = sorted(range(1, count), key=gray)
        return [block] + [lax.ppermute(block, axis, [(i, i ^ n * unit) for i in range(size)]) for n in order]

    return swap_all(jnp.concatenate(swap_all(tiles, inner, size // inner), axis=0), 1, inner)


def large_scores(tiles, query_index, per_dev, axis):
    sketches = tiles.reshape(-1, SUBLANES * LANES)
    gram = jnp.dot(sketches, sketches.T, precision=lax.Precision.HIGHEST)
    examples, fisher_dim = sketches.shape
    damping = damp_ratio * jnp.trace(gram) / fisher_dim
    factor = jnp.linalg.cholesky(gram + damping * jnp.eye(examples, dtype=jnp.float32))
    mine = lax.dynamic_slice_in_dim(gram, lax.axis_index(axis) * per_dev, per_dev, 0)
    half = lax.linalg.triangular_solve(factor, mine.T, left_side=True, lower=True)
    solved = lax.linalg.triangular_solve(factor, half, left_side=True, lower=True, transpose_a=True)
    selector = (query_index[:, None] == jnp.arange(examples, dtype=jnp.int32)[None, :]).astype(jnp.float32)
    return jnp.dot(selector, solved, precision=lax.Precision.HIGHEST).T


def local(activations, out_grads, project_in, project_out, lengths, query_index):
    per_dev = activations.shape[0]
    size = lax.axis_size("dp")
    tiles = sketch_rows(activations, out_grads, project_in, project_out, lengths)
    if size * per_dev + query_index.shape[0] <= LANES:
        inner = 4
        return gram_scores(gather_xor(tiles, "dp", size, inner), query_index, per_dev, inner, "dp")
    return large_scores(lax.all_gather(tiles, "dp", axis=0, tiled=True), query_index, per_dev, "dp")


def solution(mesh):
    return jax.shard_map(
        local,
        mesh=mesh,
        in_specs=(
            P(("groups", "dp"), None, None),
            P(("groups", "dp"), None, None),
            P(),
            P(),
            P(("groups", "dp")),
            P("groups"),
        ),
        out_specs=P(("groups", "dp"), None),
        check_vma=False,
    )
```

```python
import functools

import jax
import jax.numpy as jnp
from jax import lax
from jax.experimental import pallas as pl
from jax.experimental.pallas import tpu as pltpu
from jax.sharding import PartitionSpec as P

damp_ratio = 0.5
LANES = 128
SUBLANES = 8
NT = (((1,), (1,)), ((), ()))


def sketch_kernel(bounds, seq_len, act_hbm, out_hbm, pin_hbm, pout_hbm, lengths_hbm, sketch_ref, act, out, pin, pout, lengths_ref, sems, lengths_sem):
    rows, width = act.shape
    rank_dim = pin.shape[0]
    chunks = len(bounds) - 1
    lengths_copy = pltpu.make_async_copy(lengths_hbm, lengths_ref, lengths_sem)
    lengths_copy.start()
    copies = []
    for c in range(chunks):
        cols = pl.ds(bounds[c], bounds[c + 1] - bounds[c])
        copies.append(
            [
                pltpu.make_async_copy(src.at[:, cols], dst.at[:, cols], sems.at[n, c])
                for n, (src, dst) in enumerate(
                    ((pin_hbm, pin), (act_hbm, act), (pout_hbm, pout), (out_hbm, out))
                )
            ]
        )
        for copy in copies[-1]:
            copy.start()
    feat = jnp.zeros((rows, rank_dim), jnp.float32)
    grad = jnp.zeros((rows, rank_dim), jnp.float32)
    for c in range(chunks):
        cols = slice(bounds[c], bounds[c + 1])
        for copy in copies[c]:
            copy.wait()
        feat = feat + lax.dot_general(act[:, cols], pin[:, cols], NT, preferred_element_type=jnp.float32)
        grad = grad + lax.dot_general(out[:, cols], pout[:, cols], NT, preferred_element_type=jnp.float32)
    count = rows // seq_len
    reps = LANES // rank_dim
    lengths_copy.wait()
    position = lax.broadcasted_iota(jnp.int32, (rows, rank_dim), 0)
    masked = []
    for e in range(count):
        first = e * seq_len
        live = (position >= first) & (position < first + lengths_ref[e])
        masked.append(jnp.where(live, grad, 0.0))
    outer = lax.dot_general(
        jnp.concatenate(masked, axis=1),
        jnp.concatenate([feat] * reps, axis=1),
        (((0,), (0,)), ((), ())),
        precision=lax.Precision.HIGHEST,
        preferred_element_type=jnp.float32,
    )
    band = lax.broadcasted_iota(jnp.int32, (SUBLANES, LANES), 1) // rank_dim
    for e in range(count):
        entry = outer[e * rank_dim : e * rank_dim + SUBLANES]
        for b in range(1, reps):
            first = e * rank_dim + b * SUBLANES
            entry = jnp.where(band == b, outer[first : first + SUBLANES], entry)
        sketch_ref[e * SUBLANES : (e + 1) * SUBLANES] = entry


def sketch_rows(activations, out_grads, project_in, project_out, lengths):
    count, seq_len, width = activations.shape
    rank_dim = project_in.shape[1]
    rows = count * seq_len
    unit = width // 32
    bounds = [n * unit for n in (0, 5, 10, 15, 20, 25, 29, 31, 32)]
    chunks = len(bounds) - 1
    return pl.pallas_call(
        functools.partial(sketch_kernel, bounds, seq_len),
        out_shape=jax.ShapeDtypeStruct((count * SUBLANES, LANES), jnp.float32),
        in_specs=[pl.BlockSpec(memory_space=pltpu.HBM)] * 5,
        out_specs=pl.BlockSpec(memory_space=pltpu.VMEM),
        scratch_shapes=[
            pltpu.VMEM((rows, width), jnp.bfloat16),
            pltpu.VMEM((rows, width), jnp.bfloat16),
            pltpu.VMEM((rank_dim, width), jnp.bfloat16),
            pltpu.VMEM((rank_dim, width), jnp.bfloat16),
            pltpu.SMEM((count,), jnp.int32),
            pltpu.SemaphoreType.DMA((4, chunks)),
            pltpu.SemaphoreType.DMA,
        ],
        compiler_params=pltpu.CompilerParams(vmem_limit_bytes=16 * 2**20),
    )(
        *(
            pltpu.with_memory_space_constraint(operand, pltpu.HBM)
            for operand in (
                activations.reshape(rows, width),
                out_grads.reshape(rows, width),
                project_in.T,
                project_out.T,
                lengths,
            )
        ),
    )


def solve_first(system):
    step = 4

    def spread(column):
        return [jnp.broadcast_to(tile[:, column : column + 1], tile.shape) for tile in system]

    def row_of(tiles, number):
        tile = tiles[number // SUBLANES]
        return jnp.broadcast_to(tile[number % SUBLANES : number % SUBLANES + 1], tile.shape)

    def factor(columns, first):
        p = {(i, j): row_of(columns[j], first + i) for j in range(step) for i in range(j + 1)}
        lower, inverse = {}, []
        for k in range(step):
            inverse.append(pl.reciprocal(p[k, k]))
            for i in range(k + 1, step):
                lower[i, k] = p[k, i] * inverse[k]
            for i in range(k + 1, step):
                for j in range(i, step):
                    p[i, j] = p[i, j] - lower[i, k] * p[k, j]
        return lower, inverse

    def forward(lower, parts):
        parts = list(parts)
        for k in range(step):
            for i in range(k + 1, step):
                parts[i] = [part - lower[i, k] * other for part, other in zip(parts[i], parts[k])]
        return parts

    def update(tiles, columns, lower, inverse, rows):
        rows = forward(lower, [[r] for r in rows])
        for column, row, scale in zip(columns, rows, inverse):
            done = row[0] * scale
            tiles = [tile - c * done for tile, c in zip(tiles, column)]
        return tiles

    count = len(system) * SUBLANES
    columns = [spread(j) for j in range(count - step, count)]
    for first in range(count - step, 0, -step):
        pivots = range(first, first + step)
        left = pl.cdiv(first, SUBLANES)
        lower, inverse = factor(columns, first)
        columns = forward(lower, [c[:left] for c in columns])
        following = []
        for j in range(first - step, first):
            column = spread(j)
            following.append(update(column[:left], columns, lower, inverse, [row_of(column, i) for i in pivots]))
        system = update(system[:left], columns, lower, inverse, [row_of(system, i) for i in pivots])
        columns = following
    lower, inverse = factor(columns, 0)
    rows = forward(lower, [[row_of(system, i)] for i in range(step)])
    solved = [row[0] * scale for row, scale in zip(rows, inverse)]
    for k in reversed(range(step)):
        for i in range(k):
            solved[i] = solved[i] - lower[k, i] * solved[k]
    return solved


def solve_kernel(per_dev, inner, axis, *refs):
    tiles, (query_ref, scores_ref, gram_ref) = refs[:-3], refs[-3:]
    nq = query_ref.shape[1]
    part = tiles[0].shape[0] // SUBLANES
    examples = len(tiles) * part
    outer = examples // (inner * per_dev)
    fisher_dim = SUBLANES * LANES
    gram_ref[...] = jnp.zeros(gram_ref.shape, jnp.float32)
    slot = (query_ref[...] // per_dev) ^ lax.axis_index(axis)
    place = (gray(slot % inner) * outer + gray(slot // inner)) * per_dev + query_ref[...] % per_dev
    rest = LANES - examples - nq
    place = jnp.concatenate(
        [jnp.zeros((1, examples), jnp.int32), place] + ([jnp.zeros((1, rest), jnp.int32)] if rest else []), axis=1
    )
    lane = lax.broadcasted_iota(jnp.int32, (SUBLANES, LANES), 1)
    source = jnp.where(lane < examples, lane, jnp.broadcast_to(place, lane.shape))
    sketches = jnp.concatenate(
        [
            jnp.concatenate([tile[pl.ds(s, part, stride=SUBLANES)] for tile in tiles], axis=0)
            for s in range(SUBLANES)
        ],
        axis=1,
    )
    squares = jnp.sum(jnp.sum(sketches * sketches, axis=0, keepdims=True), axis=1, keepdims=True)
    scale = jnp.broadcast_to(1.0 / squares, (SUBLANES, LANES))
    gram_ref[:, :examples] = lax.dot_general(
        sketches, sketches, NT, precision=lax.Precision.HIGHEST, preferred_element_type=jnp.float32
    )
    row = lax.broadcasted_iota(jnp.int32, (SUBLANES, LANES), 0)
    system = []
    for first in range(0, examples, SUBLANES):
        tile = jnp.take_along_axis(gram_ref[first : first + SUBLANES], source, axis=1) * scale
        system.append(jnp.where(lane == row + first, tile + damp_ratio / fisher_dim, tile))
    solved = solve_first(system)
    scores = solved[0]
    for i in range(1, len(solved)):
        scores = jnp.where(row == i, solved[i], scores)
    scores_ref[...] = scores[:per_dev, examples : examples + nq]


def gram_scores(tiles, query_index, per_dev, inner, axis):
    nq = query_index.shape[0]
    examples = len(tiles) * tiles[0].shape[0] // SUBLANES
    return pl.pallas_call(
        functools.partial(solve_kernel, per_dev, inner, axis),
        out_shape=jax.ShapeDtypeStruct((per_dev, nq), jnp.float32),
        in_specs=[pl.BlockSpec(memory_space=pltpu.VMEM)] * (len(tiles) + 1),
        out_specs=pl.BlockSpec(memory_space=pltpu.VMEM),
        scratch_shapes=[pltpu.VMEM((examples, LANES), jnp.float32)],
        compiler_params=pltpu.CompilerParams(vmem_limit_bytes=8 * 2**20),
    )(*tiles, query_index.reshape(1, nq))


def gray(n):
    return n ^ (n >> 1)


def gather_xor(tiles, axis, size, inner):
    def swap_all(block, unit, count):
        order = sorted(range(1, count), key=gray)
        return [block] + [lax.ppermute(block, axis, [(i, i ^ n * unit) for i in range(size)]) for n in order]

    return swap_all(jnp.concatenate(swap_all(tiles, inner, size // inner), axis=0), 1, inner)


def large_scores(tiles, query_index, per_dev, axis):
    sketches = tiles.reshape(-1, SUBLANES * LANES)
    gram = jnp.dot(sketches, sketches.T, precision=lax.Precision.HIGHEST)
    examples, fisher_dim = sketches.shape
    damping = damp_ratio * jnp.trace(gram) / fisher_dim
    factor = jnp.linalg.cholesky(gram + damping * jnp.eye(examples, dtype=jnp.float32))
    mine = lax.dynamic_slice_in_dim(gram, lax.axis_index(axis) * per_dev, per_dev, 0)
    half = lax.linalg.triangular_solve(factor, mine.T, left_side=True, lower=True)
    solved = lax.linalg.triangular_solve(factor, half, left_side=True, lower=True, transpose_a=True)
    selector = (query_index[:, None] == jnp.arange(examples, dtype=jnp.int32)[None, :]).astype(jnp.float32)
    return jnp.dot(selector, solved, precision=lax.Precision.HIGHEST).T


def local(activations, out_grads, project_in, project_out, lengths, query_index):
    per_dev = activations.shape[0]
    size = lax.axis_size("dp")
    tiles = sketch_rows(activations, out_grads, project_in, project_out, lengths)
    if size * per_dev + query_index.shape[0] <= LANES:
        inner = 4
        return gram_scores(gather_xor(tiles, "dp", size, inner), query_index, per_dev, inner, "dp")
    return large_scores(lax.all_gather(tiles, "dp", axis=0, tiled=True), query_index, per_dev, "dp")


def solution(mesh):
    return jax.shard_map(
        local,
        mesh=mesh,
        in_specs=(
            P(("groups", "dp"), None, None),
            P(("groups", "dp"), None, None),
            P(),
            P(),
            P(("groups", "dp")),
            P("groups"),
        ),
        out_specs=P(("groups", "dp"), None),
        check_vma=False,
    )
```

```python
import functools

import jax
import jax.numpy as jnp
from jax import lax
from jax.experimental import pallas as pl
from jax.experimental.pallas import tpu as pltpu
from jax.sharding import PartitionSpec as P

damp_ratio = 0.5
LANES = 128
SUBLANES = 8
NT = (((1,), (1,)), ((), ()))


def sketch_kernel(bounds, seq_len, act_hbm, out_hbm, pin_hbm, pout_hbm, lengths_hbm, sketch_ref, act, out, pin, pout, lengths_ref, sems, lengths_sem):
    rows, width = act.shape
    rank_dim = pin.shape[0]
    chunks = len(bounds) - 1
    lengths_copy = pltpu.make_async_copy(lengths_hbm, lengths_ref, lengths_sem)
    lengths_copy.start()
    copies = []
    for c in range(chunks):
        cols = pl.ds(bounds[c], bounds[c + 1] - bounds[c])
        copies.append(
            [
                pltpu.make_async_copy(src.at[:, cols], dst.at[:, cols], sems.at[n, c])
                for n, (src, dst) in enumerate(
                    ((pin_hbm, pin), (act_hbm, act), (pout_hbm, pout), (out_hbm, out))
                )
            ]
        )
        for copy in copies[-1]:
            copy.start()
    feat = jnp.zeros((rows, rank_dim), jnp.float32)
    grad = jnp.zeros((rows, rank_dim), jnp.float32)
    for c in range(chunks):
        cols = slice(bounds[c], bounds[c + 1])
        for copy in copies[c]:
            copy.wait()
        feat = feat + lax.dot_general(act[:, cols], pin[:, cols], NT, preferred_element_type=jnp.float32)
        grad = grad + lax.dot_general(out[:, cols], pout[:, cols], NT, preferred_element_type=jnp.float32)
    count = rows // seq_len
    reps = LANES // rank_dim
    lengths_copy.wait()
    position = lax.broadcasted_iota(jnp.int32, (rows, rank_dim), 0)
    masked = []
    for e in range(count):
        first = e * seq_len
        live = (position >= first) & (position < first + lengths_ref[e])
        masked.append(jnp.where(live, grad, 0.0))
    outer = lax.dot_general(
        jnp.concatenate(masked, axis=1),
        jnp.concatenate([feat] * reps, axis=1),
        (((0,), (0,)), ((), ())),
        precision=lax.Precision.HIGHEST,
        preferred_element_type=jnp.float32,
    )
    band = lax.broadcasted_iota(jnp.int32, (SUBLANES, LANES), 1) // rank_dim
    for e in range(count):
        entry = outer[e * rank_dim : e * rank_dim + SUBLANES]
        for b in range(1, reps):
            first = e * rank_dim + b * SUBLANES
            entry = jnp.where(band == b, outer[first : first + SUBLANES], entry)
        sketch_ref[e * SUBLANES : (e + 1) * SUBLANES] = entry


def sketch_rows(activations, out_grads, project_in, project_out, lengths):
    count, seq_len, width = activations.shape
    rank_dim = project_in.shape[1]
    rows = count * seq_len
    chunks = 8
    bounds = [n * (width // chunks) for n in range(chunks + 1)]
    return pl.pallas_call(
        functools.partial(sketch_kernel, bounds, seq_len),
        out_shape=jax.ShapeDtypeStruct((count * SUBLANES, LANES), jnp.float32),
        in_specs=[pl.BlockSpec(memory_space=pltpu.HBM)] * 5,
        out_specs=pl.BlockSpec(memory_space=pltpu.VMEM),
        scratch_shapes=[
            pltpu.VMEM((rows, width), jnp.bfloat16),
            pltpu.VMEM((rows, width), jnp.bfloat16),
            pltpu.VMEM((rank_dim, width), jnp.bfloat16),
            pltpu.VMEM((rank_dim, width), jnp.bfloat16),
            pltpu.SMEM((count,), jnp.int32),
            pltpu.SemaphoreType.DMA((4, chunks)),
            pltpu.SemaphoreType.DMA,
        ],
        compiler_params=pltpu.CompilerParams(vmem_limit_bytes=16 * 2**20),
    )(
        *(
            pltpu.with_memory_space_constraint(operand, pltpu.HBM)
            for operand in (
                activations.reshape(rows, width),
                out_grads.reshape(rows, width),
                project_in.T,
                project_out.T,
                lengths,
            )
        ),
    )


def solve_first(system):
    step = 4

    def spread(column):
        return [jnp.broadcast_to(tile[:, column : column + 1], tile.shape) for tile in system]

    def row_of(tiles, number):
        tile = tiles[number // SUBLANES]
        return jnp.broadcast_to(tile[number % SUBLANES : number % SUBLANES + 1], tile.shape)

    def factor(columns, first):
        p = {(i, j): row_of(columns[j], first + i) for j in range(step) for i in range(j + 1)}
        lower, inverse = {}, []
        for k in range(step):
            inverse.append(pl.reciprocal(p[k, k]))
            for i in range(k + 1, step):
                lower[i, k] = p[k, i] * inverse[k]
            for i in range(k + 1, step):
                for j in range(i, step):
                    p[i, j] = p[i, j] - lower[i, k] * p[k, j]
        return lower, inverse

    def forward(lower, parts):
        parts = list(parts)
        for k in range(step):
            for i in range(k + 1, step):
                parts[i] = [part - lower[i, k] * other for part, other in zip(parts[i], parts[k])]
        return parts

    def update(tiles, columns, lower, inverse, rows):
        rows = forward(lower, [[r] for r in rows])
        for column, row, scale in zip(columns, rows, inverse):
            done = row[0] * scale
            tiles = [tile - c * done for tile, c in zip(tiles, column)]
        return tiles

    count = len(system) * SUBLANES
    columns = [spread(j) for j in range(count - step, count)]
    for first in range(count - step, 0, -step):
        pivots = range(first, first + step)
        left = pl.cdiv(first, SUBLANES)
        lower, inverse = factor(columns, first)
        columns = forward(lower, [c[:left] for c in columns])
        following = []
        for j in range(first - step, first):
            column = spread(j)
            following.append(update(column[:left], columns, lower, inverse, [row_of(column, i) for i in pivots]))
        system = update(system[:left], columns, lower, inverse, [row_of(system, i) for i in pivots])
        columns = following
    lower, inverse = factor(columns, 0)
    rows = forward(lower, [[row_of(system, i)] for i in range(step)])
    solved = [row[0] * scale for row, scale in zip(rows, inverse)]
    for k in reversed(range(step)):
        for i in range(k):
            solved[i] = solved[i] - lower[k, i] * solved[k]
    return solved


def gray(n):
    return n ^ (n >> 1)


def solve_kernel(per_dev, inner, axis, *refs):
    tiles, (query_ref, scores_ref, gram_ref) = refs[:-3], refs[-3:]
    nq = query_ref.shape[1]
    part = tiles[0].shape[0] // SUBLANES
    examples = len(tiles) * part
    outer = examples // (inner * per_dev)
    fisher_dim = SUBLANES * LANES
    gram_ref[...] = jnp.zeros(gram_ref.shape, jnp.float32)
    slot = (query_ref[...] // per_dev) ^ lax.axis_index(axis)
    place = (gray(slot % inner) * outer + (outer - slot // inner) % outer) * per_dev + query_ref[...] % per_dev
    rest = LANES - examples - nq
    place = jnp.concatenate(
        [jnp.zeros((1, examples), jnp.int32), place] + ([jnp.zeros((1, rest), jnp.int32)] if rest else []), axis=1
    )
    lane = lax.broadcasted_iota(jnp.int32, (SUBLANES, LANES), 1)
    source = jnp.where(lane < examples, lane, jnp.broadcast_to(place, lane.shape))
    sketches = jnp.concatenate(
        [
            jnp.concatenate([tile[pl.ds(s, part, stride=SUBLANES)] for tile in tiles], axis=0)
            for s in range(SUBLANES)
        ],
        axis=1,
    )
    squares = jnp.sum(jnp.sum(sketches * sketches, axis=0, keepdims=True), axis=1, keepdims=True)
    scale = jnp.broadcast_to(1.0 / squares, (SUBLANES, LANES))
    gram_ref[:, :examples] = lax.dot_general(
        sketches, sketches, NT, precision=lax.Precision.HIGHEST, preferred_element_type=jnp.float32
    )
    row = lax.broadcasted_iota(jnp.int32, (SUBLANES, LANES), 0)
    system = []
    for first in range(0, examples, SUBLANES):
        tile = jnp.take_along_axis(gram_ref[first : first + SUBLANES], source, axis=1) * scale
        system.append(jnp.where(lane == row + first, tile + damp_ratio / fisher_dim, tile))
    solved = solve_first(system)
    scores = solved[0]
    for i in range(1, len(solved)):
        scores = jnp.where(row == i, solved[i], scores)
    scores_ref[...] = scores[:per_dev, examples : examples + nq]


def gram_scores(tiles, query_index, per_dev, inner, axis):
    nq = query_index.shape[0]
    examples = len(tiles) * tiles[0].shape[0] // SUBLANES
    return pl.pallas_call(
        functools.partial(solve_kernel, per_dev, inner, axis),
        out_shape=jax.ShapeDtypeStruct((per_dev, nq), jnp.float32),
        in_specs=[pl.BlockSpec(memory_space=pltpu.VMEM)] * (len(tiles) + 1),
        out_specs=pl.BlockSpec(memory_space=pltpu.VMEM),
        scratch_shapes=[pltpu.VMEM((examples, LANES), jnp.float32)],
        compiler_params=pltpu.CompilerParams(vmem_limit_bytes=8 * 2**20),
    )(*tiles, query_index.reshape(1, nq))


def gather_xor(tiles, axis, size, inner):
    def swap(block, slot, senders=range(size)):
        return lax.ppermute(block, axis, [(i, i ^ slot) for i in senders])

    outer = size // inner
    late = size - inner
    last = swap(tiles, late, range(late))
    near = [swap(tiles, n * inner) for n in range(outer - 2, 0, -1)]
    parts = [(0, tiles), (1, last)] + list(enumerate(near, 2)) + [(1, swap(tiles, late, range(late, size)))]
    rows = tiles.shape[0]
    column = functools.reduce(
        jnp.add, [jnp.pad(part, ((n * rows, (outer - 1 - n) * rows), (0, 0))) for n, part in parts]
    )
    return [column] + [swap(column, n) for n in sorted(range(1, inner), key=gray)]


def large_scores(tiles, query_index, per_dev, axis):
    sketches = tiles.reshape(-1, SUBLANES * LANES)
    gram = jnp.dot(sketches, sketches.T, precision=lax.Precision.HIGHEST)
    examples, fisher_dim = sketches.shape
    damping = damp_ratio * jnp.trace(gram) / fisher_dim
    factor = jnp.linalg.cholesky(gram + damping * jnp.eye(examples, dtype=jnp.float32))
    mine = lax.dynamic_slice_in_dim(gram, lax.axis_index(axis) * per_dev, per_dev, 0)
    half = lax.linalg.triangular_solve(factor, mine.T, left_side=True, lower=True)
    solved = lax.linalg.triangular_solve(factor, half, left_side=True, lower=True, transpose_a=True)
    selector = (query_index[:, None] == jnp.arange(examples, dtype=jnp.int32)[None, :]).astype(jnp.float32)
    return jnp.dot(selector, solved, precision=lax.Precision.HIGHEST).T


def local(activations, out_grads, project_in, project_out, lengths, query_index):
    per_dev = activations.shape[0]
    size = lax.axis_size("dp")
    tiles = sketch_rows(activations, out_grads, project_in, project_out, lengths)
    if size * per_dev + query_index.shape[0] <= LANES:
        inner = 4
        return gram_scores(gather_xor(tiles, "dp", size, inner), query_index, per_dev, inner, "dp")
    return large_scores(lax.all_gather(tiles, "dp", axis=0, tiled=True), query_index, per_dev, "dp")


def solution(mesh):
    return jax.shard_map(
        local,
        mesh=mesh,
        in_specs=(
            P(("groups", "dp"), None, None),
            P(("groups", "dp"), None, None),
            P(),
            P(),
            P(("groups", "dp")),
            P("groups"),
        ),
        out_specs=P(("groups", "dp"), None),
        check_vma=False,
    )
```

```python
import functools

import jax
import jax.numpy as jnp
from jax import lax
from jax.experimental import pallas as pl
from jax.experimental.pallas import tpu as pltpu
from jax.sharding import PartitionSpec as P

damp_ratio = 0.5
LANES = 128
SUBLANES = 8
NT = (((1,), (1,)), ((), ()))


def sketch_kernel(bounds, seq_len, act_hbm, out_hbm, pin_hbm, pout_hbm, lengths_hbm, sketch_ref, act, out, pin, pout, lengths_ref, sems, lengths_sem):
    rows, width = act.shape
    rank_dim = pin.shape[0]
    chunks = len(bounds) - 1
    lengths_copy = pltpu.make_async_copy(lengths_hbm, lengths_ref, lengths_sem)
    lengths_copy.start()
    copies = []
    for c in range(chunks):
        cols = pl.ds(bounds[c], bounds[c + 1] - bounds[c])
        copies.append(
            [
                pltpu.make_async_copy(src.at[:, cols], dst.at[:, cols], sems.at[n, c])
                for n, (src, dst) in enumerate(
                    ((pin_hbm, pin), (act_hbm, act), (pout_hbm, pout), (out_hbm, out))
                )
            ]
        )
        for copy in copies[-1]:
            copy.start()
    feat = jnp.zeros((rows, rank_dim), jnp.float32)
    grad = jnp.zeros((rank_dim, rows), jnp.float32)
    for c in range(chunks):
        cols = slice(bounds[c], bounds[c + 1])
        for copy in copies[c]:
            copy.wait()
        feat = feat + lax.dot_general(act[:, cols], pin[:, cols], NT, preferred_element_type=jnp.float32)
        grad = grad + lax.dot_general(pout[:, cols], out[:, cols], NT, preferred_element_type=jnp.float32)
    count = rows // seq_len
    reps = LANES // rank_dim
    lengths_copy.wait()
    position = lax.broadcasted_iota(jnp.int32, (rank_dim, rows), 1)
    masked = []
    for e in range(count):
        first = e * seq_len
        live = (position >= first) & (position < first + lengths_ref[e])
        masked.append(jnp.where(live, grad, 0.0))
    outer = lax.dot_general(
        jnp.concatenate(masked, axis=0),
        jnp.concatenate([feat] * reps, axis=1),
        (((1,), (0,)), ((), ())),
        precision=lax.Precision.HIGHEST,
        preferred_element_type=jnp.float32,
    )
    band = lax.broadcasted_iota(jnp.int32, (SUBLANES, LANES), 1) // rank_dim
    for e in range(count):
        entry = outer[e * rank_dim : e * rank_dim + SUBLANES]
        for b in range(1, reps):
            first = e * rank_dim + b * SUBLANES
            entry = jnp.where(band == b, outer[first : first + SUBLANES], entry)
        sketch_ref[e * SUBLANES : (e + 1) * SUBLANES] = entry


def sketch_rows(activations, out_grads, project_in, project_out, lengths):
    count, seq_len, width = activations.shape
    rank_dim = project_in.shape[1]
    rows = count * seq_len
    unit = width // 32
    bounds = [n * unit for n in (0, 1, 4, 8, 12, 16, 20, 24, 28, 32)]
    chunks = len(bounds) - 1
    return pl.pallas_call(
        functools.partial(sketch_kernel, bounds, seq_len),
        out_shape=jax.ShapeDtypeStruct((count * SUBLANES, LANES), jnp.float32),
        in_specs=[pl.BlockSpec(memory_space=pltpu.HBM)] * 5,
        out_specs=pl.BlockSpec(memory_space=pltpu.VMEM),
        scratch_shapes=[
            pltpu.VMEM((rows, width), jnp.bfloat16),
            pltpu.VMEM((rows, width), jnp.bfloat16),
            pltpu.VMEM((rank_dim, width), jnp.bfloat16),
            pltpu.VMEM((rank_dim, width), jnp.bfloat16),
            pltpu.SMEM((count,), jnp.int32),
            pltpu.SemaphoreType.DMA((4, chunks)),
            pltpu.SemaphoreType.DMA,
        ],
        compiler_params=pltpu.CompilerParams(vmem_limit_bytes=16 * 2**20),
    )(
        *(
            pltpu.with_memory_space_constraint(operand, pltpu.HBM)
            for operand in (
                activations.reshape(rows, width),
                out_grads.reshape(rows, width),
                project_in.T,
                project_out.T,
                lengths,
            )
        ),
    )


def solve_first(system):
    step = 4

    def spread(column):
        return [jnp.broadcast_to(tile[:, column : column + 1], tile.shape) for tile in system]

    def row_of(tiles, number):
        tile = tiles[number // SUBLANES]
        return jnp.broadcast_to(tile[number % SUBLANES : number % SUBLANES + 1], tile.shape)

    def factor(columns, first):
        p = {(i, j): row_of(columns[j], first + i) for j in range(step) for i in range(j + 1)}
        lower, inverse = {}, []
        for k in range(step):
            inverse.append(pl.reciprocal(p[k, k]))
            for i in range(k + 1, step):
                lower[i, k] = p[k, i] * inverse[k]
            for i in range(k + 1, step):
                for j in range(i, step):
                    p[i, j] = p[i, j] - lower[i, k] * p[k, j]
        return lower, inverse

    def forward(lower, parts):
        parts = list(parts)
        for k in range(step):
            for i in range(k + 1, step):
                parts[i] = [part - lower[i, k] * other for part, other in zip(parts[i], parts[k])]
        return parts

    def update(tiles, columns, lower, inverse, rows):
        rows = forward(lower, [[r] for r in rows])
        for column, row, scale in zip(columns, rows, inverse):
            done = row[0] * scale
            tiles = [tile - c * done for tile, c in zip(tiles, column)]
        return tiles

    count = len(system) * SUBLANES
    columns = [spread(j) for j in range(count - step, count)]
    for first in range(count - step, 0, -step):
        pivots = range(first, first + step)
        left = pl.cdiv(first, SUBLANES)
        lower, inverse = factor(columns, first)
        columns = forward(lower, [c[:left] for c in columns])
        following = []
        for j in range(first - step, first):
            column = spread(j)
            following.append(update(column[:left], columns, lower, inverse, [row_of(column, i) for i in pivots]))
        system = update(system[:left], columns, lower, inverse, [row_of(system, i) for i in pivots])
        columns = following
    lower, inverse = factor(columns, 0)
    rows = forward(lower, [[row_of(system, i)] for i in range(step)])
    solved = [row[0] * scale for row, scale in zip(rows, inverse)]
    for k in reversed(range(step)):
        for i in range(k):
            solved[i] = solved[i] - lower[k, i] * solved[k]
    return solved


def solve_kernel(per_dev, inner, axis, *refs):
    tiles, (query_ref, scores_ref, gram_ref) = refs[:-3], refs[-3:]
    nq = query_ref.shape[1]
    part = tiles[0].shape[0] // SUBLANES
    examples = len(tiles) * part
    outer = examples // (inner * per_dev)
    fisher_dim = SUBLANES * LANES
    gram_ref[...] = jnp.zeros(gram_ref.shape, jnp.float32)
    slot = (query_ref[...] // per_dev) ^ lax.axis_index(axis)
    place = (gray(slot % inner) * outer + gray(slot // inner)) * per_dev + query_ref[...] % per_dev
    rest = LANES - examples - nq
    place = jnp.concatenate(
        [jnp.zeros((1, examples), jnp.int32), place] + ([jnp.zeros((1, rest), jnp.int32)] if rest else []), axis=1
    )
    lane = lax.broadcasted_iota(jnp.int32, (SUBLANES, LANES), 1)
    source = jnp.where(lane < examples, lane, jnp.broadcast_to(place, lane.shape))
    sketches = jnp.concatenate(
        [
            jnp.concatenate([tile[pl.ds(s, part, stride=SUBLANES)] for tile in tiles], axis=0)
            for s in range(SUBLANES)
        ],
        axis=1,
    )
    squares = jnp.sum(jnp.sum(sketches * sketches, axis=0, keepdims=True), axis=1, keepdims=True)
    scale = jnp.broadcast_to(1.0 / squares, (SUBLANES, LANES))
    gram_ref[:, :examples] = lax.dot_general(
        sketches, sketches, NT, precision=lax.Precision.HIGHEST, preferred_element_type=jnp.float32
    )
    row = lax.broadcasted_iota(jnp.int32, (SUBLANES, LANES), 0)
    system = []
    for first in range(0, examples, SUBLANES):
        tile = jnp.take_along_axis(gram_ref[first : first + SUBLANES], source, axis=1) * scale
        system.append(jnp.where(lane == row + first, tile + damp_ratio / fisher_dim, tile))
    solved = solve_first(system)
    scores = solved[0]
    for i in range(1, len(solved)):
        scores = jnp.where(row == i, solved[i], scores)
    scores_ref[...] = scores[:per_dev, examples : examples + nq]


def gram_scores(tiles, query_index, per_dev, inner, axis):
    nq = query_index.shape[0]
    examples = len(tiles) * tiles[0].shape[0] // SUBLANES
    return pl.pallas_call(
        functools.partial(solve_kernel, per_dev, inner, axis),
        out_shape=jax.ShapeDtypeStruct((per_dev, nq), jnp.float32),
        in_specs=[pl.BlockSpec(memory_space=pltpu.VMEM)] * (len(tiles) + 1),
        out_specs=pl.BlockSpec(memory_space=pltpu.VMEM),
        scratch_shapes=[pltpu.VMEM((examples, LANES), jnp.float32)],
        compiler_params=pltpu.CompilerParams(vmem_limit_bytes=8 * 2**20),
    )(*tiles, query_index.reshape(1, nq))


def gray(n):
    return n ^ (n >> 1)


def gather_xor(tiles, axis, size, inner):
    def swap_all(block, unit, count):
        order = sorted(range(1, count), key=gray)
        return [block] + [lax.ppermute(block, axis, [(i, i ^ n * unit) for i in range(size)]) for n in order]

    return swap_all(jnp.concatenate(swap_all(tiles, inner, size // inner), axis=0), 1, inner)


def large_scores(tiles, query_index, per_dev, axis):
    sketches = tiles.reshape(-1, SUBLANES * LANES)
    gram = jnp.dot(sketches, sketches.T, precision=lax.Precision.HIGHEST)
    examples, fisher_dim = sketches.shape
    damping = damp_ratio * jnp.trace(gram) / fisher_dim
    factor = jnp.linalg.cholesky(gram + damping * jnp.eye(examples, dtype=jnp.float32))
    mine = lax.dynamic_slice_in_dim(gram, lax.axis_index(axis) * per_dev, per_dev, 0)
    half = lax.linalg.triangular_solve(factor, mine.T, left_side=True, lower=True)
    solved = lax.linalg.triangular_solve(factor, half, left_side=True, lower=True, transpose_a=True)
    selector = (query_index[:, None] == jnp.arange(examples, dtype=jnp.int32)[None, :]).astype(jnp.float32)
    return jnp.dot(selector, solved, precision=lax.Precision.HIGHEST).T


def local(activations, out_grads, project_in, project_out, lengths, query_index):
    per_dev = activations.shape[0]
    size = lax.axis_size("dp")
    tiles = sketch_rows(activations, out_grads, project_in, project_out, lengths)
    if size * per_dev + query_index.shape[0] <= LANES:
        inner = 4
        return gram_scores(gather_xor(tiles, "dp", size, inner), query_index, per_dev, inner, "dp")
    return large_scores(lax.all_gather(tiles, "dp", axis=0, tiled=True), query_index, per_dev, "dp")


def solution(mesh):
    return jax.shard_map(
        local,
        mesh=mesh,
        in_specs=(
            P(("groups", "dp"), None, None),
            P(("groups", "dp"), None, None),
            P(),
            P(),
            P(("groups", "dp")),
            P("groups"),
        ),
        out_specs=P(("groups", "dp"), None),
        check_vma=False,
    )
```

```python
import functools

import jax
import jax.numpy as jnp
from jax import lax
from jax.experimental import pallas as pl
from jax.experimental.pallas import tpu as pltpu
from jax.sharding import PartitionSpec as P

damp_ratio = 0.5
LANES = 128
SUBLANES = 8
NT = (((1,), (1,)), ((), ()))


def sketch_kernel(bounds, seq_len, act_hbm, out_hbm, pin_hbm, pout_hbm, lengths_hbm, sketch_ref, act, out, pin, pout, lengths_ref, sems, lengths_sem):
    rows, width = act.shape
    rank_dim = pin.shape[0]
    chunks = len(bounds) - 1
    lengths_copy = pltpu.make_async_copy(lengths_hbm, lengths_ref, lengths_sem)
    lengths_copy.start()
    copies = []
    for c in range(chunks):
        cols = pl.ds(bounds[c], bounds[c + 1] - bounds[c])
        copies.append(
            [
                pltpu.make_async_copy(src.at[:, cols], dst.at[:, cols], sems.at[n, c])
                for n, (src, dst) in enumerate(
                    ((pin_hbm, pin), (act_hbm, act), (pout_hbm, pout), (out_hbm, out))
                )
            ]
        )
        for copy in copies[-1]:
            copy.start()
    feat = jnp.zeros((rows, rank_dim), jnp.float32)
    grad = jnp.zeros((rank_dim, rows), jnp.float32)
    for c in range(chunks):
        cols = slice(bounds[c], bounds[c + 1])
        for copy in copies[c]:
            copy.wait()
        feat = feat + lax.dot_general(act[:, cols], pin[:, cols], NT, preferred_element_type=jnp.float32)
        grad = grad + lax.dot_general(pout[:, cols], out[:, cols], NT, preferred_element_type=jnp.float32)
    lengths_copy.wait()
    count = rows // seq_len
    reps = LANES // rank_dim
    position = lax.broadcasted_iota(jnp.int32, (rows, LANES), 0)
    band = lax.broadcasted_iota(jnp.int32, (rows, LANES), 1) // rank_dim
    live = jnp.zeros((rows, LANES), jnp.bool_)
    for e in range(count):
        first = e * seq_len
        live = live | ((band == e) & (position >= first) & (position < first + lengths_ref[e]))
    outer = lax.dot_general(
        grad,
        jnp.where(live, jnp.concatenate([feat] * reps, axis=1), 0.0),
        (((1,), (0,)), ((), ())),
        precision=lax.Precision.HIGHEST,
        preferred_element_type=jnp.float32,
    )
    band = band[:SUBLANES]
    for e in range(count):
        entry = None
        for b in range(reps):
            part = outer[b * SUBLANES : (b + 1) * SUBLANES]
            if b != e:
                part = pltpu.roll(part, (b - e) * rank_dim % LANES, 1)
            entry = part if entry is None else jnp.where(band == b, part, entry)
        sketch_ref[e * SUBLANES : (e + 1) * SUBLANES] = entry


def sketch_rows(activations, out_grads, project_in, project_out, lengths):
    count, seq_len, width = activations.shape
    rank_dim = project_in.shape[1]
    rows = count * seq_len
    unit = width // 32
    bounds = [n * unit for n in (0, 2, 6, 10, 14, 18, 22, 26, 30, 32)]
    chunks = len(bounds) - 1
    return pl.pallas_call(
        functools.partial(sketch_kernel, bounds, seq_len),
        out_shape=jax.ShapeDtypeStruct((count * SUBLANES, LANES), jnp.float32),
        in_specs=[pl.BlockSpec(memory_space=pltpu.HBM)] * 5,
        out_specs=pl.BlockSpec(memory_space=pltpu.VMEM),
        scratch_shapes=[
            pltpu.VMEM((rows, width), jnp.bfloat16),
            pltpu.VMEM((rows, width), jnp.bfloat16),
            pltpu.VMEM((rank_dim, width), jnp.bfloat16),
            pltpu.VMEM((rank_dim, width), jnp.bfloat16),
            pltpu.SMEM((count,), jnp.int32),
            pltpu.SemaphoreType.DMA((4, chunks)),
            pltpu.SemaphoreType.DMA,
        ],
        compiler_params=pltpu.CompilerParams(vmem_limit_bytes=16 * 2**20),
    )(
        *(
            pltpu.with_memory_space_constraint(operand, pltpu.HBM)
            for operand in (
                activations.reshape(rows, width),
                out_grads.reshape(rows, width),
                project_in.T,
                project_out.T,
                lengths,
            )
        ),
    )


def solve_first(system):
    step = 4

    def spread(column):
        return [jnp.broadcast_to(tile[:, column : column + 1], tile.shape) for tile in system]

    def row_of(tiles, number):
        tile = tiles[number // SUBLANES]
        return jnp.broadcast_to(tile[number % SUBLANES : number % SUBLANES + 1], tile.shape)

    def factor(columns, first):
        p = {(i, j): row_of(columns[j], first + i) for j in range(step) for i in range(j + 1)}
        lower, inverse = {}, []
        for k in range(step):
            inverse.append(pl.reciprocal(p[k, k]))
            for i in range(k + 1, step):
                lower[i, k] = p[k, i] * inverse[k]
            for i in range(k + 1, step):
                for j in range(i, step):
                    p[i, j] = p[i, j] - lower[i, k] * p[k, j]
        return lower, inverse

    def forward(lower, parts):
        parts = list(parts)
        for k in range(step):
            for i in range(k + 1, step):
                parts[i] = [part - lower[i, k] * other for part, other in zip(parts[i], parts[k])]
        return parts

    def update(tiles, columns, lower, inverse, rows):
        rows = forward(lower, [[r] for r in rows])
        for column, row, scale in zip(columns, rows, inverse):
            done = row[0] * scale
            tiles = [tile - c * done for tile, c in zip(tiles, column)]
        return tiles

    count = len(system) * SUBLANES
    columns = [spread(j) for j in range(count - step, count)]
    for first in range(count - step, 0, -step):
        pivots = range(first, first + step)
        left = pl.cdiv(first, SUBLANES)
        lower, inverse = factor(columns, first)
        columns = forward(lower, [c[:left] for c in columns])
        following = []
        for j in range(first - step, first):
            column = spread(j)
            following.append(update(column[:left], columns, lower, inverse, [row_of(column, i) for i in pivots]))
        system = update(system[:left], columns, lower, inverse, [row_of(system, i) for i in pivots])
        columns = following
    lower, inverse = factor(columns, 0)
    rows = forward(lower, [[row_of(system, i)] for i in range(step)])
    solved = [row[0] * scale for row, scale in zip(rows, inverse)]
    for k in reversed(range(step)):
        for i in range(k):
            solved[i] = solved[i] - lower[k, i] * solved[k]
    return solved


def gram(x):
    high = x.astype(jnp.bfloat16)
    rest = x - high.astype(jnp.float32)
    middle = rest.astype(jnp.bfloat16)
    low = (rest - middle.astype(jnp.float32)).astype(jnp.bfloat16)
    parts = [high, middle, low]
    count = x.shape[0]
    terms = []
    for n, held in enumerate(parts):
        streamed = jnp.concatenate(parts[: len(parts) - n], axis=0)
        product = lax.dot_general(streamed, held, NT, preferred_element_type=jnp.float32)
        terms.append([product[k : k + count] for k in range(0, product.shape[0], count)])
    (hh, mh, lh), (hm, mm), (hl,) = terms
    return hh + ((mh + hm) + (lh + hl + mm))


def solve_kernel(per_dev, inner, axis, *refs):
    tiles, (query_ref, scores_ref, gram_ref) = refs[:-3], refs[-3:]
    nq = query_ref.shape[1]
    part = tiles[0].shape[0] // SUBLANES
    examples = len(tiles) * part
    outer = examples // (inner * per_dev)
    fisher_dim = SUBLANES * LANES
    gram_ref[...] = jnp.zeros(gram_ref.shape, jnp.float32)
    slot = (query_ref[...] // per_dev) ^ lax.axis_index(axis)
    place = (gray(slot % inner) * outer + gray(slot // inner)) * per_dev + query_ref[...] % per_dev
    rest = LANES - examples - nq
    place = jnp.concatenate(
        [jnp.zeros((1, examples), jnp.int32), place] + ([jnp.zeros((1, rest), jnp.int32)] if rest else []), axis=1
    )
    lane = lax.broadcasted_iota(jnp.int32, (SUBLANES, LANES), 1)
    source = jnp.where(lane < examples, lane, jnp.broadcast_to(place, lane.shape))
    sketches = jnp.concatenate(
        [
            jnp.concatenate([tile[pl.ds(s, part, stride=SUBLANES)] for tile in tiles], axis=0)
            for s in range(SUBLANES)
        ],
        axis=1,
    )
    squares = jnp.sum(jnp.sum(sketches * sketches, axis=0, keepdims=True), axis=1, keepdims=True)
    scale = jnp.broadcast_to(1.0 / squares, (SUBLANES, LANES))
    gram_ref[:, :examples] = gram(sketches)
    row = lax.broadcasted_iota(jnp.int32, (SUBLANES, LANES), 0)
    system = []
    for first in range(0, examples, SUBLANES):
        tile = jnp.take_along_axis(gram_ref[first : first + SUBLANES], source, axis=1) * scale
        system.append(jnp.where(lane == row + first, tile + damp_ratio / fisher_dim, tile))
    solved = solve_first(system)
    scores = solved[0]
    for i in range(1, len(solved)):
        scores = jnp.where(row == i, solved[i], scores)
    scores_ref[...] = scores[:per_dev, examples : examples + nq]


def gram_scores(tiles, query_index, per_dev, inner, axis):
    nq = query_index.shape[0]
    examples = len(tiles) * tiles[0].shape[0] // SUBLANES
    return pl.pallas_call(
        functools.partial(solve_kernel, per_dev, inner, axis),
        out_shape=jax.ShapeDtypeStruct((per_dev, nq), jnp.float32),
        in_specs=[pl.BlockSpec(memory_space=pltpu.VMEM)] * (len(tiles) + 1),
        out_specs=pl.BlockSpec(memory_space=pltpu.VMEM),
        scratch_shapes=[pltpu.VMEM((examples, LANES), jnp.float32)],
        compiler_params=pltpu.CompilerParams(vmem_limit_bytes=8 * 2**20),
    )(*tiles, query_index.reshape(1, nq))


def gray(n):
    return n ^ (n >> 1)


def gather_xor(tiles, axis, size, inner):
    def swap_all(block, unit, count):
        order = sorted(range(1, count), key=gray)
        return [block] + [lax.ppermute(block, axis, [(i, i ^ n * unit) for i in range(size)]) for n in order]

    return swap_all(jnp.concatenate(swap_all(tiles, inner, size // inner), axis=0), 1, inner)


def large_scores(tiles, query_index, per_dev, axis):
    sketches = tiles.reshape(-1, SUBLANES * LANES)
    gram = jnp.dot(sketches, sketches.T, precision=lax.Precision.HIGHEST)
    examples, fisher_dim = sketches.shape
    damping = damp_ratio * jnp.trace(gram) / fisher_dim
    factor = jnp.linalg.cholesky(gram + damping * jnp.eye(examples, dtype=jnp.float32))
    mine = lax.dynamic_slice_in_dim(gram, lax.axis_index(axis) * per_dev, per_dev, 0)
    half = lax.linalg.triangular_solve(factor, mine.T, left_side=True, lower=True)
    solved = lax.linalg.triangular_solve(factor, half, left_side=True, lower=True, transpose_a=True)
    selector = (query_index[:, None] == jnp.arange(examples, dtype=jnp.int32)[None, :]).astype(jnp.float32)
    return jnp.dot(selector, solved, precision=lax.Precision.HIGHEST).T


def local(activations, out_grads, project_in, project_out, lengths, query_index):
    per_dev = activations.shape[0]
    size = lax.axis_size("dp")
    tiles = sketch_rows(activations, out_grads, project_in, project_out, lengths)
    if size * per_dev + query_index.shape[0] <= LANES:
        inner = 4
        return gram_scores(gather_xor(tiles, "dp", size, inner), query_index, per_dev, inner, "dp")
    return large_scores(lax.all_gather(tiles, "dp", axis=0, tiled=True), query_index, per_dev, "dp")


def solution(mesh):
    return jax.shard_map(
        local,
        mesh=mesh,
        in_specs=(
            P(("groups", "dp"), None, None),
            P(("groups", "dp"), None, None),
            P(),
            P(),
            P(("groups", "dp")),
            P("groups"),
        ),
        out_specs=P(("groups", "dp"), None),
        check_vma=False,
    )
```

```python
import functools

import jax
import jax.numpy as jnp
from jax import lax
from jax.experimental import pallas as pl
from jax.experimental.pallas import tpu as pltpu
from jax.sharding import PartitionSpec as P

damp_ratio = 0.5
LANES = 128
SUBLANES = 8
NT = (((1,), (1,)), ((), ()))


def sketch_kernel(bounds, seq_len, act_hbm, out_hbm, pin_hbm, pout_hbm, lengths_hbm, sketch_ref, act, out, pin, pout, lengths_ref, sems, lengths_sem):
    rows, width = act.shape
    rank_dim = pin.shape[0]
    chunks = len(bounds) - 1
    lengths_copy = pltpu.make_async_copy(lengths_hbm, lengths_ref, lengths_sem)
    lengths_copy.start()
    count = rows // seq_len

    def copies(c, lengths):
        cols = pl.ds(bounds[c], bounds[c + 1] - bounds[c])
        parts = [(pin_hbm, pin, slice(None)), (pout_hbm, pout, slice(None))]
        for src, dst in ((act_hbm, act), (out_hbm, out)):
            if lengths is None:
                parts.append((src, dst, slice(None)))
            else:
                parts += [(src, dst, pl.ds(e * seq_len, lengths[e])) for e in range(count)]
        return [
            pltpu.make_async_copy(src.at[part, cols], dst.at[part, cols], sems.at[n, c])
            for n, (src, dst, part) in enumerate(parts)
        ]

    full = 3
    started = [copies(c, None) for c in range(full)]
    for copy in sum(started, []):
        copy.start()
    lengths_copy.wait()
    lengths = [pl.multiple_of((lengths_ref[e] + 15) // 16 * 16, 16) for e in range(count)]
    started += [copies(c, lengths) for c in range(full, chunks)]
    feat = jnp.zeros((rows, rank_dim), jnp.float32)
    grad = jnp.zeros((rank_dim, rows), jnp.float32)
    for c in range(chunks):
        cols = slice(bounds[c], bounds[c + 1])
        if full + c < chunks:
            for copy in started[full + c]:
                copy.start()
        for copy in started[c]:
            copy.wait()
        feat = feat + lax.dot_general(act[:, cols], pin[:, cols], NT, preferred_element_type=jnp.float32)
        grad = grad + lax.dot_general(pout[:, cols], out[:, cols], NT, preferred_element_type=jnp.float32)
    reps = LANES // rank_dim
    position = lax.broadcasted_iota(jnp.int32, (rows, LANES), 0)
    band = lax.broadcasted_iota(jnp.int32, (rows, LANES), 1) // rank_dim
    live = jnp.zeros((rows, LANES), jnp.bool_)
    for e in range(count):
        first = e * seq_len
        live = live | ((band == e) & (position >= first) & (position < first + lengths_ref[e]))
    position = lax.broadcasted_iota(jnp.int32, grad.shape, 1)
    read = position < 0
    for e in range(count):
        read = read | ((position >= e * seq_len) & (position < e * seq_len + lengths_ref[e]))
    outer = lax.dot_general(
        jnp.where(read, grad, 0.0),
        jnp.where(live, jnp.concatenate([feat] * reps, axis=1), 0.0),
        (((1,), (0,)), ((), ())),
        precision=lax.Precision.HIGHEST,
        preferred_element_type=jnp.float32,
    )
    band = band[:SUBLANES]
    for e in range(count):
        entry = None
        for b in range(reps):
            part = outer[b * SUBLANES : (b + 1) * SUBLANES]
            if b != e:
                part = pltpu.roll(part, (b - e) * rank_dim % LANES, 1)
            entry = part if entry is None else jnp.where(band == b, part, entry)
        sketch_ref[e * SUBLANES : (e + 1) * SUBLANES] = entry


def sketch_rows(activations, out_grads, project_in, project_out, lengths):
    count, seq_len, width = activations.shape
    rank_dim = project_in.shape[1]
    rows = count * seq_len
    unit = width // 32
    bounds = [n * unit for n in range(0, 33, 4)]
    chunks = len(bounds) - 1
    return pl.pallas_call(
        functools.partial(sketch_kernel, bounds, seq_len),
        out_shape=jax.ShapeDtypeStruct((count * SUBLANES, LANES), jnp.float32),
        in_specs=[pl.BlockSpec(memory_space=pltpu.HBM)] * 5,
        out_specs=pl.BlockSpec(memory_space=pltpu.VMEM),
        scratch_shapes=[
            pltpu.VMEM((rows, width), jnp.bfloat16),
            pltpu.VMEM((rows, width), jnp.bfloat16),
            pltpu.VMEM((rank_dim, width), jnp.bfloat16),
            pltpu.VMEM((rank_dim, width), jnp.bfloat16),
            pltpu.SMEM((count,), jnp.int32),
            pltpu.SemaphoreType.DMA((2 + 2 * count, chunks)),
            pltpu.SemaphoreType.DMA,
        ],
        compiler_params=pltpu.CompilerParams(vmem_limit_bytes=16 * 2**20),
    )(
        *(
            pltpu.with_memory_space_constraint(operand, pltpu.HBM)
            for operand in (
                activations.reshape(rows, width),
                out_grads.reshape(rows, width),
                project_in.T,
                project_out.T,
                lengths,
            )
        ),
    )


def solve_first(system):
    step = 4

    def spread(column):
        return [jnp.broadcast_to(tile[:, column : column + 1], tile.shape) for tile in system]

    def row_of(tiles, number):
        tile = tiles[number // SUBLANES]
        return jnp.broadcast_to(tile[number % SUBLANES : number % SUBLANES + 1], tile.shape)

    def factor(columns, first):
        p = {(i, j): row_of(columns[j], first + i) for j in range(step) for i in range(j + 1)}
        lower, inverse = {}, []
        for k in range(step):
            inverse.append(pl.reciprocal(p[k, k]))
            for i in range(k + 1, step):
                lower[i, k] = p[k, i] * inverse[k]
            for i in range(k + 1, step):
                for j in range(i, step):
                    p[i, j] = p[i, j] - lower[i, k] * p[k, j]
        return lower, inverse

    def forward(lower, parts):
        parts = list(parts)
        for k in range(step):
            for i in range(k + 1, step):
                parts[i] = [part - lower[i, k] * other for part, other in zip(parts[i], parts[k])]
        return parts

    def update(tiles, columns, lower, inverse, rows):
        rows = forward(lower, [[r] for r in rows])
        for column, row, scale in zip(columns, rows, inverse):
            done = row[0] * scale
            tiles = [tile - c * done for tile, c in zip(tiles, column)]
        return tiles

    count = len(system) * SUBLANES
    columns = [spread(j) for j in range(count - step, count)]
    for first in range(count - step, 0, -step):
        pivots = range(first, first + step)
        left = pl.cdiv(first, SUBLANES)
        lower, inverse = factor(columns, first)
        columns = forward(lower, [c[:left] for c in columns])
        following = []
        for j in range(first - step, first):
            column = spread(j)
            following.append(update(column[:left], columns, lower, inverse, [row_of(column, i) for i in pivots]))
        system = update(system[:left], columns, lower, inverse, [row_of(system, i) for i in pivots])
        columns = following
    lower, inverse = factor(columns, 0)
    rows = forward(lower, [[row_of(system, i)] for i in range(step)])
    solved = [row[0] * scale for row, scale in zip(rows, inverse)]
    for k in reversed(range(step)):
        for i in range(k):
            solved[i] = solved[i] - lower[k, i] * solved[k]
    return solved


def gram(x):
    high = x.astype(jnp.bfloat16)
    rest = x - high.astype(jnp.float32)
    middle = rest.astype(jnp.bfloat16)
    low = (rest - middle.astype(jnp.float32)).astype(jnp.bfloat16)
    parts = [high, middle, low]
    count = x.shape[0]
    terms = []
    for n, held in enumerate(parts):
        streamed = jnp.concatenate(parts[: len(parts) - n], axis=0)
        product = lax.dot_general(streamed, held, NT, preferred_element_type=jnp.float32)
        terms.append([product[k : k + count] for k in range(0, product.shape[0], count)])
    (hh, mh, lh), (hm, mm), (hl,) = terms
    return hh + ((mh + hm) + (lh + hl + mm))


def solve_kernel(per_dev, inner, axis, *refs):
    tiles, (query_ref, scores_ref, gram_ref) = refs[:-3], refs[-3:]
    nq = query_ref.shape[1]
    part = tiles[0].shape[0] // SUBLANES
    examples = len(tiles) * part
    outer = examples // (inner * per_dev)
    fisher_dim = SUBLANES * LANES
    gram_ref[...] = jnp.zeros(gram_ref.shape, jnp.float32)
    slot = (query_ref[...] // per_dev) ^ lax.axis_index(axis)
    n = slot // inner
    place = (gray((slot ^ partner(n, inner)) % inner) * outer + gray(n)) * per_dev + query_ref[...] % per_dev
    rest = LANES - examples - nq
    place = jnp.concatenate(
        [jnp.zeros((1, examples), jnp.int32), place] + ([jnp.zeros((1, rest), jnp.int32)] if rest else []), axis=1
    )
    lane = lax.broadcasted_iota(jnp.int32, (SUBLANES, LANES), 1)
    source = jnp.where(lane < examples, lane, jnp.broadcast_to(place, lane.shape))
    sketches = jnp.concatenate(
        [
            jnp.concatenate([tile[pl.ds(s, part, stride=SUBLANES)] for tile in tiles], axis=0)
            for s in range(SUBLANES)
        ],
        axis=1,
    )
    squares = jnp.sum(jnp.sum(sketches * sketches, axis=0, keepdims=True), axis=1, keepdims=True)
    scale = jnp.broadcast_to(1.0 / squares, (SUBLANES, LANES))
    gram_ref[:, :examples] = gram(sketches)
    row = lax.broadcasted_iota(jnp.int32, (SUBLANES, LANES), 0)
    system = []
    for first in range(0, examples, SUBLANES):
        tile = jnp.take_along_axis(gram_ref[first : first + SUBLANES], source, axis=1) * scale
        system.append(jnp.where(lane == row + first, tile + damp_ratio / fisher_dim, tile))
    solved = solve_first(system)
    scores = solved[0]
    for i in range(1, len(solved)):
        scores = jnp.where(row == i, solved[i], scores)
    scores_ref[...] = scores[:per_dev, examples : examples + nq]


def gram_scores(tiles, query_index, per_dev, inner, axis):
    nq = query_index.shape[0]
    examples = len(tiles) * tiles[0].shape[0] // SUBLANES
    return pl.pallas_call(
        functools.partial(solve_kernel, per_dev, inner, axis),
        out_shape=jax.ShapeDtypeStruct((per_dev, nq), jnp.float32),
        in_specs=[pl.BlockSpec(memory_space=pltpu.VMEM)] * (len(tiles) + 1),
        out_specs=pl.BlockSpec(memory_space=pltpu.VMEM),
        scratch_shapes=[pltpu.VMEM((examples, LANES), jnp.float32)],
        compiler_params=pltpu.CompilerParams(vmem_limit_bytes=8 * 2**20),
    )(*tiles, query_index.reshape(1, nq))


def gray(n):
    return n ^ (n >> 1)


def partner(n, inner):
    return n * inner ^ gray(n) & 1


def gather_xor(tiles, axis, size, inner):
    def swap(block, slot):
        return lax.ppermute(block, axis, [(i, i ^ slot) for i in range(size)])

    rows = sorted(range(1, size // inner), key=gray)
    column = jnp.concatenate([tiles] + [swap(tiles, partner(n, inner)) for n in rows], axis=0)
    return [column] + [swap(column, n) for n in sorted(range(1, inner), key=gray)]


def large_scores(tiles, query_index, per_dev, axis):
    sketches = tiles.reshape(-1, SUBLANES * LANES)
    gram = jnp.dot(sketches, sketches.T, precision=lax.Precision.HIGHEST)
    examples, fisher_dim = sketches.shape
    damping = damp_ratio * jnp.trace(gram) / fisher_dim
    factor = jnp.linalg.cholesky(gram + damping * jnp.eye(examples, dtype=jnp.float32))
    mine = lax.dynamic_slice_in_dim(gram, lax.axis_index(axis) * per_dev, per_dev, 0)
    half = lax.linalg.triangular_solve(factor, mine.T, left_side=True, lower=True)
    solved = lax.linalg.triangular_solve(factor, half, left_side=True, lower=True, transpose_a=True)
    selector = (query_index[:, None] == jnp.arange(examples, dtype=jnp.int32)[None, :]).astype(jnp.float32)
    return jnp.dot(selector, solved, precision=lax.Precision.HIGHEST).T


def local(activations, out_grads, project_in, project_out, lengths, query_index):
    per_dev = activations.shape[0]
    size = lax.axis_size("dp")
    tiles = sketch_rows(activations, out_grads, project_in, project_out, lengths)
    if size * per_dev + query_index.shape[0] <= LANES:
        inner = 4
        return gram_scores(gather_xor(tiles, "dp", size, inner), query_index, per_dev, inner, "dp")
    return large_scores(lax.all_gather(tiles, "dp", axis=0, tiled=True), query_index, per_dev, "dp")


def solution(mesh):
    return jax.shard_map(
        local,
        mesh=mesh,
        in_specs=(
            P(("groups", "dp"), None, None),
            P(("groups", "dp"), None, None),
            P(),
            P(),
            P(("groups", "dp")),
            P("groups"),
        ),
        out_specs=P(("groups", "dp"), None),
        check_vma=False,
    )
```

```python
import functools

import jax
import jax.numpy as jnp
from jax import lax
from jax.experimental import pallas as pl
from jax.experimental.pallas import tpu as pltpu
from jax.sharding import PartitionSpec as P

damp_ratio = 0.5
LANES = 128
SUBLANES = 8
NT = (((1,), (1,)), ((), ()))


def sketch_kernel(act_hbm, out_hbm, pin_hbm, pout_hbm, lengths_hbm, sketch_ref, act, out, pin, pout, lengths_ref, sems, p_sems):
    count, seq_len, width = act.shape
    rank_dim = pin.shape[0]
    reps = LANES // rank_dim
    pairs = ((pin_hbm, pin, p_sems.at[0]), (pout_hbm, pout, p_sems.at[1]), (lengths_hbm, lengths_ref, p_sems.at[2]))
    copy_in, copy_out, copy_lengths = (pltpu.make_async_copy(*pair) for pair in pairs)
    acts = [pltpu.make_async_copy(act_hbm.at[e], act.at[e], sems.at[0, e]) for e in range(count)]
    outs = [pltpu.make_async_copy(out_hbm.at[e], out.at[e], sems.at[1, e]) for e in range(count)]
    copy_lengths.start()
    copy_in.start()
    acts[0].start()
    copy_out.start()
    outs[0].start()
    for e in range(1, count):
        acts[e].start()
        outs[e].start()
    copy_in.wait()
    copy_out.wait()
    copy_lengths.wait()
    position = lax.broadcasted_iota(jnp.int32, (rank_dim, seq_len), 1)
    band = lax.broadcasted_iota(jnp.int32, (SUBLANES, LANES), 1) // rank_dim
    for e in range(count):
        acts[e].wait()
        feat = lax.dot_general(act[e], pin[...], NT, preferred_element_type=jnp.float32)
        outs[e].wait()
        grad = lax.dot_general(pout[...], out[e], NT, preferred_element_type=jnp.float32)
        outer = lax.dot_general(
            jnp.where(position < lengths_ref[e], grad, 0.0),
            jnp.concatenate([feat] * reps, axis=1),
            (((1,), (0,)), ((), ())),
            precision=lax.Precision.HIGHEST,
            preferred_element_type=jnp.float32,
        )
        entry = outer[:SUBLANES]
        for b in range(1, reps):
            entry = jnp.where(band == b, outer[b * SUBLANES : (b + 1) * SUBLANES], entry)
        sketch_ref[e * SUBLANES : (e + 1) * SUBLANES] = entry


def sketch_rows(activations, out_grads, project_in, project_out, lengths):
    count, seq_len, width = activations.shape
    rank_dim = project_in.shape[1]
    return pl.pallas_call(
        sketch_kernel,
        out_shape=jax.ShapeDtypeStruct((count * SUBLANES, LANES), jnp.float32),
        in_specs=[pl.BlockSpec(memory_space=pltpu.HBM)] * 5,
        out_specs=pl.BlockSpec(memory_space=pltpu.VMEM),
        scratch_shapes=[
            pltpu.VMEM((count, seq_len, width), jnp.bfloat16),
            pltpu.VMEM((count, seq_len, width), jnp.bfloat16),
            pltpu.VMEM((rank_dim, width), jnp.bfloat16),
            pltpu.VMEM((rank_dim, width), jnp.bfloat16),
            pltpu.SMEM((count,), jnp.int32),
            pltpu.SemaphoreType.DMA((2, count)),
            pltpu.SemaphoreType.DMA((3,)),
        ],
        compiler_params=pltpu.CompilerParams(vmem_limit_bytes=16 * 2**20),
    )(
        *(
            pltpu.with_memory_space_constraint(operand, pltpu.HBM)
            for operand in (activations, out_grads, project_in.T, project_out.T, lengths)
        )
    )


def solve_first(system):
    step = 4

    def spread(column):
        return [jnp.broadcast_to(tile[:, column : column + 1], tile.shape) for tile in system]

    def row_of(tiles, number):
        tile = tiles[number // SUBLANES]
        return jnp.broadcast_to(tile[number % SUBLANES : number % SUBLANES + 1], tile.shape)

    def factor(columns, first):
        p = {(i, j): row_of(columns[j], first + i) for j in range(step) for i in range(j + 1)}
        lower, inverse = {}, []
        for k in range(step):
            inverse.append(pl.reciprocal(p[k, k]))
            for i in range(k + 1, step):
                lower[i, k] = p[k, i] * inverse[k]
            for i in range(k + 1, step):
                for j in range(i, step):
                    p[i, j] = p[i, j] - lower[i, k] * p[k, j]
        return lower, inverse

    def forward(lower, parts):
        parts = list(parts)
        for k in range(step):
            for i in range(k + 1, step):
                parts[i] = [part - lower[i, k] * other for part, other in zip(parts[i], parts[k])]
        return parts

    def update(tiles, columns, lower, inverse, rows):
        rows = forward(lower, [[r] for r in rows])
        for column, row, scale in zip(columns, rows, inverse):
            done = row[0] * scale
            tiles = [tile - c * done for tile, c in zip(tiles, column)]
        return tiles

    count = len(system) * SUBLANES
    columns = [spread(j) for j in range(count - step, count)]
    for first in range(count - step, 0, -step):
        pivots = range(first, first + step)
        left = pl.cdiv(first, SUBLANES)
        lower, inverse = factor(columns, first)
        columns = forward(lower, [c[:left] for c in columns])
        following = []
        for j in range(first - step, first):
            column = spread(j)
            following.append(update(column[:left], columns, lower, inverse, [row_of(column, i) for i in pivots]))
        system = update(system[:left], columns, lower, inverse, [row_of(system, i) for i in pivots])
        columns = following
    lower, inverse = factor(columns, 0)
    rows = forward(lower, [[row_of(system, i)] for i in range(step)])
    solved = [row[0] * scale for row, scale in zip(rows, inverse)]
    for k in reversed(range(step)):
        for i in range(k):
            solved[i] = solved[i] - lower[k, i] * solved[k]
    return solved


def gram(x):
    high = x.astype(jnp.bfloat16)
    rest = x - high.astype(jnp.float32)
    middle = rest.astype(jnp.bfloat16)
    low = (rest - middle.astype(jnp.float32)).astype(jnp.bfloat16)
    parts = [high, middle, low]
    count = x.shape[0]
    terms = []
    for n, held in enumerate(parts):
        streamed = jnp.concatenate(parts[: len(parts) - n], axis=0)
        product = lax.dot_general(streamed, held, NT, preferred_element_type=jnp.float32)
        terms.append([product[k : k + count] for k in range(0, product.shape[0], count)])
    (hh, mh, lh), (hm, mm), (hl,) = terms
    return hh + ((mh + hm) + (lh + hl + mm))


def solve_kernel(per_dev, inner, axis, *refs):
    tiles, (query_ref, scores_ref, gram_ref) = refs[:-3], refs[-3:]
    nq = query_ref.shape[1]
    part = tiles[0].shape[0] // SUBLANES
    examples = len(tiles) * part
    outer = examples // (inner * per_dev)
    fisher_dim = SUBLANES * LANES
    gram_ref[...] = jnp.zeros(gram_ref.shape, jnp.float32)
    slot = (query_ref[...] // per_dev) ^ lax.axis_index(axis)
    n = slot // inner
    place = (gray((slot ^ partner(n, inner)) % inner) * outer + gray(n)) * per_dev + query_ref[...] % per_dev
    rest = LANES - examples - nq
    place = jnp.concatenate(
        [jnp.zeros((1, examples), jnp.int32), place] + ([jnp.zeros((1, rest), jnp.int32)] if rest else []), axis=1
    )
    lane = lax.broadcasted_iota(jnp.int32, (SUBLANES, LANES), 1)
    source = jnp.where(lane < examples, lane, jnp.broadcast_to(place, lane.shape))
    sketches = jnp.concatenate(
        [
            jnp.concatenate([tile[pl.ds(s, part, stride=SUBLANES)] for tile in tiles], axis=0)
            for s in range(SUBLANES)
        ],
        axis=1,
    )
    squares = jnp.sum(jnp.sum(sketches * sketches, axis=0, keepdims=True), axis=1, keepdims=True)
    scale = jnp.broadcast_to(1.0 / squares, (SUBLANES, LANES))
    gram_ref[:, :examples] = gram(sketches)
    row = lax.broadcasted_iota(jnp.int32, (SUBLANES, LANES), 0)
    system = []
    for first in range(0, examples, SUBLANES):
        tile = jnp.take_along_axis(gram_ref[first : first + SUBLANES], source, axis=1) * scale
        system.append(jnp.where(lane == row + first, tile + damp_ratio / fisher_dim, tile))
    solved = solve_first(system)
    scores = solved[0]
    for i in range(1, len(solved)):
        scores = jnp.where(row == i, solved[i], scores)
    scores_ref[...] = scores[:per_dev, examples : examples + nq]


def gram_scores(tiles, query_index, per_dev, inner, axis):
    nq = query_index.shape[0]
    examples = len(tiles) * tiles[0].shape[0] // SUBLANES
    return pl.pallas_call(
        functools.partial(solve_kernel, per_dev, inner, axis),
        out_shape=jax.ShapeDtypeStruct((per_dev, nq), jnp.float32),
        in_specs=[pl.BlockSpec(memory_space=pltpu.VMEM)] * (len(tiles) + 1),
        out_specs=pl.BlockSpec(memory_space=pltpu.VMEM),
        scratch_shapes=[pltpu.VMEM((examples, LANES), jnp.float32)],
        compiler_params=pltpu.CompilerParams(vmem_limit_bytes=8 * 2**20),
    )(*tiles, query_index.reshape(1, nq))


def gray(n):
    return n ^ (n >> 1)


def partner(n, inner):
    return n * inner ^ gray(n) & 1


def gather_xor(tiles, axis, size, inner):
    def swap(block, slot):
        return lax.ppermute(block, axis, [(i, i ^ slot) for i in range(size)])

    rows = sorted(range(1, size // inner), key=gray)
    column = jnp.concatenate([tiles] + [swap(tiles, partner(n, inner)) for n in rows], axis=0)
    return [column] + [swap(column, n) for n in sorted(range(1, inner), key=gray)]


def large_scores(tiles, query_index, per_dev, axis):
    sketches = tiles.reshape(-1, SUBLANES * LANES)
    gram = jnp.dot(sketches, sketches.T, precision=lax.Precision.HIGHEST)
    examples, fisher_dim = sketches.shape
    damping = damp_ratio * jnp.trace(gram) / fisher_dim
    factor = jnp.linalg.cholesky(gram + damping * jnp.eye(examples, dtype=jnp.float32))
    mine = lax.dynamic_slice_in_dim(gram, lax.axis_index(axis) * per_dev, per_dev, 0)
    half = lax.linalg.triangular_solve(factor, mine.T, left_side=True, lower=True)
    solved = lax.linalg.triangular_solve(factor, half, left_side=True, lower=True, transpose_a=True)
    selector = (query_index[:, None] == jnp.arange(examples, dtype=jnp.int32)[None, :]).astype(jnp.float32)
    return jnp.dot(selector, solved, precision=lax.Precision.HIGHEST).T


def local(activations, out_grads, project_in, project_out, lengths, query_index):
    per_dev = activations.shape[0]
    size = lax.axis_size("dp")
    tiles = sketch_rows(activations, out_grads, project_in, project_out, lengths)
    if size * per_dev + query_index.shape[0] <= LANES:
        inner = 4
        return gram_scores(gather_xor(tiles, "dp", size, inner), query_index, per_dev, inner, "dp")
    return large_scores(lax.all_gather(tiles, "dp", axis=0, tiled=True), query_index, per_dev, "dp")


def solution(mesh):
    return jax.shard_map(
        local,
        mesh=mesh,
        in_specs=(
            P(("groups", "dp"), None, None),
            P(("groups", "dp"), None, None),
            P(),
            P(),
            P(("groups", "dp")),
            P("groups"),
        ),
        out_specs=P(("groups", "dp"), None),
        check_vma=False,
    )
```

```python
import functools

import jax
import jax.numpy as jnp
from jax import lax
from jax.experimental import pallas as pl
from jax.experimental.pallas import tpu as pltpu
from jax.sharding import PartitionSpec as P

damp_ratio = 0.5
LANES = 128
SUBLANES = 8
NT = (((1,), (1,)), ((), ()))


def sketch_kernel(bounds, seq_len, act_hbm, out_hbm, pin_hbm, pout_hbm, lengths_hbm, sketch_ref, rows_ref, proj, lengths_ref, sems, lengths_sem):
    rows = rows_ref.shape[0] // 2
    rank_dim = proj.shape[0] // 2
    chunks = len(bounds) - 1
    lengths_copy = pltpu.make_async_copy(lengths_hbm, lengths_ref, lengths_sem)
    lengths_copy.start()
    copies = []
    for c in range(chunks):
        cols = pl.ds(bounds[c], bounds[c + 1] - bounds[c])
        parts = (
            (pin_hbm, proj, 0, rank_dim),
            (pout_hbm, proj, rank_dim, rank_dim),
            (act_hbm, rows_ref, 0, rows),
            (out_hbm, rows_ref, rows, rows),
        )
        copies.append(
            [
                pltpu.make_async_copy(src.at[:, cols], dst.at[pl.ds(first, size), cols], sems.at[n, c])
                for n, (src, dst, first, size) in enumerate(parts)
            ]
        )
        for copy in copies[-1]:
            copy.start()
    both = jnp.zeros((2 * rank_dim, 2 * rows), jnp.float32)
    for c in range(chunks):
        cols = slice(bounds[c], bounds[c + 1])
        for copy in copies[c]:
            copy.wait()
        both = both + lax.dot_general(proj[:, cols], rows_ref[:, cols], NT, preferred_element_type=jnp.float32)
    feat, grad = both[:rank_dim, :rows], both[rank_dim:, rows:]
    lengths_copy.wait()
    count = rows // seq_len
    reps = LANES // rank_dim
    position = lax.broadcasted_iota(jnp.int32, (rank_dim, rows), 1)
    masked = []
    for e in range(count):
        first = e * seq_len
        live = (position >= first) & (position < first + lengths_ref[e])
        masked.append(jnp.where(live, feat, 0.0))
    outer = lax.dot_general(
        grad,
        jnp.concatenate(masked, axis=0),
        NT,
        precision=lax.Precision.HIGHEST,
        preferred_element_type=jnp.float32,
    )
    band = lax.broadcasted_iota(jnp.int32, (SUBLANES, LANES), 1) // rank_dim
    for e in range(count):
        entry = None
        for b in range(reps):
            part = outer[b * SUBLANES : (b + 1) * SUBLANES]
            if b != e:
                part = pltpu.roll(part, (b - e) * rank_dim % LANES, 1)
            entry = part if entry is None else jnp.where(band == b, part, entry)
        sketch_ref[e * SUBLANES : (e + 1) * SUBLANES] = entry


def sketch_rows(activations, out_grads, project_in, project_out, lengths):
    count, seq_len, width = activations.shape
    rank_dim = project_in.shape[1]
    rows = count * seq_len
    chunks = 8
    bounds = [n * (width // chunks) for n in range(chunks + 1)]
    return pl.pallas_call(
        functools.partial(sketch_kernel, bounds, seq_len),
        out_shape=jax.ShapeDtypeStruct((count * SUBLANES, LANES), jnp.float32),
        in_specs=[pl.BlockSpec(memory_space=pltpu.HBM)] * 5,
        out_specs=pl.BlockSpec(memory_space=pltpu.VMEM),
        scratch_shapes=[
            pltpu.VMEM((2 * rows, width), jnp.bfloat16),
            pltpu.VMEM((2 * rank_dim, width), jnp.bfloat16),
            pltpu.SMEM((count,), jnp.int32),
            pltpu.SemaphoreType.DMA((4, chunks)),
            pltpu.SemaphoreType.DMA,
        ],
        compiler_params=pltpu.CompilerParams(vmem_limit_bytes=16 * 2**20),
    )(
        *(
            pltpu.with_memory_space_constraint(operand, pltpu.HBM)
            for operand in (
                activations.reshape(rows, width),
                out_grads.reshape(rows, width),
                project_in.T,
                project_out.T,
                lengths,
            )
        )
    )


def solve_first(system):
    step = 4

    def spread(column):
        return [jnp.broadcast_to(tile[:, column : column + 1], tile.shape) for tile in system]

    def row_of(tiles, number):
        tile = tiles[number // SUBLANES]
        return jnp.broadcast_to(tile[number % SUBLANES : number % SUBLANES + 1], tile.shape)

    def factor(columns, first):
        p = {(i, j): row_of(columns[j], first + i) for j in range(step) for i in range(j + 1)}
        lower, inverse = {}, []
        for k in range(step):
            inverse.append(pl.reciprocal(p[k, k]))
            for i in range(k + 1, step):
                lower[i, k] = p[k, i] * inverse[k]
            for i in range(k + 1, step):
                for j in range(i, step):
                    p[i, j] = p[i, j] - lower[i, k] * p[k, j]
        return lower, inverse

    def forward(lower, parts):
        parts = list(parts)
        for k in range(step):
            for i in range(k + 1, step):
                parts[i] = [part - lower[i, k] * other for part, other in zip(parts[i], parts[k])]
        return parts

    def update(tiles, columns, lower, inverse, rows):
        rows = forward(lower, [[r] for r in rows])
        for column, row, scale in zip(columns, rows, inverse):
            done = row[0] * scale
            tiles = [tile - c * done for tile, c in zip(tiles, column)]
        return tiles

    count = len(system) * SUBLANES
    columns = [spread(j) for j in range(count - step, count)]
    for first in range(count - step, 0, -step):
        pivots = range(first, first + step)
        left = pl.cdiv(first, SUBLANES)
        lower, inverse = factor(columns, first)
        columns = forward(lower, [c[:left] for c in columns])
        following = []
        for j in range(first - step, first):
            column = spread(j)
            following.append(update(column[:left], columns, lower, inverse, [row_of(column, i) for i in pivots]))
        system = update(system[:left], columns, lower, inverse, [row_of(system, i) for i in pivots])
        columns = following
    lower, inverse = factor(columns, 0)
    rows = forward(lower, [[row_of(system, i)] for i in range(step)])
    solved = [row[0] * scale for row, scale in zip(rows, inverse)]
    for k in reversed(range(step)):
        for i in range(k):
            solved[i] = solved[i] - lower[k, i] * solved[k]
    return solved


def gram(x):
    high = x.astype(jnp.bfloat16)
    rest = x - high.astype(jnp.float32)
    middle = rest.astype(jnp.bfloat16)
    low = (rest - middle.astype(jnp.float32)).astype(jnp.bfloat16)
    parts = [high, middle, low]
    count = x.shape[0]
    terms = []
    for n, held in enumerate(parts):
        streamed = jnp.concatenate(parts[: len(parts) - n], axis=0)
        product = lax.dot_general(streamed, held, NT, preferred_element_type=jnp.float32)
        terms.append([product[k : k + count] for k in range(0, product.shape[0], count)])
    (hh, mh, lh), (hm, mm), (hl,) = terms
    return hh + ((mh + hm) + (lh + hl + mm))


def solve_kernel(per_dev, inner, axis, *refs):
    tiles, (query_ref, scores_ref, gram_ref) = refs[:-3], refs[-3:]
    nq = query_ref.shape[1]
    part = tiles[0].shape[0] // SUBLANES
    examples = len(tiles) * part
    outer = examples // (inner * per_dev)
    fisher_dim = SUBLANES * LANES
    gram_ref[...] = jnp.zeros(gram_ref.shape, jnp.float32)
    slot = (query_ref[...] // per_dev) ^ lax.axis_index(axis)
    n = slot // inner
    place = (gray((slot ^ partner(n, inner)) % inner) * outer + gray(n)) * per_dev + query_ref[...] % per_dev
    rest = LANES - examples - nq
    place = jnp.concatenate(
        [jnp.zeros((1, examples), jnp.int32), place] + ([jnp.zeros((1, rest), jnp.int32)] if rest else []), axis=1
    )
    lane = lax.broadcasted_iota(jnp.int32, (SUBLANES, LANES), 1)
    source = jnp.where(lane < examples, lane, jnp.broadcast_to(place, lane.shape))
    sketches = jnp.concatenate(
        [
            jnp.concatenate([tile[pl.ds(s, part, stride=SUBLANES)] for tile in tiles], axis=0)
            for s in range(SUBLANES)
        ],
        axis=1,
    )
    squares = jnp.sum(jnp.sum(sketches * sketches, axis=0, keepdims=True), axis=1, keepdims=True)
    scale = jnp.broadcast_to(1.0 / squares, (SUBLANES, LANES))
    gram_ref[:, :examples] = gram(sketches)
    row = lax.broadcasted_iota(jnp.int32, (SUBLANES, LANES), 0)
    system = []
    for first in range(0, examples, SUBLANES):
        tile = jnp.take_along_axis(gram_ref[first : first + SUBLANES], source, axis=1) * scale
        system.append(jnp.where(lane == row + first, tile + damp_ratio / fisher_dim, tile))
    solved = solve_first(system)
    scores = solved[0]
    for i in range(1, len(solved)):
        scores = jnp.where(row == i, solved[i], scores)
    scores_ref[...] = scores[:per_dev, examples : examples + nq]


def gram_scores(tiles, query_index, per_dev, inner, axis):
    nq = query_index.shape[0]
    examples = len(tiles) * tiles[0].shape[0] // SUBLANES
    return pl.pallas_call(
        functools.partial(solve_kernel, per_dev, inner, axis),
        out_shape=jax.ShapeDtypeStruct((per_dev, nq), jnp.float32),
        in_specs=[pl.BlockSpec(memory_space=pltpu.VMEM)] * (len(tiles) + 1),
        out_specs=pl.BlockSpec(memory_space=pltpu.VMEM),
        scratch_shapes=[pltpu.VMEM((examples, LANES), jnp.float32)],
        compiler_params=pltpu.CompilerParams(vmem_limit_bytes=8 * 2**20),
    )(*tiles, query_index.reshape(1, nq))


def gray(n):
    return n ^ (n >> 1)


def partner(n, inner):
    return n * inner ^ gray(n) & 1


def gather_xor(tiles, axis, size, inner):
    def swap(block, slot):
        return lax.ppermute(block, axis, [(i, i ^ slot) for i in range(size)])

    rows = sorted(range(1, size // inner), key=gray)
    column = jnp.concatenate([tiles] + [swap(tiles, partner(n, inner)) for n in rows], axis=0)
    return [column] + [swap(column, n) for n in sorted(range(1, inner), key=gray)]


def large_scores(tiles, query_index, per_dev, axis):
    sketches = tiles.reshape(-1, SUBLANES * LANES)
    gram = jnp.dot(sketches, sketches.T, precision=lax.Precision.HIGHEST)
    examples, fisher_dim = sketches.shape
    damping = damp_ratio * jnp.trace(gram) / fisher_dim
    factor = jnp.linalg.cholesky(gram + damping * jnp.eye(examples, dtype=jnp.float32))
    mine = lax.dynamic_slice_in_dim(gram, lax.axis_index(axis) * per_dev, per_dev, 0)
    half = lax.linalg.triangular_solve(factor, mine.T, left_side=True, lower=True)
    solved = lax.linalg.triangular_solve(factor, half, left_side=True, lower=True, transpose_a=True)
    selector = (query_index[:, None] == jnp.arange(examples, dtype=jnp.int32)[None, :]).astype(jnp.float32)
    return jnp.dot(selector, solved, precision=lax.Precision.HIGHEST).T


def local(activations, out_grads, project_in, project_out, lengths, query_index):
    per_dev = activations.shape[0]
    size = lax.axis_size("dp")
    tiles = sketch_rows(activations, out_grads, project_in, project_out, lengths)
    if size * per_dev + query_index.shape[0] <= LANES:
        inner = 4
        return gram_scores(gather_xor(tiles, "dp", size, inner), query_index, per_dev, inner, "dp")
    return large_scores(lax.all_gather(tiles, "dp", axis=0, tiled=True), query_index, per_dev, "dp")


def solution(mesh):
    return jax.shard_map(
        local,
        mesh=mesh,
        in_specs=(
            P(("groups", "dp"), None, None),
            P(("groups", "dp"), None, None),
            P(),
            P(),
            P(("groups", "dp")),
            P("groups"),
        ),
        out_specs=P(("groups", "dp"), None),
        check_vma=False,
    )
```

```python
import functools

import jax
import jax.numpy as jnp
from jax import lax
from jax.experimental import pallas as pl
from jax.experimental.pallas import tpu as pltpu
from jax.sharding import PartitionSpec as P

damp_ratio = 0.5
LANES = 128
SUBLANES = 8
NT = (((1,), (1,)), ((), ()))


def sketch_kernel(bounds, seq_len, act_hbm, out_hbm, pin_hbm, pout_hbm, lengths_hbm, sketch_ref, act, out, pin, pout, lengths_ref, sems, lengths_sem):
    rows, width = act.shape
    rank_dim = pin.shape[0]
    chunks = len(bounds) - 1
    lengths_copy = pltpu.make_async_copy(lengths_hbm, lengths_ref, lengths_sem)
    lengths_copy.start()
    copies = []
    for c in range(chunks):
        cols = pl.ds(bounds[c], bounds[c + 1] - bounds[c])
        copies.append(
            [
                pltpu.make_async_copy(src.at[:, cols], dst.at[:, cols], sems.at[n, c])
                for n, (src, dst) in enumerate(
                    ((pin_hbm, pin), (act_hbm, act), (pout_hbm, pout), (out_hbm, out))
                )
            ]
        )
        for copy in copies[-1]:
            copy.start()
    feat = jnp.zeros((rows, rank_dim), jnp.float32)
    grad = jnp.zeros((rank_dim, rows), jnp.float32)
    for c in range(chunks):
        cols = slice(bounds[c], bounds[c + 1])
        for copy in copies[c]:
            copy.wait()
        feat = feat + lax.dot_general(act[:, cols], pin[:, cols], NT, preferred_element_type=jnp.float32)
        grad = grad + lax.dot_general(pout[:, cols], out[:, cols], NT, preferred_element_type=jnp.float32)
    lengths_copy.wait()
    count = rows // seq_len
    reps = LANES // rank_dim
    position = lax.broadcasted_iota(jnp.int32, (rows, LANES), 0)
    band = lax.broadcasted_iota(jnp.int32, (rows, LANES), 1) // rank_dim
    live = jnp.zeros((rows, LANES), jnp.bool_)
    for e in range(count):
        first = e * seq_len
        live = live | ((band == e) & (position >= first) & (position < first + lengths_ref[e]))
    outer = lax.dot_general(
        grad,
        jnp.where(live, jnp.concatenate([feat] * reps, axis=1), 0.0),
        (((1,), (0,)), ((), ())),
        precision=lax.Precision.HIGHEST,
        preferred_element_type=jnp.float32,
    )
    band = band[:SUBLANES]
    for e in range(count):
        entry = None
        for b in range(reps):
            part = outer[b * SUBLANES : (b + 1) * SUBLANES]
            if b != e:
                part = pltpu.roll(part, (b - e) * rank_dim % LANES, 1)
            entry = part if entry is None else jnp.where(band == b, part, entry)
        sketch_ref[e * SUBLANES : (e + 1) * SUBLANES] = entry


def sketch_rows(activations, out_grads, project_in, project_out, lengths):
    count, seq_len, width = activations.shape
    rank_dim = project_in.shape[1]
    rows = count * seq_len
    unit = width // 32
    bounds = [n * unit for n in (0, 2, 6, 10, 14, 18, 22, 26, 30, 32)]
    chunks = len(bounds) - 1
    return pl.pallas_call(
        functools.partial(sketch_kernel, bounds, seq_len),
        out_shape=jax.ShapeDtypeStruct((count * SUBLANES, LANES), jnp.float32),
        in_specs=[pl.BlockSpec(memory_space=pltpu.HBM)] * 5,
        out_specs=pl.BlockSpec(memory_space=pltpu.VMEM),
        scratch_shapes=[
            pltpu.VMEM((rows, width), jnp.bfloat16),
            pltpu.VMEM((rows, width), jnp.bfloat16),
            pltpu.VMEM((rank_dim, width), jnp.bfloat16),
            pltpu.VMEM((rank_dim, width), jnp.bfloat16),
            pltpu.SMEM((count,), jnp.int32),
            pltpu.SemaphoreType.DMA((4, chunks)),
            pltpu.SemaphoreType.DMA,
        ],
        compiler_params=pltpu.CompilerParams(vmem_limit_bytes=16 * 2**20),
    )(
        *(
            pltpu.with_memory_space_constraint(operand, pltpu.HBM)
            for operand in (
                activations.reshape(rows, width),
                out_grads.reshape(rows, width),
                project_in.T,
                project_out.T,
                lengths,
            )
        ),
    )


def solve_first(system):
    step = 4

    def spread(column):
        return [jnp.broadcast_to(tile[:, column : column + 1], tile.shape) for tile in system]

    def row_of(tiles, number):
        tile = tiles[number // SUBLANES]
        return jnp.broadcast_to(tile[number % SUBLANES : number % SUBLANES + 1], tile.shape)

    def factor(columns, first):
        p = {(i, j): row_of(columns[j], first + i) for j in range(step) for i in range(j + 1)}
        lower, inverse = {}, [None] * step
        for k in range(0, step, 2):
            a, b, c = p[k, k], p[k, k + 1], p[k + 1, k + 1]
            inverse[k] = pl.reciprocal(a)
            inverse[k + 1] = a * pl.reciprocal(a * c - b * b)
            for m in (k, k + 1):
                for i in range(m + 1, step):
                    lower[i, m] = p[m, i] * inverse[m]
                for i in range(m + 1, step):
                    for j in range(i, step):
                        p[i, j] = p[i, j] - lower[i, m] * p[m, j]
        return lower, inverse

    def forward(lower, parts):
        parts = list(parts)
        for k in range(step):
            for i in range(k + 1, step):
                parts[i] = [part - lower[i, k] * other for part, other in zip(parts[i], parts[k])]
        return parts

    def update(tiles, columns, lower, inverse, rows):
        rows = forward(lower, [[r] for r in rows])
        for column, row, scale in zip(columns, rows, inverse):
            done = row[0] * scale
            tiles = [tile - c * done for tile, c in zip(tiles, column)]
        return tiles

    count = len(system) * SUBLANES
    columns = [spread(j) for j in range(count - step, count)]
    for first in range(count - step, 0, -step):
        pivots = range(first, first + step)
        left = pl.cdiv(first, SUBLANES)
        lower, inverse = factor(columns, first)
        columns = forward(lower, [c[:left] for c in columns])
        following = []
        for j in range(first - step, first):
            column = spread(j)
            following.append(update(column[:left], columns, lower, inverse, [row_of(column, i) for i in pivots]))
        system = update(system[:left], columns, lower, inverse, [row_of(system, i) for i in pivots])
        columns = following
    lower, inverse = factor(columns, 0)
    rows = forward(lower, [[row_of(system, i)] for i in range(step)])
    solved = [row[0] * scale for row, scale in zip(rows, inverse)]
    for k in reversed(range(step)):
        for i in range(k):
            solved[i] = solved[i] - lower[k, i] * solved[k]
    return solved


def gram(x):
    high = x.astype(jnp.bfloat16)
    rest = x - high.astype(jnp.float32)
    middle = rest.astype(jnp.bfloat16)
    low = (rest - middle.astype(jnp.float32)).astype(jnp.bfloat16)
    parts = [high, middle, low]
    count = x.shape[0]
    terms = []
    for n, held in enumerate(parts):
        streamed = jnp.concatenate(parts[: len(parts) - n], axis=0)
        product = lax.dot_general(streamed, held, NT, preferred_element_type=jnp.float32)
        terms.append([product[k : k + count] for k in range(0, product.shape[0], count)])
    (hh, mh, lh), (hm, mm), (hl,) = terms
    return hh + ((mh + hm) + (lh + hl + mm))


def solve_kernel(per_dev, inner, axis, *refs):
    tiles, (query_ref, scores_ref, gram_ref) = refs[:-3], refs[-3:]
    nq = query_ref.shape[1]
    part = tiles[0].shape[0] // SUBLANES
    examples = len(tiles) * part
    outer = examples // (inner * per_dev)
    fisher_dim = SUBLANES * LANES
    gram_ref[...] = jnp.zeros(gram_ref.shape, jnp.float32)
    slot = (query_ref[...] // per_dev) ^ lax.axis_index(axis)
    n = slot // inner
    place = (gray((slot ^ partner(n, inner)) % inner) * outer + gray(n)) * per_dev + query_ref[...] % per_dev
    rest = LANES - examples - nq
    place = jnp.concatenate(
        [jnp.zeros((1, examples), jnp.int32), place] + ([jnp.zeros((1, rest), jnp.int32)] if rest else []), axis=1
    )
    lane = lax.broadcasted_iota(jnp.int32, (SUBLANES, LANES), 1)
    source = jnp.where(lane < examples, lane, jnp.broadcast_to(place, lane.shape))
    sketches = jnp.concatenate(
        [
            jnp.concatenate([tile[pl.ds(s, part, stride=SUBLANES)] for tile in tiles], axis=0)
            for s in range(SUBLANES)
        ],
        axis=1,
    )
    squares = jnp.sum(jnp.sum(sketches * sketches, axis=0, keepdims=True), axis=1, keepdims=True)
    scale = jnp.broadcast_to(1.0 / squares, (SUBLANES, LANES))
    gram_ref[:, :examples] = gram(sketches)
    row = lax.broadcasted_iota(jnp.int32, (SUBLANES, LANES), 0)
    system = []
    for first in range(0, examples, SUBLANES):
        tile = jnp.take_along_axis(gram_ref[first : first + SUBLANES], source, axis=1) * scale
        system.append(jnp.where(lane == row + first, tile + damp_ratio / fisher_dim, tile))
    solved = solve_first(system)
    scores = solved[0]
    for i in range(1, len(solved)):
        scores = jnp.where(row == i, solved[i], scores)
    scores_ref[...] = scores[:per_dev, examples : examples + nq]


def gram_scores(tiles, query_index, per_dev, inner, axis):
    nq = query_index.shape[0]
    examples = len(tiles) * tiles[0].shape[0] // SUBLANES
    return pl.pallas_call(
        functools.partial(solve_kernel, per_dev, inner, axis),
        out_shape=jax.ShapeDtypeStruct((per_dev, nq), jnp.float32),
        in_specs=[pl.BlockSpec(memory_space=pltpu.VMEM)] * (len(tiles) + 1),
        out_specs=pl.BlockSpec(memory_space=pltpu.VMEM),
        scratch_shapes=[pltpu.VMEM((examples, LANES), jnp.float32)],
        compiler_params=pltpu.CompilerParams(vmem_limit_bytes=8 * 2**20),
    )(*tiles, query_index.reshape(1, nq))


def gray(n):
    return n ^ (n >> 1)


def partner(n, inner):
    return n * inner ^ gray(n) & 1


def gather_xor(tiles, axis, size, inner):
    def swap(block, slot):
        return lax.ppermute(block, axis, [(i, i ^ slot) for i in range(size)])

    rows = sorted(range(1, size // inner), key=gray)
    column = jnp.concatenate([tiles] + [swap(tiles, partner(n, inner)) for n in rows], axis=0)
    return [column] + [swap(column, n) for n in sorted(range(1, inner), key=gray)]


def large_scores(tiles, query_index, per_dev, axis):
    sketches = tiles.reshape(-1, SUBLANES * LANES)
    gram = jnp.dot(sketches, sketches.T, precision=lax.Precision.HIGHEST)
    examples, fisher_dim = sketches.shape
    damping = damp_ratio * jnp.trace(gram) / fisher_dim
    factor = jnp.linalg.cholesky(gram + damping * jnp.eye(examples, dtype=jnp.float32))
    mine = lax.dynamic_slice_in_dim(gram, lax.axis_index(axis) * per_dev, per_dev, 0)
    half = lax.linalg.triangular_solve(factor, mine.T, left_side=True, lower=True)
    solved = lax.linalg.triangular_solve(factor, half, left_side=True, lower=True, transpose_a=True)
    selector = (query_index[:, None] == jnp.arange(examples, dtype=jnp.int32)[None, :]).astype(jnp.float32)
    return jnp.dot(selector, solved, precision=lax.Precision.HIGHEST).T


def local(activations, out_grads, project_in, project_out, lengths, query_index):
    per_dev = activations.shape[0]
    size = lax.axis_size("dp")
    tiles = sketch_rows(activations, out_grads, project_in, project_out, lengths)
    if size * per_dev + query_index.shape[0] <= LANES:
        inner = 4
        return gram_scores(gather_xor(tiles, "dp", size, inner), query_index, per_dev, inner, "dp")
    return large_scores(lax.all_gather(tiles, "dp", axis=0, tiled=True), query_index, per_dev, "dp")


def solution(mesh):
    return jax.shard_map(
        local,
        mesh=mesh,
        in_specs=(
            P(("groups", "dp"), None, None),
            P(("groups", "dp"), None, None),
            P(),
            P(),
            P(("groups", "dp")),
            P("groups"),
        ),
        out_specs=P(("groups", "dp"), None),
        check_vma=False,
    )
```

```python
import functools

import jax
import jax.numpy as jnp
from jax import lax
from jax.experimental import pallas as pl
from jax.experimental.pallas import tpu as pltpu
from jax.sharding import PartitionSpec as P

damp_ratio = 0.5
ROUTES = (
    ((1, 0), (3, 1), (2, 0), (0, 0)),
    ((2, 1), (1, 0), (0, 0), (3, 0)),
    ((3, 1), (0, 0), (1, 0), (2, 0)),
    ((0, 0), (2, 0), (3, 1), (1, 0)),
)
LANES = 128
SUBLANES = 8
NT = (((1,), (1,)), ((), ()))


def sketch_kernel(bounds, seq_len, act_hbm, out_hbm, pin_hbm, pout_hbm, lengths_hbm, sketch_ref, act, out, pin, pout, lengths_ref, sems, lengths_sem):
    rows, width = act.shape
    rank_dim = pin.shape[0]
    chunks = len(bounds) - 1
    lengths_copy = pltpu.make_async_copy(lengths_hbm, lengths_ref, lengths_sem)
    lengths_copy.start()
    copies = []
    for c in range(chunks):
        cols = pl.ds(bounds[c], bounds[c + 1] - bounds[c])
        copies.append(
            [
                pltpu.make_async_copy(src.at[:, cols], dst.at[:, cols], sems.at[n, c])
                for n, (src, dst) in enumerate(
                    ((pin_hbm, pin), (act_hbm, act), (pout_hbm, pout), (out_hbm, out))
                )
            ]
        )
        for copy in copies[-1]:
            copy.start()
    feat = jnp.zeros((rows, rank_dim), jnp.float32)
    grad = jnp.zeros((rank_dim, rows), jnp.float32)
    for c in range(chunks):
        cols = slice(bounds[c], bounds[c + 1])
        for copy in copies[c]:
            copy.wait()
        feat = feat + lax.dot_general(act[:, cols], pin[:, cols], NT, preferred_element_type=jnp.float32)
        grad = grad + lax.dot_general(pout[:, cols], out[:, cols], NT, preferred_element_type=jnp.float32)
    lengths_copy.wait()
    count = rows // seq_len
    reps = LANES // rank_dim
    position = lax.broadcasted_iota(jnp.int32, (rows, LANES), 0)
    band = lax.broadcasted_iota(jnp.int32, (rows, LANES), 1) // rank_dim
    live = jnp.zeros((rows, LANES), jnp.bool_)
    for e in range(count):
        first = e * seq_len
        live = live | ((band == e) & (position >= first) & (position < first + lengths_ref[e]))
    outer = lax.dot_general(
        grad,
        jnp.where(live, jnp.concatenate([feat] * reps, axis=1), 0.0),
        (((1,), (0,)), ((), ())),
        precision=lax.Precision.HIGHEST,
        preferred_element_type=jnp.float32,
    )
    band = band[:SUBLANES]
    for e in range(count):
        entry = None
        for b in range(reps):
            part = outer[b * SUBLANES : (b + 1) * SUBLANES]
            if b != e:
                part = pltpu.roll(part, (b - e) * rank_dim % LANES, 1)
            entry = part if entry is None else jnp.where(band == b, part, entry)
        sketch_ref[e * SUBLANES : (e + 1) * SUBLANES] = entry


def sketch_rows(activations, out_grads, project_in, project_out, lengths):
    count, seq_len, width = activations.shape
    rank_dim = project_in.shape[1]
    rows = count * seq_len
    unit = width // 32
    bounds = [n * unit for n in (0, 2, 6, 10, 14, 18, 22, 26, 30, 32)]
    chunks = len(bounds) - 1
    return pl.pallas_call(
        functools.partial(sketch_kernel, bounds, seq_len),
        out_shape=jax.ShapeDtypeStruct((count * SUBLANES, LANES), jnp.float32),
        in_specs=[pl.BlockSpec(memory_space=pltpu.HBM)] * 5,
        out_specs=pl.BlockSpec(memory_space=pltpu.VMEM),
        scratch_shapes=[
            pltpu.VMEM((rows, width), jnp.bfloat16),
            pltpu.VMEM((rows, width), jnp.bfloat16),
            pltpu.VMEM((rank_dim, width), jnp.bfloat16),
            pltpu.VMEM((rank_dim, width), jnp.bfloat16),
            pltpu.SMEM((count,), jnp.int32),
            pltpu.SemaphoreType.DMA((4, chunks)),
            pltpu.SemaphoreType.DMA,
        ],
        compiler_params=pltpu.CompilerParams(vmem_limit_bytes=16 * 2**20),
    )(
        *(
            pltpu.with_memory_space_constraint(operand, pltpu.HBM)
            for operand in (
                activations.reshape(rows, width),
                out_grads.reshape(rows, width),
                project_in.T,
                project_out.T,
                lengths,
            )
        ),
    )


def solve_first(system):
    step = 4

    def spread(column):
        return [jnp.broadcast_to(tile[:, column : column + 1], tile.shape) for tile in system]

    def row_of(tiles, number):
        tile = tiles[number // SUBLANES]
        return jnp.broadcast_to(tile[number % SUBLANES : number % SUBLANES + 1], tile.shape)

    def factor(columns, first):
        p = {(i, j): row_of(columns[j], first + i) for j in range(step) for i in range(j + 1)}
        lower, inverse = {}, [None] * step
        for k in range(0, step, 2):
            a, b, c = p[k, k], p[k, k + 1], p[k + 1, k + 1]
            inverse[k] = pl.reciprocal(a)
            inverse[k + 1] = a * pl.reciprocal(a * c - b * b)
            for m in (k, k + 1):
                for i in range(m + 1, step):
                    lower[i, m] = p[m, i] * inverse[m]
                for i in range(m + 1, step):
                    for j in range(i, step):
                        p[i, j] = p[i, j] - lower[i, m] * p[m, j]
        return lower, inverse

    def forward(lower, parts):
        parts = list(parts)
        for k in range(step):
            for i in range(k + 1, step):
                parts[i] = [part - lower[i, k] * other for part, other in zip(parts[i], parts[k])]
        return parts

    def update(tiles, columns, lower, inverse, rows):
        rows = forward(lower, [[r] for r in rows])
        for column, row, scale in zip(columns, rows, inverse):
            done = row[0] * scale
            tiles = [tile - c * done for tile, c in zip(tiles, column)]
        return tiles

    count = len(system) * SUBLANES
    columns = [spread(j) for j in range(count - step, count)]
    for first in range(count - step, 0, -step):
        pivots = range(first, first + step)
        left = pl.cdiv(first, SUBLANES)
        lower, inverse = factor(columns, first)
        columns = forward(lower, [c[:left] for c in columns])
        following = []
        for j in range(first - step, first):
            column = spread(j)
            following.append(update(column[:left], columns, lower, inverse, [row_of(column, i) for i in pivots]))
        system = update(system[:left], columns, lower, inverse, [row_of(system, i) for i in pivots])
        columns = following
    lower, inverse = factor(columns, 0)
    rows = forward(lower, [[row_of(system, i)] for i in range(step)])
    solved = [row[0] * scale for row, scale in zip(rows, inverse)]
    for k in reversed(range(step)):
        for i in range(k):
            solved[i] = solved[i] - lower[k, i] * solved[k]
    return solved


def gram(x):
    high = x.astype(jnp.bfloat16)
    rest = x - high.astype(jnp.float32)
    middle = rest.astype(jnp.bfloat16)
    low = (rest - middle.astype(jnp.float32)).astype(jnp.bfloat16)
    parts = [high, middle, low]
    count = x.shape[0]
    terms = []
    for n, held in enumerate(parts):
        streamed = jnp.concatenate(parts[: len(parts) - n], axis=0)
        product = lax.dot_general(streamed, held, NT, preferred_element_type=jnp.float32)
        terms.append([product[k : k + count] for k in range(0, product.shape[0], count)])
    (hh, mh, lh), (hm, mm), (hl,) = terms
    return hh + ((mh + hm) + (lh + hl + mm))


def solve_kernel(per_dev, inner, axis, *refs):
    tiles, (query_ref, scores_ref, gram_ref) = refs[:-3], refs[-3:]
    nq = query_ref.shape[1]
    held = tiles[0].shape[0] // SUBLANES
    examples = len(tiles) * held
    fisher_dim = SUBLANES * LANES
    gram_ref[...] = jnp.zeros(gram_ref.shape, jnp.float32)
    mine = lax.axis_index(axis)
    device = query_ref[...] // per_dev
    part = part_of(device // inner, mine // inner)
    place = gray((device ^ mine ^ (part & 1)) % inner) * len(ROUTES) + (part >> 1)
    place = place * per_dev + query_ref[...] % per_dev
    rest = LANES - examples - nq
    place = jnp.concatenate(
        [jnp.zeros((1, examples), jnp.int32), place] + ([jnp.zeros((1, rest), jnp.int32)] if rest else []), axis=1
    )
    lane = lax.broadcasted_iota(jnp.int32, (SUBLANES, LANES), 1)
    own = part_of(mine // inner, mine // inner) >> 1
    source = jnp.where(lane < len(ROUTES) * per_dev, lane ^ (own * per_dev), lane)
    source = jnp.where(lane < examples, source, jnp.broadcast_to(place, lane.shape))
    sketches = jnp.concatenate(
        [
            jnp.concatenate([tile[pl.ds(s, held, stride=SUBLANES)] for tile in tiles], axis=0)
            for s in range(SUBLANES)
        ],
        axis=1,
    )
    squares = jnp.sum(jnp.sum(sketches * sketches, axis=0, keepdims=True), axis=1, keepdims=True)
    scale = jnp.broadcast_to(1.0 / squares, (SUBLANES, LANES))
    gram_ref[:, :examples] = gram(sketches)
    row = lax.broadcasted_iota(jnp.int32, (SUBLANES, LANES), 0)
    system = []
    for first in range(0, examples, SUBLANES):
        if first < len(ROUTES) * per_dev:
            tile = gram_ref[pl.ds(pl.multiple_of(first ^ (own // 2 * SUBLANES), SUBLANES), SUBLANES)]
            tile = jnp.where(own % 2 == 1, pltpu.roll(tile, per_dev, 0), tile)
        else:
            tile = gram_ref[first : first + SUBLANES]
        tile = jnp.take_along_axis(tile, source, axis=1) * scale
        system.append(jnp.where(lane == row + first, tile + damp_ratio / fisher_dim, tile))
    solved = solve_first(system)
    scores = solved[0]
    for i in range(1, len(solved)):
        scores = jnp.where(row == i, solved[i], scores)
    scores_ref[...] = scores[:per_dev, examples : examples + nq]


def gram_scores(tiles, query_index, per_dev, inner, axis):
    nq = query_index.shape[0]
    examples = len(tiles) * tiles[0].shape[0] // SUBLANES
    return pl.pallas_call(
        functools.partial(solve_kernel, per_dev, inner, axis),
        out_shape=jax.ShapeDtypeStruct((per_dev, nq), jnp.float32),
        in_specs=[pl.BlockSpec(memory_space=pltpu.VMEM)] * (len(tiles) + 1),
        out_specs=pl.BlockSpec(memory_space=pltpu.VMEM),
        scratch_shapes=[pltpu.VMEM((examples, LANES), jnp.float32)],
        compiler_params=pltpu.CompilerParams(vmem_limit_bytes=8 * 2**20),
    )(*tiles, query_index.reshape(1, nq))


def gray(n):
    return n ^ (n >> 1)


def gather_rows(tiles, axis, size, inner):
    rows = range(size // inner)
    parts = []
    for routes in ROUTES:
        pairs = [(z * inner + k, routes[z][0] * inner + (k ^ routes[z][1])) for z in rows for k in range(inner)]
        parts.append(lax.ppermute(tiles, axis, pairs))
    column = jnp.concatenate(parts[::-1], axis=0)
    order = sorted(range(1, inner), key=gray)
    return [column] + [lax.ppermute(column, axis, [(i, i ^ n) for i in range(size)]) for n in order]


def part_of(row, mine):
    found = jnp.zeros_like(row)
    for n, routes in enumerate(ROUTES):
        for z, (target, flip) in enumerate(routes):
            found = jnp.where((row == z) & (mine == target), (len(ROUTES) - 1 - n) * 2 + flip, found)
    return found


def large_scores(tiles, query_index, per_dev, axis):
    sketches = tiles.reshape(-1, SUBLANES * LANES)
    gram = jnp.dot(sketches, sketches.T, precision=lax.Precision.HIGHEST)
    examples, fisher_dim = sketches.shape
    damping = damp_ratio * jnp.trace(gram) / fisher_dim
    factor = jnp.linalg.cholesky(gram + damping * jnp.eye(examples, dtype=jnp.float32))
    mine = lax.dynamic_slice_in_dim(gram, lax.axis_index(axis) * per_dev, per_dev, 0)
    half = lax.linalg.triangular_solve(factor, mine.T, left_side=True, lower=True)
    solved = lax.linalg.triangular_solve(factor, half, left_side=True, lower=True, transpose_a=True)
    selector = (query_index[:, None] == jnp.arange(examples, dtype=jnp.int32)[None, :]).astype(jnp.float32)
    return jnp.dot(selector, solved, precision=lax.Precision.HIGHEST).T


def local(activations, out_grads, project_in, project_out, lengths, query_index):
    per_dev = activations.shape[0]
    size = lax.axis_size("dp")
    tiles = sketch_rows(activations, out_grads, project_in, project_out, lengths)
    inner = 4
    if size == len(ROUTES) * inner and size * per_dev + query_index.shape[0] <= LANES:
        return gram_scores(gather_rows(tiles, "dp", size, inner), query_index, per_dev, inner, "dp")
    return large_scores(lax.all_gather(tiles, "dp", axis=0, tiled=True), query_index, per_dev, "dp")


def solution(mesh):
    return jax.shard_map(
        local,
        mesh=mesh,
        in_specs=(
            P(("groups", "dp"), None, None),
            P(("groups", "dp"), None, None),
            P(),
            P(),
            P(("groups", "dp")),
            P("groups"),
        ),
        out_specs=P(("groups", "dp"), None),
        check_vma=False,
    )
```

```python
import functools

import jax
import jax.numpy as jnp
from jax import lax
from jax.experimental import pallas as pl
from jax.experimental.pallas import tpu as pltpu
from jax.sharding import PartitionSpec as P

damp_ratio = 0.5
ROUTES = (
    ((1, 0), (3, 1), (2, 0), (0, 0)),
    ((2, 1), (1, 0), (0, 0), (3, 0)),
    ((3, 1), (0, 0), (1, 0), (2, 0)),
    ((0, 0), (2, 0), (3, 1), (1, 0)),
)
LANES = 128
SUBLANES = 8
NT = (((1,), (1,)), ((), ()))


def sketch_kernel(bounds, seq_len, act_hbm, out_hbm, pin_hbm, pout_hbm, lengths_hbm, sketch_ref, act, out, pin, pout, lengths_ref, sems, lengths_sem):
    rows, width = act.shape
    rank_dim = pin.shape[0]
    chunks = len(bounds) - 1
    lengths_copy = pltpu.make_async_copy(lengths_hbm, lengths_ref, lengths_sem)
    lengths_copy.start()
    copies = []
    for c in range(chunks):
        cols = pl.ds(bounds[c], bounds[c + 1] - bounds[c])
        copies.append(
            [
                pltpu.make_async_copy(src.at[:, cols], dst.at[:, cols], sems.at[n, c])
                for n, (src, dst) in enumerate(
                    ((pin_hbm, pin), (act_hbm, act), (pout_hbm, pout), (out_hbm, out))
                )
            ]
        )
        for copy in copies[-1]:
            copy.start()
    feat = jnp.zeros((rows, rank_dim), jnp.float32)
    grad = jnp.zeros((rank_dim, rows), jnp.float32)
    for c in range(chunks):
        cols = slice(bounds[c], bounds[c + 1])
        for copy in copies[c]:
            copy.wait()
        feat = feat + lax.dot_general(act[:, cols], pin[:, cols], NT, preferred_element_type=jnp.float32)
        grad = grad + lax.dot_general(pout[:, cols], out[:, cols], NT, preferred_element_type=jnp.float32)
    lengths_copy.wait()
    count = rows // seq_len
    reps = LANES // rank_dim
    position = lax.broadcasted_iota(jnp.int32, (rows, LANES), 0)
    band = lax.broadcasted_iota(jnp.int32, (rows, LANES), 1) // rank_dim
    live = jnp.zeros((rows, LANES), jnp.bool_)
    for e in range(count):
        first = e * seq_len
        live = live | ((band == e) & (position >= first) & (position < first + lengths_ref[e]))
    outer = lax.dot_general(
        grad,
        jnp.where(live, jnp.concatenate([feat] * reps, axis=1), 0.0),
        (((1,), (0,)), ((), ())),
        precision=lax.Precision.HIGHEST,
        preferred_element_type=jnp.float32,
    )
    band = band[:SUBLANES]
    for e in range(count):
        entry = None
        for b in range(reps):
            part = outer[b * SUBLANES : (b + 1) * SUBLANES]
            if b != e:
                part = pltpu.roll(part, (b - e) * rank_dim % LANES, 1)
            entry = part if entry is None else jnp.where(band == b, part, entry)
        sketch_ref[e * SUBLANES : (e + 1) * SUBLANES] = entry


def sketch_rows(activations, out_grads, project_in, project_out, lengths):
    count, seq_len, width = activations.shape
    rank_dim = project_in.shape[1]
    rows = count * seq_len
    unit = width // 32
    bounds = [n * unit for n in (0, 2, 6, 10, 14, 18, 22, 26, 30, 32)]
    chunks = len(bounds) - 1
    return pl.pallas_call(
        functools.partial(sketch_kernel, bounds, seq_len),
        out_shape=jax.ShapeDtypeStruct((count * SUBLANES, LANES), jnp.float32),
        in_specs=[pl.BlockSpec(memory_space=pltpu.HBM)] * 5,
        out_specs=pl.BlockSpec(memory_space=pltpu.VMEM),
        scratch_shapes=[
            pltpu.VMEM((rows, width), jnp.bfloat16),
            pltpu.VMEM((rows, width), jnp.bfloat16),
            pltpu.VMEM((rank_dim, width), jnp.bfloat16),
            pltpu.VMEM((rank_dim, width), jnp.bfloat16),
            pltpu.SMEM((count,), jnp.int32),
            pltpu.SemaphoreType.DMA((4, chunks)),
            pltpu.SemaphoreType.DMA,
        ],
        compiler_params=pltpu.CompilerParams(vmem_limit_bytes=16 * 2**20),
    )(
        *(
            pltpu.with_memory_space_constraint(operand, pltpu.HBM)
            for operand in (
                activations.reshape(rows, width),
                out_grads.reshape(rows, width),
                project_in.T,
                project_out.T,
                lengths,
            )
        ),
    )


def solve_first(system):
    step = 4

    def spread(column):
        return [jnp.broadcast_to(tile[:, column : column + 1], tile.shape) for tile in system]

    def row_of(tiles, number):
        tile = tiles[number // SUBLANES]
        return jnp.broadcast_to(tile[number % SUBLANES : number % SUBLANES + 1], tile.shape)

    def factor(columns, first):
        p = {(i, j): row_of(columns[j], first + i) for j in range(step) for i in range(j + 1)}
        lower, inverse = {}, [None] * step
        for k in range(0, step, 2):
            a, b, c = p[k, k], p[k, k + 1], p[k + 1, k + 1]
            inverse[k] = pl.reciprocal(a)
            inverse[k + 1] = a * pl.reciprocal(a * c - b * b)
            for m in (k, k + 1):
                for i in range(m + 1, step):
                    lower[i, m] = p[m, i] * inverse[m]
                for i in range(m + 1, step):
                    for j in range(i, step):
                        p[i, j] = p[i, j] - lower[i, m] * p[m, j]
        return lower, inverse

    def forward(lower, parts):
        parts = list(parts)
        for k in range(step):
            for i in range(k + 1, step):
                parts[i] = [part - lower[i, k] * other for part, other in zip(parts[i], parts[k])]
        return parts

    def update(tiles, columns, lower, inverse, rows):
        rows = forward(lower, [[r] for r in rows])
        for column, row, scale in zip(columns, rows, inverse):
            done = row[0] * scale
            tiles = [tile - c * done for tile, c in zip(tiles, column)]
        return tiles

    count = len(system) * SUBLANES
    columns = [spread(j) for j in range(count - step, count)]
    for first in range(count - step, 0, -step):
        pivots = range(first, first + step)
        left = pl.cdiv(first, SUBLANES)
        lower, inverse = factor(columns, first)
        columns = forward(lower, [c[:left] for c in columns])
        following = []
        for j in range(first - step, first):
            column = spread(j)
            following.append(update(column[:left], columns, lower, inverse, [row_of(column, i) for i in pivots]))
        system = update(system[:left], columns, lower, inverse, [row_of(system, i) for i in pivots])
        columns = following
    lower, inverse = factor(columns, 0)
    rows = forward(lower, [[row_of(system, i)] for i in range(step)])
    solved = [row[0] * scale for row, scale in zip(rows, inverse)]
    for k in reversed(range(step)):
        for i in range(k):
            solved[i] = solved[i] - lower[k, i] * solved[k]
    return solved


def gram(x):
    high = x.astype(jnp.bfloat16)
    rest = x - high.astype(jnp.float32)
    middle = rest.astype(jnp.bfloat16)
    low = (rest - middle.astype(jnp.float32)).astype(jnp.bfloat16)
    parts = [high, middle, low]
    count = x.shape[0]
    terms = []
    for n, held in enumerate(parts):
        streamed = jnp.concatenate(parts[: len(parts) - n], axis=0)
        product = lax.dot_general(streamed, held, NT, preferred_element_type=jnp.float32)
        terms.append([product[k : k + count] for k in range(0, product.shape[0], count)])
    (hh, mh, lh), (hm, mm), (hl,) = terms
    return hh + ((mh + hm) + (lh + hl + mm))


def solve_kernel(per_dev, inner, axis, *refs):
    tiles, (query_ref, scores_ref, gram_ref) = refs[:-3], refs[-3:]
    nq = query_ref.shape[1]
    held = tiles[0].shape[0] // SUBLANES
    examples = len(tiles) * held
    fisher_dim = SUBLANES * LANES
    gram_ref[...] = jnp.zeros(gram_ref.shape, jnp.float32)
    mine = lax.axis_index(axis)
    device = query_ref[...] // per_dev
    part = part_of(device // inner, mine // inner)
    place = gray((device ^ mine ^ (part & 1)) % inner) * len(ROUTES) + (part >> 1)
    place = place * per_dev + query_ref[...] % per_dev
    rest = LANES - examples - nq
    place = jnp.concatenate(
        [jnp.zeros((1, examples), jnp.int32), place] + ([jnp.zeros((1, rest), jnp.int32)] if rest else []), axis=1
    )
    lane = lax.broadcasted_iota(jnp.int32, (SUBLANES, LANES), 1)
    own = part_of(mine // inner, mine // inner) >> 1
    source = jnp.where(lane < len(ROUTES) * per_dev, lane ^ (own * per_dev), lane)
    source = jnp.where(lane < examples, source, jnp.broadcast_to(place, lane.shape))
    sketches = jnp.concatenate(
        [
            jnp.concatenate([tile[pl.ds(s, held, stride=SUBLANES)] for tile in tiles], axis=0)
            for s in range(SUBLANES)
        ],
        axis=1,
    )
    squares = jnp.sum(jnp.sum(sketches * sketches, axis=0, keepdims=True), axis=1, keepdims=True)
    scale = jnp.broadcast_to(1.0 / squares, (SUBLANES, LANES))
    gram_ref[:, :examples] = gram(sketches)
    row = lax.broadcasted_iota(jnp.int32, (SUBLANES, LANES), 0)
    system = []
    for first in range(0, examples, SUBLANES):
        if first < len(ROUTES) * per_dev:
            tile = gram_ref[pl.ds(pl.multiple_of(first ^ (own // 2 * SUBLANES), SUBLANES), SUBLANES)]
            tile = jnp.where(own % 2 == 1, pltpu.roll(tile, per_dev, 0), tile)
        else:
            tile = gram_ref[first : first + SUBLANES]
        tile = jnp.take_along_axis(tile, source, axis=1) * scale
        system.append(jnp.where(lane == row + first, tile + damp_ratio / fisher_dim, tile))
    solved = solve_first(system)
    scores = solved[0]
    for i in range(1, len(solved)):
        scores = jnp.where(row == i, solved[i], scores)
    scores_ref[...] = scores[:per_dev, examples : examples + nq]


def gram_scores(tiles, query_index, per_dev, inner, axis):
    nq = query_index.shape[0]
    examples = len(tiles) * tiles[0].shape[0] // SUBLANES
    return pl.pallas_call(
        functools.partial(solve_kernel, per_dev, inner, axis),
        out_shape=jax.ShapeDtypeStruct((per_dev, nq), jnp.float32),
        in_specs=[pl.BlockSpec(memory_space=pltpu.VMEM)] * (len(tiles) + 1),
        out_specs=pl.BlockSpec(memory_space=pltpu.VMEM),
        scratch_shapes=[pltpu.VMEM((examples, LANES), jnp.float32)],
        compiler_params=pltpu.CompilerParams(vmem_limit_bytes=8 * 2**20),
    )(*tiles, query_index.reshape(1, nq))


def gray(n):
    return n ^ (n >> 1)


def gather_rows(tiles, axis, size, inner):
    rows = range(size // inner)
    parts = []
    for routes in ROUTES:
        pairs = [(z * inner + k, routes[z][0] * inner + (k ^ routes[z][1])) for z in rows for k in range(inner)]
        parts.append(lax.ppermute(tiles, axis, pairs))
    block = tiles.shape[0]
    last = len(parts) - 1
    column = functools.reduce(
        jnp.add,
        [jnp.pad(parts[last - n], ((n * block, (last - n) * block), (0, 0))) for n in range(len(parts))],
    )
    order = sorted(range(1, inner), key=gray)
    return [column] + [lax.ppermute(column, axis, [(i, i ^ n) for i in range(size)]) for n in order]


def part_of(row, mine):
    found = jnp.zeros_like(row)
    for n, routes in enumerate(ROUTES):
        for z, (target, flip) in enumerate(routes):
            found = jnp.where((row == z) & (mine == target), (len(ROUTES) - 1 - n) * 2 + flip, found)
    return found


def large_scores(tiles, query_index, per_dev, axis):
    sketches = tiles.reshape(-1, SUBLANES * LANES)
    gram = jnp.dot(sketches, sketches.T, precision=lax.Precision.HIGHEST)
    examples, fisher_dim = sketches.shape
    damping = damp_ratio * jnp.trace(gram) / fisher_dim
    factor = jnp.linalg.cholesky(gram + damping * jnp.eye(examples, dtype=jnp.float32))
    mine = lax.dynamic_slice_in_dim(gram, lax.axis_index(axis) * per_dev, per_dev, 0)
    half = lax.linalg.triangular_solve(factor, mine.T, left_side=True, lower=True)
    solved = lax.linalg.triangular_solve(factor, half, left_side=True, lower=True, transpose_a=True)
    selector = (query_index[:, None] == jnp.arange(examples, dtype=jnp.int32)[None, :]).astype(jnp.float32)
    return jnp.dot(selector, solved, precision=lax.Precision.HIGHEST).T


def local(activations, out_grads, project_in, project_out, lengths, query_index):
    per_dev = activations.shape[0]
    size = lax.axis_size("dp")
    tiles = sketch_rows(activations, out_grads, project_in, project_out, lengths)
    inner = 4
    if size == len(ROUTES) * inner and size * per_dev + query_index.shape[0] <= LANES:
        return gram_scores(gather_rows(tiles, "dp", size, inner), query_index, per_dev, inner, "dp")
    return large_scores(lax.all_gather(tiles, "dp", axis=0, tiled=True), query_index, per_dev, "dp")


def solution(mesh):
    return jax.shard_map(
        local,
        mesh=mesh,
        in_specs=(
            P(("groups", "dp"), None, None),
            P(("groups", "dp"), None, None),
            P(),
            P(),
            P(("groups", "dp")),
            P("groups"),
        ),
        out_specs=P(("groups", "dp"), None),
        check_vma=False,
    )
```

```python
import functools

import jax
import jax.numpy as jnp
from jax import lax
from jax.experimental import pallas as pl
from jax.experimental.pallas import tpu as pltpu
from jax.sharding import PartitionSpec as P

damp_ratio = 0.5
LANES = 128
SUBLANES = 8
NT = (((1,), (1,)), ((), ()))


def sketch_kernel(bounds, seq_len, act_hbm, out_hbm, pin_hbm, pout_hbm, lengths_hbm, sketch_ref, act, out, pin, pout, lengths_ref, sems, lengths_sem):
    rows, width = act.shape
    rank_dim = pin.shape[0]
    chunks = len(bounds) - 1
    lengths_copy = pltpu.make_async_copy(lengths_hbm, lengths_ref, lengths_sem)
    lengths_copy.start()
    copies = []
    for c in range(chunks):
        cols = pl.ds(bounds[c], bounds[c + 1] - bounds[c])
        copies.append(
            [
                pltpu.make_async_copy(src.at[:, cols], dst.at[:, cols], sems.at[n, c])
                for n, (src, dst) in enumerate(
                    ((pin_hbm, pin), (act_hbm, act), (pout_hbm, pout), (out_hbm, out))
                )
            ]
        )
        for copy in copies[-1]:
            copy.start()
    feat = jnp.zeros((rows, rank_dim), jnp.float32)
    grad = jnp.zeros((rank_dim, rows), jnp.float32)
    for c in range(chunks):
        cols = slice(bounds[c], bounds[c + 1])
        for copy in copies[c]:
            copy.wait()
        feat = feat + lax.dot_general(act[:, cols], pin[:, cols], NT, preferred_element_type=jnp.float32)
        grad = grad + lax.dot_general(pout[:, cols], out[:, cols], NT, preferred_element_type=jnp.float32)
    lengths_copy.wait()
    count = rows // seq_len
    reps = LANES // rank_dim
    position = lax.broadcasted_iota(jnp.int32, (rows, LANES), 0)
    band = lax.broadcasted_iota(jnp.int32, (rows, LANES), 1) // rank_dim
    live = jnp.zeros((rows, LANES), jnp.bool_)
    for e in range(count):
        first = e * seq_len
        live = live | ((band == e) & (position >= first) & (position < first + lengths_ref[e]))
    outer = lax.dot_general(
        grad,
        jnp.where(live, jnp.concatenate([feat] * reps, axis=1), 0.0),
        (((1,), (0,)), ((), ())),
        precision=lax.Precision.HIGHEST,
        preferred_element_type=jnp.float32,
    )
    band = band[:SUBLANES]
    for e in range(count):
        entry = None
        for b in range(reps):
            part = outer[b * SUBLANES : (b + 1) * SUBLANES]
            if b != e:
                part = pltpu.roll(part, (b - e) * rank_dim % LANES, 1)
            entry = part if entry is None else jnp.where(band == b, part, entry)
        sketch_ref[e * SUBLANES : (e + 1) * SUBLANES] = entry


def sketch_rows(activations, out_grads, project_in, project_out, lengths):
    count, seq_len, width = activations.shape
    rank_dim = project_in.shape[1]
    rows = count * seq_len
    unit = width // 32
    bounds = [n * unit for n in (0, 2, 6, 10, 14, 18, 22, 26, 30, 32)]
    chunks = len(bounds) - 1
    return pl.pallas_call(
        functools.partial(sketch_kernel, bounds, seq_len),
        out_shape=jax.ShapeDtypeStruct((count * SUBLANES, LANES), jnp.float32),
        in_specs=[pl.BlockSpec(memory_space=pltpu.HBM)] * 5,
        out_specs=pl.BlockSpec(memory_space=pltpu.VMEM),
        scratch_shapes=[
            pltpu.VMEM((rows, width), jnp.bfloat16),
            pltpu.VMEM((rows, width), jnp.bfloat16),
            pltpu.VMEM((rank_dim, width), jnp.bfloat16),
            pltpu.VMEM((rank_dim, width), jnp.bfloat16),
            pltpu.SMEM((count,), jnp.int32),
            pltpu.SemaphoreType.DMA((4, chunks)),
            pltpu.SemaphoreType.DMA,
        ],
        compiler_params=pltpu.CompilerParams(vmem_limit_bytes=16 * 2**20),
    )(
        *(
            pltpu.with_memory_space_constraint(operand, pltpu.HBM)
            for operand in (
                activations.reshape(rows, width),
                out_grads.reshape(rows, width),
                project_in.T,
                project_out.T,
                lengths,
            )
        ),
    )


def solve_first(system):
    step = 4

    def spread(column):
        return [jnp.broadcast_to(tile[:, column : column + 1], tile.shape) for tile in system]

    def row_of(tiles, number):
        tile = tiles[number // SUBLANES]
        return jnp.broadcast_to(tile[number % SUBLANES : number % SUBLANES + 1], tile.shape)

    def factor(columns, first):
        p = {(i, j): row_of(columns[j], first + i) for j in range(step) for i in range(j + 1)}
        lower, inverse = {}, [None] * step
        for k in range(0, step, 2):
            a, b, c = p[k, k], p[k, k + 1], p[k + 1, k + 1]
            inverse[k] = pl.reciprocal(a)
            inverse[k + 1] = a * pl.reciprocal(a * c - b * b)
            for m in (k, k + 1):
                for i in range(m + 1, step):
                    lower[i, m] = p[m, i] * inverse[m]
                for i in range(m + 1, step):
                    for j in range(i, step):
                        p[i, j] = p[i, j] - lower[i, m] * p[m, j]
        return lower, inverse

    def forward(lower, parts):
        parts = list(parts)
        for k in range(step):
            for i in range(k + 1, step):
                parts[i] = [part - lower[i, k] * other for part, other in zip(parts[i], parts[k])]
        return parts

    def update(tiles, columns, lower, inverse, rows):
        rows = forward(lower, [[r] for r in rows])
        for column, row, scale in zip(columns, rows, inverse):
            done = row[0] * scale
            tiles = [tile - c * done for tile, c in zip(tiles, column)]
        return tiles

    count = len(system) * SUBLANES
    columns = [spread(j) for j in range(count - step, count)]
    for first in range(count - step, 0, -step):
        pivots = range(first, first + step)
        left = pl.cdiv(first, SUBLANES)
        lower, inverse = factor(columns, first)
        across = {j: [row_of(column, j) for column in columns] for j in range(first - step, first)}
        columns = forward(lower, [c[:left] for c in columns])
        following = [update(spread(j)[:left], columns, lower, inverse, across[j]) for j in across]
        system = update(system[:left], columns, lower, inverse, [row_of(system, i) for i in pivots])
        columns = following
    lower, inverse = factor(columns, 0)
    rows = forward(lower, [[row_of(system, i)] for i in range(step)])
    solved = [row[0] * scale for row, scale in zip(rows, inverse)]
    for k in reversed(range(step)):
        for i in range(k):
            solved[i] = solved[i] - lower[k, i] * solved[k]
    return solved


def gram(x):
    high = x.astype(jnp.bfloat16)
    rest = x - high.astype(jnp.float32)
    middle = rest.astype(jnp.bfloat16)
    low = (rest - middle.astype(jnp.float32)).astype(jnp.bfloat16)
    parts = [high, middle, low]
    count = x.shape[0]
    terms = []
    for n, held in enumerate(parts):
        streamed = jnp.concatenate(parts[: len(parts) - n], axis=0)
        product = lax.dot_general(streamed, held, NT, preferred_element_type=jnp.float32)
        terms.append([product[k : k + count] for k in range(0, product.shape[0], count)])
    (hh, mh, lh), (hm, mm), (hl,) = terms
    return hh + ((mh + hm) + (lh + hl + mm))


def solve_kernel(per_dev, inner, axis, *refs):
    tiles, (query_ref, scores_ref, gram_ref) = refs[:-3], refs[-3:]
    nq = query_ref.shape[1]
    part = tiles[0].shape[0] // SUBLANES
    examples = len(tiles) * part
    outer = examples // (inner * per_dev)
    fisher_dim = SUBLANES * LANES
    gram_ref[...] = jnp.zeros(gram_ref.shape, jnp.float32)
    slot = (query_ref[...] // per_dev) ^ lax.axis_index(axis)
    n = slot // inner
    place = (gray((slot ^ partner(n, inner)) % inner) * outer + gray(n)) * per_dev + query_ref[...] % per_dev
    rest = LANES - examples - nq
    place = jnp.concatenate(
        [jnp.zeros((1, examples), jnp.int32), place] + ([jnp.zeros((1, rest), jnp.int32)] if rest else []), axis=1
    )
    lane = lax.broadcasted_iota(jnp.int32, (SUBLANES, LANES), 1)
    source = jnp.where(lane < examples, lane, jnp.broadcast_to(place, lane.shape))
    sketches = jnp.concatenate(
        [
            jnp.concatenate([tile[pl.ds(s, part, stride=SUBLANES)] for tile in tiles], axis=0)
            for s in range(SUBLANES)
        ],
        axis=1,
    )
    squares = jnp.sum(jnp.sum(sketches * sketches, axis=0, keepdims=True), axis=1, keepdims=True)
    scale = jnp.broadcast_to(1.0 / squares, (SUBLANES, LANES))
    gram_ref[:, :examples] = gram(sketches)
    row = lax.broadcasted_iota(jnp.int32, (SUBLANES, LANES), 0)
    system = []
    for first in range(0, examples, SUBLANES):
        tile = jnp.take_along_axis(gram_ref[first : first + SUBLANES], source, axis=1) * scale
        system.append(jnp.where(lane == row + first, tile + damp_ratio / fisher_dim, tile))
    solved = solve_first(system)
    scores = solved[0]
    for i in range(1, len(solved)):
        scores = jnp.where(row == i, solved[i], scores)
    scores_ref[...] = scores[:per_dev, examples : examples + nq]


def gram_scores(tiles, query_index, per_dev, inner, axis):
    nq = query_index.shape[0]
    examples = len(tiles) * tiles[0].shape[0] // SUBLANES
    return pl.pallas_call(
        functools.partial(solve_kernel, per_dev, inner, axis),
        out_shape=jax.ShapeDtypeStruct((per_dev, nq), jnp.float32),
        in_specs=[pl.BlockSpec(memory_space=pltpu.VMEM)] * (len(tiles) + 1),
        out_specs=pl.BlockSpec(memory_space=pltpu.VMEM),
        scratch_shapes=[pltpu.VMEM((examples, LANES), jnp.float32)],
        compiler_params=pltpu.CompilerParams(vmem_limit_bytes=8 * 2**20),
    )(*tiles, query_index.reshape(1, nq))


def gray(n):
    return n ^ (n >> 1)


def partner(n, inner):
    return n * inner ^ gray(n) & 1


def gather_xor(tiles, axis, size, inner):
    def swap(block, slot):
        return lax.ppermute(block, axis, [(i, i ^ slot) for i in range(size)])

    rows = sorted(range(1, size // inner), key=gray)
    column = jnp.concatenate([tiles] + [swap(tiles, partner(n, inner)) for n in rows], axis=0)
    return [column] + [swap(column, n) for n in sorted(range(1, inner), key=gray)]


def large_scores(tiles, query_index, per_dev, axis):
    sketches = tiles.reshape(-1, SUBLANES * LANES)
    gram = jnp.dot(sketches, sketches.T, precision=lax.Precision.HIGHEST)
    examples, fisher_dim = sketches.shape
    damping = damp_ratio * jnp.trace(gram) / fisher_dim
    factor = jnp.linalg.cholesky(gram + damping * jnp.eye(examples, dtype=jnp.float32))
    mine = lax.dynamic_slice_in_dim(gram, lax.axis_index(axis) * per_dev, per_dev, 0)
    half = lax.linalg.triangular_solve(factor, mine.T, left_side=True, lower=True)
    solved = lax.linalg.triangular_solve(factor, half, left_side=True, lower=True, transpose_a=True)
    selector = (query_index[:, None] == jnp.arange(examples, dtype=jnp.int32)[None, :]).astype(jnp.float32)
    return jnp.dot(selector, solved, precision=lax.Precision.HIGHEST).T


def local(activations, out_grads, project_in, project_out, lengths, query_index):
    per_dev = activations.shape[0]
    size = lax.axis_size("dp")
    tiles = sketch_rows(activations, out_grads, project_in, project_out, lengths)
    if size * per_dev + query_index.shape[0] <= LANES:
        inner = 4
        return gram_scores(gather_xor(tiles, "dp", size, inner), query_index, per_dev, inner, "dp")
    return large_scores(lax.all_gather(tiles, "dp", axis=0, tiled=True), query_index, per_dev, "dp")


def solution(mesh):
    return jax.shard_map(
        local,
        mesh=mesh,
        in_specs=(
            P(("groups", "dp"), None, None),
            P(("groups", "dp"), None, None),
            P(),
            P(),
            P(("groups", "dp")),
            P("groups"),
        ),
        out_specs=P(("groups", "dp"), None),
        check_vma=False,
    )
```

```python
import functools

import jax
import jax.numpy as jnp
from jax import lax
from jax.experimental import pallas as pl
from jax.experimental.pallas import tpu as pltpu
from jax.sharding import PartitionSpec as P

damp_ratio = 0.5
LANES = 128
SUBLANES = 8
NT = (((1,), (1,)), ((), ()))


def sketch_kernel(bounds, seq_len, act_hbm, out_hbm, pin_hbm, pout_hbm, lengths_hbm, sketch_ref, act, out, pin, pout, lengths_ref, sems, lengths_sem):
    rows, width = act.shape
    rank_dim = pin.shape[0]
    chunks = len(bounds) - 1
    lengths_copy = pltpu.make_async_copy(lengths_hbm, lengths_ref, lengths_sem)
    lengths_copy.start()
    copies = []
    for c in range(chunks):
        cols = pl.ds(bounds[c], bounds[c + 1] - bounds[c])
        copies.append(
            [
                pltpu.make_async_copy(src.at[:, cols], dst.at[:, cols], sems.at[n, c])
                for n, (src, dst) in enumerate(
                    ((pin_hbm, pin), (act_hbm, act), (pout_hbm, pout), (out_hbm, out))
                )
            ]
        )
        for copy in copies[-1]:
            copy.start()
    feat = jnp.zeros((rows, rank_dim), jnp.float32)
    grad = jnp.zeros((rank_dim, rows), jnp.float32)
    for c in range(chunks):
        cols = slice(bounds[c], bounds[c + 1])
        for copy in copies[c]:
            copy.wait()
        feat = feat + lax.dot_general(act[:, cols], pin[:, cols], NT, preferred_element_type=jnp.float32)
        grad = grad + lax.dot_general(pout[:, cols], out[:, cols], NT, preferred_element_type=jnp.float32)
    lengths_copy.wait()
    count = rows // seq_len
    reps = LANES // rank_dim
    position = lax.broadcasted_iota(jnp.int32, (rows, LANES), 0)
    band = lax.broadcasted_iota(jnp.int32, (rows, LANES), 1) // rank_dim
    live = jnp.zeros((rows, LANES), jnp.bool_)
    for e in range(count):
        first = e * seq_len
        live = live | ((band == e) & (position >= first) & (position < first + lengths_ref[e]))
    outer = lax.dot_general(
        grad,
        jnp.where(live, jnp.concatenate([feat] * reps, axis=1), 0.0),
        (((1,), (0,)), ((), ())),
        precision=lax.Precision.HIGHEST,
        preferred_element_type=jnp.float32,
    )
    band = band[:SUBLANES]
    for e in range(count):
        entry = None
        for b in range(reps):
            part = outer[b * SUBLANES : (b + 1) * SUBLANES]
            if b != e:
                part = pltpu.roll(part, (b - e) * rank_dim % LANES, 1)
            entry = part if entry is None else jnp.where(band == b, part, entry)
        sketch_ref[e * SUBLANES : (e + 1) * SUBLANES] = entry


def sketch_rows(activations, out_grads, project_in, project_out, lengths):
    count, seq_len, width = activations.shape
    rank_dim = project_in.shape[1]
    rows = count * seq_len
    unit = width // 32
    bounds = [n * unit for n in (0, 2, 6, 10, 14, 18, 22, 26, 30, 32)]
    chunks = len(bounds) - 1
    return pl.pallas_call(
        functools.partial(sketch_kernel, bounds, seq_len),
        out_shape=jax.ShapeDtypeStruct((count * SUBLANES, LANES), jnp.float32),
        in_specs=[pl.BlockSpec(memory_space=pltpu.HBM)] * 5,
        out_specs=pl.BlockSpec(memory_space=pltpu.VMEM),
        scratch_shapes=[
            pltpu.VMEM((rows, width), jnp.bfloat16),
            pltpu.VMEM((rows, width), jnp.bfloat16),
            pltpu.VMEM((rank_dim, width), jnp.bfloat16),
            pltpu.VMEM((rank_dim, width), jnp.bfloat16),
            pltpu.SMEM((count,), jnp.int32),
            pltpu.SemaphoreType.DMA((4, chunks)),
            pltpu.SemaphoreType.DMA,
        ],
        compiler_params=pltpu.CompilerParams(vmem_limit_bytes=16 * 2**20),
    )(
        *(
            pltpu.with_memory_space_constraint(operand, pltpu.HBM)
            for operand in (
                activations.reshape(rows, width),
                out_grads.reshape(rows, width),
                project_in.T,
                project_out.T,
                lengths,
            )
        ),
    )


def solve_first(system, scratch):
    step = 4

    def spread(column):
        return [jnp.broadcast_to(tile[:, column : column + 1], tile.shape) for tile in system]

    stored = {}

    def row_of(tiles, number):
        tile = tiles[number // SUBLANES]
        if id(tile) not in stored:
            slot = len(stored)
            scratch[slot] = tile
            stored[id(tile)] = slot, tile
        slot, _ = stored[id(tile)]
        row = scratch[slot, number % SUBLANES : number % SUBLANES + 1]
        return jnp.broadcast_to(row, tile.shape)

    def factor(columns, first):
        p = {(i, j): row_of(columns[j], first + i) for j in range(step) for i in range(j + 1)}
        lower, inverse = {}, [None] * step
        for k in range(0, step, 2):
            a, b, c = p[k, k], p[k, k + 1], p[k + 1, k + 1]
            inverse[k] = pl.reciprocal(a)
            inverse[k + 1] = a * pl.reciprocal(a * c - b * b)
            for m in (k, k + 1):
                for i in range(m + 1, step):
                    lower[i, m] = p[m, i] * inverse[m]
                for i in range(m + 1, step):
                    for j in range(i, step):
                        p[i, j] = p[i, j] - lower[i, m] * p[m, j]
        return lower, inverse

    def forward(lower, parts):
        parts = list(parts)
        for k in range(step):
            for i in range(k + 1, step):
                parts[i] = [part - lower[i, k] * other for part, other in zip(parts[i], parts[k])]
        return parts

    def update(tiles, columns, lower, inverse, rows):
        rows = forward(lower, [[r] for r in rows])
        for column, row, scale in zip(columns, rows, inverse):
            done = row[0] * scale
            tiles = [tile - c * done for tile, c in zip(tiles, column)]
        return tiles

    count = len(system) * SUBLANES
    columns = [spread(j) for j in range(count - step, count)]
    for first in range(count - step, 0, -step):
        pivots = range(first, first + step)
        left = pl.cdiv(first, SUBLANES)
        lower, inverse = factor(columns, first)
        across = {j: [row_of(column, j) for column in columns] for j in range(first - step, first)}
        columns = forward(lower, [c[:left] for c in columns])
        following = [update(spread(j)[:left], columns, lower, inverse, across[j]) for j in across]
        system = update(system[:left], columns, lower, inverse, [row_of(system, i) for i in pivots])
        columns = following
    lower, inverse = factor(columns, 0)
    rows = forward(lower, [[row_of(system, i)] for i in range(step)])
    solved = [row[0] * scale for row, scale in zip(rows, inverse)]
    for k in reversed(range(step)):
        for i in range(k):
            solved[i] = solved[i] - lower[k, i] * solved[k]
    return solved


def gram(x):
    high = x.astype(jnp.bfloat16)
    rest = x - high.astype(jnp.float32)
    middle = rest.astype(jnp.bfloat16)
    low = (rest - middle.astype(jnp.float32)).astype(jnp.bfloat16)
    parts = [high, middle, low]
    count = x.shape[0]
    terms = []
    for n, held in enumerate(parts):
        streamed = jnp.concatenate(parts[: len(parts) - n], axis=0)
        product = lax.dot_general(streamed, held, NT, preferred_element_type=jnp.float32)
        terms.append([product[k : k + count] for k in range(0, product.shape[0], count)])
    (hh, mh, lh), (hm, mm), (hl,) = terms
    return hh + ((mh + hm) + (lh + hl + mm))


def solve_kernel(per_dev, inner, axis, *refs):
    tiles, (query_ref, scores_ref, gram_ref, scratch) = refs[:-4], refs[-4:]
    nq = query_ref.shape[1]
    part = tiles[0].shape[0] // SUBLANES
    examples = len(tiles) * part
    outer = examples // (inner * per_dev)
    fisher_dim = SUBLANES * LANES
    gram_ref[...] = jnp.zeros(gram_ref.shape, jnp.float32)
    slot = (query_ref[...] // per_dev) ^ lax.axis_index(axis)
    n = slot // inner
    place = (gray((slot ^ partner(n, inner)) % inner) * outer + gray(n)) * per_dev + query_ref[...] % per_dev
    rest = LANES - examples - nq
    place = jnp.concatenate(
        [jnp.zeros((1, examples), jnp.int32), place] + ([jnp.zeros((1, rest), jnp.int32)] if rest else []), axis=1
    )
    lane = lax.broadcasted_iota(jnp.int32, (SUBLANES, LANES), 1)
    source = jnp.where(lane < examples, lane, jnp.broadcast_to(place, lane.shape))
    sketches = jnp.concatenate(
        [
            jnp.concatenate([tile[pl.ds(s, part, stride=SUBLANES)] for tile in tiles], axis=0)
            for s in range(SUBLANES)
        ],
        axis=1,
    )
    squares = jnp.sum(jnp.sum(sketches * sketches, axis=0, keepdims=True), axis=1, keepdims=True)
    scale = jnp.broadcast_to(1.0 / squares, (SUBLANES, LANES))
    gram_ref[:, :examples] = gram(sketches)
    row = lax.broadcasted_iota(jnp.int32, (SUBLANES, LANES), 0)
    system = []
    for first in range(0, examples, SUBLANES):
        tile = jnp.take_along_axis(gram_ref[first : first + SUBLANES], source, axis=1) * scale
        system.append(jnp.where(lane == row + first, tile + damp_ratio / fisher_dim, tile))
    solved = solve_first(system, scratch)
    scores = solved[0]
    for i in range(1, len(solved)):
        scores = jnp.where(row == i, solved[i], scores)
    scores_ref[...] = scores[:per_dev, examples : examples + nq]


def gram_scores(tiles, query_index, per_dev, inner, axis):
    nq = query_index.shape[0]
    examples = len(tiles) * tiles[0].shape[0] // SUBLANES
    return pl.pallas_call(
        functools.partial(solve_kernel, per_dev, inner, axis),
        out_shape=jax.ShapeDtypeStruct((per_dev, nq), jnp.float32),
        in_specs=[pl.BlockSpec(memory_space=pltpu.VMEM)] * (len(tiles) + 1),
        out_specs=pl.BlockSpec(memory_space=pltpu.VMEM),
        scratch_shapes=[
            pltpu.VMEM((examples, LANES), jnp.float32),
            pltpu.VMEM((3 * examples, SUBLANES, LANES), jnp.float32),
        ],
        compiler_params=pltpu.CompilerParams(vmem_limit_bytes=8 * 2**20),
    )(*tiles, query_index.reshape(1, nq))


def gray(n):
    return n ^ (n >> 1)


def partner(n, inner):
    return n * inner ^ gray(n) & 1


def gather_xor(tiles, axis, size, inner):
    def swap(block, slot):
        return lax.ppermute(block, axis, [(i, i ^ slot) for i in range(size)])

    rows = sorted(range(1, size // inner), key=gray)
    column = jnp.concatenate([tiles] + [swap(tiles, partner(n, inner)) for n in rows], axis=0)
    return [column] + [swap(column, n) for n in sorted(range(1, inner), key=gray)]


def large_scores(tiles, query_index, per_dev, axis):
    sketches = tiles.reshape(-1, SUBLANES * LANES)
    gram = jnp.dot(sketches, sketches.T, precision=lax.Precision.HIGHEST)
    examples, fisher_dim = sketches.shape
    damping = damp_ratio * jnp.trace(gram) / fisher_dim
    factor = jnp.linalg.cholesky(gram + damping * jnp.eye(examples, dtype=jnp.float32))
    mine = lax.dynamic_slice_in_dim(gram, lax.axis_index(axis) * per_dev, per_dev, 0)
    half = lax.linalg.triangular_solve(factor, mine.T, left_side=True, lower=True)
    solved = lax.linalg.triangular_solve(factor, half, left_side=True, lower=True, transpose_a=True)
    selector = (query_index[:, None] == jnp.arange(examples, dtype=jnp.int32)[None, :]).astype(jnp.float32)
    return jnp.dot(selector, solved, precision=lax.Precision.HIGHEST).T


def local(activations, out_grads, project_in, project_out, lengths, query_index):
    per_dev = activations.shape[0]
    size = lax.axis_size("dp")
    tiles = sketch_rows(activations, out_grads, project_in, project_out, lengths)
    if size * per_dev + query_index.shape[0] <= LANES:
        inner = 4
        return gram_scores(gather_xor(tiles, "dp", size, inner), query_index, per_dev, inner, "dp")
    return large_scores(lax.all_gather(tiles, "dp", axis=0, tiled=True), query_index, per_dev, "dp")


def solution(mesh):
    return jax.shard_map(
        local,
        mesh=mesh,
        in_specs=(
            P(("groups", "dp"), None, None),
            P(("groups", "dp"), None, None),
            P(),
            P(),
            P(("groups", "dp")),
            P("groups"),
        ),
        out_specs=P(("groups", "dp"), None),
        check_vma=False,
    )
```

```python
import functools

import jax
import jax.numpy as jnp
from jax import lax
from jax.experimental import pallas as pl
from jax.experimental.pallas import tpu as pltpu
from jax.sharding import PartitionSpec as P

damp_ratio = 0.5
LANES = 128
SUBLANES = 8
NT = (((1,), (1,)), ((), ()))


def sketch_kernel(bounds, seq_len, act_hbm, out_hbm, pin_hbm, pout_hbm, lengths_hbm, sketch_ref, act, out, pin, pout, lengths_ref, sems, lengths_sem):
    rows, width = act.shape
    rank_dim = pin.shape[0]
    chunks = len(bounds) - 1
    lengths_copy = pltpu.make_async_copy(lengths_hbm, lengths_ref, lengths_sem)
    lengths_copy.start()
    copies = []
    for c in range(chunks):
        cols = pl.ds(bounds[c], bounds[c + 1] - bounds[c])
        copies.append(
            [
                pltpu.make_async_copy(src.at[:, cols], dst.at[:, cols], sems.at[n, c])
                for n, (src, dst) in enumerate(
                    ((pin_hbm, pin), (act_hbm, act), (pout_hbm, pout), (out_hbm, out))
                )
            ]
        )
        for copy in copies[-1]:
            copy.start()
    feat = jnp.zeros((rows, rank_dim), jnp.float32)
    grad = jnp.zeros((rank_dim, rows), jnp.float32)
    for c in range(chunks):
        cols = slice(bounds[c], bounds[c + 1])
        for copy in copies[c]:
            copy.wait()
        feat = feat + lax.dot_general(act[:, cols], pin[:, cols], NT, preferred_element_type=jnp.float32)
        grad = grad + lax.dot_general(pout[:, cols], out[:, cols], NT, preferred_element_type=jnp.float32)
    lengths_copy.wait()
    count = rows // seq_len
    reps = LANES // rank_dim
    position = lax.broadcasted_iota(jnp.int32, (rows, LANES), 0)
    band = lax.broadcasted_iota(jnp.int32, (rows, LANES), 1) // rank_dim
    live = jnp.zeros((rows, LANES), jnp.bool_)
    for e in range(count):
        first = e * seq_len
        live = live | ((band == e) & (position >= first) & (position < first + lengths_ref[e]))
    outer = lax.dot_general(
        grad,
        jnp.where(live, jnp.concatenate([feat] * reps, axis=1), 0.0),
        (((1,), (0,)), ((), ())),
        precision=lax.Precision.HIGHEST,
        preferred_element_type=jnp.float32,
    )
    band = band[:SUBLANES]
    for e in range(count):
        entry = None
        for b in range(reps):
            part = outer[b * SUBLANES : (b + 1) * SUBLANES]
            if b != e:
                part = pltpu.roll(part, (b - e) * rank_dim % LANES, 1)
            entry = part if entry is None else jnp.where(band == b, part, entry)
        sketch_ref[e * SUBLANES : (e + 1) * SUBLANES] = entry


def sketch_rows(activations, out_grads, project_in, project_out, lengths):
    count, seq_len, width = activations.shape
    rank_dim = project_in.shape[1]
    rows = count * seq_len
    unit = width // 32
    bounds = [n * unit for n in (0, 2, 6, 10, 14, 18, 22, 26, 30, 32)]
    chunks = len(bounds) - 1
    return pl.pallas_call(
        functools.partial(sketch_kernel, bounds, seq_len),
        out_shape=jax.ShapeDtypeStruct((count * SUBLANES, LANES), jnp.float32),
        in_specs=[pl.BlockSpec(memory_space=pltpu.HBM)] * 5,
        out_specs=pl.BlockSpec(memory_space=pltpu.VMEM),
        scratch_shapes=[
            pltpu.VMEM((rows, width), jnp.bfloat16),
            pltpu.VMEM((rows, width), jnp.bfloat16),
            pltpu.VMEM((rank_dim, width), jnp.bfloat16),
            pltpu.VMEM((rank_dim, width), jnp.bfloat16),
            pltpu.SMEM((count,), jnp.int32),
            pltpu.SemaphoreType.DMA((4, chunks)),
            pltpu.SemaphoreType.DMA,
        ],
        compiler_params=pltpu.CompilerParams(vmem_limit_bytes=16 * 2**20),
    )(
        *(
            pltpu.with_memory_space_constraint(operand, pltpu.HBM)
            for operand in (
                activations.reshape(rows, width),
                out_grads.reshape(rows, width),
                project_in.T,
                project_out.T,
                lengths,
            )
        ),
    )


def solve_first(system, scratch):
    step = 4

    def spread(column):
        return [jnp.broadcast_to(tile[:, column : column + 1], tile.shape) for tile in system]

    stored = {}

    def row_of(tiles, number):
        tile = tiles[number // SUBLANES]
        if id(tile) not in stored:
            slot = len(stored)
            scratch[slot] = tile
            stored[id(tile)] = slot, tile
        slot, _ = stored[id(tile)]
        row = scratch[slot, number % SUBLANES : number % SUBLANES + 1]
        return jnp.broadcast_to(row, tile.shape)

    def factor(columns, first):
        p = {(i, j): row_of(columns[j], first + i) for j in range(step) for i in range(j + 1)}
        lower, inverse = {}, [None] * step
        for k in range(0, step, 2):
            a, b, c = p[k, k], p[k, k + 1], p[k + 1, k + 1]
            inverse[k] = pl.reciprocal(a)
            inverse[k + 1] = a * pl.reciprocal(a * c - b * b)
            for m in (k, k + 1):
                for i in range(m + 1, step):
                    lower[i, m] = p[m, i] * inverse[m]
                for i in range(m + 1, step):
                    for j in range(i, step):
                        p[i, j] = p[i, j] - lower[i, m] * p[m, j]
        return lower, inverse

    def forward(lower, parts):
        parts = list(parts)
        for k in range(step):
            for i in range(k + 1, step):
                parts[i] = [part - lower[i, k] * other for part, other in zip(parts[i], parts[k])]
        return parts

    def update(tiles, columns, lower, inverse, rows):
        rows = forward(lower, [[r] for r in rows])
        for column, row, scale in zip(columns, rows, inverse):
            done = row[0] * scale
            tiles = [tile - c * done for tile, c in zip(tiles, column)]
        return tiles

    count = len(system) * SUBLANES
    columns = [spread(j) for j in range(count - step, count)]
    for first in range(count - step, 0, -step):
        pivots = range(first, first + step)
        left = pl.cdiv(first, SUBLANES)
        lower, inverse = factor(columns, first)
        across = {j: [row_of(column, j) for column in columns] for j in range(first - step, first)}
        columns = forward(lower, [c[:left] for c in columns])
        following = [update(spread(j)[:left], columns, lower, inverse, across[j]) for j in across]
        system = update(system[:left], columns, lower, inverse, [row_of(system, i) for i in pivots])
        columns = following
    lower, inverse = factor(columns, 0)
    rows = forward(lower, [[row_of(system, i)] for i in range(step)])
    solved = [row[0] * scale for row, scale in zip(rows, inverse)]
    for k in reversed(range(step)):
        for i in range(k):
            solved[i] = solved[i] - lower[k, i] * solved[k]
    return solved


def split(x):
    high = x.astype(jnp.bfloat16)
    rest = x - high.astype(jnp.float32)
    middle = rest.astype(jnp.bfloat16)
    return [high, middle, (rest - middle.astype(jnp.float32)).astype(jnp.bfloat16)]


def products(left, right):
    count = left[0].shape[0]
    terms = []
    for n, held in enumerate(right):
        streamed = jnp.concatenate(left[: len(left) - n], axis=0)
        product = lax.dot_general(streamed, held, NT, preferred_element_type=jnp.float32)
        terms.append([product[k : k + count] for k in range(0, product.shape[0], count)])
    (hh, mh, lh), (hm, mm), (hl,) = terms
    return hh + ((mh + hm) + (lh + hl + mm))


def sketch_matrix(tile):
    count = tile.shape[0] // SUBLANES
    return jnp.concatenate([tile[pl.ds(s, count, stride=SUBLANES)] for s in range(SUBLANES)], axis=1)


def square_sums(x):
    sums = jnp.sum(x * x, axis=0, keepdims=True)
    return functools.reduce(jnp.add, [sums[:, k : k + LANES] for k in range(0, x.shape[1], LANES)])


def early_kernel(own_ref, across_ref, gram_ref, squares_ref, high_ref, middle_ref, low_ref):
    own, across = sketch_matrix(own_ref), sketch_matrix(across_ref)
    late = jnp.zeros_like(own)
    sketches = jnp.concatenate([own, late, late, across], axis=0)
    parts = split(sketches)
    for ref, part in zip((high_ref, middle_ref, low_ref), parts):
        ref[...] = part
    squares_ref[...] = square_sums(sketches)
    gram_ref[...] = jnp.zeros(gram_ref.shape, jnp.float32)
    gram_ref[:, : sketches.shape[0]] = products(parts, parts)


def solve_kernel(per_dev, inner, axis, late_ref, last_ref, gram_ref, squares_ref, high_ref, middle_ref, low_ref, query_ref, scores_ref, late_rows, scratch):
    nq = query_ref.shape[1]
    held_rows = late_ref.shape[0] // SUBLANES
    examples = gram_ref.shape[0]
    late = slice(held_rows, examples - held_rows)
    outer = examples // (inner * per_dev)
    fisher_dim = SUBLANES * LANES
    late_rows[...] = jnp.zeros(late_rows.shape, jnp.float32)
    slot = (query_ref[...] // per_dev) ^ lax.axis_index(axis)
    n = slot // inner
    place = block_of((slot ^ partner(n, inner)) % inner) * outer + (outer - gray(n)) % outer
    place = place * per_dev + query_ref[...] % per_dev
    rest = LANES - examples - nq
    place = jnp.concatenate(
        [jnp.zeros((1, examples), jnp.int32), place] + ([jnp.zeros((1, rest), jnp.int32)] if rest else []), axis=1
    )
    lane = lax.broadcasted_iota(jnp.int32, (SUBLANES, LANES), 1)
    source = jnp.where(lane < examples, lane, jnp.broadcast_to(place, lane.shape))
    sketches = jnp.concatenate([sketch_matrix(late_ref), sketch_matrix(last_ref)], axis=0)
    parts = split(sketches)
    held = [
        jnp.concatenate([ref[: late.start], part, ref[late.stop :]], axis=0)
        for ref, part in zip((high_ref, middle_ref, low_ref), parts)
    ]
    squares = jnp.sum(squares_ref[...] + square_sums(sketches), axis=1, keepdims=True)
    scale = jnp.broadcast_to(1.0 / squares, (SUBLANES, LANES))
    late_rows[late, :examples] = products(parts, held)
    turned = jnp.transpose(late_rows[...])
    row = lax.broadcasted_iota(jnp.int32, (SUBLANES, LANES), 0)
    system = []
    for first in range(0, examples, SUBLANES):
        own = slice(first, first + SUBLANES)
        if late.start <= first < late.stop:
            tile = late_rows[own]
        else:
            tile = gram_ref[own] + turned[own]
        tile = jnp.take_along_axis(tile, source, axis=1) * scale
        system.append(jnp.where(lane == row + first, tile + damp_ratio / fisher_dim, tile))
    solved = solve_first(system, scratch)
    scores = solved[0]
    for i in range(1, len(solved)):
        scores = jnp.where(row == i, solved[i], scores)
    scores_ref[...] = scores[:per_dev, examples : examples + nq]


def gram_scores(columns, query_index, per_dev, inner, axis):
    own, late, last, across = columns
    nq = query_index.shape[0]
    examples = len(columns) * own.shape[0] // SUBLANES
    width = SUBLANES * LANES
    vmem = pl.BlockSpec(memory_space=pltpu.VMEM)
    early = pl.pallas_call(
        early_kernel,
        out_shape=[
            jax.ShapeDtypeStruct((examples, LANES), jnp.float32),
            jax.ShapeDtypeStruct((1, LANES), jnp.float32),
        ]
        + [jax.ShapeDtypeStruct((examples, width), jnp.bfloat16)] * 3,
        in_specs=[vmem] * 2,
        out_specs=[vmem] * 5,
        compiler_params=pltpu.CompilerParams(vmem_limit_bytes=8 * 2**20),
        cost_estimate=pl.CostEstimate(
            flops=12 * examples * examples * width, bytes_accessed=10 * examples * width, transcendentals=0
        ),
    )(own, across)
    return pl.pallas_call(
        functools.partial(solve_kernel, per_dev, inner, axis),
        out_shape=jax.ShapeDtypeStruct((per_dev, nq), jnp.float32),
        in_specs=[vmem] * 8,
        out_specs=vmem,
        scratch_shapes=[
            pltpu.VMEM((LANES, LANES), jnp.float32),
            pltpu.VMEM((3 * examples, SUBLANES, LANES), jnp.float32),
        ],
        compiler_params=pltpu.CompilerParams(vmem_limit_bytes=8 * 2**20),
    )(late, last, *early, query_index.reshape(1, nq))


def gray(n):
    return n ^ (n >> 1)


def partner(n, inner):
    return n * inner ^ gray(n) & 1


def block_of(n):
    return jnp.where(n == 0, 0, n % 3 + 1)


def gather_xor(tiles, axis, size, inner):
    def swap(block, slot):
        return lax.ppermute(block, axis, [(i, i ^ slot) for i in range(size)])

    rows = sorted(range(1, size // inner), key=gray, reverse=True)
    column = jnp.concatenate([tiles] + [swap(tiles, partner(n, inner)) for n in rows], axis=0)
    return [column, swap(column, 3), swap(column, 1), swap(column, 2)]


def large_scores(tiles, query_index, per_dev, axis):
    sketches = tiles.reshape(-1, SUBLANES * LANES)
    gram = jnp.dot(sketches, sketches.T, precision=lax.Precision.HIGHEST)
    examples, fisher_dim = sketches.shape
    damping = damp_ratio * jnp.trace(gram) / fisher_dim
    factor = jnp.linalg.cholesky(gram + damping * jnp.eye(examples, dtype=jnp.float32))
    mine = lax.dynamic_slice_in_dim(gram, lax.axis_index(axis) * per_dev, per_dev, 0)
    half = lax.linalg.triangular_solve(factor, mine.T, left_side=True, lower=True)
    solved = lax.linalg.triangular_solve(factor, half, left_side=True, lower=True, transpose_a=True)
    selector = (query_index[:, None] == jnp.arange(examples, dtype=jnp.int32)[None, :]).astype(jnp.float32)
    return jnp.dot(selector, solved, precision=lax.Precision.HIGHEST).T


def local(activations, out_grads, project_in, project_out, lengths, query_index):
    per_dev = activations.shape[0]
    size = lax.axis_size("dp")
    tiles = sketch_rows(activations, out_grads, project_in, project_out, lengths)
    if size * per_dev + query_index.shape[0] <= LANES:
        inner = 4
        return gram_scores(gather_xor(tiles, "dp", size, inner), query_index, per_dev, inner, "dp")
    return large_scores(lax.all_gather(tiles, "dp", axis=0, tiled=True), query_index, per_dev, "dp")


def solution(mesh):
    return jax.shard_map(
        local,
        mesh=mesh,
        in_specs=(
            P(("groups", "dp"), None, None),
            P(("groups", "dp"), None, None),
            P(),
            P(),
            P(("groups", "dp")),
            P("groups"),
        ),
        out_specs=P(("groups", "dp"), None),
        check_vma=False,
    )
```

```python
import functools

import jax
import jax.numpy as jnp
from jax import lax
from jax.experimental import pallas as pl
from jax.experimental.pallas import tpu as pltpu
from jax.sharding import PartitionSpec as P

damp_ratio = 0.5
LANES = 128
SUBLANES = 8
NT = (((1,), (1,)), ((), ()))


def sketch_kernel(bounds, seq_len, act_hbm, out_hbm, pin_hbm, pout_hbm, lengths_hbm, sketch_ref, act, out, pin, pout, lengths_ref, sems, lengths_sem):
    rows, width = act.shape
    rank_dim = pin.shape[0]
    chunks = len(bounds) - 1
    lengths_copy = pltpu.make_async_copy(lengths_hbm, lengths_ref, lengths_sem)
    lengths_copy.start()
    copies = []
    for c in range(chunks):
        cols = pl.ds(bounds[c], bounds[c + 1] - bounds[c])
        copies.append(
            [
                pltpu.make_async_copy(src.at[:, cols], dst.at[:, cols], sems.at[n, c])
                for n, (src, dst) in enumerate(
                    ((pin_hbm, pin), (act_hbm, act), (pout_hbm, pout), (out_hbm, out))
                )
            ]
        )
        for copy in copies[-1]:
            copy.start()
    feat = jnp.zeros((rows, rank_dim), jnp.float32)
    grad = jnp.zeros((rank_dim, rows), jnp.float32)
    for c in range(chunks):
        cols = slice(bounds[c], bounds[c + 1])
        for copy in copies[c]:
            copy.wait()
        feat = feat + lax.dot_general(act[:, cols], pin[:, cols], NT, preferred_element_type=jnp.float32)
        grad = grad + lax.dot_general(pout[:, cols], out[:, cols], NT, preferred_element_type=jnp.float32)
    lengths_copy.wait()
    count = rows // seq_len
    reps = LANES // rank_dim
    position = lax.broadcasted_iota(jnp.int32, (rows, LANES), 0)
    band = lax.broadcasted_iota(jnp.int32, (rows, LANES), 1) // rank_dim
    live = jnp.zeros((rows, LANES), jnp.bool_)
    for e in range(count):
        first = e * seq_len
        live = live | ((band == e) & (position >= first) & (position < first + lengths_ref[e]))
    outer = lax.dot_general(
        grad,
        jnp.where(live, jnp.concatenate([feat] * reps, axis=1), 0.0),
        (((1,), (0,)), ((), ())),
        precision=lax.Precision.HIGHEST,
        preferred_element_type=jnp.float32,
    )
    band = band[:SUBLANES]
    for e in range(count):
        entry = None
        for b in range(reps):
            part = outer[b * SUBLANES : (b + 1) * SUBLANES]
            if b != e:
                part = pltpu.roll(part, (b - e) * rank_dim % LANES, 1)
            entry = part if entry is None else jnp.where(band == b, part, entry)
        sketch_ref[e * SUBLANES : (e + 1) * SUBLANES] = entry


def sketch_rows(activations, out_grads, project_in, project_out, lengths):
    count, seq_len, width = activations.shape
    rank_dim = project_in.shape[1]
    rows = count * seq_len
    unit = width // 32
    bounds = [n * unit for n in (0, 2, 6, 10, 14, 18, 22, 26, 30, 32)]
    chunks = len(bounds) - 1
    return pl.pallas_call(
        functools.partial(sketch_kernel, bounds, seq_len),
        out_shape=jax.ShapeDtypeStruct((count * SUBLANES, LANES), jnp.float32),
        in_specs=[pl.BlockSpec(memory_space=pltpu.HBM)] * 5,
        out_specs=pl.BlockSpec(memory_space=pltpu.VMEM),
        scratch_shapes=[
            pltpu.VMEM((rows, width), jnp.bfloat16),
            pltpu.VMEM((rows, width), jnp.bfloat16),
            pltpu.VMEM((rank_dim, width), jnp.bfloat16),
            pltpu.VMEM((rank_dim, width), jnp.bfloat16),
            pltpu.SMEM((count,), jnp.int32),
            pltpu.SemaphoreType.DMA((4, chunks)),
            pltpu.SemaphoreType.DMA,
        ],
        compiler_params=pltpu.CompilerParams(vmem_limit_bytes=16 * 2**20),
    )(
        *(
            pltpu.with_memory_space_constraint(operand, pltpu.HBM)
            for operand in (
                activations.reshape(rows, width),
                out_grads.reshape(rows, width),
                project_in.T,
                project_out.T,
                lengths,
            )
        ),
    )


def solve_first(system, scratch, wanted):
    step = 2

    def spread(column):
        return [jnp.broadcast_to(tile[:, column : column + 1], tile.shape) for tile in system]

    stored = {}

    def row_of(tiles, number):
        tile = tiles[number // SUBLANES]
        if id(tile) not in stored:
            slot = len(stored)
            scratch[slot] = tile
            stored[id(tile)] = slot, tile
        slot, _ = stored[id(tile)]
        row = scratch[slot, number % SUBLANES : number % SUBLANES + 1]
        return jnp.broadcast_to(row, tile.shape)

    def factor(columns, first):
        size = len(columns)
        p = {(i, j): row_of(columns[j], first + i) for j in range(size) for i in range(j + 1)}
        lower, inverse = {}, [None] * size
        for k in range(0, size, 2):
            a, b, c = p[k, k], p[k, k + 1], p[k + 1, k + 1]
            inverse[k] = pl.reciprocal(a)
            inverse[k + 1] = a * pl.reciprocal(a * c - b * b)
            for m in (k, k + 1):
                for i in range(m + 1, size):
                    lower[i, m] = p[m, i] * inverse[m]
                for i in range(m + 1, size):
                    for j in range(i, size):
                        p[i, j] = p[i, j] - lower[i, m] * p[m, j]
        return lower, inverse

    def forward(lower, parts):
        parts = list(parts)
        for k in range(len(parts)):
            for i in range(k + 1, len(parts)):
                parts[i] = [part - lower[i, k] * other for part, other in zip(parts[i], parts[k])]
        return parts

    def update(tiles, columns, lower, inverse, rows):
        rows = forward(lower, [[r] for r in rows])
        for column, row, scale in zip(columns, rows, inverse):
            done = row[0] * scale
            tiles = [tile - c * done for tile, c in zip(tiles, column)]
        return tiles

    first = len(system) * SUBLANES - step
    columns = [spread(j) for j in range(first, first + step)]
    while first >= wanted:
        left = pl.cdiv(first, SUBLANES)
        following = range(first - step, first) if first > wanted else range(wanted)
        lower, inverse = factor(columns, first)
        across = {j: [row_of(column, j) for column in columns] for j in following}
        size = len(columns)
        columns = forward(lower, [c[:left] for c in columns])
        updated = [update(spread(j)[:left], columns, lower, inverse, across[j]) for j in following]
        system = update(system[:left], columns, lower, inverse, [row_of(system, first + i) for i in range(size)])
        columns = updated
        first -= len(following)
    lower, inverse = factor(columns, 0)
    rows = forward(lower, [[row_of(system, i)] for i in range(wanted)])
    solved = [row[0] * scale for row, scale in zip(rows, inverse)]
    for k in reversed(range(wanted)):
        for i in range(k):
            solved[i] = solved[i] - lower[k, i] * solved[k]
    return solved


def gram(x):
    high = x.astype(jnp.bfloat16)
    rest = x - high.astype(jnp.float32)
    middle = rest.astype(jnp.bfloat16)
    low = (rest - middle.astype(jnp.float32)).astype(jnp.bfloat16)
    parts = [high, middle, low]
    count = x.shape[0]
    terms = []
    for n, held in enumerate(parts):
        streamed = jnp.concatenate(parts[: len(parts) - n], axis=0)
        product = lax.dot_general(streamed, held, NT, preferred_element_type=jnp.float32)
        terms.append([product[k : k + count] for k in range(0, product.shape[0], count)])
    (hh, mh, lh), (hm, mm), (hl,) = terms
    return hh + ((mh + hm) + (lh + hl + mm))


def solve_kernel(per_dev, inner, axis, *refs):
    tiles, (query_ref, scores_ref, gram_ref, scratch) = refs[:-4], refs[-4:]
    nq = query_ref.shape[1]
    part = tiles[0].shape[0] // SUBLANES
    examples = len(tiles) * part
    outer = examples // (inner * per_dev)
    fisher_dim = SUBLANES * LANES
    gram_ref[...] = jnp.zeros(gram_ref.shape, jnp.float32)
    slot = (query_ref[...] // per_dev) ^ lax.axis_index(axis)
    n = slot // inner
    place = (gray((slot ^ partner(n, inner)) % inner) * outer + gray(n)) * per_dev + query_ref[...] % per_dev
    rest = LANES - examples - nq
    place = jnp.concatenate(
        [jnp.zeros((1, examples), jnp.int32), place] + ([jnp.zeros((1, rest), jnp.int32)] if rest else []), axis=1
    )
    lane = lax.broadcasted_iota(jnp.int32, (SUBLANES, LANES), 1)
    source = jnp.where(lane < examples, lane, jnp.broadcast_to(place, lane.shape))
    sketches = jnp.concatenate(
        [
            jnp.concatenate([tile[pl.ds(s, part, stride=SUBLANES)] for tile in tiles], axis=0)
            for s in range(SUBLANES)
        ],
        axis=1,
    )
    squares = jnp.sum(jnp.sum(sketches * sketches, axis=0, keepdims=True), axis=1, keepdims=True)
    scale = jnp.broadcast_to(1.0 / squares, (SUBLANES, LANES))
    gram_ref[:, :examples] = gram(sketches)
    row = lax.broadcasted_iota(jnp.int32, (SUBLANES, LANES), 0)
    system = []
    for first in range(0, examples, SUBLANES):
        tile = jnp.take_along_axis(gram_ref[first : first + SUBLANES], source, axis=1) * scale
        system.append(jnp.where(lane == row + first, tile + damp_ratio / fisher_dim, tile))
    solved = solve_first(system, scratch, per_dev)
    scores = solved[0]
    for i in range(1, len(solved)):
        scores = jnp.where(row == i, solved[i], scores)
    scores_ref[...] = scores[:per_dev, examples : examples + nq]


def gram_scores(tiles, query_index, per_dev, inner, axis):
    nq = query_index.shape[0]
    examples = len(tiles) * tiles[0].shape[0] // SUBLANES
    return pl.pallas_call(
        functools.partial(solve_kernel, per_dev, inner, axis),
        out_shape=jax.ShapeDtypeStruct((per_dev, nq), jnp.float32),
        in_specs=[pl.BlockSpec(memory_space=pltpu.VMEM)] * (len(tiles) + 1),
        out_specs=pl.BlockSpec(memory_space=pltpu.VMEM),
        scratch_shapes=[
            pltpu.VMEM((examples, LANES), jnp.float32),
            pltpu.VMEM((4 * examples, SUBLANES, LANES), jnp.float32),
        ],
        compiler_params=pltpu.CompilerParams(vmem_limit_bytes=8 * 2**20),
    )(*tiles, query_index.reshape(1, nq))


def gray(n):
    return n ^ (n >> 1)


def partner(n, inner):
    return n * inner ^ gray(n) & 1


def gather_xor(tiles, axis, size, inner):
    def swap(block, slot):
        return lax.ppermute(block, axis, [(i, i ^ slot) for i in range(size)])

    rows = sorted(range(1, size // inner), key=gray)
    column = jnp.concatenate([tiles] + [swap(tiles, partner(n, inner)) for n in rows], axis=0)
    return [column] + [swap(column, n) for n in sorted(range(1, inner), key=gray)]


def large_scores(tiles, query_index, per_dev, axis):
    sketches = tiles.reshape(-1, SUBLANES * LANES)
    gram = jnp.dot(sketches, sketches.T, precision=lax.Precision.HIGHEST)
    examples, fisher_dim = sketches.shape
    damping = damp_ratio * jnp.trace(gram) / fisher_dim
    factor = jnp.linalg.cholesky(gram + damping * jnp.eye(examples, dtype=jnp.float32))
    mine = lax.dynamic_slice_in_dim(gram, lax.axis_index(axis) * per_dev, per_dev, 0)
    half = lax.linalg.triangular_solve(factor, mine.T, left_side=True, lower=True)
    solved = lax.linalg.triangular_solve(factor, half, left_side=True, lower=True, transpose_a=True)
    selector = (query_index[:, None] == jnp.arange(examples, dtype=jnp.int32)[None, :]).astype(jnp.float32)
    return jnp.dot(selector, solved, precision=lax.Precision.HIGHEST).T


def local(activations, out_grads, project_in, project_out, lengths, query_index):
    per_dev = activations.shape[0]
    size = lax.axis_size("dp")
    tiles = sketch_rows(activations, out_grads, project_in, project_out, lengths)
    if size * per_dev + query_index.shape[0] <= LANES:
        inner = 4
        return gram_scores(gather_xor(tiles, "dp", size, inner), query_index, per_dev, inner, "dp")
    return large_scores(lax.all_gather(tiles, "dp", axis=0, tiled=True), query_index, per_dev, "dp")


def solution(mesh):
    return jax.shard_map(
        local,
        mesh=mesh,
        in_specs=(
            P(("groups", "dp"), None, None),
            P(("groups", "dp"), None, None),
            P(),
            P(),
            P(("groups", "dp")),
            P("groups"),
        ),
        out_specs=P(("groups", "dp"), None),
        check_vma=False,
    )
```

```python
import functools

import jax
import jax.numpy as jnp
from jax import lax
from jax.experimental import pallas as pl
from jax.experimental.pallas import tpu as pltpu
from jax.sharding import PartitionSpec as P

damp_ratio = 0.5
LANES = 128
SUBLANES = 8
NT = (((1,), (1,)), ((), ()))


def sketch_kernel(bounds, seq_len, act_hbm, out_hbm, pin_hbm, pout_hbm, lengths_hbm, sketch_ref, act, out, pin, pout, lengths_ref, sems, lengths_sem):
    rows, width = act.shape
    rank_dim = pin.shape[0]
    chunks = len(bounds) - 1
    lengths_copy = pltpu.make_async_copy(lengths_hbm, lengths_ref, lengths_sem)
    lengths_copy.start()
    copies = []
    for c in range(chunks):
        cols = pl.ds(bounds[c], bounds[c + 1] - bounds[c])
        copies.append(
            [
                pltpu.make_async_copy(src.at[:, cols], dst.at[:, cols], sems.at[n, c])
                for n, (src, dst) in enumerate(
                    ((pin_hbm, pin), (act_hbm, act), (pout_hbm, pout), (out_hbm, out))
                )
            ]
        )
        for copy in copies[-1]:
            copy.start()
    feat = jnp.zeros((rank_dim, rows), jnp.float32)
    grad = jnp.zeros((rank_dim, rows), jnp.float32)
    for c in range(chunks):
        cols = slice(bounds[c], bounds[c + 1])
        for copy in copies[c]:
            copy.wait()
        feat = feat + lax.dot_general(pin[:, cols], act[:, cols], NT, preferred_element_type=jnp.float32)
        grad = grad + lax.dot_general(pout[:, cols], out[:, cols], NT, preferred_element_type=jnp.float32)
    lengths_copy.wait()
    count = rows // seq_len
    reps = LANES // rank_dim
    position = lax.broadcasted_iota(jnp.int32, (rank_dim, rows), 1)
    masked = []
    for e in range(count):
        first = e * seq_len
        live = (position >= first) & (position < first + lengths_ref[e])
        masked.append(jnp.where(live, feat, 0.0))
    outer = lax.dot_general(
        grad,
        jnp.concatenate(masked, axis=0),
        NT,
        precision=lax.Precision.HIGHEST,
        preferred_element_type=jnp.float32,
    )
    band = lax.broadcasted_iota(jnp.int32, (SUBLANES, LANES), 1) // rank_dim
    for e in range(count):
        entry = None
        for b in range(reps):
            part = outer[b * SUBLANES : (b + 1) * SUBLANES]
            if b != e:
                part = pltpu.roll(part, (b - e) * rank_dim % LANES, 1)
            entry = part if entry is None else jnp.where(band == b, part, entry)
        sketch_ref[e * SUBLANES : (e + 1) * SUBLANES] = entry


def sketch_rows(activations, out_grads, project_in, project_out, lengths):
    count, seq_len, width = activations.shape
    rank_dim = project_in.shape[1]
    rows = count * seq_len
    unit = width // 32
    bounds = [n * unit for n in (0, 1, 3, 6, 10, 14, 18, 22, 26, 30, 32)]
    chunks = len(bounds) - 1
    return pl.pallas_call(
        functools.partial(sketch_kernel, bounds, seq_len),
        out_shape=jax.ShapeDtypeStruct((count * SUBLANES, LANES), jnp.float32),
        in_specs=[pl.BlockSpec(memory_space=pltpu.HBM)] * 5,
        out_specs=pl.BlockSpec(memory_space=pltpu.VMEM),
        scratch_shapes=[
            pltpu.VMEM((rows, width), jnp.bfloat16),
            pltpu.VMEM((rows, width), jnp.bfloat16),
            pltpu.VMEM((rank_dim, width), jnp.bfloat16),
            pltpu.VMEM((rank_dim, width), jnp.bfloat16),
            pltpu.SMEM((count,), jnp.int32),
            pltpu.SemaphoreType.DMA((4, chunks)),
            pltpu.SemaphoreType.DMA,
        ],
        compiler_params=pltpu.CompilerParams(vmem_limit_bytes=16 * 2**20),
    )(
        *(
            pltpu.with_memory_space_constraint(operand, pltpu.HBM)
            for operand in (
                activations.reshape(rows, width),
                out_grads.reshape(rows, width),
                project_in.T,
                project_out.T,
                lengths,
            )
        ),
    )


def solve_first(system, plain, scratch):
    step = 4

    def spread(column):
        return [jnp.broadcast_to(tile[:, column : column + 1], tile.shape) for tile in plain]

    stored = {}

    def row_of(tiles, number):
        tile = tiles[number // SUBLANES]
        if id(tile) not in stored:
            slot = len(stored)
            scratch[slot] = tile
            stored[id(tile)] = slot, tile
        slot, _ = stored[id(tile)]
        row = scratch[slot, number % SUBLANES : number % SUBLANES + 1]
        return jnp.broadcast_to(row, tile.shape)

    def factor(columns, first):
        p = {(i, j): row_of(columns[j], first + i) for j in range(step) for i in range(j + 1)}
        lower, inverse = {}, [None] * step
        for k in range(0, step, 2):
            a, b, c = p[k, k], p[k, k + 1], p[k + 1, k + 1]
            inverse[k] = pl.reciprocal(a)
            inverse[k + 1] = a * pl.reciprocal(a * c - b * b)
            for m in (k, k + 1):
                for i in range(m + 1, step):
                    lower[i, m] = p[m, i] * inverse[m]
                for i in range(m + 1, step):
                    for j in range(i, step):
                        p[i, j] = p[i, j] - lower[i, m] * p[m, j]
        return lower, inverse

    def forward(lower, parts):
        parts = list(parts)
        for k in range(step):
            for i in range(k + 1, step):
                parts[i] = [part - lower[i, k] * other for part, other in zip(parts[i], parts[k])]
        return parts

    def update(tiles, columns, lower, inverse, rows):
        rows = forward(lower, [[r] for r in rows])
        for column, row, scale in zip(columns, rows, inverse):
            done = row[0] * scale
            tiles = [tile - c * done for tile, c in zip(tiles, column)]
        return tiles

    count = len(system) * SUBLANES
    columns = [spread(j) for j in range(count - step, count)]
    for first in range(count - step, 0, -step):
        pivots = range(first, first + step)
        left = pl.cdiv(first, SUBLANES)
        lower, inverse = factor(columns, first)
        across = {j: [row_of(column, j) for column in columns] for j in range(first - step, first)}
        columns = forward(lower, [c[:left] for c in columns])
        following = [update(spread(j)[:left], columns, lower, inverse, across[j]) for j in across]
        system = plain = update(system[:left], columns, lower, inverse, [row_of(system, i) for i in pivots])
        columns = following
    lower, inverse = factor(columns, 0)
    rows = forward(lower, [[row_of(system, i)] for i in range(step)])
    solved = [row[0] * scale for row, scale in zip(rows, inverse)]
    for k in reversed(range(step)):
        for i in range(k):
            solved[i] = solved[i] - lower[k, i] * solved[k]
    return solved


def gram(x):
    high = x.astype(jnp.bfloat16)
    rest = x - high.astype(jnp.float32)
    middle = rest.astype(jnp.bfloat16)
    low = (rest - middle.astype(jnp.float32)).astype(jnp.bfloat16)
    parts = [high, middle, low]
    count = x.shape[0]
    terms = []
    for n, held in enumerate(parts):
        streamed = jnp.concatenate(parts[: len(parts) - n], axis=0)
        product = lax.dot_general(streamed, held, NT, preferred_element_type=jnp.float32)
        terms.append([product[k : k + count] for k in range(0, product.shape[0], count)])
    (hh, mh, lh), (hm, mm), (hl,) = terms
    return hh + ((mh + hm) + (lh + hl + mm))


def solve_kernel(per_dev, inner, axis, *refs):
    tiles, (query_ref, scores_ref, gram_ref, scratch) = refs[:-4], refs[-4:]
    nq = query_ref.shape[1]
    part = tiles[0].shape[0] // SUBLANES
    examples = len(tiles) * part
    outer = examples // (inner * per_dev)
    fisher_dim = SUBLANES * LANES
    gram_ref[...] = jnp.zeros(gram_ref.shape, jnp.float32)
    slot = (query_ref[...] // per_dev) ^ lax.axis_index(axis)
    n = slot // inner
    place = (gray((slot ^ partner(n, inner)) % inner) * outer + gray(n)) * per_dev + query_ref[...] % per_dev
    rest = LANES - examples - nq
    place = jnp.concatenate(
        [jnp.zeros((1, examples), jnp.int32), place] + ([jnp.zeros((1, rest), jnp.int32)] if rest else []), axis=1
    )
    lane = lax.broadcasted_iota(jnp.int32, (SUBLANES, LANES), 1)
    source = jnp.where(lane < examples, lane, jnp.broadcast_to(place, lane.shape))
    sketches = jnp.concatenate(
        [
            jnp.concatenate([tile[pl.ds(s, part, stride=SUBLANES)] for tile in tiles], axis=0)
            for s in range(SUBLANES)
        ],
        axis=1,
    )
    squares = jnp.sum(jnp.sum(sketches * sketches, axis=0, keepdims=True), axis=1, keepdims=True)
    scale = jnp.broadcast_to(1.0 / squares, (SUBLANES, LANES))
    gram_ref[:, :examples] = gram(sketches)
    row = lax.broadcasted_iota(jnp.int32, (SUBLANES, LANES), 0)
    system, plain = [], []
    for first in range(0, examples, SUBLANES):
        tile = gram_ref[first : first + SUBLANES] * scale
        plain.append(jnp.where(lane == row + first, tile + damp_ratio / fisher_dim, tile))
        system.append(jnp.where(lane < examples, plain[-1], jnp.take_along_axis(tile, source, axis=1)))
    solved = solve_first(system, plain, scratch)
    scores = solved[0]
    for i in range(1, len(solved)):
        scores = jnp.where(row == i, solved[i], scores)
    scores_ref[...] = scores[:per_dev, examples : examples + nq]


def gram_scores(tiles, query_index, per_dev, inner, axis):
    nq = query_index.shape[0]
    examples = len(tiles) * tiles[0].shape[0] // SUBLANES
    return pl.pallas_call(
        functools.partial(solve_kernel, per_dev, inner, axis),
        out_shape=jax.ShapeDtypeStruct((per_dev, nq), jnp.float32),
        in_specs=[pl.BlockSpec(memory_space=pltpu.VMEM)] * (len(tiles) + 1),
        out_specs=pl.BlockSpec(memory_space=pltpu.VMEM),
        scratch_shapes=[
            pltpu.VMEM((examples, LANES), jnp.float32),
            pltpu.VMEM((3 * examples, SUBLANES, LANES), jnp.float32),
        ],
        compiler_params=pltpu.CompilerParams(vmem_limit_bytes=8 * 2**20),
    )(*tiles, query_index.reshape(1, nq))


def gray(n):
    return n ^ (n >> 1)


def partner(n, inner):
    return n * inner ^ gray(n) & 1


def gather_xor(tiles, axis, size, inner):
    def swap(block, slot):
        return lax.ppermute(block, axis, [(i, i ^ slot) for i in range(size)])

    rows = sorted(range(1, size // inner), key=gray)
    column = jnp.concatenate([tiles] + [swap(tiles, partner(n, inner)) for n in rows], axis=0)
    return [column] + [swap(column, n) for n in sorted(range(1, inner), key=gray)]


def large_scores(tiles, query_index, per_dev, axis):
    sketches = tiles.reshape(-1, SUBLANES * LANES)
    gram = jnp.dot(sketches, sketches.T, precision=lax.Precision.HIGHEST)
    examples, fisher_dim = sketches.shape
    damping = damp_ratio * jnp.trace(gram) / fisher_dim
    factor = jnp.linalg.cholesky(gram + damping * jnp.eye(examples, dtype=jnp.float32))
    mine = lax.dynamic_slice_in_dim(gram, lax.axis_index(axis) * per_dev, per_dev, 0)
    half = lax.linalg.triangular_solve(factor, mine.T, left_side=True, lower=True)
    solved = lax.linalg.triangular_solve(factor, half, left_side=True, lower=True, transpose_a=True)
    selector = (query_index[:, None] == jnp.arange(examples, dtype=jnp.int32)[None, :]).astype(jnp.float32)
    return jnp.dot(selector, solved, precision=lax.Precision.HIGHEST).T


def local(activations, out_grads, project_in, project_out, lengths, query_index):
    per_dev = activations.shape[0]
    size = lax.axis_size("dp")
    tiles = sketch_rows(activations, out_grads, project_in, project_out, lengths)
    if size * per_dev + query_index.shape[0] <= LANES:
        inner = 4
        return gram_scores(gather_xor(tiles, "dp", size, inner), query_index, per_dev, inner, "dp")
    return large_scores(lax.all_gather(tiles, "dp", axis=0, tiled=True), query_index, per_dev, "dp")


def solution(mesh):
    return jax.shard_map(
        local,
        mesh=mesh,
        in_specs=(
            P(("groups", "dp"), None, None),
            P(("groups", "dp"), None, None),
            P(),
            P(),
            P(("groups", "dp")),
            P("groups"),
        ),
        out_specs=P(("groups", "dp"), None),
        check_vma=False,
    )
```

```python
import functools

import jax
import jax.numpy as jnp
from jax import lax
from jax.experimental import pallas as pl
from jax.experimental.pallas import tpu as pltpu
from jax.sharding import PartitionSpec as P

damp_ratio = 0.5
LANES = 128
SUBLANES = 8
NT = (((1,), (1,)), ((), ()))


def sketch_kernel(bounds, seq_len, act_hbm, out_hbm, pin_hbm, pout_hbm, lengths_hbm, sketch_ref, act, out, pin, pout, lengths_ref, sems, lengths_sem):
    rows, width = act.shape
    rank_dim = pin.shape[0]
    chunks = len(bounds) - 1
    lengths_copy = pltpu.make_async_copy(lengths_hbm, lengths_ref, lengths_sem)
    lengths_copy.start()
    copies = []
    for c in range(chunks):
        cols = pl.ds(bounds[c], bounds[c + 1] - bounds[c])
        copies.append(
            [
                pltpu.make_async_copy(src.at[:, cols], dst.at[:, cols], sems.at[n, c])
                for n, (src, dst) in enumerate(
                    ((pin_hbm, pin), (act_hbm, act), (pout_hbm, pout), (out_hbm, out))
                )
            ]
        )
        for copy in copies[-1]:
            copy.start()
    feat = jnp.zeros((rows, rank_dim), jnp.float32)
    grad = jnp.zeros((rank_dim, rows), jnp.float32)
    for c in range(chunks):
        cols = slice(bounds[c], bounds[c + 1])
        for copy in copies[c]:
            copy.wait()
        feat = feat + lax.dot_general(act[:, cols], pin[:, cols], NT, preferred_element_type=jnp.float32)
        grad = grad + lax.dot_general(pout[:, cols], out[:, cols], NT, preferred_element_type=jnp.float32)
    lengths_copy.wait()
    count = rows // seq_len
    reps = LANES // rank_dim
    position = lax.broadcasted_iota(jnp.int32, (rows, LANES), 0)
    band = lax.broadcasted_iota(jnp.int32, (rows, LANES), 1) // rank_dim
    live = jnp.zeros((rows, LANES), jnp.bool_)
    for e in range(count):
        first = e * seq_len
        live = live | ((band == e) & (position >= first) & (position < first + lengths_ref[e]))
    outer = lax.dot_general(
        grad,
        jnp.where(live, jnp.concatenate([feat] * reps, axis=1), 0.0),
        (((1,), (0,)), ((), ())),
        precision=lax.Precision.HIGHEST,
        preferred_element_type=jnp.float32,
    )
    band = band[:SUBLANES]
    for e in range(count):
        entry = None
        for b in range(reps):
            part = outer[b * SUBLANES : (b + 1) * SUBLANES]
            if b != e:
                part = pltpu.roll(part, (b - e) * rank_dim % LANES, 1)
            entry = part if entry is None else jnp.where(band == b, part, entry)
        sketch_ref[e * SUBLANES : (e + 1) * SUBLANES] = entry


def sketch_rows(activations, out_grads, project_in, project_out, lengths):
    count, seq_len, width = activations.shape
    rank_dim = project_in.shape[1]
    rows = count * seq_len
    unit = width // 32
    bounds = [n * unit for n in (0, 2, 6, 10, 14, 18, 22, 26, 30, 32)]
    chunks = len(bounds) - 1
    return pl.pallas_call(
        functools.partial(sketch_kernel, bounds, seq_len),
        out_shape=jax.ShapeDtypeStruct((count * SUBLANES, LANES), jnp.float32),
        in_specs=[pl.BlockSpec(memory_space=pltpu.HBM)] * 5,
        out_specs=pl.BlockSpec(memory_space=pltpu.VMEM),
        scratch_shapes=[
            pltpu.VMEM((rows, width), jnp.bfloat16),
            pltpu.VMEM((rows, width), jnp.bfloat16),
            pltpu.VMEM((rank_dim, width), jnp.bfloat16),
            pltpu.VMEM((rank_dim, width), jnp.bfloat16),
            pltpu.SMEM((count,), jnp.int32),
            pltpu.SemaphoreType.DMA((4, chunks)),
            pltpu.SemaphoreType.DMA,
        ],
        compiler_params=pltpu.CompilerParams(vmem_limit_bytes=16 * 2**20),
    )(
        *(
            pltpu.with_memory_space_constraint(operand, pltpu.HBM)
            for operand in (
                activations.reshape(rows, width),
                out_grads.reshape(rows, width),
                project_in.T,
                project_out.T,
                lengths,
            )
        ),
    )


def solve_first(system, plain, scratch):
    step = 4

    def spread(column):
        return [jnp.broadcast_to(tile[:, column : column + 1], tile.shape) for tile in plain]

    stored = {}

    def row_of(tiles, number):
        tile = tiles[number // SUBLANES]
        if id(tile) not in stored:
            slot = len(stored)
            scratch[slot] = tile
            stored[id(tile)] = slot, tile
        slot, _ = stored[id(tile)]
        row = scratch[slot, number % SUBLANES : number % SUBLANES + 1]
        return jnp.broadcast_to(row, tile.shape)

    def factor(columns, first):
        p = {(i, j): row_of(columns[j], first + i) for j in range(step) for i in range(j + 1)}
        lower, inverse = {}, [None] * step
        for k in range(0, step, 2):
            a, b, c = p[k, k], p[k, k + 1], p[k + 1, k + 1]
            inverse[k] = pl.reciprocal(a)
            inverse[k + 1] = a * pl.reciprocal(a * c - b * b)
            for m in (k, k + 1):
                for i in range(m + 1, step):
                    lower[i, m] = p[m, i] * inverse[m]
                for i in range(m + 1, step):
                    for j in range(i, step):
                        p[i, j] = p[i, j] - lower[i, m] * p[m, j]
        return lower, inverse

    def forward(lower, parts):
        parts = list(parts)
        for k in range(step):
            for i in range(k + 1, step):
                parts[i] = [part - lower[i, k] * other for part, other in zip(parts[i], parts[k])]
        return parts

    def update(tiles, columns, lower, inverse, rows):
        rows = forward(lower, [[r] for r in rows])
        for column, row, scale in zip(columns, rows, inverse):
            done = row[0] * scale
            tiles = [tile - c * done for tile, c in zip(tiles, column)]
        return tiles

    count = len(system) * SUBLANES
    columns = [spread(j) for j in range(count - step, count)]
    for first in range(count - step, 0, -step):
        pivots = range(first, first + step)
        left = pl.cdiv(first, SUBLANES)
        lower, inverse = factor(columns, first)
        across = {j: [row_of(column, j) for column in columns] for j in range(first - step, first)}
        columns = forward(lower, [c[:left] for c in columns])
        following = [update(spread(j)[:left], columns, lower, inverse, across[j]) for j in across]
        system = plain = update(system[:left], columns, lower, inverse, [row_of(system, i) for i in pivots])
        columns = following
    lower, inverse = factor(columns, 0)
    rows = forward(lower, [[row_of(system, i)] for i in range(step)])
    solved = [row[0] * scale for row, scale in zip(rows, inverse)]
    for k in reversed(range(step)):
        for i in range(k):
            solved[i] = solved[i] - lower[k, i] * solved[k]
    return solved


def gram(x):
    high = x.astype(jnp.bfloat16)
    rest = x - high.astype(jnp.float32)
    middle = rest.astype(jnp.bfloat16)
    low = (rest - middle.astype(jnp.float32)).astype(jnp.bfloat16)
    parts = [high, middle, low]
    count = x.shape[0]
    terms = []
    for n, held in enumerate(parts):
        streamed = jnp.concatenate(parts[: len(parts) - n], axis=0)
        product = lax.dot_general(streamed, held, NT, preferred_element_type=jnp.float32)
        terms.append([product[k : k + count] for k in range(0, product.shape[0], count)])
    (hh, mh, lh), (hm, mm), (hl,) = terms
    return hh + ((mh + hm) + (lh + hl + mm))


def solve_kernel(per_dev, inner, axis, *refs):
    tiles, (query_ref, scores_ref, gram_ref, scratch) = refs[:-4], refs[-4:]
    nq = query_ref.shape[1]
    part = tiles[0].shape[0] // SUBLANES
    examples = len(tiles) * part
    outer = examples // (inner * per_dev)
    fisher_dim = SUBLANES * LANES
    gram_ref[...] = jnp.zeros(gram_ref.shape, jnp.float32)
    slot = (query_ref[...] // per_dev) ^ lax.axis_index(axis)
    n = slot // inner
    place = ((slot ^ partner(n, inner)) % inner * outer + gray(n)) * per_dev + query_ref[...] % per_dev
    rest = LANES - examples - nq
    place = jnp.concatenate(
        [jnp.zeros((1, examples), jnp.int32), place] + ([jnp.zeros((1, rest), jnp.int32)] if rest else []), axis=1
    )
    lane = lax.broadcasted_iota(jnp.int32, (SUBLANES, LANES), 1)
    source = jnp.where(lane < examples, lane, jnp.broadcast_to(place, lane.shape))
    sketches = jnp.concatenate(
        [
            jnp.concatenate([tile[pl.ds(s, part, stride=SUBLANES)] for tile in tiles], axis=0)
            for s in range(SUBLANES)
        ],
        axis=1,
    )
    squares = jnp.sum(jnp.sum(sketches * sketches, axis=0, keepdims=True), axis=1, keepdims=True)
    scale = jnp.broadcast_to(1.0 / squares, (SUBLANES, LANES))
    gram_ref[:, :examples] = gram(sketches)
    row = lax.broadcasted_iota(jnp.int32, (SUBLANES, LANES), 0)
    system, plain = [], []
    for first in range(0, examples, SUBLANES):
        tile = gram_ref[first : first + SUBLANES] * scale
        plain.append(jnp.where(lane == row + first, tile + damp_ratio / fisher_dim, tile))
        system.append(jnp.where(lane < examples, plain[-1], jnp.take_along_axis(tile, source, axis=1)))
    solved = solve_first(system, plain, scratch)
    scores = solved[0]
    for i in range(1, len(solved)):
        scores = jnp.where(row == i, solved[i], scores)
    scores_ref[...] = scores[:per_dev, examples : examples + nq]


def gram_scores(tiles, query_index, per_dev, inner, axis):
    nq = query_index.shape[0]
    examples = len(tiles) * tiles[0].shape[0] // SUBLANES
    return pl.pallas_call(
        functools.partial(solve_kernel, per_dev, inner, axis),
        out_shape=jax.ShapeDtypeStruct((per_dev, nq), jnp.float32),
        in_specs=[pl.BlockSpec(memory_space=pltpu.VMEM)] * (len(tiles) + 1),
        out_specs=pl.BlockSpec(memory_space=pltpu.VMEM),
        scratch_shapes=[
            pltpu.VMEM((examples, LANES), jnp.float32),
            pltpu.VMEM((3 * examples, SUBLANES, LANES), jnp.float32),
        ],
        compiler_params=pltpu.CompilerParams(vmem_limit_bytes=8 * 2**20),
    )(*tiles, query_index.reshape(1, nq))


def gray(n):
    return n ^ (n >> 1)


def partner(n, inner):
    return n * inner ^ gray(n) & 1


def gather_xor(tiles, axis, size, inner):
    def swap(block, slot):
        return lax.ppermute(block, axis, [(i, i ^ slot) for i in range(size)])

    rows = sorted(range(1, size // inner), key=gray)
    column = jnp.concatenate([tiles] + [swap(tiles, partner(n, inner)) for n in rows], axis=0)
    return [column] + [swap(column, n) for n in range(1, inner)]


def large_scores(tiles, query_index, per_dev, axis):
    sketches = tiles.reshape(-1, SUBLANES * LANES)
    gram = jnp.dot(sketches, sketches.T, precision=lax.Precision.HIGHEST)
    examples, fisher_dim = sketches.shape
    damping = damp_ratio * jnp.trace(gram) / fisher_dim
    factor = jnp.linalg.cholesky(gram + damping * jnp.eye(examples, dtype=jnp.float32))
    mine = lax.dynamic_slice_in_dim(gram, lax.axis_index(axis) * per_dev, per_dev, 0)
    half = lax.linalg.triangular_solve(factor, mine.T, left_side=True, lower=True)
    solved = lax.linalg.triangular_solve(factor, half, left_side=True, lower=True, transpose_a=True)
    selector = (query_index[:, None] == jnp.arange(examples, dtype=jnp.int32)[None, :]).astype(jnp.float32)
    return jnp.dot(selector, solved, precision=lax.Precision.HIGHEST).T


def local(activations, out_grads, project_in, project_out, lengths, query_index):
    per_dev = activations.shape[0]
    size = lax.axis_size("dp")
    tiles = sketch_rows(activations, out_grads, project_in, project_out, lengths)
    if size * per_dev + query_index.shape[0] <= LANES:
        inner = 4
        return gram_scores(gather_xor(tiles, "dp", size, inner), query_index, per_dev, inner, "dp")
    return large_scores(lax.all_gather(tiles, "dp", axis=0, tiled=True), query_index, per_dev, "dp")


def solution(mesh):
    return jax.shard_map(
        local,
        mesh=mesh,
        in_specs=(
            P(("groups", "dp"), None, None),
            P(("groups", "dp"), None, None),
            P(),
            P(),
            P(("groups", "dp")),
            P("groups"),
        ),
        out_specs=P(("groups", "dp"), None),
        check_vma=False,
    )
```

```python
import functools

import jax
import jax.numpy as jnp
from jax import lax
from jax.experimental import pallas as pl
from jax.experimental.pallas import tpu as pltpu
from jax.sharding import PartitionSpec as P

damp_ratio = 0.5
LANES = 128
SUBLANES = 8
NT = (((1,), (1,)), ((), ()))


def sketch_kernel(bounds, seq_len, act_hbm, out_hbm, pin_hbm, pout_hbm, lengths_hbm, sketch_ref, act, out, pin, pout, lengths_ref, sems, lengths_sem):
    rows, width = act.shape
    rank_dim = pin.shape[0]
    chunks = len(bounds) - 1
    lengths_copy = pltpu.make_async_copy(lengths_hbm, lengths_ref, lengths_sem)
    lengths_copy.start()
    copies = []
    for c in range(chunks):
        cols = pl.ds(bounds[c], bounds[c + 1] - bounds[c])
        copies.append(
            [
                pltpu.make_async_copy(src.at[:, cols], dst.at[:, cols], sems.at[n, c])
                for n, (src, dst) in enumerate(
                    ((pin_hbm, pin), (act_hbm, act), (pout_hbm, pout), (out_hbm, out))
                )
            ]
        )
        for copy in copies[-1]:
            copy.start()
    feat = jnp.zeros((rows, rank_dim), jnp.float32)
    grad = jnp.zeros((rank_dim, rows), jnp.float32)
    for c in range(chunks):
        cols = slice(bounds[c], bounds[c + 1])
        for copy in copies[c]:
            copy.wait()
        feat = feat + lax.dot_general(act[:, cols], pin[:, cols], NT, preferred_element_type=jnp.float32)
        grad = grad + lax.dot_general(pout[:, cols], out[:, cols], NT, preferred_element_type=jnp.float32)
    lengths_copy.wait()
    count = rows // seq_len
    reps = LANES // rank_dim
    position = lax.broadcasted_iota(jnp.int32, (rows, LANES), 0)
    band = lax.broadcasted_iota(jnp.int32, (rows, LANES), 1) // rank_dim
    live = jnp.zeros((rows, LANES), jnp.bool_)
    for e in range(count):
        first = e * seq_len
        live = live | ((band == e) & (position >= first) & (position < first + lengths_ref[e]))
    outer = lax.dot_general(
        grad,
        jnp.where(live, jnp.concatenate([feat] * reps, axis=1), 0.0),
        (((1,), (0,)), ((), ())),
        precision=lax.Precision.HIGHEST,
        preferred_element_type=jnp.float32,
    )
    band = band[:SUBLANES]
    for e in range(count):
        entry = None
        for b in range(reps):
            part = outer[b * SUBLANES : (b + 1) * SUBLANES]
            if b != e:
                part = pltpu.roll(part, (b - e) * rank_dim % LANES, 1)
            entry = part if entry is None else jnp.where(band == b, part, entry)
        sketch_ref[e * SUBLANES : (e + 1) * SUBLANES] = entry


def sketch_rows(activations, out_grads, project_in, project_out, lengths):
    count, seq_len, width = activations.shape
    rank_dim = project_in.shape[1]
    rows = count * seq_len
    unit = width // 32
    bounds = [n * unit for n in (0, 2, 6, 10, 14, 18, 22, 26, 30, 32)]
    chunks = len(bounds) - 1
    return pl.pallas_call(
        functools.partial(sketch_kernel, bounds, seq_len),
        out_shape=jax.ShapeDtypeStruct((count * SUBLANES, LANES), jnp.float32),
        in_specs=[pl.BlockSpec(memory_space=pltpu.HBM)] * 5,
        out_specs=pl.BlockSpec(memory_space=pltpu.VMEM),
        scratch_shapes=[
            pltpu.VMEM((rows, width), jnp.bfloat16),
            pltpu.VMEM((rows, width), jnp.bfloat16),
            pltpu.VMEM((rank_dim, width), jnp.bfloat16),
            pltpu.VMEM((rank_dim, width), jnp.bfloat16),
            pltpu.SMEM((count,), jnp.int32),
            pltpu.SemaphoreType.DMA((4, chunks)),
            pltpu.SemaphoreType.DMA,
        ],
        compiler_params=pltpu.CompilerParams(vmem_limit_bytes=16 * 2**20),
    )(
        *(
            pltpu.with_memory_space_constraint(operand, pltpu.HBM)
            for operand in (
                activations.reshape(rows, width),
                out_grads.reshape(rows, width),
                project_in.T,
                project_out.T,
                lengths,
            )
        ),
    )


def solve_first(system, plain, scratch):
    step = 4

    def spread(column):
        return [jnp.broadcast_to(tile[:, column : column + 1], tile.shape) for tile in plain]

    stored = {}

    def row_of(tiles, number):
        tile = tiles[number // SUBLANES]
        if id(tile) not in stored:
            slot = len(stored)
            scratch[slot] = tile
            stored[id(tile)] = slot, tile
        slot, _ = stored[id(tile)]
        row = scratch[slot, number % SUBLANES : number % SUBLANES + 1]
        return jnp.broadcast_to(row, tile.shape)

    def factor(columns, first):
        p = {(i, j): row_of(columns[j], first + i) for j in range(step) for i in range(j + 1)}
        lower, inverse = {}, [None] * step
        for k in range(0, step, 2):
            a, b, c = p[k, k], p[k, k + 1], p[k + 1, k + 1]
            inverse[k] = pl.reciprocal(a)
            inverse[k + 1] = a * pl.reciprocal(a * c - b * b)
            for m in (k, k + 1):
                for i in range(m + 1, step):
                    lower[i, m] = p[m, i] * inverse[m]
                for i in range(m + 1, step):
                    for j in range(i, step):
                        p[i, j] = p[i, j] - lower[i, m] * p[m, j]
        return lower, inverse

    def forward(lower, parts):
        parts = list(parts)
        for k in range(step):
            for i in range(k + 1, step):
                parts[i] = [part - lower[i, k] * other for part, other in zip(parts[i], parts[k])]
        return parts

    def update(tiles, columns, lower, inverse, rows):
        rows = forward(lower, [[r] for r in rows])
        for column, row, scale in zip(columns, rows, inverse):
            done = row[0] * scale
            tiles = [tile - c * done for tile, c in zip(tiles, column)]
        return tiles

    count = len(system) * SUBLANES
    columns = [spread(j) for j in range(count - step, count)]
    for first in range(count - step, 0, -step):
        pivots = range(first, first + step)
        left = pl.cdiv(first, SUBLANES)
        lower, inverse = factor(columns, first)
        across = {j: [row_of(column, j) for column in columns] for j in range(first - step, first)}
        columns = forward(lower, [c[:left] for c in columns])
        following = [update(spread(j)[:left], columns, lower, inverse, across[j]) for j in across]
        system = plain = update(system[:left], columns, lower, inverse, [row_of(system, i) for i in pivots])
        columns = following
    lower, inverse = factor(columns, 0)
    rows = forward(lower, [[row_of(system, i)] for i in range(step)])
    solved = [row[0] * scale for row, scale in zip(rows, inverse)]
    for k in reversed(range(step)):
        for i in range(k):
            solved[i] = solved[i] - lower[k, i] * solved[k]
    return solved


def gram(x):
    high = x.astype(jnp.bfloat16)
    rest = x - high.astype(jnp.float32)
    middle = rest.astype(jnp.bfloat16)
    low = (rest - middle.astype(jnp.float32)).astype(jnp.bfloat16)
    parts = [high, middle, low]
    count = x.shape[0]
    terms = []
    for n, held in enumerate(parts):
        streamed = jnp.concatenate(parts[: len(parts) - n], axis=0)
        product = lax.dot_general(streamed, held, NT, preferred_element_type=jnp.float32)
        terms.append([product[k : k + count] for k in range(0, product.shape[0], count)])
    (hh, mh, lh), (hm, mm), (hl,) = terms
    return hh + ((mh + hm) + (lh + hl + mm))


def solve_kernel(per_dev, inner, axis, *refs):
    tiles, (query_ref, scores_ref, gram_ref, scratch) = refs[:-4], refs[-4:]
    nq = query_ref.shape[1]
    part = tiles[0].shape[0] // SUBLANES
    examples = len(tiles) * part
    outer = examples // (inner * per_dev)
    fisher_dim = SUBLANES * LANES
    gram_ref[...] = jnp.zeros(gram_ref.shape, jnp.float32)
    slot = (query_ref[...] // per_dev) ^ lax.axis_index(axis)
    n = slot // inner
    place = (gray((slot ^ partner(n, inner)) % inner) * outer + gray(n)) * per_dev + query_ref[...] % per_dev
    rest = LANES - examples - nq
    place = jnp.concatenate(
        [jnp.zeros((1, examples), jnp.int32), place] + ([jnp.zeros((1, rest), jnp.int32)] if rest else []), axis=1
    )
    lane = lax.broadcasted_iota(jnp.int32, (SUBLANES, LANES), 1)
    source = jnp.where(lane < examples, lane, jnp.broadcast_to(place, lane.shape))
    sketches = jnp.concatenate(
        [
            jnp.concatenate([tile[pl.ds(s, part, stride=SUBLANES)] for tile in tiles], axis=0)
            for s in range(SUBLANES)
        ],
        axis=1,
    )
    squares = jnp.sum(jnp.sum(sketches * sketches, axis=0, keepdims=True), axis=1, keepdims=True)
    scale = jnp.broadcast_to(1.0 / squares, (SUBLANES, LANES))
    gram_ref[:, :examples] = gram(sketches)
    row = lax.broadcasted_iota(jnp.int32, (SUBLANES, LANES), 0)
    system, plain = [], []
    for first in range(0, examples, SUBLANES):
        tile = gram_ref[first : first + SUBLANES] * scale
        plain.append(jnp.where(lane == row + first, tile + damp_ratio / fisher_dim, tile))
        system.append(jnp.where(lane < examples, plain[-1], jnp.take_along_axis(tile, source, axis=1)))
    solved = solve_first(system, plain, scratch)
    scores = solved[0]
    for i in range(1, len(solved)):
        scores = jnp.where(row == i, solved[i], scores)
    scores_ref[...] = scores[:per_dev, examples : examples + nq]


def gram_scores(tiles, query_index, per_dev, inner, axis):
    nq = query_index.shape[0]
    examples = len(tiles) * tiles[0].shape[0] // SUBLANES
    return pl.pallas_call(
        functools.partial(solve_kernel, per_dev, inner, axis),
        out_shape=jax.ShapeDtypeStruct((per_dev, nq), jnp.float32),
        in_specs=[pl.BlockSpec(memory_space=pltpu.VMEM)] * (len(tiles) + 1),
        out_specs=pl.BlockSpec(memory_space=pltpu.VMEM),
        scratch_shapes=[
            pltpu.VMEM((examples, LANES), jnp.float32),
            pltpu.VMEM((3 * examples, SUBLANES, LANES), jnp.float32),
        ],
        compiler_params=pltpu.CompilerParams(vmem_limit_bytes=8 * 2**20),
    )(*tiles, query_index.reshape(1, nq))


def gray(n):
    return n ^ (n >> 1)


def partner(n, inner):
    return n * inner ^ gray(n) & 1


def gather_xor(tiles, axis, size, inner):
    def swap(block, slot):
        return lax.ppermute(block, axis, [(i, i ^ slot) for i in range(size)])

    rows = sorted(range(1, size // inner), key=gray)
    column = jnp.concatenate([tiles] + [swap(tiles, partner(n, inner)) for n in rows], axis=0)
    return [column] + [swap(column, n) for n in sorted(range(1, inner), key=gray)]


def large_scores(tiles, query_index, per_dev, axis):
    sketches = tiles.reshape(-1, SUBLANES * LANES)
    gram = jnp.dot(sketches, sketches.T, precision=lax.Precision.HIGHEST)
    examples, fisher_dim = sketches.shape
    damping = damp_ratio * jnp.trace(gram) / fisher_dim
    factor = jnp.linalg.cholesky(gram + damping * jnp.eye(examples, dtype=jnp.float32))
    mine = lax.dynamic_slice_in_dim(gram, lax.axis_index(axis) * per_dev, per_dev, 0)
    half = lax.linalg.triangular_solve(factor, mine.T, left_side=True, lower=True)
    solved = lax.linalg.triangular_solve(factor, half, left_side=True, lower=True, transpose_a=True)
    selector = (query_index[:, None] == jnp.arange(examples, dtype=jnp.int32)[None, :]).astype(jnp.float32)
    return jnp.dot(selector, solved, precision=lax.Precision.HIGHEST).T


def local(activations, out_grads, project_in, project_out, lengths, query_index):
    per_dev = activations.shape[0]
    size = lax.axis_size("dp")
    tiles = sketch_rows(activations, out_grads, project_in, project_out, lengths)
    if size * per_dev + query_index.shape[0] <= LANES:
        inner = 4
        return gram_scores(gather_xor(tiles, "dp", size, inner), query_index, per_dev, inner, "dp")
    return large_scores(lax.all_gather(tiles, "dp", axis=0, tiled=True), query_index, per_dev, "dp")


def solution(mesh):
    return jax.shard_map(
        local,
        mesh=mesh,
        in_specs=(
            P(("groups", "dp"), None, None),
            P(("groups", "dp"), None, None),
            P(),
            P(),
            P(("groups", "dp")),
            P("groups"),
        ),
        out_specs=P(("groups", "dp"), None),
        check_vma=False,
    )
```

```python
import functools

import jax
import jax.numpy as jnp
from jax import lax
from jax.experimental import pallas as pl
from jax.experimental.pallas import tpu as pltpu
from jax.sharding import PartitionSpec as P

damp_ratio = 0.5
LANES = 128
SUBLANES = 8
NT = (((1,), (1,)), ((), ()))


def sketch_kernel(bounds, seq_len, act_hbm, out_hbm, pin_hbm, pout_hbm, lengths_hbm, sketch_ref, act, out, pin, pout, lengths_ref, sems, lengths_sem):
    rows, width = act.shape
    rank_dim = pin.shape[0]
    chunks = len(bounds) - 1
    lengths_copy = pltpu.make_async_copy(lengths_hbm, lengths_ref, lengths_sem)
    lengths_copy.start()
    copies = []
    for c in range(chunks):
        cols = pl.ds(bounds[c], bounds[c + 1] - bounds[c])
        copies.append(
            [
                pltpu.make_async_copy(src.at[:, cols], dst.at[:, cols], sems.at[n, c])
                for n, (src, dst) in enumerate(
                    ((pin_hbm, pin), (act_hbm, act), (pout_hbm, pout), (out_hbm, out))
                )
            ]
        )
        for copy in copies[-1]:
            copy.start()
    feat = jnp.zeros((rows, rank_dim), jnp.float32)
    grad = jnp.zeros((rank_dim, rows), jnp.float32)
    for c in range(chunks):
        cols = slice(bounds[c], bounds[c + 1])
        for copy in copies[c]:
            copy.wait()
        feat = feat + lax.dot_general(act[:, cols], pin[:, cols], NT, preferred_element_type=jnp.float32)
        grad = grad + lax.dot_general(pout[:, cols], out[:, cols], NT, preferred_element_type=jnp.float32)
    lengths_copy.wait()
    count = rows // seq_len
    reps = LANES // rank_dim
    position = lax.broadcasted_iota(jnp.int32, (rows, LANES), 0)
    band = lax.broadcasted_iota(jnp.int32, (rows, LANES), 1) // rank_dim
    live = jnp.zeros((rows, LANES), jnp.bool_)
    for e in range(count):
        first = e * seq_len
        live = live | ((band == e) & (position >= first) & (position < first + lengths_ref[e]))
    outer = lax.dot_general(
        grad,
        jnp.where(live, jnp.concatenate([feat] * reps, axis=1), 0.0),
        (((1,), (0,)), ((), ())),
        precision=lax.Precision.HIGHEST,
        preferred_element_type=jnp.float32,
    )
    band = band[:SUBLANES]
    for e in range(count):
        entry = None
        for b in range(reps):
            part = outer[b * SUBLANES : (b + 1) * SUBLANES]
            if b != e:
                part = pltpu.roll(part, (b - e) * rank_dim % LANES, 1)
            entry = part if entry is None else jnp.where(band == b, part, entry)
        sketch_ref[e * SUBLANES : (e + 1) * SUBLANES] = entry


def sketch_rows(activations, out_grads, project_in, project_out, lengths):
    count, seq_len, width = activations.shape
    rank_dim = project_in.shape[1]
    rows = count * seq_len
    unit = width // 32
    bounds = [n * unit for n in (0, 2, 6, 10, 14, 18, 22, 26, 30, 32)]
    chunks = len(bounds) - 1
    return pl.pallas_call(
        functools.partial(sketch_kernel, bounds, seq_len),
        out_shape=jax.ShapeDtypeStruct((count * SUBLANES, LANES), jnp.float32),
        in_specs=[pl.BlockSpec(memory_space=pltpu.HBM)] * 5,
        out_specs=pl.BlockSpec(memory_space=pltpu.VMEM),
        scratch_shapes=[
            pltpu.VMEM((rows, width), jnp.bfloat16),
            pltpu.VMEM((rows, width), jnp.bfloat16),
            pltpu.VMEM((rank_dim, width), jnp.bfloat16),
            pltpu.VMEM((rank_dim, width), jnp.bfloat16),
            pltpu.SMEM((count,), jnp.int32),
            pltpu.SemaphoreType.DMA((4, chunks)),
            pltpu.SemaphoreType.DMA,
        ],
        compiler_params=pltpu.CompilerParams(vmem_limit_bytes=16 * 2**20),
    )(
        *(
            pltpu.with_memory_space_constraint(operand, pltpu.HBM)
            for operand in (
                activations.reshape(rows, width),
                out_grads.reshape(rows, width),
                project_in.T,
                project_out.T,
                lengths,
            )
        ),
    )


def solve_first(system, plain, scratch):
    step = 4

    def spread(column):
        return [jnp.broadcast_to(tile[:, column : column + 1], tile.shape) for tile in plain]

    stored = {}

    def row_of(tiles, number):
        tile = tiles[number // SUBLANES]
        if id(tile) not in stored:
            slot = len(stored)
            scratch[slot] = tile
            stored[id(tile)] = slot, tile
        slot, _ = stored[id(tile)]
        row = scratch[slot, number % SUBLANES : number % SUBLANES + 1]
        return jnp.broadcast_to(row, tile.shape)

    def factor(columns, first):
        p = {(i, j): row_of(columns[j], first + i) for j in range(step) for i in range(j + 1)}
        lower, inverse = {}, [None] * step
        for k in range(0, step, 2):
            a, b, c = p[k, k], p[k, k + 1], p[k + 1, k + 1]
            inverse[k] = pl.reciprocal(a)
            inverse[k + 1] = a * pl.reciprocal(a * c - b * b)
            for m in (k, k + 1):
                for i in range(m + 1, step):
                    lower[i, m] = p[m, i] * inverse[m]
                for i in range(m + 1, step):
                    for j in range(i, step):
                        p[i, j] = p[i, j] - lower[i, m] * p[m, j]
        return lower, inverse

    def forward(lower, parts):
        parts = list(parts)
        for k in range(step):
            for i in range(k + 1, step):
                parts[i] = [part - lower[i, k] * other for part, other in zip(parts[i], parts[k])]
        return parts

    def update(tiles, columns, lower, inverse, rows):
        rows = forward(lower, [[r] for r in rows])
        for column, row, scale in zip(columns, rows, inverse):
            done = row[0] * scale
            tiles = [tile - c * done for tile, c in zip(tiles, column)]
        return tiles

    count = len(system) * SUBLANES
    columns = [spread(j) for j in range(count - step, count)]
    for first in range(count - step, 0, -step):
        pivots = range(first, first + step)
        left = pl.cdiv(first, SUBLANES)
        lower, inverse = factor(columns, first)
        across = {j: [row_of(column, j) for column in columns] for j in range(first - step, first)}
        columns = forward(lower, [c[:left] for c in columns])
        following = [update(spread(j)[:left], columns, lower, inverse, across[j]) for j in across]
        system = plain = update(system[:left], columns, lower, inverse, [row_of(system, i) for i in pivots])
        columns = following
    lower, inverse = factor(columns, 0)
    rows = forward(lower, [[row_of(system, i)] for i in range(step)])
    solved = [row[0] * scale for row, scale in zip(rows, inverse)]
    for k in reversed(range(step)):
        for i in range(k):
            solved[i] = solved[i] - lower[k, i] * solved[k]
    return solved


def gram(x):
    high = x.astype(jnp.bfloat16)
    rest = x - high.astype(jnp.float32)
    middle = rest.astype(jnp.bfloat16)
    low = (rest - middle.astype(jnp.float32)).astype(jnp.bfloat16)
    parts = [high, middle, low]
    count = x.shape[0]
    terms = []
    for n, held in enumerate(parts):
        streamed = jnp.concatenate(parts[: len(parts) - n], axis=0)
        product = lax.dot_general(streamed, held, NT, preferred_element_type=jnp.float32)
        terms.append([product[k : k + count] for k in range(0, product.shape[0], count)])
    (hh, mh, lh), (hm, mm), (hl,) = terms
    return hh + ((mh + hm) + (lh + hl + mm))


def solve_kernel(per_dev, inner, axis, *refs):
    tiles, (query_ref, scores_ref, gram_ref, scratch) = refs[:-4], refs[-4:]
    nq = query_ref.shape[1]
    part = tiles[0].shape[0] // SUBLANES
    examples = len(tiles) * part
    outer = examples // (inner * per_dev)
    fisher_dim = SUBLANES * LANES
    gram_ref[...] = jnp.zeros(gram_ref.shape, jnp.float32)
    slot = (query_ref[...] // per_dev) ^ lax.axis_index(axis)
    n = slot // inner
    place = (gray((slot ^ partner(n, inner)) % inner) * outer + gray(n)) * per_dev + query_ref[...] % per_dev
    rest = LANES - examples - nq
    place = jnp.concatenate(
        [jnp.zeros((1, examples), jnp.int32), place] + ([jnp.zeros((1, rest), jnp.int32)] if rest else []), axis=1
    )
    lane = lax.broadcasted_iota(jnp.int32, (SUBLANES, LANES), 1)
    source = jnp.where(lane < examples, lane, jnp.broadcast_to(place, lane.shape))
    sketches = jnp.concatenate(
        [
            jnp.concatenate([tile[pl.ds(s, part, stride=SUBLANES)] for tile in tiles], axis=0)
            for s in range(SUBLANES)
        ],
        axis=1,
    )
    squares = jnp.sum(jnp.sum(sketches * sketches, axis=0, keepdims=True), axis=1, keepdims=True)
    scale = jnp.broadcast_to(1.0 / squares, (SUBLANES, LANES))
    gram_ref[:, :examples] = gram(sketches)
    row = lax.broadcasted_iota(jnp.int32, (SUBLANES, LANES), 0)
    system, plain = [], []
    for first in range(0, examples, SUBLANES):
        tile = gram_ref[first : first + SUBLANES] * scale
        plain.append(jnp.where(lane == row + first, tile + damp_ratio / fisher_dim, tile))
        system.append(jnp.where(lane < examples, plain[-1], jnp.take_along_axis(tile, source, axis=1)))
    solved = solve_first(system, plain, scratch)
    scores = solved[0]
    for i in range(1, len(solved)):
        scores = jnp.where(row == i, solved[i], scores)
    scores_ref[...] = scores[:per_dev, examples : examples + nq]


def gram_scores(tiles, query_index, per_dev, inner, axis):
    nq = query_index.shape[0]
    examples = len(tiles) * tiles[0].shape[0] // SUBLANES
    return pl.pallas_call(
        functools.partial(solve_kernel, per_dev, inner, axis),
        out_shape=jax.ShapeDtypeStruct((per_dev, nq), jnp.float32),
        in_specs=[pl.BlockSpec(memory_space=pltpu.VMEM)] * (len(tiles) + 1),
        out_specs=pl.BlockSpec(memory_space=pltpu.VMEM),
        scratch_shapes=[
            pltpu.VMEM((examples, LANES), jnp.float32),
            pltpu.VMEM((3 * examples, SUBLANES, LANES), jnp.float32),
        ],
        compiler_params=pltpu.CompilerParams(vmem_limit_bytes=8 * 2**20),
    )(*tiles, query_index.reshape(1, nq))


def gray(n):
    return n ^ (n >> 1)


def partner(n, inner):
    return n * inner ^ (n >> 1) & ~n & 1


def gather_xor(tiles, axis, size, inner):
    def swap(block, slot):
        return lax.ppermute(block, axis, [(i, i ^ slot) for i in range(size)])

    rows = sorted(range(1, size // inner), key=gray)
    column = jnp.concatenate([tiles] + [swap(tiles, partner(n, inner)) for n in rows], axis=0)
    return [column] + [swap(column, n) for n in sorted(range(1, inner), key=gray)]


def large_scores(tiles, query_index, per_dev, axis):
    sketches = tiles.reshape(-1, SUBLANES * LANES)
    gram = jnp.dot(sketches, sketches.T, precision=lax.Precision.HIGHEST)
    examples, fisher_dim = sketches.shape
    damping = damp_ratio * jnp.trace(gram) / fisher_dim
    factor = jnp.linalg.cholesky(gram + damping * jnp.eye(examples, dtype=jnp.float32))
    mine = lax.dynamic_slice_in_dim(gram, lax.axis_index(axis) * per_dev, per_dev, 0)
    half = lax.linalg.triangular_solve(factor, mine.T, left_side=True, lower=True)
    solved = lax.linalg.triangular_solve(factor, half, left_side=True, lower=True, transpose_a=True)
    selector = (query_index[:, None] == jnp.arange(examples, dtype=jnp.int32)[None, :]).astype(jnp.float32)
    return jnp.dot(selector, solved, precision=lax.Precision.HIGHEST).T


def local(activations, out_grads, project_in, project_out, lengths, query_index):
    per_dev = activations.shape[0]
    size = lax.axis_size("dp")
    tiles = sketch_rows(activations, out_grads, project_in, project_out, lengths)
    if size * per_dev + query_index.shape[0] <= LANES:
        inner = 4
        return gram_scores(gather_xor(tiles, "dp", size, inner), query_index, per_dev, inner, "dp")
    return large_scores(lax.all_gather(tiles, "dp", axis=0, tiled=True), query_index, per_dev, "dp")


def solution(mesh):
    return jax.shard_map(
        local,
        mesh=mesh,
        in_specs=(
            P(("groups", "dp"), None, None),
            P(("groups", "dp"), None, None),
            P(),
            P(),
            P(("groups", "dp")),
            P("groups"),
        ),
        out_specs=P(("groups", "dp"), None),
        check_vma=False,
    )
```

```python
import functools

import jax
import jax.numpy as jnp
from jax import lax
from jax.experimental import pallas as pl
from jax.experimental.pallas import tpu as pltpu
from jax.sharding import PartitionSpec as P

damp_ratio = 0.5
LANES = 128
SUBLANES = 8
NT = (((1,), (1,)), ((), ()))


def sketch_kernel(bounds, seq_len, act_hbm, out_hbm, pin_hbm, pout_hbm, lengths_hbm, sketch_ref, act, out, pin, pout, lengths_ref, sems, lengths_sem):
    rows, width = act.shape
    rank_dim = pin.shape[0]
    chunks = len(bounds) - 1
    lengths_copy = pltpu.make_async_copy(lengths_hbm, lengths_ref, lengths_sem)
    lengths_copy.start()
    copies = []
    for c in range(chunks):
        cols = pl.ds(bounds[c], bounds[c + 1] - bounds[c])
        copies.append(
            [
                pltpu.make_async_copy(src.at[:, cols], dst.at[:, cols], sems.at[n, c])
                for n, (src, dst) in enumerate(
                    ((pin_hbm, pin), (act_hbm, act), (pout_hbm, pout), (out_hbm, out))
                )
            ]
        )
        for copy in copies[-1]:
            copy.start()
    feat = [jnp.zeros((rows, rank_dim), jnp.float32)] * 2
    grad = [jnp.zeros((rank_dim, rows), jnp.float32)] * 2
    for c in range(chunks):
        middle = (bounds[c] + bounds[c + 1]) // 2
        for copy in copies[c]:
            copy.wait()
        for n, cols in enumerate((slice(bounds[c], middle), slice(middle, bounds[c + 1]))):
            feat[n] = feat[n] + lax.dot_general(act[:, cols], pin[:, cols], NT, preferred_element_type=jnp.float32)
            grad[n] = grad[n] + lax.dot_general(pout[:, cols], out[:, cols], NT, preferred_element_type=jnp.float32)
    feat, grad = feat[0] + feat[1], grad[0] + grad[1]
    lengths_copy.wait()
    count = rows // seq_len
    reps = LANES // rank_dim
    position = lax.broadcasted_iota(jnp.int32, (rows, LANES), 0)
    band = lax.broadcasted_iota(jnp.int32, (rows, LANES), 1) // rank_dim
    live = jnp.zeros((rows, LANES), jnp.bool_)
    for e in range(count):
        first = e * seq_len
        live = live | ((band == e) & (position >= first) & (position < first + lengths_ref[e]))
    outer = lax.dot_general(
        grad,
        jnp.where(live, jnp.concatenate([feat] * reps, axis=1), 0.0),
        (((1,), (0,)), ((), ())),
        precision=lax.Precision.HIGHEST,
        preferred_element_type=jnp.float32,
    )
    band = band[:SUBLANES]
    for e in range(count):
        entry = None
        for b in range(reps):
            part = outer[b * SUBLANES : (b + 1) * SUBLANES]
            if b != e:
                part = pltpu.roll(part, (b - e) * rank_dim % LANES, 1)
            entry = part if entry is None else jnp.where(band == b, part, entry)
        sketch_ref[e * SUBLANES : (e + 1) * SUBLANES] = entry


def sketch_rows(activations, out_grads, project_in, project_out, lengths):
    count, seq_len, width = activations.shape
    rank_dim = project_in.shape[1]
    rows = count * seq_len
    unit = width // 32
    bounds = [n * unit for n in (0, 2, 6, 10, 14, 18, 22, 26, 30, 32)]
    chunks = len(bounds) - 1
    return pl.pallas_call(
        functools.partial(sketch_kernel, bounds, seq_len),
        out_shape=jax.ShapeDtypeStruct((count * SUBLANES, LANES), jnp.float32),
        in_specs=[pl.BlockSpec(memory_space=pltpu.HBM)] * 5,
        out_specs=pl.BlockSpec(memory_space=pltpu.VMEM),
        scratch_shapes=[
            pltpu.VMEM((rows, width), jnp.bfloat16),
            pltpu.VMEM((rows, width), jnp.bfloat16),
            pltpu.VMEM((rank_dim, width), jnp.bfloat16),
            pltpu.VMEM((rank_dim, width), jnp.bfloat16),
            pltpu.SMEM((count,), jnp.int32),
            pltpu.SemaphoreType.DMA((4, chunks)),
            pltpu.SemaphoreType.DMA,
        ],
        compiler_params=pltpu.CompilerParams(vmem_limit_bytes=16 * 2**20),
    )(
        *(
            pltpu.with_memory_space_constraint(operand, pltpu.HBM)
            for operand in (
                activations.reshape(rows, width),
                out_grads.reshape(rows, width),
                project_in.T,
                project_out.T,
                lengths,
            )
        ),
    )


def solve_first(system, plain, scratch):
    step = 4

    def spread(column):
        return [jnp.broadcast_to(tile[:, column : column + 1], tile.shape) for tile in plain]

    stored = {}

    def row_of(tiles, number):
        tile = tiles[number // SUBLANES]
        if id(tile) not in stored:
            slot = len(stored)
            scratch[slot] = tile
            stored[id(tile)] = slot, tile
        slot, _ = stored[id(tile)]
        row = scratch[slot, number % SUBLANES : number % SUBLANES + 1]
        return jnp.broadcast_to(row, tile.shape)

    def factor(columns, first):
        p = {(i, j): row_of(columns[j], first + i) for j in range(step) for i in range(j + 1)}
        lower, inverse = {}, [None] * step
        for k in range(0, step, 2):
            a, b, c = p[k, k], p[k, k + 1], p[k + 1, k + 1]
            inverse[k] = pl.reciprocal(a)
            inverse[k + 1] = a * pl.reciprocal(a * c - b * b)
            for m in (k, k + 1):
                for i in range(m + 1, step):
                    lower[i, m] = p[m, i] * inverse[m]
                for i in range(m + 1, step):
                    for j in range(i, step):
                        p[i, j] = p[i, j] - lower[i, m] * p[m, j]
        return lower, inverse

    def forward(lower, parts):
        parts = list(parts)
        for k in range(step):
            for i in range(k + 1, step):
                parts[i] = [part - lower[i, k] * other for part, other in zip(parts[i], parts[k])]
        return parts

    def update(tiles, columns, lower, inverse, rows):
        rows = forward(lower, [[r] for r in rows])
        for column, row, scale in zip(columns, rows, inverse):
            done = row[0] * scale
            tiles = [tile - c * done for tile, c in zip(tiles, column)]
        return tiles

    count = len(system) * SUBLANES
    columns = [spread(j) for j in range(count - step, count)]
    for first in range(count - step, 0, -step):
        pivots = range(first, first + step)
        left = pl.cdiv(first, SUBLANES)
        lower, inverse = factor(columns, first)
        across = {j: [row_of(column, j) for column in columns] for j in range(first - step, first)}
        columns = forward(lower, [c[:left] for c in columns])
        following = [update(spread(j)[:left], columns, lower, inverse, across[j]) for j in across]
        system = plain = update(system[:left], columns, lower, inverse, [row_of(system, i) for i in pivots])
        columns = following
    lower, inverse = factor(columns, 0)
    rows = forward(lower, [[row_of(system, i)] for i in range(step)])
    solved = [row[0] * scale for row, scale in zip(rows, inverse)]
    for k in reversed(range(step)):
        for i in range(k):
            solved[i] = solved[i] - lower[k, i] * solved[k]
    return solved


def gram(x):
    high = x.astype(jnp.bfloat16)
    rest = x - high.astype(jnp.float32)
    middle = rest.astype(jnp.bfloat16)
    low = (rest - middle.astype(jnp.float32)).astype(jnp.bfloat16)
    parts = [high, middle, low]
    count = x.shape[0]
    terms = []
    for n, held in enumerate(parts):
        streamed = jnp.concatenate(parts[: len(parts) - n], axis=0)
        product = lax.dot_general(streamed, held, NT, preferred_element_type=jnp.float32)
        terms.append([product[k : k + count] for k in range(0, product.shape[0], count)])
    (hh, mh, lh), (hm, mm), (hl,) = terms
    return hh + ((mh + hm) + (lh + hl + mm))


def solve_kernel(per_dev, inner, axis, *refs):
    tiles, (query_ref, scores_ref, gram_ref, scratch) = refs[:-4], refs[-4:]
    nq = query_ref.shape[1]
    part = tiles[0].shape[0] // SUBLANES
    examples = len(tiles) * part
    outer = examples // (inner * per_dev)
    fisher_dim = SUBLANES * LANES
    gram_ref[...] = jnp.zeros(gram_ref.shape, jnp.float32)
    slot = (query_ref[...] // per_dev) ^ lax.axis_index(axis)
    n = slot // inner
    place = (gray((slot ^ partner(n, inner)) % inner) * outer + gray(n)) * per_dev + query_ref[...] % per_dev
    rest = LANES - examples - nq
    place = jnp.concatenate(
        [jnp.zeros((1, examples), jnp.int32), place] + ([jnp.zeros((1, rest), jnp.int32)] if rest else []), axis=1
    )
    lane = lax.broadcasted_iota(jnp.int32, (SUBLANES, LANES), 1)
    source = jnp.where(lane < examples, lane, jnp.broadcast_to(place, lane.shape))
    sketches = jnp.concatenate(
        [
            jnp.concatenate([tile[pl.ds(s, part, stride=SUBLANES)] for tile in tiles], axis=0)
            for s in range(SUBLANES)
        ],
        axis=1,
    )
    squares = jnp.sum(jnp.sum(sketches * sketches, axis=0, keepdims=True), axis=1, keepdims=True)
    scale = jnp.broadcast_to(1.0 / squares, (SUBLANES, LANES))
    gram_ref[:, :examples] = gram(sketches)
    row = lax.broadcasted_iota(jnp.int32, (SUBLANES, LANES), 0)
    system, plain = [], []
    for first in range(0, examples, SUBLANES):
        tile = gram_ref[first : first + SUBLANES] * scale
        plain.append(jnp.where(lane == row + first, tile + damp_ratio / fisher_dim, tile))
        system.append(jnp.where(lane < examples, plain[-1], jnp.take_along_axis(tile, source, axis=1)))
    solved = solve_first(system, plain, scratch)
    scores = solved[0]
    for i in range(1, len(solved)):
        scores = jnp.where(row == i, solved[i], scores)
    scores_ref[...] = scores[:per_dev, examples : examples + nq]


def gram_scores(tiles, query_index, per_dev, inner, axis):
    nq = query_index.shape[0]
    examples = len(tiles) * tiles[0].shape[0] // SUBLANES
    return pl.pallas_call(
        functools.partial(solve_kernel, per_dev, inner, axis),
        out_shape=jax.ShapeDtypeStruct((per_dev, nq), jnp.float32),
        in_specs=[pl.BlockSpec(memory_space=pltpu.VMEM)] * (len(tiles) + 1),
        out_specs=pl.BlockSpec(memory_space=pltpu.VMEM),
        scratch_shapes=[
            pltpu.VMEM((examples, LANES), jnp.float32),
            pltpu.VMEM((3 * examples, SUBLANES, LANES), jnp.float32),
        ],
        compiler_params=pltpu.CompilerParams(vmem_limit_bytes=8 * 2**20),
    )(*tiles, query_index.reshape(1, nq))


def gray(n):
    return n ^ (n >> 1)


def partner(n, inner):
    return n * inner ^ (n >> 1) & ~n & 1


def gather_xor(tiles, axis, size, inner):
    def swap(block, slot):
        return lax.ppermute(block, axis, [(i, i ^ slot) for i in range(size)])

    rows = sorted(range(1, size // inner), key=gray)
    column = jnp.concatenate([tiles] + [swap(tiles, partner(n, inner)) for n in rows], axis=0)
    return [column] + [swap(column, n) for n in sorted(range(1, inner), key=gray)]


def large_scores(tiles, query_index, per_dev, axis):
    sketches = tiles.reshape(-1, SUBLANES * LANES)
    gram = jnp.dot(sketches, sketches.T, precision=lax.Precision.HIGHEST)
    examples, fisher_dim = sketches.shape
    damping = damp_ratio * jnp.trace(gram) / fisher_dim
    factor = jnp.linalg.cholesky(gram + damping * jnp.eye(examples, dtype=jnp.float32))
    mine = lax.dynamic_slice_in_dim(gram, lax.axis_index(axis) * per_dev, per_dev, 0)
    half = lax.linalg.triangular_solve(factor, mine.T, left_side=True, lower=True)
    solved = lax.linalg.triangular_solve(factor, half, left_side=True, lower=True, transpose_a=True)
    selector = (query_index[:, None] == jnp.arange(examples, dtype=jnp.int32)[None, :]).astype(jnp.float32)
    return jnp.dot(selector, solved, precision=lax.Precision.HIGHEST).T


def local(activations, out_grads, project_in, project_out, lengths, query_index):
    per_dev = activations.shape[0]
    size = lax.axis_size("dp")
    tiles = sketch_rows(activations, out_grads, project_in, project_out, lengths)
    if size * per_dev + query_index.shape[0] <= LANES:
        inner = 4
        return gram_scores(gather_xor(tiles, "dp", size, inner), query_index, per_dev, inner, "dp")
    return large_scores(lax.all_gather(tiles, "dp", axis=0, tiled=True), query_index, per_dev, "dp")


def solution(mesh):
    return jax.shard_map(
        local,
        mesh=mesh,
        in_specs=(
            P(("groups", "dp"), None, None),
            P(("groups", "dp"), None, None),
            P(),
            P(),
            P(("groups", "dp")),
            P("groups"),
        ),
        out_specs=P(("groups", "dp"), None),
        check_vma=False,
    )
```

```python
import functools

import jax
import jax.numpy as jnp
from jax import lax
from jax.experimental import pallas as pl
from jax.experimental.pallas import tpu as pltpu
from jax.sharding import PartitionSpec as P

damp_ratio = 0.5
LANES = 128
SUBLANES = 8
NT = (((1,), (1,)), ((), ()))


def sketch_kernel(bounds, seq_len, act_hbm, out_hbm, pin_hbm, pout_hbm, lengths_hbm, sketch_ref, act, out, pin, pout, lengths_ref, sems, lengths_sem):
    rows, width = act.shape
    rank_dim = pin.shape[0]
    chunks = len(bounds) - 1
    lengths_copy = pltpu.make_async_copy(lengths_hbm, lengths_ref, lengths_sem)
    lengths_copy.start()
    copies = []
    for c in range(chunks):
        cols = pl.ds(bounds[c], bounds[c + 1] - bounds[c])
        copies.append(
            [
                pltpu.make_async_copy(src.at[:, cols], dst.at[:, cols], sems.at[n, c])
                for n, (src, dst) in enumerate(
                    ((pin_hbm, pin), (act_hbm, act), (pout_hbm, pout), (out_hbm, out))
                )
            ]
        )
        for copy in copies[-1]:
            copy.start()
    feat = [jnp.zeros((rows, rank_dim), jnp.float32)] * 2
    grad = [jnp.zeros((rank_dim, rows), jnp.float32)] * 2
    for c in range(chunks):
        middle = (bounds[c] + bounds[c + 1]) // 2
        for copy in copies[c]:
            copy.wait()
        for n, cols in enumerate((slice(bounds[c], middle), slice(middle, bounds[c + 1]))):
            feat[n] = feat[n] + lax.dot_general(act[:, cols], pin[:, cols], NT, preferred_element_type=jnp.float32)
            grad[n] = grad[n] + lax.dot_general(pout[:, cols], out[:, cols], NT, preferred_element_type=jnp.float32)
    feat, grad = feat[0] + feat[1], grad[0] + grad[1]
    lengths_copy.wait()
    count = rows // seq_len
    reps = LANES // rank_dim
    position = lax.broadcasted_iota(jnp.int32, (rows, LANES), 0)
    band = lax.broadcasted_iota(jnp.int32, (rows, LANES), 1) // rank_dim
    live = jnp.zeros((rows, LANES), jnp.bool_)
    for e in range(count):
        first = e * seq_len
        live = live | ((band == e) & (position >= first) & (position < first + lengths_ref[e]))
    outer = lax.dot_general(
        grad,
        jnp.where(live, jnp.concatenate([feat] * reps, axis=1), 0.0),
        (((1,), (0,)), ((), ())),
        precision=lax.Precision.HIGHEST,
        preferred_element_type=jnp.float32,
    )
    band = band[:SUBLANES]
    for e in range(count):
        entry = None
        for b in range(reps):
            part = outer[b * SUBLANES : (b + 1) * SUBLANES]
            if b != e:
                part = pltpu.roll(part, (b - e) * rank_dim % LANES, 1)
            entry = part if entry is None else jnp.where(band == b, part, entry)
        sketch_ref[e * SUBLANES : (e + 1) * SUBLANES] = entry


def sketch_rows(activations, out_grads, project_in, project_out, lengths):
    count, seq_len, width = activations.shape
    rank_dim = project_in.shape[1]
    rows = count * seq_len
    unit = width // 32
    bounds = [n * unit for n in (0, 2, 6, 10, 14, 18, 22, 26, 30, 32)]
    chunks = len(bounds) - 1
    return pl.pallas_call(
        functools.partial(sketch_kernel, bounds, seq_len),
        out_shape=jax.ShapeDtypeStruct((count * SUBLANES, LANES), jnp.float32),
        in_specs=[pl.BlockSpec(memory_space=pltpu.HBM)] * 5,
        out_specs=pl.BlockSpec(memory_space=pltpu.VMEM),
        scratch_shapes=[
            pltpu.VMEM((rows, width), jnp.bfloat16),
            pltpu.VMEM((rows, width), jnp.bfloat16),
            pltpu.VMEM((rank_dim, width), jnp.bfloat16),
            pltpu.VMEM((rank_dim, width), jnp.bfloat16),
            pltpu.SMEM((count,), jnp.int32),
            pltpu.SemaphoreType.DMA((4, chunks)),
            pltpu.SemaphoreType.DMA,
        ],
        compiler_params=pltpu.CompilerParams(vmem_limit_bytes=16 * 2**20),
    )(
        *(
            pltpu.with_memory_space_constraint(operand, pltpu.HBM)
            for operand in (
                activations.reshape(rows, width),
                out_grads.reshape(rows, width),
                project_in.T,
                project_out.T,
                lengths,
            )
        ),
    )


def solve_first(system, plain, scratch):
    step = 4

    def spread(column):
        index = jnp.full((SUBLANES, LANES), column, jnp.int32)
        return [jnp.take_along_axis(tile, index, axis=1) for tile in plain]

    stored = {}

    def row_of(tiles, number):
        tile = tiles[number // SUBLANES]
        if id(tile) not in stored:
            slot = len(stored)
            scratch[slot] = tile
            stored[id(tile)] = slot, tile
        slot, _ = stored[id(tile)]
        row = scratch[slot, number % SUBLANES : number % SUBLANES + 1]
        return jnp.broadcast_to(row, tile.shape)

    def factor(columns, first):
        p = {(i, j): row_of(columns[j], first + i) for j in range(step) for i in range(j + 1)}
        lower, inverse = {}, [None] * step
        for k in range(0, step, 2):
            a, b, c = p[k, k], p[k, k + 1], p[k + 1, k + 1]
            inverse[k] = pl.reciprocal(a)
            inverse[k + 1] = a * pl.reciprocal(a * c - b * b)
            for m in (k, k + 1):
                for i in range(m + 1, step):
                    lower[i, m] = p[m, i] * inverse[m]
                for i in range(m + 1, step):
                    for j in range(i, step):
                        p[i, j] = p[i, j] - lower[i, m] * p[m, j]
        return lower, inverse

    def forward(lower, parts):
        parts = list(parts)
        for k in range(step):
            for i in range(k + 1, step):
                parts[i] = [part - lower[i, k] * other for part, other in zip(parts[i], parts[k])]
        return parts

    def update(tiles, columns, lower, inverse, rows):
        rows = forward(lower, [[r] for r in rows])
        for column, row, scale in zip(columns, rows, inverse):
            done = row[0] * scale
            tiles = [tile - c * done for tile, c in zip(tiles, column)]
        return tiles

    count = len(system) * SUBLANES
    columns = [spread(j) for j in range(count - step, count)]
    for first in range(count - step, 0, -step):
        pivots = range(first, first + step)
        left = pl.cdiv(first, SUBLANES)
        lower, inverse = factor(columns, first)
        across = {j: [row_of(column, j) for column in columns] for j in range(first - step, first)}
        columns = forward(lower, [c[:left] for c in columns])
        following = [update(spread(j)[:left], columns, lower, inverse, across[j]) for j in across]
        system = plain = update(system[:left], columns, lower, inverse, [row_of(system, i) for i in pivots])
        columns = following
    lower, inverse = factor(columns, 0)
    rows = forward(lower, [[row_of(system, i)] for i in range(step)])
    solved = [row[0] * scale for row, scale in zip(rows, inverse)]
    for k in reversed(range(step)):
        for i in range(k):
            solved[i] = solved[i] - lower[k, i] * solved[k]
    return solved


def gram(x):
    high = x.astype(jnp.bfloat16)
    rest = x - high.astype(jnp.float32)
    middle = rest.astype(jnp.bfloat16)
    low = (rest - middle.astype(jnp.float32)).astype(jnp.bfloat16)
    parts = [high, middle, low]
    count = x.shape[0]
    terms = []
    for n, held in enumerate(parts):
        streamed = jnp.concatenate(parts[: len(parts) - n], axis=0)
        product = lax.dot_general(streamed, held, NT, preferred_element_type=jnp.float32)
        terms.append([product[k : k + count] for k in range(0, product.shape[0], count)])
    (hh, mh, lh), (hm, mm), (hl,) = terms
    return hh + ((mh + hm) + (lh + hl + mm))


def solve_kernel(per_dev, inner, axis, *refs):
    tiles, (query_ref, scores_ref, gram_ref, scratch) = refs[:-4], refs[-4:]
    nq = query_ref.shape[1]
    part = tiles[0].shape[0] // SUBLANES
    examples = len(tiles) * part
    outer = examples // (inner * per_dev)
    fisher_dim = SUBLANES * LANES
    gram_ref[...] = jnp.zeros(gram_ref.shape, jnp.float32)
    slot = (query_ref[...] // per_dev) ^ lax.axis_index(axis)
    n = slot // inner
    place = (gray((slot ^ partner(n, inner)) % inner) * outer + gray(n)) * per_dev + query_ref[...] % per_dev
    rest = LANES - examples - nq
    place = jnp.concatenate(
        [jnp.zeros((1, examples), jnp.int32), place] + ([jnp.zeros((1, rest), jnp.int32)] if rest else []), axis=1
    )
    lane = lax.broadcasted_iota(jnp.int32, (SUBLANES, LANES), 1)
    source = jnp.where(lane < examples, lane, jnp.broadcast_to(place, lane.shape))
    sketches = jnp.concatenate(
        [
            jnp.concatenate([tile[pl.ds(s, part, stride=SUBLANES)] for tile in tiles], axis=0)
            for s in range(SUBLANES)
        ],
        axis=1,
    )
    squares = jnp.sum(jnp.sum(sketches * sketches, axis=0, keepdims=True), axis=1, keepdims=True)
    scale = jnp.broadcast_to(1.0 / squares, (SUBLANES, LANES))
    gram_ref[:, :examples] = gram(sketches)
    row = lax.broadcasted_iota(jnp.int32, (SUBLANES, LANES), 0)
    system, plain = [], []
    for first in range(0, examples, SUBLANES):
        tile = gram_ref[first : first + SUBLANES] * scale
        plain.append(jnp.where(lane == row + first, tile + damp_ratio / fisher_dim, tile))
        system.append(jnp.where(lane < examples, plain[-1], jnp.take_along_axis(tile, source, axis=1)))
    solved = solve_first(system, plain, scratch)
    scores = solved[0]
    for i in range(1, len(solved)):
        scores = jnp.where(row == i, solved[i], scores)
    scores_ref[...] = scores[:per_dev, examples : examples + nq]


def gram_scores(tiles, query_index, per_dev, inner, axis):
    nq = query_index.shape[0]
    examples = len(tiles) * tiles[0].shape[0] // SUBLANES
    return pl.pallas_call(
        functools.partial(solve_kernel, per_dev, inner, axis),
        out_shape=jax.ShapeDtypeStruct((per_dev, nq), jnp.float32),
        in_specs=[pl.BlockSpec(memory_space=pltpu.VMEM)] * (len(tiles) + 1),
        out_specs=pl.BlockSpec(memory_space=pltpu.VMEM),
        scratch_shapes=[
            pltpu.VMEM((examples, LANES), jnp.float32),
            pltpu.VMEM((3 * examples, SUBLANES, LANES), jnp.float32),
        ],
        compiler_params=pltpu.CompilerParams(vmem_limit_bytes=8 * 2**20),
    )(*tiles, query_index.reshape(1, nq))


def gray(n):
    return n ^ (n >> 1)


def partner(n, inner):
    return n * inner ^ (n >> 1) & ~n & 1


def gather_xor(tiles, axis, size, inner):
    def swap(block, slot):
        return lax.ppermute(block, axis, [(i, i ^ slot) for i in range(size)])

    rows = sorted(range(1, size // inner), key=gray)
    column = jnp.concatenate([tiles] + [swap(tiles, partner(n, inner)) for n in rows], axis=0)
    return [column] + [swap(column, n) for n in sorted(range(1, inner), key=gray)]


def large_scores(tiles, query_index, per_dev, axis):
    sketches = tiles.reshape(-1, SUBLANES * LANES)
    gram = jnp.dot(sketches, sketches.T, precision=lax.Precision.HIGHEST)
    examples, fisher_dim = sketches.shape
    damping = damp_ratio * jnp.trace(gram) / fisher_dim
    factor = jnp.linalg.cholesky(gram + damping * jnp.eye(examples, dtype=jnp.float32))
    mine = lax.dynamic_slice_in_dim(gram, lax.axis_index(axis) * per_dev, per_dev, 0)
    half = lax.linalg.triangular_solve(factor, mine.T, left_side=True, lower=True)
    solved = lax.linalg.triangular_solve(factor, half, left_side=True, lower=True, transpose_a=True)
    selector = (query_index[:, None] == jnp.arange(examples, dtype=jnp.int32)[None, :]).astype(jnp.float32)
    return jnp.dot(selector, solved, precision=lax.Precision.HIGHEST).T


def local(activations, out_grads, project_in, project_out, lengths, query_index):
    per_dev = activations.shape[0]
    size = lax.axis_size("dp")
    tiles = sketch_rows(activations, out_grads, project_in, project_out, lengths)
    if size * per_dev + query_index.shape[0] <= LANES:
        inner = 4
        return gram_scores(gather_xor(tiles, "dp", size, inner), query_index, per_dev, inner, "dp")
    return large_scores(lax.all_gather(tiles, "dp", axis=0, tiled=True), query_index, per_dev, "dp")


def solution(mesh):
    return jax.shard_map(
        local,
        mesh=mesh,
        in_specs=(
            P(("groups", "dp"), None, None),
            P(("groups", "dp"), None, None),
            P(),
            P(),
            P(("groups", "dp")),
            P("groups"),
        ),
        out_specs=P(("groups", "dp"), None),
        check_vma=False,
    )
```

```python
import functools

import jax
import jax.numpy as jnp
from jax import lax
from jax.experimental import pallas as pl
from jax.experimental.pallas import tpu as pltpu
from jax.sharding import PartitionSpec as P

damp_ratio = 0.5
LANES = 128
SUBLANES = 8
NT = (((1,), (1,)), ((), ()))


def sketch_kernel(bounds, seq_len, act_hbm, out_hbm, pin_hbm, pout_hbm, lengths_hbm, sketch_ref, act, out, pin, pout, lengths_ref, sems, lengths_sem):
    rows, width = act.shape
    rank_dim = pin.shape[0]
    chunks = len(bounds) - 1
    lengths_copy = pltpu.make_async_copy(lengths_hbm, lengths_ref, lengths_sem)
    lengths_copy.start()
    copies = []
    early = 2
    for c in range(chunks):
        cols = pl.ds(bounds[c], bounds[c + 1] - bounds[c])
        operands = [(act_hbm, act, cols), (out_hbm, out, cols)]
        if c in (0, early):
            cols = pl.ds(bounds[c], (width if c else bounds[early]) - bounds[c])
            operands = [(pin_hbm, pin, cols), (pout_hbm, pout, cols)] + operands
        copies.append(
            [
                pltpu.make_async_copy(src.at[:, part], dst.at[:, part], sems.at[n, c])
                for n, (src, dst, part) in enumerate(operands)
            ]
        )
        for copy in copies[-1]:
            copy.start()
    feat = [jnp.zeros((rows, rank_dim), jnp.float32)] * 2
    grad = [jnp.zeros((rank_dim, rows), jnp.float32)] * 2
    for c in range(chunks):
        middle = (bounds[c] + bounds[c + 1]) // 2
        for copy in copies[c]:
            copy.wait()
        for n, cols in enumerate((slice(bounds[c], middle), slice(middle, bounds[c + 1]))):
            feat[n] = feat[n] + lax.dot_general(act[:, cols], pin[:, cols], NT, preferred_element_type=jnp.float32)
            grad[n] = grad[n] + lax.dot_general(pout[:, cols], out[:, cols], NT, preferred_element_type=jnp.float32)
    feat, grad = feat[0] + feat[1], grad[0] + grad[1]
    lengths_copy.wait()
    count = rows // seq_len
    reps = LANES // rank_dim
    position = lax.broadcasted_iota(jnp.int32, (rows, LANES), 0)
    band = lax.broadcasted_iota(jnp.int32, (rows, LANES), 1) // rank_dim
    live = jnp.zeros((rows, LANES), jnp.bool_)
    for e in range(count):
        first = e * seq_len
        live = live | ((band == e) & (position >= first) & (position < first + lengths_ref[e]))
    outer = lax.dot_general(
        grad,
        jnp.where(live, jnp.concatenate([feat] * reps, axis=1), 0.0),
        (((1,), (0,)), ((), ())),
        precision=lax.Precision.HIGHEST,
        preferred_element_type=jnp.float32,
    )
    band = band[:SUBLANES]
    for e in range(count):
        entry = None
        for b in range(reps):
            part = outer[b * SUBLANES : (b + 1) * SUBLANES]
            if b != e:
                part = pltpu.roll(part, (b - e) * rank_dim % LANES, 1)
            entry = part if entry is None else jnp.where(band == b, part, entry)
        sketch_ref[e * SUBLANES : (e + 1) * SUBLANES] = entry


def sketch_rows(activations, out_grads, project_in, project_out, lengths):
    count, seq_len, width = activations.shape
    rank_dim = project_in.shape[1]
    rows = count * seq_len
    unit = width // 32
    bounds = [n * unit for n in (0, 2, 6, 10, 14, 18, 22, 26, 30, 32)]
    chunks = len(bounds) - 1
    return pl.pallas_call(
        functools.partial(sketch_kernel, bounds, seq_len),
        out_shape=jax.ShapeDtypeStruct((count * SUBLANES, LANES), jnp.float32),
        in_specs=[pl.BlockSpec(memory_space=pltpu.HBM)] * 5,
        out_specs=pl.BlockSpec(memory_space=pltpu.VMEM),
        scratch_shapes=[
            pltpu.VMEM((rows, width), jnp.bfloat16),
            pltpu.VMEM((rows, width), jnp.bfloat16),
            pltpu.VMEM((rank_dim, width), jnp.bfloat16),
            pltpu.VMEM((rank_dim, width), jnp.bfloat16),
            pltpu.SMEM((count,), jnp.int32),
            pltpu.SemaphoreType.DMA((4, chunks)),
            pltpu.SemaphoreType.DMA,
        ],
        compiler_params=pltpu.CompilerParams(vmem_limit_bytes=16 * 2**20),
    )(
        *(
            pltpu.with_memory_space_constraint(operand, pltpu.HBM)
            for operand in (
                activations.reshape(rows, width),
                out_grads.reshape(rows, width),
                project_in.T,
                project_out.T,
                lengths,
            )
        ),
    )


def solve_first(system, plain, scratch):
    step = 4

    def spread(column):
        return [jnp.broadcast_to(tile[:, column : column + 1], tile.shape) for tile in plain]

    stored = {}

    def row_of(tiles, number):
        tile = tiles[number // SUBLANES]
        if id(tile) not in stored:
            slot = len(stored)
            scratch[slot] = tile
            stored[id(tile)] = slot, tile
        slot, _ = stored[id(tile)]
        row = scratch[slot, number % SUBLANES : number % SUBLANES + 1]
        return jnp.broadcast_to(row, tile.shape)

    def factor(columns, first):
        p = {(i, j): row_of(columns[j], first + i) for j in range(step) for i in range(j + 1)}
        lower, inverse = {}, [None] * step
        for k in range(0, step, 2):
            a, b, c = p[k, k], p[k, k + 1], p[k + 1, k + 1]
            inverse[k] = pl.reciprocal(a)
            inverse[k + 1] = a * pl.reciprocal(a * c - b * b)
            for m in (k, k + 1):
                for i in range(m + 1, step):
                    lower[i, m] = p[m, i] * inverse[m]
                for i in range(m + 1, step):
                    for j in range(i, step):
                        p[i, j] = p[i, j] - lower[i, m] * p[m, j]
        return lower, inverse

    def forward(lower, parts):
        parts = list(parts)
        for k in range(step):
            for i in range(k + 1, step):
                parts[i] = [part - lower[i, k] * other for part, other in zip(parts[i], parts[k])]
        return parts

    def update(tiles, columns, lower, inverse, rows):
        rows = forward(lower, [[r] for r in rows])
        for column, row, scale in zip(columns, rows, inverse):
            done = row[0] * scale
            tiles = [tile - c * done for tile, c in zip(tiles, column)]
        return tiles

    count = len(system) * SUBLANES
    columns = [spread(j) for j in range(count - step, count)]
    for first in range(count - step, 0, -step):
        pivots = range(first, first + step)
        left = pl.cdiv(first, SUBLANES)
        lower, inverse = factor(columns, first)
        across = {j: [row_of(column, j) for column in columns] for j in range(first - step, first)}
        columns = forward(lower, [c[:left] for c in columns])
        following = [update(spread(j)[:left], columns, lower, inverse, across[j]) for j in across]
        system = plain = update(system[:left], columns, lower, inverse, [row_of(system, i) for i in pivots])
        columns = following
    lower, inverse = factor(columns, 0)
    rows = forward(lower, [[row_of(system, i)] for i in range(step)])
    solved = [row[0] * scale for row, scale in zip(rows, inverse)]
    for k in reversed(range(step)):
        for i in range(k):
            solved[i] = solved[i] - lower[k, i] * solved[k]
    return solved


def gram(x):
    high = x.astype(jnp.bfloat16)
    rest = x - high.astype(jnp.float32)
    middle = rest.astype(jnp.bfloat16)
    low = (rest - middle.astype(jnp.float32)).astype(jnp.bfloat16)
    parts = [high, middle, low]
    count = x.shape[0]
    terms = []
    for n, held in enumerate(parts):
        streamed = jnp.concatenate(parts[: len(parts) - n], axis=0)
        product = lax.dot_general(streamed, held, NT, preferred_element_type=jnp.float32)
        terms.append([product[k : k + count] for k in range(0, product.shape[0], count)])
    (hh, mh, lh), (hm, mm), (hl,) = terms
    return hh + ((mh + hm) + (lh + hl + mm))


def solve_kernel(per_dev, inner, axis, *refs):
    tiles, (query_ref, scores_ref, gram_ref, scratch) = refs[:-4], refs[-4:]
    nq = query_ref.shape[1]
    part = tiles[0].shape[0] // SUBLANES
    examples = len(tiles) * part
    outer = examples // (inner * per_dev)
    fisher_dim = SUBLANES * LANES
    gram_ref[...] = jnp.zeros(gram_ref.shape, jnp.float32)
    slot = (query_ref[...] // per_dev) ^ lax.axis_index(axis)
    n = slot // inner
    place = (gray((slot ^ partner(n, inner)) % inner) * outer + gray(n)) * per_dev + query_ref[...] % per_dev
    rest = LANES - examples - nq
    place = jnp.concatenate(
        [jnp.zeros((1, examples), jnp.int32), place] + ([jnp.zeros((1, rest), jnp.int32)] if rest else []), axis=1
    )
    lane = lax.broadcasted_iota(jnp.int32, (SUBLANES, LANES), 1)
    source = jnp.where(lane < examples, lane, jnp.broadcast_to(place, lane.shape))
    sketches = jnp.concatenate(
        [
            jnp.concatenate([tile[pl.ds(s, part, stride=SUBLANES)] for tile in tiles], axis=0)
            for s in range(SUBLANES)
        ],
        axis=1,
    )
    squares = jnp.sum(jnp.sum(sketches * sketches, axis=0, keepdims=True), axis=1, keepdims=True)
    scale = jnp.broadcast_to(1.0 / squares, (SUBLANES, LANES))
    gram_ref[:, :examples] = gram(sketches)
    row = lax.broadcasted_iota(jnp.int32, (SUBLANES, LANES), 0)
    system, plain = [], []
    for first in range(0, examples, SUBLANES):
        tile = gram_ref[first : first + SUBLANES] * scale
        plain.append(jnp.where(lane == row + first, tile + damp_ratio / fisher_dim, tile))
        system.append(jnp.where(lane < examples, plain[-1], jnp.take_along_axis(tile, source, axis=1)))
    solved = solve_first(system, plain, scratch)
    scores = solved[0]
    for i in range(1, len(solved)):
        scores = jnp.where(row == i, solved[i], scores)
    scores_ref[...] = scores[:per_dev, examples : examples + nq]


def gram_scores(tiles, query_index, per_dev, inner, axis):
    nq = query_index.shape[0]
    examples = len(tiles) * tiles[0].shape[0] // SUBLANES
    return pl.pallas_call(
        functools.partial(solve_kernel, per_dev, inner, axis),
        out_shape=jax.ShapeDtypeStruct((per_dev, nq), jnp.float32),
        in_specs=[pl.BlockSpec(memory_space=pltpu.VMEM)] * (len(tiles) + 1),
        out_specs=pl.BlockSpec(memory_space=pltpu.VMEM),
        scratch_shapes=[
            pltpu.VMEM((examples, LANES), jnp.float32),
            pltpu.VMEM((3 * examples, SUBLANES, LANES), jnp.float32),
        ],
        compiler_params=pltpu.CompilerParams(vmem_limit_bytes=8 * 2**20),
    )(*tiles, query_index.reshape(1, nq))


def gray(n):
    return n ^ (n >> 1)


def partner(n, inner):
    return n * inner ^ (n >> 1) & ~n & 1


def gather_xor(tiles, axis, size, inner):
    def swap(block, slot):
        return lax.ppermute(block, axis, [(i, i ^ slot) for i in range(size)])

    rows = sorted(range(1, size // inner), key=gray)
    column = jnp.concatenate([tiles] + [swap(tiles, partner(n, inner)) for n in rows], axis=0)
    return [column] + [swap(column, n) for n in sorted(range(1, inner), key=gray)]


def large_scores(tiles, query_index, per_dev, axis):
    sketches = tiles.reshape(-1, SUBLANES * LANES)
    gram = jnp.dot(sketches, sketches.T, precision=lax.Precision.HIGHEST)
    examples, fisher_dim = sketches.shape
    damping = damp_ratio * jnp.trace(gram) / fisher_dim
    factor = jnp.linalg.cholesky(gram + damping * jnp.eye(examples, dtype=jnp.float32))
    mine = lax.dynamic_slice_in_dim(gram, lax.axis_index(axis) * per_dev, per_dev, 0)
    half = lax.linalg.triangular_solve(factor, mine.T, left_side=True, lower=True)
    solved = lax.linalg.triangular_solve(factor, half, left_side=True, lower=True, transpose_a=True)
    selector = (query_index[:, None] == jnp.arange(examples, dtype=jnp.int32)[None, :]).astype(jnp.float32)
    return jnp.dot(selector, solved, precision=lax.Precision.HIGHEST).T


def local(activations, out_grads, project_in, project_out, lengths, query_index):
    per_dev = activations.shape[0]
    size = lax.axis_size("dp")
    tiles = sketch_rows(activations, out_grads, project_in, project_out, lengths)
    if size * per_dev + query_index.shape[0] <= LANES:
        inner = 4
        return gram_scores(gather_xor(tiles, "dp", size, inner), query_index, per_dev, inner, "dp")
    return large_scores(lax.all_gather(tiles, "dp", axis=0, tiled=True), query_index, per_dev, "dp")


def solution(mesh):
    return jax.shard_map(
        local,
        mesh=mesh,
        in_specs=(
            P(("groups", "dp"), None, None),
            P(("groups", "dp"), None, None),
            P(),
            P(),
            P(("groups", "dp")),
            P("groups"),
        ),
        out_specs=P(("groups", "dp"), None),
        check_vma=False,
    )
```

```python
import functools

import jax
import jax.numpy as jnp
from jax import lax
from jax.experimental import pallas as pl
from jax.experimental.pallas import tpu as pltpu
from jax.sharding import PartitionSpec as P

damp_ratio = 0.5
LANES = 128
SUBLANES = 8
NT = (((1,), (1,)), ((), ()))


def sketch_kernel(bounds, seq_len, act_hbm, out_hbm, pin_hbm, pout_hbm, lengths_hbm, sketch_ref, act, out, pin, pout, lengths_ref, sems, lengths_sem):
    rows, width = act.shape
    rank_dim = pin.shape[0]
    chunks = len(bounds) - 1
    lengths_copy = pltpu.make_async_copy(lengths_hbm, lengths_ref, lengths_sem)
    lengths_copy.start()
    copies = []
    for c in range(chunks):
        cols = pl.ds(bounds[c], bounds[c + 1] - bounds[c])
        copies.append(
            [
                pltpu.make_async_copy(src.at[:, cols], dst.at[:, cols], sems.at[n, c])
                for n, (src, dst) in enumerate(
                    ((pin_hbm, pin), (act_hbm, act), (pout_hbm, pout), (out_hbm, out))
                )
            ]
        )
        for copy in copies[-1]:
            copy.start()
    feat = [jnp.zeros((rows, rank_dim), jnp.float32)] * 2
    grad = [jnp.zeros((rank_dim, rows), jnp.float32)] * 2
    for c in range(chunks):
        middle = (bounds[c] + bounds[c + 1]) // 2
        for copy in copies[c]:
            copy.wait()
        for n, cols in enumerate((slice(bounds[c], middle), slice(middle, bounds[c + 1]))):
            feat[n] = feat[n] + lax.dot_general(act[:, cols], pin[:, cols], NT, preferred_element_type=jnp.float32)
            grad[n] = grad[n] + lax.dot_general(pout[:, cols], out[:, cols], NT, preferred_element_type=jnp.float32)
    feat, grad = feat[0] + feat[1], grad[0] + grad[1]
    lengths_copy.wait()
    count = rows // seq_len
    reps = LANES // rank_dim
    position = lax.broadcasted_iota(jnp.int32, (rows, LANES), 0)
    band = lax.broadcasted_iota(jnp.int32, (rows, LANES), 1) // rank_dim
    live = jnp.zeros((rows, LANES), jnp.bool_)
    for e in range(count):
        first = e * seq_len
        live = live | ((band == e) & (position >= first) & (position < first + lengths_ref[e]))
    outer = lax.dot_general(
        grad,
        jnp.where(live, jnp.concatenate([feat] * reps, axis=1), 0.0),
        (((1,), (0,)), ((), ())),
        precision=lax.Precision.HIGHEST,
        preferred_element_type=jnp.float32,
    )
    band = band[:SUBLANES]
    for e in range(count):
        entry = None
        for b in range(reps):
            part = outer[b * SUBLANES : (b + 1) * SUBLANES]
            if b != e:
                part = pltpu.roll(part, (b - e) * rank_dim % LANES, 1)
            entry = part if entry is None else jnp.where(band == b, part, entry)
        sketch_ref[e * SUBLANES : (e + 1) * SUBLANES] = entry


def sketch_rows(activations, out_grads, project_in, project_out, lengths):
    count, seq_len, width = activations.shape
    rank_dim = project_in.shape[1]
    rows = count * seq_len
    unit = width // 32
    bounds = [n * unit for n in (0, 2, 6, 10, 14, 18, 22, 26, 30, 32)]
    chunks = len(bounds) - 1
    return pl.pallas_call(
        functools.partial(sketch_kernel, bounds, seq_len),
        out_shape=jax.ShapeDtypeStruct((count * SUBLANES, LANES), jnp.float32),
        in_specs=[pl.BlockSpec(memory_space=pltpu.HBM)] * 5,
        out_specs=pl.BlockSpec(memory_space=pltpu.VMEM),
        scratch_shapes=[
            pltpu.VMEM((rows, width), jnp.bfloat16),
            pltpu.VMEM((rows, width), jnp.bfloat16),
            pltpu.VMEM((rank_dim, width), jnp.bfloat16),
            pltpu.VMEM((rank_dim, width), jnp.bfloat16),
            pltpu.SMEM((count,), jnp.int32),
            pltpu.SemaphoreType.DMA((4, chunks)),
            pltpu.SemaphoreType.DMA,
        ],
        compiler_params=pltpu.CompilerParams(vmem_limit_bytes=16 * 2**20),
    )(
        *(
            pltpu.with_memory_space_constraint(operand, pltpu.HBM)
            for operand in (
                activations.reshape(rows, width),
                out_grads.reshape(rows, width),
                project_in.T,
                project_out.T,
                lengths,
            )
        ),
    )


def solve_first(system, plain, scratch):
    step = 4

    def spread(column):
        return [jnp.broadcast_to(tile[:, column : column + 1], tile.shape) for tile in plain]

    stored = {}

    def row_of(tiles, number):
        tile = tiles[number // SUBLANES]
        if id(tile) not in stored:
            slot = len(stored)
            scratch[slot] = tile
            stored[id(tile)] = slot, tile
        slot, _ = stored[id(tile)]
        row = scratch[slot, number % SUBLANES : number % SUBLANES + 1]
        return jnp.broadcast_to(row, tile.shape)

    def factor(columns, first):
        p = {(i, j): row_of(columns[j], first + i) for j in range(step) for i in range(j + 1)}
        lower, inverse = {}, [None] * step
        for k in range(0, step, 2):
            a, b, c = p[k, k], p[k, k + 1], p[k + 1, k + 1]
            inverse[k] = pl.reciprocal(a)
            inverse[k + 1] = a * pl.reciprocal(a * c - b * b)
            for m in (k, k + 1):
                for i in range(m + 1, step):
                    lower[i, m] = p[m, i] * inverse[m]
                for i in range(m + 1, step):
                    for j in range(i, step):
                        p[i, j] = p[i, j] - lower[i, m] * p[m, j]
        return lower, inverse

    def forward(lower, parts):
        parts = list(parts)
        for k in range(step):
            for i in range(k + 1, step):
                parts[i] = [part - lower[i, k] * other for part, other in zip(parts[i], parts[k])]
        return parts

    def update(tiles, columns, lower, inverse, rows):
        rows = forward(lower, [[r] for r in rows])
        for column, row, scale in zip(columns, rows, inverse):
            done = row[0] * scale
            tiles = [tile - c * done for tile, c in zip(tiles, column)]
        return tiles

    count = len(system) * SUBLANES
    columns = [spread(j) for j in range(count - step, count)]
    for first in range(count - step, 0, -step):
        pivots = range(first, first + step)
        left = pl.cdiv(first, SUBLANES)
        lower, inverse = factor(columns, first)
        across = {j: [row_of(column, j) for column in columns] for j in range(first - step, first)}
        columns = forward(lower, [c[:left] for c in columns])
        following = [update(spread(j)[:left], columns, lower, inverse, across[j]) for j in across]
        system = plain = update(system[:left], columns, lower, inverse, [row_of(system, i) for i in pivots])
        columns = following
    lower, inverse = factor(columns, 0)
    rows = forward(lower, [[row_of(system, i)] for i in range(step)])
    solved = [row[0] * scale for row, scale in zip(rows, inverse)]
    for k in reversed(range(step)):
        for i in range(k):
            solved[i] = solved[i] - lower[k, i] * solved[k]
    return solved


def gram(x):
    high = x.astype(jnp.bfloat16)
    rest = x - high.astype(jnp.float32)
    middle = rest.astype(jnp.bfloat16)
    low = (rest - middle.astype(jnp.float32)).astype(jnp.bfloat16)
    parts = [high, middle, low]
    count = x.shape[0]
    terms = []
    for n, held in enumerate(parts):
        streamed = jnp.concatenate(parts[: len(parts) - n], axis=0)
        product = lax.dot_general(streamed, held, NT, preferred_element_type=jnp.float32)
        terms.append([product[k : k + count] for k in range(0, product.shape[0], count)])
    (hh, mh, lh), (hm, mm), (hl,) = terms
    return hh + ((mh + hm) + (lh + hl + mm))


def solve_kernel(per_dev, inner, axis, *refs):
    tiles, (query_ref, scores_ref, gram_ref, scratch) = refs[:-4], refs[-4:]
    nq = query_ref.shape[1]
    part = tiles[0].shape[0] // SUBLANES
    examples = len(tiles) * part
    outer = examples // (inner * per_dev)
    fisher_dim = SUBLANES * LANES
    gram_ref[...] = jnp.zeros(gram_ref.shape, jnp.float32)
    slot = (query_ref[...] // per_dev) ^ lax.axis_index(axis)
    n = slot // inner
    place = (gray((slot ^ partner(n, inner)) % inner) * outer + gray(n)) * per_dev + query_ref[...] % per_dev
    rest = LANES - examples - nq
    place = jnp.concatenate(
        [jnp.zeros((1, examples), jnp.int32), place] + ([jnp.zeros((1, rest), jnp.int32)] if rest else []), axis=1
    )
    lane = lax.broadcasted_iota(jnp.int32, (SUBLANES, LANES), 1)
    source = jnp.where(lane < examples, lane, jnp.broadcast_to(place, lane.shape))
    sketches = jnp.concatenate(
        [
            jnp.concatenate([tile[pl.ds(s, part, stride=SUBLANES)] for tile in tiles], axis=0)
            for s in range(SUBLANES)
        ],
        axis=1,
    )
    squares = jnp.sum(jnp.sum(sketches * sketches, axis=0, keepdims=True), axis=1, keepdims=True)
    scale = jnp.broadcast_to(1.0 / squares, (SUBLANES, LANES))
    gram_ref[:, :examples] = gram(sketches)
    row = lax.broadcasted_iota(jnp.int32, (SUBLANES, LANES), 0)
    system, plain = [], []
    for first in range(0, examples, SUBLANES):
        tile = gram_ref[first : first + SUBLANES] * scale
        plain.append(jnp.where(lane == row + first, tile + damp_ratio / fisher_dim, tile))
        system.append(jnp.where(lane < examples, plain[-1], jnp.take_along_axis(tile, source, axis=1)))
    solved = solve_first(system, plain, scratch)
    scores = solved[0]
    for i in range(1, len(solved)):
        scores = jnp.where(row == i, solved[i], scores)
    scores_ref[...] = scores[:per_dev, examples : examples + nq]


def gram_scores(tiles, query_index, per_dev, inner, axis):
    nq = query_index.shape[0]
    examples = len(tiles) * tiles[0].shape[0] // SUBLANES
    return pl.pallas_call(
        functools.partial(solve_kernel, per_dev, inner, axis),
        out_shape=jax.ShapeDtypeStruct((per_dev, nq), jnp.float32),
        in_specs=[pl.BlockSpec(memory_space=pltpu.VMEM)] * (len(tiles) + 1),
        out_specs=pl.BlockSpec(memory_space=pltpu.VMEM),
        scratch_shapes=[
            pltpu.VMEM((examples, LANES), jnp.float32),
            pltpu.VMEM((3 * examples, SUBLANES, LANES), jnp.float32),
        ],
        compiler_params=pltpu.CompilerParams(vmem_limit_bytes=8 * 2**20),
    )(*tiles, query_index.reshape(1, nq))


def gray(n):
    return n ^ (n >> 1)


def partner(n, inner):
    return n * inner ^ (n >> 1) & 1


def gather_xor(tiles, axis, size, inner):
    def swap(block, slot):
        return lax.ppermute(block, axis, [(i, i ^ slot) for i in range(size)])

    rows = sorted(range(1, size // inner), key=gray)
    column = jnp.concatenate([tiles] + [swap(tiles, partner(n, inner)) for n in rows], axis=0)
    return [column] + [swap(column, n) for n in sorted(range(1, inner), key=gray)]


def large_scores(tiles, query_index, per_dev, axis):
    sketches = tiles.reshape(-1, SUBLANES * LANES)
    gram = jnp.dot(sketches, sketches.T, precision=lax.Precision.HIGHEST)
    examples, fisher_dim = sketches.shape
    damping = damp_ratio * jnp.trace(gram) / fisher_dim
    factor = jnp.linalg.cholesky(gram + damping * jnp.eye(examples, dtype=jnp.float32))
    mine = lax.dynamic_slice_in_dim(gram, lax.axis_index(axis) * per_dev, per_dev, 0)
    half = lax.linalg.triangular_solve(factor, mine.T, left_side=True, lower=True)
    solved = lax.linalg.triangular_solve(factor, half, left_side=True, lower=True, transpose_a=True)
    selector = (query_index[:, None] == jnp.arange(examples, dtype=jnp.int32)[None, :]).astype(jnp.float32)
    return jnp.dot(selector, solved, precision=lax.Precision.HIGHEST).T


def local(activations, out_grads, project_in, project_out, lengths, query_index):
    per_dev = activations.shape[0]
    size = lax.axis_size("dp")
    tiles = sketch_rows(activations, out_grads, project_in, project_out, lengths)
    if size * per_dev + query_index.shape[0] <= LANES:
        inner = 4
        return gram_scores(gather_xor(tiles, "dp", size, inner), query_index, per_dev, inner, "dp")
    return large_scores(lax.all_gather(tiles, "dp", axis=0, tiled=True), query_index, per_dev, "dp")


def solution(mesh):
    return jax.shard_map(
        local,
        mesh=mesh,
        in_specs=(
            P(("groups", "dp"), None, None),
            P(("groups", "dp"), None, None),
            P(),
            P(),
            P(("groups", "dp")),
            P("groups"),
        ),
        out_specs=P(("groups", "dp"), None),
        check_vma=False,
    )
```

```python
import functools

import jax
import jax.numpy as jnp
from jax import lax
from jax.experimental import pallas as pl
from jax.experimental.pallas import tpu as pltpu
from jax.sharding import PartitionSpec as P

damp_ratio = 0.5
LANES = 128
SUBLANES = 8
NT = (((1,), (1,)), ((), ()))


def sketch_kernel(bounds, seq_len, act_hbm, out_hbm, pin_hbm, pout_hbm, lengths_hbm, sketch_ref, act, out, pin, pout, lengths_ref, sems, lengths_sem):
    rows, width = act.shape
    rank_dim = pin.shape[0]
    chunks = len(bounds) - 1
    lengths_copy = pltpu.make_async_copy(lengths_hbm, lengths_ref, lengths_sem)
    lengths_copy.start()
    copies = []
    for c in range(chunks):
        cols = pl.ds(bounds[c], bounds[c + 1] - bounds[c])
        copies.append(
            [
                pltpu.make_async_copy(src.at[:, cols], dst.at[:, cols], sems.at[n, c])
                for n, (src, dst) in enumerate(
                    ((pin_hbm, pin), (act_hbm, act), (pout_hbm, pout), (out_hbm, out))
                )
            ]
        )
        for copy in copies[-1]:
            copy.start()
    feat = [jnp.zeros((rows, rank_dim), jnp.float32)] * 2
    grad = [jnp.zeros((rank_dim, rows), jnp.float32)] * 2
    for c in range(chunks):
        middle = (bounds[c] + bounds[c + 1]) // 2
        for copy in copies[c]:
            copy.wait()
        for n, cols in enumerate((slice(bounds[c], middle), slice(middle, bounds[c + 1]))):
            feat[n] = feat[n] + lax.dot_general(act[:, cols], pin[:, cols], NT, preferred_element_type=jnp.float32)
            grad[n] = grad[n] + lax.dot_general(pout[:, cols], out[:, cols], NT, preferred_element_type=jnp.float32)
    feat, grad = feat[0] + feat[1], grad[0] + grad[1]
    lengths_copy.wait()
    count = rows // seq_len
    reps = LANES // rank_dim
    position = lax.broadcasted_iota(jnp.int32, (rows, LANES), 0)
    band = lax.broadcasted_iota(jnp.int32, (rows, LANES), 1) // rank_dim
    live = jnp.zeros((rows, LANES), jnp.bool_)
    for e in range(count):
        first = e * seq_len
        live = live | ((band == e) & (position >= first) & (position < first + lengths_ref[e]))
    outer = lax.dot_general(
        grad,
        jnp.where(live, jnp.concatenate([feat] * reps, axis=1), 0.0),
        (((1,), (0,)), ((), ())),
        precision=lax.Precision.HIGHEST,
        preferred_element_type=jnp.float32,
    )
    band = band[:SUBLANES]
    for e in range(count):
        entry = None
        for b in range(reps):
            part = outer[b * SUBLANES : (b + 1) * SUBLANES]
            if b != e:
                part = pltpu.roll(part, (b - e) * rank_dim % LANES, 1)
            entry = part if entry is None else jnp.where(band == b, part, entry)
        sketch_ref[e * SUBLANES : (e + 1) * SUBLANES] = entry


def sketch_rows(activations, out_grads, project_in, project_out, lengths):
    count, seq_len, width = activations.shape
    rank_dim = project_in.shape[1]
    rows = count * seq_len
    unit = width // 32
    bounds = [n * unit for n in (0, 2, 6, 10, 14, 18, 22, 26, 30, 32)]
    chunks = len(bounds) - 1
    return pl.pallas_call(
        functools.partial(sketch_kernel, bounds, seq_len),
        out_shape=jax.ShapeDtypeStruct((count * SUBLANES, LANES), jnp.float32),
        in_specs=[pl.BlockSpec(memory_space=pltpu.HBM)] * 5,
        out_specs=pl.BlockSpec(memory_space=pltpu.VMEM),
        scratch_shapes=[
            pltpu.VMEM((rows, width), jnp.bfloat16),
            pltpu.VMEM((rows, width), jnp.bfloat16),
            pltpu.VMEM((rank_dim, width), jnp.bfloat16),
            pltpu.VMEM((rank_dim, width), jnp.bfloat16),
            pltpu.SMEM((count,), jnp.int32),
            pltpu.SemaphoreType.DMA((4, chunks)),
            pltpu.SemaphoreType.DMA,
        ],
        compiler_params=pltpu.CompilerParams(vmem_limit_bytes=16 * 2**20),
    )(
        *(
            pltpu.with_memory_space_constraint(operand, pltpu.HBM)
            for operand in (
                activations.reshape(rows, width),
                out_grads.reshape(rows, width),
                project_in.T,
                project_out.T,
                lengths,
            )
        ),
    )


def solve_first(system, plain, scratch):
    step = 4

    def spread(column):
        return [jnp.broadcast_to(tile[:, column : column + 1], tile.shape) for tile in plain]

    stored = {}

    def row_of(tiles, number):
        tile = tiles[number // SUBLANES]
        if id(tile) not in stored:
            slot = len(stored)
            scratch[slot] = tile
            stored[id(tile)] = slot, tile
        slot, _ = stored[id(tile)]
        row = scratch[slot, number % SUBLANES : number % SUBLANES + 1]
        return jnp.broadcast_to(row, tile.shape)

    def factor(columns, first):
        p = {(i, j): row_of(columns[j], first + i) for j in range(step) for i in range(j + 1)}
        lower, inverse = {}, [None] * step
        for k in range(0, step, 2):
            a, b, c = p[k, k], p[k, k + 1], p[k + 1, k + 1]
            inverse[k] = pl.reciprocal(a)
            inverse[k + 1] = a * pl.reciprocal(a * c - b * b)
            for m in (k, k + 1):
                for i in range(m + 1, step):
                    lower[i, m] = p[m, i] * inverse[m]
                for i in range(m + 1, step):
                    for j in range(i, step):
                        p[i, j] = p[i, j] - lower[i, m] * p[m, j]
        return lower, inverse

    def forward(lower, parts):
        parts = list(parts)
        for k in range(step):
            for i in range(k + 1, step):
                parts[i] = [part - lower[i, k] * other for part, other in zip(parts[i], parts[k])]
        return parts

    def update(tiles, columns, lower, inverse, rows):
        rows = forward(lower, [[r] for r in rows])
        for column, row, scale in zip(columns, rows, inverse):
            done = row[0] * scale
            tiles = [tile - c * done for tile, c in zip(tiles, column)]
        return tiles

    count = len(system) * SUBLANES
    columns = [spread(j) for j in range(count - step, count)]
    for first in range(count - step, 0, -step):
        pivots = range(first, first + step)
        left = pl.cdiv(first, SUBLANES)
        lower, inverse = factor(columns, first)
        across = {j: [row_of(column, j) for column in columns] for j in range(first - step, first)}
        columns = forward(lower, [c[:left] for c in columns])
        following = [update(spread(j)[:left], columns, lower, inverse, across[j]) for j in across]
        system = plain = update(system[:left], columns, lower, inverse, [row_of(system, i) for i in pivots])
        columns = following
    lower, inverse = factor(columns, 0)
    rows = forward(lower, [[row_of(system, i)] for i in range(step)])
    solved = [row[0] * scale for row, scale in zip(rows, inverse)]
    for k in reversed(range(step)):
        for i in range(k):
            solved[i] = solved[i] - lower[k, i] * solved[k]
    return solved


def gram(x):
    high = x.astype(jnp.bfloat16)
    rest = x - high.astype(jnp.float32)
    middle = rest.astype(jnp.bfloat16)
    low = (rest - middle.astype(jnp.float32)).astype(jnp.bfloat16)
    parts = [high, middle, low]
    count = x.shape[0]
    terms = []
    for n, held in enumerate(parts):
        streamed = jnp.concatenate(parts[: len(parts) - n], axis=0)
        product = lax.dot_general(streamed, held, NT, preferred_element_type=jnp.float32)
        terms.append([product[k : k + count] for k in range(0, product.shape[0], count)])
    (hh, mh, lh), (hm, mm), (hl,) = terms
    return hh + ((mh + hm) + (lh + hl + mm))


def solve_kernel(per_dev, inner, axis, *refs):
    tiles, (query_ref, scores_ref, gram_ref, scratch) = refs[:-4], refs[-4:]
    nq = query_ref.shape[1]
    part = tiles[0].shape[0] // SUBLANES
    examples = len(tiles) * part
    outer = examples // (inner * per_dev)
    fisher_dim = SUBLANES * LANES
    gram_ref[...] = jnp.zeros(gram_ref.shape, jnp.float32)
    slot = (query_ref[...] // per_dev) ^ lax.axis_index(axis)
    n = slot // inner
    place = (gray((slot ^ partner(n, inner)) % inner) * outer + gray(n)) * per_dev + query_ref[...] % per_dev
    rest = LANES - examples - nq
    place = jnp.concatenate(
        [jnp.zeros((1, examples), jnp.int32), place] + ([jnp.zeros((1, rest), jnp.int32)] if rest else []), axis=1
    )
    lane = lax.broadcasted_iota(jnp.int32, (SUBLANES, LANES), 1)
    source = jnp.where(lane < examples, lane, jnp.broadcast_to(place, lane.shape))
    sketches = jnp.concatenate(
        [
            jnp.concatenate([tile[pl.ds(s, part, stride=SUBLANES)] for tile in tiles], axis=0)
            for s in range(SUBLANES)
        ],
        axis=1,
    )
    squares = jnp.sum(jnp.sum(sketches * sketches, axis=0, keepdims=True), axis=1, keepdims=True)
    scale = jnp.broadcast_to(1.0 / squares, (SUBLANES, LANES))
    gram_ref[:, :examples] = gram(sketches)
    row = lax.broadcasted_iota(jnp.int32, (SUBLANES, LANES), 0)
    system, plain = [], []
    for first in range(0, examples, SUBLANES):
        tile = gram_ref[first : first + SUBLANES] * scale
        plain.append(jnp.where(lane == row + first, tile + damp_ratio / fisher_dim, tile))
        system.append(jnp.where(lane < examples, plain[-1], jnp.take_along_axis(tile, source, axis=1)))
    solved = solve_first(system, plain, scratch)
    scores = solved[0]
    for i in range(1, len(solved)):
        scores = jnp.where(row == i, solved[i], scores)
    scores_ref[...] = scores[:per_dev, examples : examples + nq]


def gram_scores(tiles, query_index, per_dev, inner, axis):
    nq = query_index.shape[0]
    examples = len(tiles) * tiles[0].shape[0] // SUBLANES
    return pl.pallas_call(
        functools.partial(solve_kernel, per_dev, inner, axis),
        out_shape=jax.ShapeDtypeStruct((per_dev, nq), jnp.float32),
        in_specs=[pl.BlockSpec(memory_space=pltpu.VMEM)] * (len(tiles) + 1),
        out_specs=pl.BlockSpec(memory_space=pltpu.VMEM),
        scratch_shapes=[
            pltpu.VMEM((examples, LANES), jnp.float32),
            pltpu.VMEM((3 * examples, SUBLANES, LANES), jnp.float32),
        ],
        compiler_params=pltpu.CompilerParams(vmem_limit_bytes=8 * 2**20),
    )(*tiles, query_index.reshape(1, nq))


def gray(n):
    return n ^ (n >> 1)


def partner(n, inner):
    return n * inner ^ (n | n >> 1) & 1


def gather_xor(tiles, axis, size, inner):
    def swap(block, slot):
        return lax.ppermute(block, axis, [(i, i ^ slot) for i in range(size)])

    rows = sorted(range(1, size // inner), key=gray)
    column = jnp.concatenate([tiles] + [swap(tiles, partner(n, inner)) for n in rows], axis=0)
    return [column] + [swap(column, n) for n in sorted(range(1, inner), key=gray)]


def large_scores(tiles, query_index, per_dev, axis):
    sketches = tiles.reshape(-1, SUBLANES * LANES)
    gram = jnp.dot(sketches, sketches.T, precision=lax.Precision.HIGHEST)
    examples, fisher_dim = sketches.shape
    damping = damp_ratio * jnp.trace(gram) / fisher_dim
    factor = jnp.linalg.cholesky(gram + damping * jnp.eye(examples, dtype=jnp.float32))
    mine = lax.dynamic_slice_in_dim(gram, lax.axis_index(axis) * per_dev, per_dev, 0)
    half = lax.linalg.triangular_solve(factor, mine.T, left_side=True, lower=True)
    solved = lax.linalg.triangular_solve(factor, half, left_side=True, lower=True, transpose_a=True)
    selector = (query_index[:, None] == jnp.arange(examples, dtype=jnp.int32)[None, :]).astype(jnp.float32)
    return jnp.dot(selector, solved, precision=lax.Precision.HIGHEST).T


def local(activations, out_grads, project_in, project_out, lengths, query_index):
    per_dev = activations.shape[0]
    size = lax.axis_size("dp")
    tiles = sketch_rows(activations, out_grads, project_in, project_out, lengths)
    if size * per_dev + query_index.shape[0] <= LANES:
        inner = 4
        return gram_scores(gather_xor(tiles, "dp", size, inner), query_index, per_dev, inner, "dp")
    return large_scores(lax.all_gather(tiles, "dp", axis=0, tiled=True), query_index, per_dev, "dp")


def solution(mesh):
    return jax.shard_map(
        local,
        mesh=mesh,
        in_specs=(
            P(("groups", "dp"), None, None),
            P(("groups", "dp"), None, None),
            P(),
            P(),
            P(("groups", "dp")),
            P("groups"),
        ),
        out_specs=P(("groups", "dp"), None),
        check_vma=False,
    )
```

```python
import functools

import jax
import jax.numpy as jnp
from jax import lax
from jax.experimental import pallas as pl
from jax.experimental.pallas import tpu as pltpu
from jax.sharding import PartitionSpec as P

damp_ratio = 0.5
LANES = 128
SUBLANES = 8
NT = (((1,), (1,)), ((), ()))


def sketch_kernel(bounds, seq_len, act_hbm, out_hbm, pin_hbm, pout_hbm, lengths_hbm, sketch_ref, act, out, pin, pout, lengths_ref, sems, lengths_sem):
    rows, width = act.shape
    rank_dim = pin.shape[0]
    chunks = len(bounds) - 1
    lengths_copy = pltpu.make_async_copy(lengths_hbm, lengths_ref, lengths_sem)
    lengths_copy.start()
    copies = []
    for c in range(chunks):
        cols = pl.ds(bounds[c], bounds[c + 1] - bounds[c])
        copies.append(
            [
                pltpu.make_async_copy(src.at[:, cols], dst.at[:, cols], sems.at[n, c])
                for n, (src, dst) in enumerate(
                    ((pin_hbm, pin), (act_hbm, act), (pout_hbm, pout), (out_hbm, out))
                )
            ]
        )
        for copy in copies[-1]:
            copy.start()
    feat = [jnp.zeros((rows, rank_dim), jnp.float32)] * 2
    grad = [jnp.zeros((rank_dim, rows), jnp.float32)] * 2
    for c in range(chunks):
        middle = (bounds[c] + bounds[c + 1]) // 2
        for copy in copies[c]:
            copy.wait()
        for n, cols in enumerate((slice(bounds[c], middle), slice(middle, bounds[c + 1]))):
            feat[n] = feat[n] + lax.dot_general(act[:, cols], pin[:, cols], NT, preferred_element_type=jnp.float32)
            grad[n] = grad[n] + lax.dot_general(pout[:, cols], out[:, cols], NT, preferred_element_type=jnp.float32)
    feat, grad = feat[0] + feat[1], grad[0] + grad[1]
    lengths_copy.wait()
    count = rows // seq_len
    reps = LANES // rank_dim
    position = lax.broadcasted_iota(jnp.int32, (rows, LANES), 0)
    band = lax.broadcasted_iota(jnp.int32, (rows, LANES), 1) // rank_dim
    live = jnp.zeros((rows, LANES), jnp.bool_)
    for e in range(count):
        first = e * seq_len
        live = live | ((band == e) & (position >= first) & (position < first + lengths_ref[e]))
    outer = lax.dot_general(
        grad,
        jnp.where(live, jnp.concatenate([feat] * reps, axis=1), 0.0),
        (((1,), (0,)), ((), ())),
        precision=lax.Precision.HIGHEST,
        preferred_element_type=jnp.float32,
    )
    band = band[:SUBLANES]
    for e in range(count):
        entry = None
        for b in range(reps):
            part = outer[b * SUBLANES : (b + 1) * SUBLANES]
            if b != e:
                part = pltpu.roll(part, (b - e) * rank_dim % LANES, 1)
            entry = part if entry is None else jnp.where(band == b, part, entry)
        sketch_ref[e * SUBLANES : (e + 1) * SUBLANES] = entry


def sketch_rows(activations, out_grads, project_in, project_out, lengths):
    count, seq_len, width = activations.shape
    rank_dim = project_in.shape[1]
    rows = count * seq_len
    unit = width // 32
    bounds = [n * unit for n in (0, 2, 6, 10, 14, 18, 22, 26, 30, 32)]
    chunks = len(bounds) - 1
    return pl.pallas_call(
        functools.partial(sketch_kernel, bounds, seq_len),
        out_shape=jax.ShapeDtypeStruct((count * SUBLANES, LANES), jnp.float32),
        in_specs=[pl.BlockSpec(memory_space=pltpu.HBM)] * 5,
        out_specs=pl.BlockSpec(memory_space=pltpu.VMEM),
        scratch_shapes=[
            pltpu.VMEM((rows, width), jnp.bfloat16),
            pltpu.VMEM((rows, width), jnp.bfloat16),
            pltpu.VMEM((rank_dim, width), jnp.bfloat16),
            pltpu.VMEM((rank_dim, width), jnp.bfloat16),
            pltpu.SMEM((count,), jnp.int32),
            pltpu.SemaphoreType.DMA((4, chunks)),
            pltpu.SemaphoreType.DMA,
        ],
        compiler_params=pltpu.CompilerParams(vmem_limit_bytes=16 * 2**20),
    )(
        *(
            pltpu.with_memory_space_constraint(operand, pltpu.HBM)
            for operand in (
                activations.reshape(rows, width),
                out_grads.reshape(rows, width),
                project_in.T,
                project_out.T,
                lengths,
            )
        ),
    )


def solve_first(system, plain, scratch):
    step = 4

    def spread(column):
        return [jnp.broadcast_to(tile[:, column : column + 1], tile.shape) for tile in plain]

    stored = {}

    def row_of(tiles, number):
        tile = tiles[number // SUBLANES]
        if id(tile) not in stored:
            slot = len(stored)
            scratch[slot] = tile
            stored[id(tile)] = slot, tile
        slot, _ = stored[id(tile)]
        row = scratch[slot, number % SUBLANES : number % SUBLANES + 1]
        return jnp.broadcast_to(row, tile.shape)

    def factor(columns, first):
        p = {(i, j): row_of(columns[j], first + i) for j in range(step) for i in range(j + 1)}
        lower, inverse = {}, [None] * step
        for k in range(0, step, 2):
            a, b, c = p[k, k], p[k, k + 1], p[k + 1, k + 1]
            inverse[k] = pl.reciprocal(a)
            inverse[k + 1] = a * pl.reciprocal(a * c - b * b)
            for m in (k, k + 1):
                for i in range(m + 1, step):
                    lower[i, m] = p[m, i] * inverse[m]
                for i in range(m + 1, step):
                    for j in range(i, step):
                        p[i, j] = p[i, j] - lower[i, m] * p[m, j]
        return lower, inverse

    def forward(lower, parts):
        parts = list(parts)
        for k in range(step):
            for i in range(k + 1, step):
                parts[i] = [part - lower[i, k] * other for part, other in zip(parts[i], parts[k])]
        return parts

    def update(tiles, columns, lower, inverse, rows):
        rows = forward(lower, [[r] for r in rows])
        for column, row, scale in zip(columns, rows, inverse):
            done = row[0] * scale
            tiles = [tile - c * done for tile, c in zip(tiles, column)]
        return tiles

    count = len(system) * SUBLANES
    columns = [spread(j) for j in range(count - step, count)]
    for first in range(count - step, 0, -step):
        pivots = range(first, first + step)
        left = pl.cdiv(first, SUBLANES)
        lower, inverse = factor(columns, first)
        across = {j: [row_of(column, j) for column in columns] for j in range(first - step, first)}
        columns = forward(lower, [c[:left] for c in columns])
        following = [update(spread(j)[:left], columns, lower, inverse, across[j]) for j in across]
        system = plain = update(system[:left], columns, lower, inverse, [row_of(system, i) for i in pivots])
        columns = following
    lower, inverse = factor(columns, 0)
    rows = forward(lower, [[row_of(system, i)] for i in range(step)])
    solved = [row[0] * scale for row, scale in zip(rows, inverse)]
    for k in reversed(range(step)):
        for i in range(k):
            solved[i] = solved[i] - lower[k, i] * solved[k]
    return solved


def gram(x):
    high = x.astype(jnp.bfloat16)
    rest = x - high.astype(jnp.float32)
    middle = rest.astype(jnp.bfloat16)
    low = (rest - middle.astype(jnp.float32)).astype(jnp.bfloat16)
    parts = [high, middle, low]
    count = x.shape[0]
    terms = []
    for n, held in enumerate(parts):
        streamed = jnp.concatenate(parts[: len(parts) - n], axis=0)
        product = lax.dot_general(streamed, held, NT, preferred_element_type=jnp.float32)
        terms.append([product[k : k + count] for k in range(0, product.shape[0], count)])
    (hh, mh, lh), (hm, mm), (hl,) = terms
    return hh + ((mh + hm) + (lh + hl + mm))


def solve_kernel(per_dev, inner, axis, *refs):
    tiles, (query_ref, scores_ref, gram_ref, scratch) = refs[:-4], refs[-4:]
    nq = query_ref.shape[1]
    part = tiles[0].shape[0] // SUBLANES
    examples = len(tiles) * part
    outer = examples // (inner * per_dev)
    fisher_dim = SUBLANES * LANES
    gram_ref[...] = jnp.zeros(gram_ref.shape, jnp.float32)
    slot = (query_ref[...] // per_dev) ^ lax.axis_index(axis)
    n = slot // inner
    place = ((slot ^ partner(n, inner)) % inner * outer + gray(n)) * per_dev + query_ref[...] % per_dev
    rest = LANES - examples - nq
    place = jnp.concatenate(
        [jnp.zeros((1, examples), jnp.int32), place] + ([jnp.zeros((1, rest), jnp.int32)] if rest else []), axis=1
    )
    lane = lax.broadcasted_iota(jnp.int32, (SUBLANES, LANES), 1)
    source = jnp.where(lane < examples, lane, jnp.broadcast_to(place, lane.shape))
    sketches = jnp.concatenate(
        [
            jnp.concatenate([tile[pl.ds(s, part, stride=SUBLANES)] for tile in tiles], axis=0)
            for s in range(SUBLANES)
        ],
        axis=1,
    )
    squares = jnp.sum(jnp.sum(sketches * sketches, axis=0, keepdims=True), axis=1, keepdims=True)
    scale = jnp.broadcast_to(1.0 / squares, (SUBLANES, LANES))
    gram_ref[:, :examples] = gram(sketches)
    row = lax.broadcasted_iota(jnp.int32, (SUBLANES, LANES), 0)
    system, plain = [], []
    for first in range(0, examples, SUBLANES):
        tile = gram_ref[first : first + SUBLANES] * scale
        plain.append(jnp.where(lane == row + first, tile + damp_ratio / fisher_dim, tile))
        system.append(jnp.where(lane < examples, plain[-1], jnp.take_along_axis(tile, source, axis=1)))
    solved = solve_first(system, plain, scratch)
    scores = solved[0]
    for i in range(1, len(solved)):
        scores = jnp.where(row == i, solved[i], scores)
    scores_ref[...] = scores[:per_dev, examples : examples + nq]


def gram_scores(tiles, query_index, per_dev, inner, axis):
    nq = query_index.shape[0]
    examples = len(tiles) * tiles[0].shape[0] // SUBLANES
    return pl.pallas_call(
        functools.partial(solve_kernel, per_dev, inner, axis),
        out_shape=jax.ShapeDtypeStruct((per_dev, nq), jnp.float32),
        in_specs=[pl.BlockSpec(memory_space=pltpu.VMEM)] * (len(tiles) + 1),
        out_specs=pl.BlockSpec(memory_space=pltpu.VMEM),
        scratch_shapes=[
            pltpu.VMEM((examples, LANES), jnp.float32),
            pltpu.VMEM((3 * examples, SUBLANES, LANES), jnp.float32),
        ],
        compiler_params=pltpu.CompilerParams(vmem_limit_bytes=8 * 2**20),
    )(*tiles, query_index.reshape(1, nq))


def gray(n):
    return n ^ (n >> 1)


def partner(n, inner):
    return n * inner ^ (n | n >> 1) & 1


def gather_xor(tiles, axis, size, inner):
    def swap(block, slot):
        return lax.ppermute(block, axis, [(i, i ^ slot) for i in range(size)])

    rows = sorted(range(1, size // inner), key=gray)
    column = jnp.concatenate([tiles] + [swap(tiles, partner(n, inner)) for n in rows], axis=0)
    return [column] + [swap(column, n) for n in range(1, inner)]


def large_scores(tiles, query_index, per_dev, axis):
    sketches = tiles.reshape(-1, SUBLANES * LANES)
    gram = jnp.dot(sketches, sketches.T, precision=lax.Precision.HIGHEST)
    examples, fisher_dim = sketches.shape
    damping = damp_ratio * jnp.trace(gram) / fisher_dim
    factor = jnp.linalg.cholesky(gram + damping * jnp.eye(examples, dtype=jnp.float32))
    mine = lax.dynamic_slice_in_dim(gram, lax.axis_index(axis) * per_dev, per_dev, 0)
    half = lax.linalg.triangular_solve(factor, mine.T, left_side=True, lower=True)
    solved = lax.linalg.triangular_solve(factor, half, left_side=True, lower=True, transpose_a=True)
    selector = (query_index[:, None] == jnp.arange(examples, dtype=jnp.int32)[None, :]).astype(jnp.float32)
    return jnp.dot(selector, solved, precision=lax.Precision.HIGHEST).T


def local(activations, out_grads, project_in, project_out, lengths, query_index):
    per_dev = activations.shape[0]
    size = lax.axis_size("dp")
    tiles = sketch_rows(activations, out_grads, project_in, project_out, lengths)
    if size * per_dev + query_index.shape[0] <= LANES:
        inner = 4
        return gram_scores(gather_xor(tiles, "dp", size, inner), query_index, per_dev, inner, "dp")
    return large_scores(lax.all_gather(tiles, "dp", axis=0, tiled=True), query_index, per_dev, "dp")


def solution(mesh):
    return jax.shard_map(
        local,
        mesh=mesh,
        in_specs=(
            P(("groups", "dp"), None, None),
            P(("groups", "dp"), None, None),
            P(),
            P(),
            P(("groups", "dp")),
            P("groups"),
        ),
        out_specs=P(("groups", "dp"), None),
        check_vma=False,
    )
```
